32 devices in a mesh: fsdp: 16 (over z, y, x), replica: 2 (over core).
Axes of the slice: x: 2, y: 2, z: 4, core: 2. Of those that a mesh axis runs over, the one named last changes fastest.
Arguments:
- master: float32 [1024, 8192], P('fsdp', 'replica'), may hold values from -6 to 6
- moment_one: float32 [1024, 8192], P('fsdp', 'replica'), may hold values from -6 to 6
- moment_two: float32 [1024, 8192], P('fsdp', 'replica'), may hold values from 0.5 to 8
- gradients: float32 [2, 1024, 8192], P('replica', 'fsdp'), may hold values from -6 to 6
- new_row: int32 [1024], P('fsdp'), may hold values from 0 to 1023, as said below
Outputs:
- new_master: float32 [1024, 8192], P('fsdp', 'replica')
- new_moment_one: float32 [1024, 8192], P('fsdp', 'replica')
- new_moment_two: float32 [1024, 8192], P('fsdp', 'replica')
- params: bfloat16 [1024, 8192], P('fsdp')
- checksum: float32 [1024], P('fsdp')
The draws below stay inside these ranges and needn't reach their ends.
Inputs may be any that keep to these rules, and one draw needn't show every extreme that they name: new_row is a permutation; the 64 old rows of one fsdp index send at most 8 rows to the 64 new rows of any one fsdp index, and this most is reached.
All inputs are finite; a program needn't handle non-finite values.
Results may differ from the reference program's by a relative error of at most 0.0025.
Values may be sent and summed in bfloat16 or wider, within the bound.
No kernel may reach another device: no remote copies, remote signals or barrier semaphores. Data moves between devices by JAX's collectives and lax.ppermute only.
A program may use at most 128 MiB of HBM per device.

```python
import math
import jax
import jax.numpy as jnp
from jax import lax

D = 8192
ROWS_DEV = 64
ROWS = 1024
N_FSDP = 16
N_REPLICA = 2


def draw_new_row(key, part):
    key = jax.random.fold_in(key, 11)
    capacity = max(2, 2 * ROWS_DEV // N_FSDP)
    groups = ROWS_DEV // capacity
    key_shift, key_source, key_target = jax.random.split(key, 3)
    shuffled = jax.random.permutation(key_shift, N_FSDP).astype(jnp.int32)
    position = jnp.arange(N_FSDP, dtype=jnp.int32)
    score = jnp.where(shuffled == N_FSDP // 2, -2, jnp.where(shuffled == N_FSDP - 1, -1, position))
    shifts = shuffled[jnp.argsort(score, stable=True)][:groups]
    source_order = jax.vmap(lambda k: jax.random.permutation(k, ROWS_DEV))(jax.random.split(key_source, N_FSDP))
    target_order = jax.vmap(lambda k: jax.random.permutation(k, ROWS_DEV))(jax.random.split(key_target, N_FSDP))
    slot = jnp.arange(ROWS_DEV, dtype=jnp.int32)
    block = jnp.arange(N_FSDP, dtype=jnp.int32)[:, None]
    target = (block + shifts[slot // capacity][None, :]) % N_FSDP
    value = target * ROWS_DEV + target_order[target, slot[None, :]]
    where_row = block * ROWS_DEV + source_order
    result = jnp.zeros((ROWS,), jnp.int32).at[where_row.reshape(-1)].set(value.reshape(-1).astype(jnp.int32))
    return result


def raised(values, own_key, source, target, parts, factor):
    owner, partner = [(jnp.arange(values.shape[axis_at]) // (values.shape[axis_at] // parts)).reshape([-1 if axis == axis_at else 1 for axis in range(values.ndim)]) for axis_at in (source, target)]
    chosen = jax.random.permutation(own_key, parts)[partner]
    strong = (owner == chosen) | (owner == (partner + parts // 2) % parts)
    return jnp.where(strong, factor * values, values)


def shard_levels(key, extent, cuts, smallest, top_value):
    gain, own = 1.0, jax.random.fold_in(key, 6)
    for axis_at, parts in cuts:
        heights = jnp.exp(jax.random.uniform(jax.random.fold_in(own, axis_at), (parts,), jnp.float32, smallest / len(cuts), top_value / len(cuts)))
        gain = gain * jnp.repeat(heights, extent[axis_at] // parts).reshape([-1 if axis == axis_at else 1 for axis in range(len(extent))])
    return gain


def noise(stream_key, shape, width, bound, pieces=(), kind=jnp.bfloat16):
    values = jax.random.normal(stream_key, shape, jnp.float32) * width
    if len(pieces) > 0:
        values = shard_levels(stream_key, shape, pieces, -0.22, 0.18) * values
    return jnp.clip(values, min=-bound, max=bound).astype(kind)


def gaussian_with(stream_key, extent, deviation, most, pieces, heavy, kind=jnp.bfloat16):
    entries = deviation * jax.random.normal(stream_key, extent, jnp.float32)
    if pieces:
        entries = entries * shard_levels(stream_key, extent, pieces, -0.22, 0.18)
    return jnp.clip(raised(entries, jax.random.fold_in(stream_key, 3), *heavy), -most, most).astype(kind)


def setup_inputs(seed: int = 0) -> dict:
    seeds = jax.random.split(jax.random.key(seed), 6)
    master = noise(seeds[0], (ROWS, D), 1.0, 6.0, ((0, 16), (1, 2)), jnp.float32)
    moment_one = noise(seeds[1], (ROWS, D), 1.0, 6.0, ((0, 16), (1, 2)), jnp.float32)
    moment_two = jnp.clip(jnp.exp(math.log(8.0) - 2.7725887 * jax.random.uniform(seeds[2], (ROWS, D), jnp.float32) ** shard_levels(seeds[2], (ROWS, D), ((0, 16), (1, 2)), -0.2, 0.2)), 0.5, 8.0)
    gradients = gaussian_with(seeds[3], (N_REPLICA, ROWS, D), 1.0, 6.0, ((0, 2), (1, 16)), (0, 2, 2, 2.0), jnp.float32)
    new_row = draw_new_row(jax.random.fold_in(seeds[5], 71), 0)
    return {"master": master, "moment_one": moment_one, "moment_two": moment_two, "gradients": gradients, "new_row": new_row}


def reference(master, moment_one, moment_two, gradients, new_row):
    source = jnp.zeros((ROWS,), jnp.int32).at[new_row].set(jnp.arange(ROWS, dtype=jnp.int32))
    moved_master = jnp.take(master, source, axis=0)
    moved_one = jnp.take(moment_one, source, axis=0)
    moved_two = jnp.take(moment_two, source, axis=0)
    summed = jnp.take(lax.optimization_barrier(jnp.sum(gradients, axis=0)), source, axis=0)
    column = jnp.arange(D, dtype=jnp.int32)
    weights = 1.0 + (column % 7).astype(jnp.float32) / 7.0
    checksum = lax.optimization_barrier(jnp.sum(moved_master * weights[None, :], axis=1)) / jnp.sqrt(jnp.float32(D))
    new_one = 0.9 * moved_one + 0.1 * summed
    new_two = 0.95 * moved_two + 0.05 * summed * summed
    update = new_one / (1.0 - 0.9 ** 10) / (jnp.sqrt(new_two / (1.0 - 0.95 ** 10)) + 1e-08)
    new_master = moved_master - 0.05 * (update + 0.1 * moved_master)
    return (new_master, new_one, new_two, new_master.astype(jnp.bfloat16), checksum)
```

```python
import functools
import math

import jax
import jax.numpy as jnp
from jax import lax
from jax.experimental import pallas as pl
from jax.experimental.pallas import tpu as pltpu
from jax.sharding import PartitionSpec as P

LANES = 128
TILE_ROWS = 16
VMEM_BYTES = 40 * 1024 * 1024
F32 = jnp.float32
BF16 = jnp.bfloat16


def iota(shape, axis):
    return lax.broadcasted_iota(jnp.int32, shape, axis)


def prepare_kernel(rows, cap, lines, scale, rep_ref, new_row_ref, master_ref, pick_ref, meta_ref):
    width = master_ref.shape[1]
    slots, stacked = pick_ref.shape
    column = iota((1, width), 1) + rep_ref[0] * width
    weights = 1.0 + (column % 7).astype(F32) / 7.0
    part = jnp.sum(master_ref[...] * weights, axis=1, keepdims=True) * scale
    line = new_row_ref[...]
    target = line // rows
    at_row, at_lane = iota((rows, stacked), 0), iota((rows, stacked), 1)
    diagonal = at_row == at_lane
    as_column = jnp.sum(jnp.where(diagonal, line.astype(F32), 0.0), axis=1, keepdims=True).astype(jnp.int32)
    target_column = as_column // rows
    earlier = (target_column == target) & (at_row < at_lane % rows)
    rank = jnp.sum(jnp.where(earlier, 1.0, 0.0), axis=0, keepdims=True).astype(jnp.int32)
    slot = target * lines + (iota((1, stacked), 1) // rows) * cap + rank
    pick = jnp.where(iota((slots, stacked), 0) == slot, 1.0, 0.0).astype(BF16)
    pick_ref[...] = pick
    offset = (as_column - target_column * rows + 1).astype(F32)
    high = part.astype(BF16).astype(F32)
    middle = (part - high).astype(BF16).astype(F32)
    low = part - high - middle
    lane = iota((rows, LANES), 1)
    meta = jnp.where(
        lane == 0, offset, jnp.where(lane == 1, high, jnp.where(lane == 2, middle, jnp.where(lane == 3, low, 0.0)))
    ).astype(BF16)
    meta = jnp.concatenate([meta] * (stacked // rows), axis=0)
    meta_ref[...] = jnp.dot(pick, meta, preferred_element_type=F32).astype(BF16)


def update_kernel(split, cb, body_cols, rep_ref, pick_ref, meta_ref, master_ref, one_ref, two_ref, own_ref, *rest):
    received, (master_out, moments_out) = rest[:-2], rest[-2:]
    j = pl.program_id(0)
    pieces = ([], [], [])
    for h in range(split):
        cols = slice(h * cb, (h + 1) * cb)
        summed = own_ref[:, cols]
        for other in received:
            summed = summed + other[:, cols].astype(F32)
        moved = master_ref[:, cols]
        new_one = 0.9 * one_ref[:, cols] + 0.1 * summed
        new_two = 0.95 * two_ref[:, cols] + 0.05 * summed * summed
        update = new_one / (1.0 - 0.9**10) / (jnp.sqrt(new_two / (1.0 - 0.95**10)) + 1e-08)
        new_master = moved - 0.05 * (update + 0.1 * moved)
        for piece, value in zip(pieces, (new_master, new_one, new_two)):
            piece.append(value.astype(BF16))
    pick = pick_ref[...]
    packed = [jnp.dot(pick, jnp.concatenate(piece, axis=0), preferred_element_type=F32).astype(BF16) for piece in pieces]
    master_out[:, pl.ds(pl.multiple_of(j * cb, LANES), cb)] = packed[0]
    moments_out[:, :cb] = packed[1]
    moments_out[:, cb:] = packed[2]

    @pl.when(j == 0)
    def _():
        master_out[:, body_cols:] = meta_ref[...]


def placing(meta, rows, cap, lines, stacked):
    shape = (meta.shape[0], stacked)
    offset = meta[:, :1].astype(F32).astype(jnp.int32)
    piece = (iota((meta.shape[0], 1), 0) % lines) // cap
    wanted = jnp.where(offset > 0, offset - 1 + piece * rows, -1)
    return jnp.where(iota(shape, 1) == wanted, 1.0, 0.0).astype(BF16)


def placed(place, values):
    return lax.dot_general(place, values, (((0,), (0,)), ((), ())), preferred_element_type=F32)


def master_kernel(rows, cap, lines, cb, blocks, rep_ref, *refs):
    received, (new_master, params, checksum) = refs[:-3], refs[-3:]
    copies = len(received)
    split = lines // cap
    body_cols = blocks * cb
    width = split * body_cols
    place = placing(received[0][:, body_cols:], rows, cap, lines, split * rows)
    total = jnp.zeros((1, rows), F32)
    for k, ref in enumerate(received):
        replica = lax.rem(rep_ref[0] + copies - k, copies)
        base = pl.multiple_of(replica * width, LANES)
        for j in range(blocks):
            rows_out = placed(place, ref[:, j * cb : (j + 1) * cb])
            for h in range(split):
                values = rows_out[h * rows : (h + 1) * rows]
                at = (j * split + h) * cb
                if k == 0:
                    new_master[:, at : at + cb] = values
                params[:, pl.ds(base + at, cb)] = values.astype(BF16)
        sums = placed(ref[:, body_cols:], place)
        total = total + (sums[1:2, :rows] + sums[2:3, :rows] + sums[3:4, :rows])
    checksum[...] = total


def moments_kernel(rows, cap, lines, cb, meta_ref, moments_ref, one_out, two_out):
    split = lines // cap
    place = placing(meta_ref[...], rows, cap, lines, split * rows)
    for at, out in ((0, one_out), (cb, two_out)):
        rows_out = placed(place, moments_ref[:, at : at + cb])
        for h in range(split):
            out[:, h * cb : (h + 1) * cb] = rows_out[h * rows : (h + 1) * rows]


def whole(shape):
    return pl.BlockSpec(shape, lambda *_: (0,) * len(shape))


def shards(master, moment_one, moment_two, gradients, new_row):
    rows, width = master.shape
    peers = lax.axis_size("fsdp")
    copies = lax.axis_size("replica")
    cap = max(2, 2 * rows // peers)
    split = max(1, TILE_ROWS // cap)
    lines = cap * split
    slots = peers * lines
    stacked = split * rows
    body_cols = width // split
    cb = math.gcd(body_cols, 512)
    blocks = body_cols // cb
    span = split * cb
    params_compiler = pltpu.CompilerParams(vmem_limit_bytes=VMEM_BYTES)
    smem = pl.BlockSpec(memory_space=pltpu.SMEM)
    vmem = pl.BlockSpec(memory_space=pltpu.VMEM)

    replica = lax.axis_index("replica").astype(jnp.int32)
    rep = replica.reshape(1)
    full = gradients[0]
    received = []
    for k in range(1, copies):
        other = lax.rem(replica + k, copies)
        part = lax.dynamic_slice(full, (0, other * width), (rows, width)).astype(BF16)
        received.append(lax.ppermute(part, "replica", [(i, (i + k) % copies) for i in range(copies)]))

    pick, meta = pl.pallas_call(
        functools.partial(prepare_kernel, rows, cap, lines, 1.0 / math.sqrt(width * copies)),
        out_shape=(jax.ShapeDtypeStruct((slots, stacked), BF16), jax.ShapeDtypeStruct((slots, LANES), BF16)),
        in_specs=[smem, vmem, vmem],
        out_specs=(vmem, vmem),
        compiler_params=params_compiler,
        cost_estimate=pl.CostEstimate(flops=4 * rows * width, bytes_accessed=4 * rows * width, transcendentals=0),
        name="prepare",
    )(rep, jnp.tile(new_row, split).reshape(1, stacked), master)

    block = pl.BlockSpec((rows, span), lambda j, rep: (0, j))
    send_master, send_moments = pl.pallas_call(
        functools.partial(update_kernel, split, cb, body_cols),
        out_shape=(
            jax.ShapeDtypeStruct((slots, body_cols + LANES), BF16),
            jax.ShapeDtypeStruct((slots, 2 * body_cols), BF16),
        ),
        grid_spec=pltpu.PrefetchScalarGridSpec(
            num_scalar_prefetch=1,
            grid=(blocks,),
            in_specs=[
                whole((slots, stacked)),
                whole((slots, LANES)),
                block,
                block,
                block,
                pl.BlockSpec((rows, span), lambda j, rep: (0, rep[0] * blocks + j)),
            ]
            + [block] * (copies - 1),
            out_specs=(
                whole((slots, body_cols + LANES)),
                pl.BlockSpec((slots, 2 * cb), lambda j, rep: (0, j)),
            ),
        ),
        compiler_params=params_compiler,
        cost_estimate=pl.CostEstimate(
            flops=6 * slots * stacked * body_cols, bytes_accessed=24 * rows * width, transcendentals=rows * width
        ),
        name="update",
    )(rep, pick, meta, master, moment_one, moment_two, full, *received)

    got_master = lax.all_to_all(send_master, "fsdp", split_axis=0, concat_axis=0, tiled=True)
    got_moments = lax.all_to_all(send_moments, "fsdp", split_axis=0, concat_axis=0, tiled=True)

    got = [got_master] + [
        lax.ppermute(got_master, "replica", [(i, (i + k) % copies) for i in range(copies)]) for k in range(1, copies)
    ]
    new_master, params, checksum = pl.pallas_call(
        functools.partial(master_kernel, rows, cap, lines, cb, blocks),
        out_shape=(
            jax.ShapeDtypeStruct((rows, width), F32),
            jax.ShapeDtypeStruct((rows, width * copies), BF16),
            jax.ShapeDtypeStruct((1, rows), F32),
        ),
        in_specs=[smem] + [vmem] * copies,
        out_specs=(vmem, vmem, vmem),
        compiler_params=params_compiler,
        cost_estimate=pl.CostEstimate(
            flops=2 * copies * slots * stacked * body_cols, bytes_accessed=12 * rows * width, transcendentals=0
        ),
        name="place_master",
    )(rep, *got)

    new_one, new_two = pl.pallas_call(
        functools.partial(moments_kernel, rows, cap, lines, cb),
        out_shape=(jax.ShapeDtypeStruct((rows, width), F32), jax.ShapeDtypeStruct((rows, width), F32)),
        grid=(blocks,),
        in_specs=[
            pl.BlockSpec((slots, LANES), lambda j: (0, body_cols // LANES)),
            pl.BlockSpec((slots, 2 * cb), lambda j: (0, j)),
        ],
        out_specs=(pl.BlockSpec((rows, span), lambda j: (0, j)), pl.BlockSpec((rows, span), lambda j: (0, j))),
        compiler_params=params_compiler,
        cost_estimate=pl.CostEstimate(
            flops=4 * slots * stacked * body_cols, bytes_accessed=16 * rows * width, transcendentals=0
        ),
        name="place_moments",
    )(got_master, got_moments)
    return (new_master, new_one, new_two, params, checksum.reshape(rows))


def solution(mesh):
    return jax.shard_map(
        shards,
        mesh=mesh,
        in_specs=(
            P("fsdp", "replica"),
            P("fsdp", "replica"),
            P("fsdp", "replica"),
            P("replica", "fsdp", None),
            P("fsdp"),
        ),
        out_specs=(
            P("fsdp", "replica"),
            P("fsdp", "replica"),
            P("fsdp", "replica"),
            P("fsdp", None),
            P("fsdp"),
        ),
        check_vma=False,
    )
```

```python
import functools
import math

import jax
import jax.numpy as jnp
from jax import lax
from jax.experimental import pallas as pl
from jax.experimental.pallas import tpu as pltpu
from jax.sharding import PartitionSpec as P

LANES = 128
TILE_ROWS = 16
VMEM_BYTES = 48 * 1024 * 1024
MOST_SHIFT_PEERS = 16
GROUP = 5
F32 = jnp.float32
BF16 = jnp.bfloat16


def iota(shape, axis):
    return lax.broadcasted_iota(jnp.int32, shape, axis)


class Sizes:
    def __init__(self, rows, width, peers, copies):
        self.rows, self.width, self.peers, self.copies = rows, width, peers, copies
        self.cap = max(2, 2 * rows // peers)
        self.split = max(1, TILE_ROWS // self.cap)
        self.lines = self.cap * self.split
        self.slots = peers * self.lines
        self.stacked = self.split * rows
        self.body = width // self.split
        self.cb = math.gcd(self.body, 512)
        self.blocks = self.body // self.cb
        self.span = self.split * self.cb
        self.sub = math.gcd(self.cb, 256)
        self.payload = 3 * self.body + LANES


def prepare_kernel(z, origin_ref, new_row_ref, pick_ref, info_ref, mask_ref):
    line = new_row_ref[...]
    at_row, at_lane = iota((z.rows, z.rows), 0), iota((z.rows, z.rows), 1)
    column = jnp.sum(jnp.where(at_row == at_lane, line.astype(F32), 0.0), axis=1, keepdims=True).astype(jnp.int32)
    target, target_column = line // z.rows, column // z.rows
    earlier = (target_column == target) & (at_row < at_lane)
    rank = jnp.sum(jnp.where(earlier, 1.0, 0.0), axis=0, keepdims=True).astype(jnp.int32)
    shift = lax.rem(target - origin_ref[0] + z.peers, z.peers)
    shift_column = lax.rem(target_column - origin_ref[0] + z.peers, z.peers)
    for h in range(z.split):
        slot = shift * z.lines + h * z.cap + rank
        pick_ref[h] = jnp.where(iota((z.slots, z.rows), 0) == slot, 1.0, 0.0).astype(BF16)
    lane = iota((z.rows, LANES), 1)
    info_ref[...] = jnp.where(lane == 0, (column - target_column * z.rows + 1).astype(F32), 0.0)
    used = jnp.where(lane == shift_column, 1.0, 0.0)
    mask_ref[...] = jnp.max(used, axis=0, keepdims=True).astype(jnp.int32)


def update_kernel(z, rep_ref, pick_ref, info_ref, master_hbm, one_hbm, two_hbm, full_hbm, *refs):
    received, refs = refs[: z.copies - 1], refs[z.copies - 1 :]
    outs, (master_buf, one_buf, two_buf, own_buf, rows_buf, sems) = refs[: z.peers], refs[z.peers :]
    base = rep_ref[0] * z.width

    def copies_of(j):
        at = pl.ds(j * z.span, z.span)
        own = pl.ds(pl.multiple_of(base + j * z.span, LANES), z.span)
        pairs = (
            (full_hbm.at[:, own], own_buf),
            (one_hbm.at[:, at], one_buf),
            (two_hbm.at[:, at], two_buf),
            (master_hbm.at[:, at], master_buf),
        )
        return [pltpu.make_async_copy(src, dst.at[:, at], sems.at[i, j]) for i, (src, dst) in enumerate(pairs)]

    for j in range(z.blocks):
        for copy in copies_of(j):
            copy.start()
    pick = jnp.concatenate([pick_ref[h] for h in range(z.split)], axis=1)
    part = jnp.zeros((z.rows, LANES), F32)
    for j in range(z.blocks):
        for copy in copies_of(j):
            copy.wait()
        for h in range(z.split):
            for c in range(0, z.cb, z.sub):
                at = j * z.span + h * z.cb + c
                cols = slice(at, at + z.sub)
                summed = own_buf[:, cols]
                for other in received:
                    summed = summed + other[:, cols].astype(F32)
                moved = master_buf[:, cols]
                weights = 1.0 + ((iota((1, z.sub), 1) + (base + at)) % 7).astype(F32) / 7.0
                weighted = moved * weights
                for lane in range(0, z.sub, LANES):
                    part = part + weighted[:, lane : lane + LANES]
                new_one = 0.9 * one_buf[:, cols] + 0.1 * summed
                new_two = 0.95 * two_buf[:, cols] + 0.05 * summed * summed
                update = new_one / (1.0 - 0.9**10) / (jnp.sqrt(new_two / (1.0 - 0.95**10)) + 1e-08)
                new_master = moved - 0.05 * (update + 0.1 * moved)
                for i, value in enumerate((new_master, new_one, new_two)):
                    rows_buf[h * z.rows : (h + 1) * z.rows, i * z.cb + c : i * z.cb + c + z.sub] = value.astype(BF16)
        for i in range(3):
            packed = jnp.dot(pick, rows_buf[:, i * z.cb : (i + 1) * z.cb], preferred_element_type=F32).astype(BF16)
            at = i * z.body + j * z.cb
            for s, out in enumerate(outs):
                out[:, at : at + z.cb] = packed[s * z.lines : (s + 1) * z.lines]
    total = jnp.sum(part, axis=1, keepdims=True) * (1.0 / math.sqrt(z.width * z.copies))
    high = total.astype(BF16).astype(F32)
    middle = (total - high).astype(BF16).astype(F32)
    low = total - high - middle
    lane = iota((z.rows, LANES), 1)
    meta = jnp.where(lane == 1, high, jnp.where(lane == 2, middle, jnp.where(lane == 3, low, info_ref[...])))
    meta = jnp.concatenate([meta.astype(BF16)] * z.split, axis=0)
    packed = jnp.dot(pick, meta, preferred_element_type=F32).astype(BF16)
    for s, out in enumerate(outs):
        out[:, 3 * z.body :] = packed[s * z.lines : (s + 1) * z.lines]


def gathered(refs, cols):
    return jnp.concatenate([ref[:, cols] for ref in refs], axis=0)


def placing(z, meta):
    offset = meta[:, :1].astype(F32).astype(jnp.int32)
    piece = lax.rem(iota((z.slots, 1), 0), z.lines) // z.cap
    wanted = jnp.where(offset > 0, offset - 1 + piece * z.rows, -1)
    return jnp.where(iota((z.slots, z.stacked), 1) == wanted, 1.0, 0.0).astype(BF16)


def placed(place, values):
    return lax.dot_general(place, values, (((0,), (0,)), ((), ())), preferred_element_type=F32)


def master_kernel(z, rep_ref, *refs):
    got, (new_master, params, half, master_buf, sems) = refs[: z.peers], refs[z.peers :]
    meta = gathered(got, slice(3 * z.body, 3 * z.body + LANES))
    place = placing(z, meta)
    copies = []
    for j in range(z.blocks):
        rows_out = placed(place, gathered(got, slice(j * z.cb, (j + 1) * z.cb)))
        for h in range(z.split):
            values = rows_out[h * z.rows : (h + 1) * z.rows]
            at = j * z.span + h * z.cb
            master_buf[:, at : at + z.cb] = values
            half[:, at : at + z.cb] = values.astype(BF16)
        at = pl.ds(j * z.span, z.span)
        there = pl.ds(pl.multiple_of(rep_ref[0] * z.width + j * z.span, LANES), z.span)
        copies.append(pltpu.make_async_copy(master_buf.at[:, at], new_master.at[:, at], sems.at[0, j]))
        copies.append(pltpu.make_async_copy(half.at[:, at], params.at[:, there], sems.at[1, j]))
        copies[-2].start()
        copies[-1].start()
    half[:, z.width :] = placed(place, meta)[: z.rows].astype(BF16)
    for copy in copies:
        copy.wait()


def moments_kernel(z, *refs):
    got, (one_out, two_out, one_buf, two_buf, sems) = refs[: z.peers], refs[z.peers :]
    place = placing(z, gathered(got, slice(3 * z.body, 3 * z.body + LANES)))
    copies = []
    for i, (out, buf) in enumerate(((one_out, one_buf), (two_out, two_buf))):
        for j in range(z.blocks):
            at = (i + 1) * z.body + j * z.cb
            rows_out = placed(place, gathered(got, slice(at, at + z.cb)))
            for h in range(z.split):
                col = j * z.span + h * z.cb
                buf[:, col : col + z.cb] = rows_out[h * z.rows : (h + 1) * z.rows]
            cols = pl.ds(j * z.span, z.span)
            copies.append(pltpu.make_async_copy(buf.at[:, cols], out.at[:, cols], sems.at[i, j]))
            copies[-1].start()
    for copy in copies:
        copy.wait()


def finish_kernel(z, rep_ref, half, *refs):
    others, (_, params, checksum, sems) = refs[: z.copies - 1], refs[z.copies - 1 :]
    copies = []
    for k, other in enumerate(others):
        replica = lax.rem(rep_ref[0] + z.copies - (k + 1), z.copies)
        there = pl.ds(pl.multiple_of(replica * z.width, LANES), z.width)
        copies.append(pltpu.make_async_copy(other.at[:, : z.width], params.at[:, there], sems.at[k]))
        copies[-1].start()
    sums = half[:, z.width :].astype(F32)
    for other in others:
        sums = sums + other[:, z.width :].astype(F32)
    lane = iota((z.rows, LANES), 1)
    column = jnp.sum(jnp.where((lane >= 1) & (lane <= 3), sums, 0.0), axis=1, keepdims=True)
    diagonal = iota((z.rows, z.rows), 0) == iota((z.rows, z.rows), 1)
    checksum[...] = jnp.sum(jnp.where(diagonal, column, 0.0), axis=0, keepdims=True)
    for copy in copies:
        copy.wait()


def shifted(value, axis, k, count):
    return lax.ppermute(value, axis, [(i, (i + k) % count) for i in range(count)])


def send_used(peers, group, mask, chunks):
    return tuple(
        shifted(chunk, "fsdp", s, peers) if mask >> i & 1 else chunk for i, (s, chunk) in enumerate(zip(group, chunks))
    )


def move(z, chunks, mask):
    if z.peers > MOST_SHIFT_PEERS:
        got = lax.all_to_all(jnp.concatenate(chunks, axis=0), "fsdp", split_axis=0, concat_axis=0, tiled=True)
        return [got[s * z.lines : (s + 1) * z.lines] for s in range(z.peers)]
    got = list(chunks)
    groups = -(-(z.peers - 1) // GROUP)
    for g in range(groups):
        group = list(range(1 + g, z.peers, groups))
        bits = sum(mask[0, s] << i for i, s in enumerate(group))
        branches = [
            lambda *values, used=used: send_used(z.peers, group, used, values) for used in range(1 << len(group))
        ]
        for s, value in zip(group, lax.switch(bits, branches, *[chunks[s] for s in group])):
            got[s] = value
    return got


def shards(master, moment_one, moment_two, gradients, new_row):
    rows, width = master.shape
    peers, copies = lax.axis_size("fsdp"), lax.axis_size("replica")
    z = Sizes(rows, width, peers, copies)
    compiler_params = pltpu.CompilerParams(vmem_limit_bytes=VMEM_BYTES)
    smem = pl.BlockSpec(memory_space=pltpu.SMEM)
    vmem = pl.BlockSpec(memory_space=pltpu.VMEM)
    hbm = pl.BlockSpec(memory_space=pl.ANY)
    dma = pltpu.SemaphoreType.DMA

    replica = lax.axis_index("replica").astype(jnp.int32)
    rep = replica.reshape(1)
    by_shift = peers <= MOST_SHIFT_PEERS
    origin = (lax.axis_index("fsdp").astype(jnp.int32) if by_shift else jnp.int32(0)).reshape(1)
    full = gradients[0]

    pick, info, used = pl.pallas_call(
        functools.partial(prepare_kernel, z),
        out_shape=(
            jax.ShapeDtypeStruct((z.split, z.slots, rows), BF16),
            jax.ShapeDtypeStruct((rows, LANES), F32),
            jax.ShapeDtypeStruct((1, LANES), jnp.int32),
        ),
        in_specs=[smem, vmem],
        out_specs=(vmem, vmem, vmem),
        compiler_params=compiler_params,
        name="prepare",
    )(origin, new_row.reshape(1, rows))

    received = []
    for k in range(1, copies):
        other = lax.rem(replica + k, copies)
        part = lax.dynamic_slice(full, (0, other * width), (rows, width)).astype(BF16)
        received.append(shifted(part, "replica", k, copies))
    mask = lax.pmax(used, "fsdp") if by_shift else None

    chunks = pl.pallas_call(
        functools.partial(update_kernel, z),
        out_shape=[jax.ShapeDtypeStruct((z.lines, z.payload), BF16)] * peers,
        in_specs=[smem, vmem, vmem, hbm, hbm, hbm, hbm] + [vmem] * (copies - 1),
        out_specs=[vmem] * peers,
        scratch_shapes=[pltpu.VMEM((rows, width), F32)] * 4
        + [pltpu.VMEM((z.stacked, 3 * z.cb), BF16), dma((4, z.blocks))],
        compiler_params=compiler_params,
        cost_estimate=pl.CostEstimate(
            flops=6 * z.slots * z.stacked * z.body, bytes_accessed=24 * rows * width, transcendentals=rows * width
        ),
        name="update",
    )(rep, pick, info, master, moment_one, moment_two, full, *received)

    got = move(z, chunks, mask)

    new_master, params, half = pl.pallas_call(
        functools.partial(master_kernel, z),
        out_shape=(
            jax.ShapeDtypeStruct((rows, width), F32),
            jax.ShapeDtypeStruct((rows, width * copies), BF16),
            jax.ShapeDtypeStruct((rows, width + LANES), BF16),
        ),
        in_specs=[smem] + [vmem] * peers,
        out_specs=(hbm, hbm, vmem),
        scratch_shapes=[pltpu.VMEM((rows, width), F32), dma((2, z.blocks))],
        compiler_params=compiler_params,
        cost_estimate=pl.CostEstimate(
            flops=2 * z.slots * z.stacked * z.body, bytes_accessed=10 * rows * width, transcendentals=0
        ),
        name="place_master",
    )(rep, *got)
    others = [shifted(half, "replica", k, copies) for k in range(1, copies)]

    new_one, new_two = pl.pallas_call(
        functools.partial(moments_kernel, z),
        out_shape=(jax.ShapeDtypeStruct((rows, width), F32), jax.ShapeDtypeStruct((rows, width), F32)),
        in_specs=[vmem] * peers,
        out_specs=(hbm, hbm),
        scratch_shapes=[pltpu.VMEM((rows, width), F32)] * 2 + [dma((2, z.blocks))],
        compiler_params=compiler_params,
        cost_estimate=pl.CostEstimate(
            flops=4 * z.slots * z.stacked * z.body, bytes_accessed=16 * rows * width, transcendentals=0
        ),
        name="place_moments",
    )(*got)

    params, checksum = pl.pallas_call(
        functools.partial(finish_kernel, z),
        out_shape=(jax.ShapeDtypeStruct((rows, width * copies), BF16), jax.ShapeDtypeStruct((1, rows), F32)),
        in_specs=[smem, vmem] + [vmem] * (copies - 1) + [hbm],
        out_specs=(hbm, vmem),
        scratch_shapes=[dma((max(1, copies - 1),))],
        input_output_aliases={copies + 1: 0},
        compiler_params=compiler_params,
        cost_estimate=pl.CostEstimate(flops=0, bytes_accessed=4 * rows * width, transcendentals=0),
        name="finish",
    )(rep, half, *others, params)
    return (new_master, new_one, new_two, params, checksum.reshape(rows))


def solution(mesh):
    return jax.shard_map(
        shards,
        mesh=mesh,
        in_specs=(
            P("fsdp", "replica"),
            P("fsdp", "replica"),
            P("fsdp", "replica"),
            P("replica", "fsdp", None),
            P("fsdp"),
        ),
        out_specs=(
            P("fsdp", "replica"),
            P("fsdp", "replica"),
            P("fsdp", "replica"),
            P("fsdp", None),
            P("fsdp"),
        ),
        check_vma=False,
    )
```

```python
import functools
import math

import jax
import jax.numpy as jnp
from jax import lax
from jax.experimental import pallas as pl
from jax.experimental.pallas import tpu as pltpu
from jax.sharding import PartitionSpec as P

LANES = 128
TILE_ROWS = 16
VMEM_BYTES = 48 * 1024 * 1024
MOST_SHIFT_PEERS = 16
GROUP = 5
F32 = jnp.float32
BF16 = jnp.bfloat16


def iota(shape, axis):
    return lax.broadcasted_iota(jnp.int32, shape, axis)


class Sizes:
    def __init__(self, rows, width, peers, copies):
        self.rows, self.width, self.peers, self.copies = rows, width, peers, copies
        self.cap = max(2, 2 * rows // peers)
        self.split = max(1, TILE_ROWS // self.cap)
        self.lines = self.cap * self.split
        self.slots = peers * self.lines
        self.stacked = self.split * rows
        self.body = width // self.split
        self.cb = math.gcd(self.body, 512)
        self.blocks = self.body // self.cb
        self.span = self.split * self.cb
        self.sub = math.gcd(self.cb, 256)
        self.payload = 3 * self.body + LANES


def prepare_kernel(z, origin_ref, new_row_ref, pick_ref, info_ref, mask_ref):
    line = new_row_ref[...]
    at_row, at_lane = iota((z.rows, z.rows), 0), iota((z.rows, z.rows), 1)
    column = jnp.sum(jnp.where(at_row == at_lane, line.astype(F32), 0.0), axis=1, keepdims=True).astype(jnp.int32)
    target, target_column = line // z.rows, column // z.rows
    earlier = (target_column == target) & (at_row < at_lane)
    rank = jnp.sum(jnp.where(earlier, 1.0, 0.0), axis=0, keepdims=True).astype(jnp.int32)
    shift = lax.rem(target - origin_ref[0] + z.peers, z.peers)
    shift_column = lax.rem(target_column - origin_ref[0] + z.peers, z.peers)
    for h in range(z.split):
        slot = shift * z.lines + h * z.cap + rank
        pick_ref[h] = jnp.where(iota((z.slots, z.rows), 0) == slot, 1.0, 0.0).astype(BF16)
    lane = iota((z.rows, LANES), 1)
    info_ref[...] = jnp.where(lane == 0, (column - target_column * z.rows + 1).astype(F32), 0.0)
    used = jnp.where(lane == shift_column, 1.0, 0.0)
    mask_ref[...] = jnp.max(used, axis=0, keepdims=True).astype(jnp.int32)


def agree_kernel(*refs):
    total = refs[0][...]
    for ref in refs[1:-1]:
        total = jnp.maximum(total, ref[...])
    refs[-1][...] = total


def choose_kernel(groups, *refs):
    masks, outs = refs[: -len(groups)], refs[-len(groups) :]
    total = masks[0][...]
    for ref in masks[1:]:
        total = jnp.maximum(total, ref[...])
    lane = iota(total.shape, 1)
    for group, out in zip(groups, outs):
        value = jnp.zeros(total.shape, jnp.int32)
        for i, s in enumerate(group):
            value = value + jnp.where(lane == s, total << i, 0)
        out[0] = jnp.sum(value.astype(F32)).astype(jnp.int32)


def load_kernel(z, rep_ref, info_ref, master_hbm, one_hbm, two_hbm, full_hbm, master, one, two, own, meta_ref, sems):
    base = rep_ref[0] * z.width
    step = z.width // z.blocks
    copies = []
    for j in range(z.blocks):
        at = pl.ds(j * step, step)
        mine = pl.ds(pl.multiple_of(base + j * step, LANES), step)
        copies.append(
            [
                pltpu.make_async_copy(master_hbm.at[:, at], master.at[:, at], sems.at[0, j]),
                pltpu.make_async_copy(one_hbm.at[:, at], one.at[:, at], sems.at[1, j]),
                pltpu.make_async_copy(two_hbm.at[:, at], two.at[:, at], sems.at[2, j]),
                pltpu.make_async_copy(full_hbm.at[:, mine], own.at[:, at], sems.at[3, j]),
            ]
        )
    for i in range(4):
        for j in range(z.blocks):
            copies[j][i].start()
    part = jnp.zeros((z.rows, LANES), F32)
    for j in range(z.blocks):
        copies[j][0].wait()
        for at in range(j * step, (j + 1) * step, LANES):
            weights = 1.0 + ((iota((1, LANES), 1) + (base + at)) % 7).astype(F32) / 7.0
            part = part + master[:, at : at + LANES] * weights
    total = jnp.sum(part, axis=1, keepdims=True) * (1.0 / math.sqrt(z.width * z.copies))
    high = total.astype(BF16).astype(F32)
    middle = (total - high).astype(BF16).astype(F32)
    low = total - high - middle
    lane = iota((z.rows, LANES), 1)
    meta = jnp.where(lane == 1, high, jnp.where(lane == 2, middle, jnp.where(lane == 3, low, info_ref[...])))
    meta_ref[...] = meta.astype(BF16)
    for j in range(z.blocks):
        for i in range(1, 4):
            copies[j][i].wait()


def update_kernel(z, pick_ref, meta_ref, master, one, two, own, *refs):
    received, refs = refs[: z.copies - 1], refs[z.copies - 1 :]
    outs, rows_buf = refs[: z.peers], refs[z.peers]
    pick = jnp.concatenate([pick_ref[h] for h in range(z.split)], axis=1)
    for j in range(z.blocks):
        for h in range(z.split):
            for c in range(0, z.cb, z.sub):
                at = j * z.span + h * z.cb + c
                cols = slice(at, at + z.sub)
                summed = own[:, cols]
                for other in received:
                    summed = summed + other[:, cols].astype(F32)
                moved = master[:, cols]
                new_one = 0.9 * one[:, cols] + 0.1 * summed
                new_two = 0.95 * two[:, cols] + 0.05 * summed * summed
                update = new_one * (1.0 / (1.0 - 0.9**10)) / (jnp.sqrt(new_two * (1.0 / (1.0 - 0.95**10))) + 1e-08)
                new_master = moved - 0.05 * (update + 0.1 * moved)
                for i, value in enumerate((new_master, new_one, new_two)):
                    to = i * z.body + j * z.cb + c
                    rows_buf[h * z.rows : (h + 1) * z.rows, to : to + z.sub] = value.astype(BF16)
        for i in range(3):
            at = i * z.body + j * z.cb
            packed = jnp.dot(pick, rows_buf[:, at : at + z.cb], preferred_element_type=F32).astype(BF16)
            for s, out in enumerate(outs):
                out[:, at : at + z.cb] = packed[s * z.lines : (s + 1) * z.lines]
    meta = jnp.concatenate([meta_ref[...]] * z.split, axis=0)
    packed = jnp.dot(pick, meta, preferred_element_type=F32).astype(BF16)
    for s, out in enumerate(outs):
        out[:, 3 * z.body :] = packed[s * z.lines : (s + 1) * z.lines]


def gathered(refs, cols):
    return jnp.concatenate([ref[:, cols] for ref in refs], axis=0)


def placing(z, meta):
    offset = meta[:, :1].astype(F32).astype(jnp.int32)
    piece = lax.rem(iota((z.slots, 1), 0), z.lines) // z.cap
    wanted = jnp.where(offset > 0, offset - 1 + piece * z.rows, -1)
    return jnp.where(iota((z.slots, z.stacked), 1) == wanted, 1.0, 0.0).astype(BF16)


def placed(place, values):
    return lax.dot_general(place, values, (((0,), (0,)), ((), ())), preferred_element_type=F32)


def master_kernel(z, rep_ref, *refs):
    got, (new_master, params, half, master_buf, sems) = refs[: z.peers], refs[z.peers :]
    meta = gathered(got, slice(3 * z.body, 3 * z.body + LANES))
    place = placing(z, meta)
    copies = []
    for j in range(z.blocks):
        rows_out = placed(place, gathered(got, slice(j * z.cb, (j + 1) * z.cb)))
        for h in range(z.split):
            values = rows_out[h * z.rows : (h + 1) * z.rows]
            at = j * z.span + h * z.cb
            master_buf[:, at : at + z.cb] = values
            half[:, at : at + z.cb] = values.astype(BF16)
        at = pl.ds(j * z.span, z.span)
        there = pl.ds(pl.multiple_of(rep_ref[0] * z.width + j * z.span, LANES), z.span)
        copies.append(pltpu.make_async_copy(master_buf.at[:, at], new_master.at[:, at], sems.at[0, j]))
        copies.append(pltpu.make_async_copy(half.at[:, at], params.at[:, there], sems.at[1, j]))
        copies[-2].start()
        copies[-1].start()
    half[:, z.width :] = placed(place, meta)[: z.rows].astype(BF16)
    for copy in copies:
        copy.wait()


def moments_kernel(z, *refs):
    got, (one_out, two_out, one_buf, two_buf, sems) = refs[: z.peers], refs[z.peers :]
    place = placing(z, gathered(got, slice(3 * z.body, 3 * z.body + LANES)))
    copies = []
    for i, (out, buf) in enumerate(((one_out, one_buf), (two_out, two_buf))):
        for j in range(z.blocks):
            at = (i + 1) * z.body + j * z.cb
            rows_out = placed(place, gathered(got, slice(at, at + z.cb)))
            for h in range(z.split):
                col = j * z.span + h * z.cb
                buf[:, col : col + z.cb] = rows_out[h * z.rows : (h + 1) * z.rows]
            cols = pl.ds(j * z.span, z.span)
            copies.append(pltpu.make_async_copy(buf.at[:, cols], out.at[:, cols], sems.at[i, j]))
            copies[-1].start()
    for copy in copies:
        copy.wait()


def finish_kernel(z, rep_ref, half, *refs):
    others, (_, params, checksum, sems) = refs[: z.copies - 1], refs[z.copies - 1 :]
    copies = []
    for k, other in enumerate(others):
        replica = lax.rem(rep_ref[0] + z.copies - (k + 1), z.copies)
        there = pl.ds(pl.multiple_of(replica * z.width, LANES), z.width)
        copies.append(pltpu.make_async_copy(other.at[:, : z.width], params.at[:, there], sems.at[k]))
        copies[-1].start()
    sums = half[:, z.width :].astype(F32)
    for other in others:
        sums = sums + other[:, z.width :].astype(F32)
    lane = iota((z.rows, LANES), 1)
    column = jnp.sum(jnp.where((lane >= 1) & (lane <= 3), sums, 0.0), axis=1, keepdims=True)
    diagonal = iota((z.rows, z.rows), 0) == iota((z.rows, z.rows), 1)
    checksum[...] = jnp.sum(jnp.where(diagonal, column, 0.0), axis=0, keepdims=True)
    for copy in copies:
        copy.wait()


def shifted(value, axis, k, count):
    return lax.ppermute(value, axis, [(i, (i + k) % count) for i in range(count)])


def send_used(peers, group, mask, chunks):
    return tuple(
        shifted(chunk, "fsdp", s, peers) if mask >> i & 1 else chunk for i, (s, chunk) in enumerate(zip(group, chunks))
    )


def shift_groups(peers):
    groups = -(-(peers - 1) // GROUP)
    return [list(range(1 + g, peers, groups)) for g in range(groups)]


def swapped(value, k, peers):
    return lax.ppermute(value, "fsdp", [(i, i ^ k) for i in range(peers)])


def choose_branches(used, peers, compiler_params):
    vmem = pl.BlockSpec(memory_space=pltpu.VMEM)
    smem = pl.BlockSpec(memory_space=pltpu.SMEM)
    groups = shift_groups(peers)
    masks = [used]
    stride = 1
    while stride < peers:
        radix = min(4, peers // stride)
        if stride > 1:
            used = pl.pallas_call(
                agree_kernel,
                out_shape=jax.ShapeDtypeStruct((1, LANES), jnp.int32),
                in_specs=[vmem] * len(masks),
                out_specs=vmem,
                compiler_params=compiler_params,
                name="agree",
            )(*masks)
        masks = [used] + [swapped(used, k * stride, peers) for k in range(1, radix)]
        stride *= radix
    return pl.pallas_call(
        functools.partial(choose_kernel, groups),
        out_shape=[jax.ShapeDtypeStruct((1,), jnp.int32)] * len(groups),
        in_specs=[vmem] * len(masks),
        out_specs=[smem] * len(groups),
        compiler_params=compiler_params,
        name="choose",
    )(*masks)


def move(z, chunks, chosen):
    if chosen is None:
        got = lax.all_to_all(jnp.concatenate(chunks, axis=0), "fsdp", split_axis=0, concat_axis=0, tiled=True)
        return [got[s * z.lines : (s + 1) * z.lines] for s in range(z.peers)]
    got = list(chunks)
    for group, bits in zip(shift_groups(z.peers), chosen):
        branches = [
            lambda *values, used=used: send_used(z.peers, group, used, values) for used in range(1 << len(group))
        ]
        for s, value in zip(group, lax.switch(bits[0], branches, *[chunks[s] for s in group])):
            got[s] = value
    return got


def shards(master, moment_one, moment_two, gradients, new_row):
    rows, width = master.shape
    peers, copies = lax.axis_size("fsdp"), lax.axis_size("replica")
    z = Sizes(rows, width, peers, copies)
    compiler_params = pltpu.CompilerParams(vmem_limit_bytes=VMEM_BYTES)
    smem = pl.BlockSpec(memory_space=pltpu.SMEM)
    vmem = pl.BlockSpec(memory_space=pltpu.VMEM)
    hbm = pl.BlockSpec(memory_space=pltpu.HBM)
    dma = pltpu.SemaphoreType.DMA

    replica = lax.axis_index("replica").astype(jnp.int32)
    rep = replica.reshape(1)
    by_shift = peers <= MOST_SHIFT_PEERS and peers & (peers - 1) == 0
    origin = (lax.axis_index("fsdp").astype(jnp.int32) if by_shift else jnp.int32(0)).reshape(1)
    full = gradients[0]

    pick, info, used = pl.pallas_call(
        functools.partial(prepare_kernel, z),
        out_shape=(
            jax.ShapeDtypeStruct((z.split, z.slots, rows), BF16),
            jax.ShapeDtypeStruct((rows, LANES), F32),
            jax.ShapeDtypeStruct((1, LANES), jnp.int32),
        ),
        in_specs=[smem, vmem],
        out_specs=(vmem, vmem, vmem),
        compiler_params=compiler_params,
        name="prepare",
    )(origin, new_row.reshape(1, rows))

    received = []
    for k in range(1, copies):
        other = lax.rem(replica + k, copies)
        part = lax.dynamic_slice(full, (0, other * width), (rows, width)).astype(BF16)
        received.append(shifted(part, "replica", k, copies))
    chosen = choose_branches(used, peers, compiler_params) if by_shift else None

    loaded = jax.ShapeDtypeStruct((rows, width), F32)
    *state, meta = pl.pallas_call(
        functools.partial(load_kernel, z),
        out_shape=[loaded, loaded, loaded, loaded, jax.ShapeDtypeStruct((rows, LANES), BF16)],
        in_specs=[smem, vmem, hbm, hbm, hbm, hbm],
        out_specs=[vmem] * 5,
        scratch_shapes=[dma((4, z.blocks))],
        compiler_params=compiler_params,
        cost_estimate=pl.CostEstimate(flops=4 * rows * width, bytes_accessed=16 * rows * width, transcendentals=0),
        name="load",
    )(rep, info, master, moment_one, moment_two, full)

    chunks = pl.pallas_call(
        functools.partial(update_kernel, z),
        out_shape=[jax.ShapeDtypeStruct((z.lines, z.payload), BF16)] * peers,
        in_specs=[vmem] * (5 + copies),
        out_specs=[vmem] * peers,
        scratch_shapes=[pltpu.VMEM((z.stacked, 3 * z.body), BF16)],
        compiler_params=compiler_params,
        cost_estimate=pl.CostEstimate(
            flops=6 * z.slots * z.stacked * z.body, bytes_accessed=24 * rows * width, transcendentals=rows * width
        ),
        name="update",
    )(pick, meta, *state, *received)

    got = move(z, chunks, chosen)

    new_master, params, half = pl.pallas_call(
        functools.partial(master_kernel, z),
        out_shape=(
            jax.ShapeDtypeStruct((rows, width), F32),
            jax.ShapeDtypeStruct((rows, width * copies), BF16),
            jax.ShapeDtypeStruct((rows, width + LANES), BF16),
        ),
        in_specs=[smem] + [vmem] * peers,
        out_specs=(hbm, hbm, vmem),
        scratch_shapes=[pltpu.VMEM((rows, width), F32), dma((2, z.blocks))],
        compiler_params=compiler_params,
        cost_estimate=pl.CostEstimate(
            flops=2 * z.slots * z.stacked * z.body, bytes_accessed=10 * rows * width, transcendentals=0
        ),
        name="place_master",
    )(rep, *got)
    others = [shifted(half, "replica", k, copies) for k in range(1, copies)]

    new_one, new_two = pl.pallas_call(
        functools.partial(moments_kernel, z),
        out_shape=(jax.ShapeDtypeStruct((rows, width), F32), jax.ShapeDtypeStruct((rows, width), F32)),
        in_specs=[vmem] * peers,
        out_specs=(hbm, hbm),
        scratch_shapes=[pltpu.VMEM((rows, width), F32)] * 2 + [dma((2, z.blocks))],
        compiler_params=compiler_params,
        cost_estimate=pl.CostEstimate(
            flops=4 * z.slots * z.stacked * z.body, bytes_accessed=16 * rows * width, transcendentals=0
        ),
        name="place_moments",
    )(*got)

    params, checksum = pl.pallas_call(
        functools.partial(finish_kernel, z),
        out_shape=(jax.ShapeDtypeStruct((rows, width * copies), BF16), jax.ShapeDtypeStruct((1, rows), F32)),
        in_specs=[smem, vmem] + [vmem] * (copies - 1) + [hbm],
        out_specs=(hbm, vmem),
        scratch_shapes=[dma((max(1, copies - 1),))],
        input_output_aliases={copies + 1: 0},
        compiler_params=compiler_params,
        cost_estimate=pl.CostEstimate(flops=0, bytes_accessed=4 * rows * width, transcendentals=0),
        name="finish",
    )(rep, half, *others, params)
    return (new_master, new_one, new_two, params, checksum.reshape(rows))


def solution(mesh):
    return jax.shard_map(
        shards,
        mesh=mesh,
        in_specs=(
            P("fsdp", "replica"),
            P("fsdp", "replica"),
            P("fsdp", "replica"),
            P("replica", "fsdp", None),
            P("fsdp"),
        ),
        out_specs=(
            P("fsdp", "replica"),
            P("fsdp", "replica"),
            P("fsdp", "replica"),
            P("fsdp", None),
            P("fsdp"),
        ),
        check_vma=False,
    )
```

```python
import functools
import math

import jax
import jax.numpy as jnp
from jax import lax
from jax.experimental import pallas as pl
from jax.experimental.pallas import tpu as pltpu
from jax.sharding import PartitionSpec as P

LANES = 128
TILE_ROWS = 16
MIB = 1024 * 1024
VMEM_BYTES = 48 * MIB
MOST_SHIFT_PEERS = 16
GROUP = 7
F32 = jnp.float32
BF16 = jnp.bfloat16


def iota(shape, axis):
    return lax.broadcasted_iota(jnp.int32, shape, axis)


class Sizes:
    def __init__(self, rows, width, peers, copies):
        self.rows, self.width, self.peers, self.copies = rows, width, peers, copies
        self.cap = max(2, 2 * rows // peers)
        self.split = max(1, TILE_ROWS // self.cap)
        self.lines = self.cap * self.split
        self.slots = peers * self.lines
        self.stacked = self.split * rows
        self.body = width // self.split
        self.cb = math.gcd(self.body, 512)
        self.blocks = self.body // self.cb
        self.span = self.split * self.cb
        self.sub = math.gcd(self.cb, 256)
        self.payload = 3 * self.body + LANES


def prepare_kernel(z, rep_ref, origin_ref, new_row_hbm, full_hbm, pick_ref, info_ref, mask_ref, *refs):
    parts, (full_buf, line_buf, sems, line_sem) = refs[: z.copies - 1], refs[z.copies - 1 :]
    step = z.width // z.blocks
    line_copy = pltpu.make_async_copy(new_row_hbm, line_buf, line_sem)
    line_copy.start()
    copies = []
    for k in range(1, z.copies):
        other = lax.rem(rep_ref[0] + k, z.copies)
        for j in range(z.blocks):
            there = pl.ds(pl.multiple_of(other * z.width + j * step, LANES), step)
            copies.append(
                pltpu.make_async_copy(
                    full_hbm.at[:, there], full_buf.at[k - 1, :, pl.ds(j * step, step)], sems.at[k - 1, j]
                )
            )
            copies[-1].start()
    line_copy.wait()
    line = line_buf[...]
    at_row, at_lane = iota((z.rows, z.rows), 0), iota((z.rows, z.rows), 1)
    column = jnp.sum(jnp.where(at_row == at_lane, line.astype(F32), 0.0), axis=1, keepdims=True).astype(jnp.int32)
    target, target_column = line // z.rows, column // z.rows
    earlier = (target_column == target) & (at_row < at_lane)
    rank = jnp.sum(jnp.where(earlier, 1.0, 0.0), axis=0, keepdims=True).astype(jnp.int32)
    shift = lax.rem(target - origin_ref[0] + z.peers, z.peers)
    shift_column = lax.rem(target_column - origin_ref[0] + z.peers, z.peers)
    for h in range(z.split):
        slot = shift * z.lines + h * z.cap + rank
        pick_ref[h] = jnp.where(iota((z.slots, z.rows), 0) == slot, 1.0, 0.0).astype(BF16)
    lane = iota((z.rows, LANES), 1)
    info_ref[...] = jnp.where(lane == 0, (column - target_column * z.rows + 1).astype(F32), 0.0)
    used = jnp.where(lane == shift_column, 1.0, 0.0)
    mask_ref[...] = jnp.max(used, axis=0, keepdims=True).astype(jnp.int32)
    for k in range(1, z.copies):
        for j in range(z.blocks):
            copies[(k - 1) * z.blocks + j].wait()
            at = slice(j * step, (j + 1) * step)
            parts[k - 1][:, at] = full_buf[k - 1, :, at].astype(BF16)


def agree_kernel(left, right, _, out):
    out[...] = jnp.maximum(left[...], right[...])


def choose_kernel(groups, *refs):
    masks, outs = refs[: -len(groups)], refs[-len(groups) :]
    total = masks[0][...]
    for ref in masks[1:]:
        total = jnp.maximum(total, ref[...])
    lane = iota(total.shape, 1)
    for group, out in zip(groups, outs):
        value = jnp.zeros(total.shape, jnp.int32)
        for i, s in enumerate(group):
            value = value + jnp.where(lane == s, total << i, 0)
        out[0] = jnp.sum(value.astype(F32)).astype(jnp.int32)


def load_kernel(z, rep_ref, info_ref, master_hbm, one_hbm, two_hbm, full_hbm, master, one, two, own, meta_ref, sems):
    base = rep_ref[0] * z.width
    step = z.width // z.blocks
    copies = []
    for j in range(z.blocks):
        at = pl.ds(j * step, step)
        mine = pl.ds(pl.multiple_of(base + j * step, LANES), step)
        copies.append(
            [
                pltpu.make_async_copy(master_hbm.at[:, at], master.at[:, at], sems.at[0, j]),
                pltpu.make_async_copy(one_hbm.at[:, at], one.at[:, at], sems.at[1, j]),
                pltpu.make_async_copy(two_hbm.at[:, at], two.at[:, at], sems.at[2, j]),
                pltpu.make_async_copy(full_hbm.at[:, mine], own.at[:, at], sems.at[3, j]),
            ]
        )
    for i in range(4):
        for j in range(z.blocks):
            copies[j][i].start()
    part = jnp.zeros((z.rows, LANES), F32)
    for j in range(z.blocks):
        copies[j][0].wait()
        for at in range(j * step, (j + 1) * step, LANES):
            weights = 1.0 + ((iota((1, LANES), 1) + (base + at)) % 7).astype(F32) / 7.0
            part = part + master[:, at : at + LANES] * weights
    total = jnp.sum(part, axis=1, keepdims=True) * (1.0 / math.sqrt(z.width * z.copies))
    high = total.astype(BF16).astype(F32)
    middle = (total - high).astype(BF16).astype(F32)
    low = total - high - middle
    lane = iota((z.rows, LANES), 1)
    meta = jnp.where(lane == 1, high, jnp.where(lane == 2, middle, jnp.where(lane == 3, low, info_ref[...])))
    meta_ref[...] = meta.astype(BF16)
    for j in range(z.blocks):
        for i in range(1, 4):
            copies[j][i].wait()


def update_kernel(z, pick_ref, meta_ref, master, one, two, own, *refs):
    received, refs = refs[: z.copies - 1], refs[z.copies :]
    outs, rows_buf = refs[: z.peers], refs[z.peers]
    pick = jnp.concatenate([pick_ref[h] for h in range(z.split)], axis=1)
    for j in range(z.blocks):
        for h in range(z.split):
            for c in range(0, z.cb, z.sub):
                at = j * z.span + h * z.cb + c
                cols = slice(at, at + z.sub)
                summed = own[:, cols]
                for other in received:
                    summed = summed + other[:, cols].astype(F32)
                moved = master[:, cols]
                new_one = 0.9 * one[:, cols] + 0.1 * summed
                new_two = 0.95 * two[:, cols] + 0.05 * summed * summed
                update = new_one * (1.0 / (1.0 - 0.9**10)) / (jnp.sqrt(new_two * (1.0 / (1.0 - 0.95**10))) + 1e-08)
                new_master = moved - 0.05 * (update + 0.1 * moved)
                for i, value in enumerate((new_master, new_one, new_two)):
                    to = i * z.body + j * z.cb + c
                    rows_buf[h * z.rows : (h + 1) * z.rows, to : to + z.sub] = value.astype(BF16)
        for i in range(3):
            at = i * z.body + j * z.cb
            packed = jnp.dot(pick, rows_buf[:, at : at + z.cb], preferred_element_type=F32).astype(BF16)
            for s, out in enumerate(outs):
                out[:, at : at + z.cb] = packed[s * z.lines : (s + 1) * z.lines]
    meta = jnp.concatenate([meta_ref[...]] * z.split, axis=0)
    packed = jnp.dot(pick, meta, preferred_element_type=F32).astype(BF16)
    for s, out in enumerate(outs):
        out[:, 3 * z.body :] = packed[s * z.lines : (s + 1) * z.lines]


def gathered(refs, cols):
    return jnp.concatenate([ref[:, cols] for ref in refs], axis=0)


def placing(z, meta):
    offset = meta[:, :1].astype(F32).astype(jnp.int32)
    piece = lax.rem(iota((z.slots, 1), 0), z.lines) // z.cap
    wanted = jnp.where(offset > 0, offset - 1 + piece * z.rows, -1)
    return jnp.where(iota((z.slots, z.stacked), 1) == wanted, 1.0, 0.0).astype(BF16)


def placed(place, values):
    return lax.dot_general(place, values, (((0,), (0,)), ((), ())), preferred_element_type=F32)


def master_kernel(z, rep_ref, *refs):
    got, (new_master, params, half, master_buf, sems) = refs[: z.peers], refs[z.peers :]
    meta = gathered(got, slice(3 * z.body, 3 * z.body + LANES))
    place = placing(z, meta)
    copies = []
    for j in range(z.blocks):
        rows_out = placed(place, gathered(got, slice(j * z.cb, (j + 1) * z.cb)))
        for h in range(z.split):
            values = rows_out[h * z.rows : (h + 1) * z.rows]
            at = j * z.span + h * z.cb
            master_buf[:, at : at + z.cb] = values
            half[:, at : at + z.cb] = values.astype(BF16)
        at = pl.ds(j * z.span, z.span)
        there = pl.ds(pl.multiple_of(rep_ref[0] * z.width + j * z.span, LANES), z.span)
        copies.append(pltpu.make_async_copy(master_buf.at[:, at], new_master.at[:, at], sems.at[0, j]))
        copies.append(pltpu.make_async_copy(half.at[:, at], params.at[:, there], sems.at[1, j]))
        copies[-2].start()
        copies[-1].start()
    half[:, z.width :] = placed(place, meta)[: z.rows].astype(BF16)
    for copy in copies:
        copy.wait()


def place_one(z, i, got, out, buf, sems):
    place = placing(z, gathered(got, slice(3 * z.body, 3 * z.body + LANES)))
    copies = []
    for j in range(z.blocks):
        at = i * z.body + j * z.cb
        rows_out = placed(place, gathered(got, slice(at, at + z.cb)))
        for h in range(z.split):
            col = j * z.span + h * z.cb
            buf[:, col : col + z.cb] = rows_out[h * z.rows : (h + 1) * z.rows]
        cols = pl.ds(j * z.span, z.span)
        copies.append(pltpu.make_async_copy(buf.at[:, cols], out.at[:, cols], sems.at[j]))
        copies[-1].start()
    return copies


def one_kernel(z, *refs):
    got, (one_out, buf, sems) = refs[: z.peers], refs[z.peers :]
    for copy in place_one(z, 1, got, one_out, buf, sems):
        copy.wait()


def two_kernel(z, rep_ref, half, *refs):
    others, refs = refs[: z.copies - 1], refs[z.copies - 1 :]
    got, (_, params, two_out, checksum, buf, sems, param_sems) = refs[: z.peers], refs[z.peers :]
    copies = []
    for k, other in enumerate(others):
        replica = lax.rem(rep_ref[0] + z.copies - (k + 1), z.copies)
        there = pl.ds(pl.multiple_of(replica * z.width, LANES), z.width)
        copies.append(pltpu.make_async_copy(other.at[:, : z.width], params.at[:, there], param_sems.at[k]))
        copies[-1].start()
    copies += place_one(z, 2, got, two_out, buf, sems)
    sums = half[:, z.width :].astype(F32)
    for other in others:
        sums = sums + other[:, z.width :].astype(F32)
    lane = iota((z.rows, LANES), 1)
    column = jnp.sum(jnp.where((lane >= 1) & (lane <= 3), sums, 0.0), axis=1, keepdims=True)
    diagonal = iota((z.rows, z.rows), 0) == iota((z.rows, z.rows), 1)
    checksum[...] = jnp.sum(jnp.where(diagonal, column, 0.0), axis=0, keepdims=True)
    for copy in copies:
        copy.wait()


def shifted(value, axis, k, count):
    return lax.ppermute(value, axis, [(i, (i + k) % count) for i in range(count)])


def send_used(peers, group, mask, chunks):
    return tuple(
        shifted(chunk, "fsdp", s, peers) if mask >> i & 1 else chunk for i, (s, chunk) in enumerate(zip(group, chunks))
    )


def always_sent(peers):
    return sorted({peers // 2, peers - 1})


def shift_groups(peers):
    rest = [s for s in range(1, peers) if s not in always_sent(peers)]
    groups = -(-len(rest) // GROUP)
    return [rest[g::groups] for g in range(groups)]


def agree(used, stride, peers, after, compiler_params):
    vmem = pl.BlockSpec(memory_space=pltpu.VMEM)
    other = lax.ppermute(used, "fsdp", [(i, i ^ stride) for i in range(peers)])
    return pl.pallas_call(
        agree_kernel,
        out_shape=jax.ShapeDtypeStruct((1, LANES), jnp.int32),
        in_specs=[vmem, vmem, pl.BlockSpec(memory_space=pl.ANY)],
        out_specs=vmem,
        compiler_params=compiler_params,
        name="agree",
    )(used, other, after)


def choose_branches(used, after, peers, compiler_params):
    vmem = pl.BlockSpec(memory_space=pltpu.VMEM)
    smem = pl.BlockSpec(memory_space=pltpu.SMEM)
    groups = shift_groups(peers)
    stride = 2
    while 2 * stride < peers:
        used = agree(used, stride, peers, after, compiler_params)
        stride *= 2
    other = lax.ppermute(used, "fsdp", [(i, i ^ stride) for i in range(peers)])
    return pl.pallas_call(
        functools.partial(choose_kernel, groups),
        out_shape=[jax.ShapeDtypeStruct((1,), jnp.int32)] * len(groups),
        in_specs=[vmem, vmem],
        out_specs=[smem] * len(groups),
        compiler_params=compiler_params,
        name="choose",
    )(used, other)


def move(z, chunks, chosen):
    if chosen is None:
        got = lax.all_to_all(jnp.concatenate(chunks, axis=0), "fsdp", split_axis=0, concat_axis=0, tiled=True)
        return [got[s * z.lines : (s + 1) * z.lines] for s in range(z.peers)]
    got = list(chunks)
    always = always_sent(z.peers)
    for s in always:
        got[s] = shifted(chunks[s], "fsdp", s, z.peers)
    barred = lax.optimization_barrier((*chosen, *[got[s] for s in always]))
    chosen, moved = barred[: len(chosen)], barred[len(chosen) :]
    for s, value in zip(always, moved):
        got[s] = value
    for group, bits in zip(shift_groups(z.peers), chosen):
        branches = [
            lambda *values, used=used: send_used(z.peers, group, used, values) for used in range(1 << len(group))
        ]
        for s, value in zip(group, lax.switch(bits[0], branches, *[chunks[s] for s in group])):
            got[s] = value
    return got


def shards(master, moment_one, moment_two, gradients, new_row):
    rows, width = master.shape
    peers, copies = lax.axis_size("fsdp"), lax.axis_size("replica")
    z = Sizes(rows, width, peers, copies)
    compiler_params = pltpu.CompilerParams(vmem_limit_bytes=VMEM_BYTES)
    smem = pl.BlockSpec(memory_space=pltpu.SMEM)
    vmem = pl.BlockSpec(memory_space=pltpu.VMEM)
    hbm = pl.BlockSpec(memory_space=pl.ANY)
    dma = pltpu.SemaphoreType.DMA

    replica = lax.axis_index("replica").astype(jnp.int32)
    rep = replica.reshape(1)
    by_shift = peers <= MOST_SHIFT_PEERS and peers & (peers - 1) == 0
    origin = (lax.axis_index("fsdp").astype(jnp.int32) if by_shift else jnp.int32(0)).reshape(1)
    state_in = [pltpu.with_memory_space_constraint(x, pltpu.HBM) for x in (master, moment_one, moment_two)]
    full = pltpu.with_memory_space_constraint(gradients[0], pltpu.HBM)

    part = jax.ShapeDtypeStruct((rows, width), BF16)
    pick, info, used, *parts = pl.pallas_call(
        functools.partial(prepare_kernel, z),
        out_shape=[
            jax.ShapeDtypeStruct((z.split, z.slots, rows), BF16),
            jax.ShapeDtypeStruct((rows, LANES), F32),
            jax.ShapeDtypeStruct((1, LANES), jnp.int32),
        ]
        + [part] * (copies - 1),
        in_specs=[smem, smem, hbm, hbm],
        out_specs=[vmem] * (copies + 2),
        scratch_shapes=[
            pltpu.VMEM((copies - 1, rows, width), F32),
            pltpu.VMEM((1, rows), jnp.int32),
            dma((copies - 1, z.blocks)),
            dma,
        ],
        compiler_params=compiler_params,
        cost_estimate=pl.CostEstimate(flops=1 << 30, bytes_accessed=1, transcendentals=0),
        name="prepare",
    )(rep, origin, pltpu.with_memory_space_constraint(new_row.reshape(1, rows), pltpu.HBM), full)
    received = [shifted(value, "replica", k + 1, copies) for k, value in enumerate(parts)]

    loaded = jax.ShapeDtypeStruct((rows, width), F32)
    *state, meta = pl.pallas_call(
        functools.partial(load_kernel, z),
        out_shape=[loaded, loaded, loaded, loaded, jax.ShapeDtypeStruct((rows, LANES), BF16)],
        in_specs=[smem, vmem, hbm, hbm, hbm, hbm],
        out_specs=[vmem] * 5,
        scratch_shapes=[dma((4, z.blocks))],
        compiler_params=compiler_params,
        cost_estimate=pl.CostEstimate(flops=1 << 30, bytes_accessed=1, transcendentals=0),
        name="load",
    )(rep, info, *state_in, full)

    if by_shift:
        used = agree(used, 1, peers, meta, compiler_params)
    chunks = pl.pallas_call(
        functools.partial(update_kernel, z),
        out_shape=[jax.ShapeDtypeStruct((z.lines, z.payload), BF16)] * peers,
        in_specs=[vmem] * (5 + copies) + [hbm],
        out_specs=[vmem] * peers,
        scratch_shapes=[pltpu.VMEM((z.stacked, 3 * z.body), BF16)],
        compiler_params=compiler_params,
        cost_estimate=pl.CostEstimate(
            flops=6 * z.slots * z.stacked * z.body, bytes_accessed=24 * rows * width, transcendentals=rows * width
        ),
        name="update",
    )(pick, meta, *state, *received, used)

    chosen = choose_branches(used, chunks[0], peers, compiler_params) if by_shift else None
    got = move(z, chunks, chosen)

    new_master, params, half = pl.pallas_call(
        functools.partial(master_kernel, z),
        out_shape=(
            jax.ShapeDtypeStruct((rows, width), F32),
            jax.ShapeDtypeStruct((rows, width * copies), BF16),
            jax.ShapeDtypeStruct((rows, width + LANES), BF16),
        ),
        in_specs=[smem] + [vmem] * peers,
        out_specs=(hbm, hbm, vmem),
        scratch_shapes=[pltpu.VMEM((rows, width), F32), dma((2, z.blocks))],
        compiler_params=compiler_params,
        cost_estimate=pl.CostEstimate(
            flops=2 * z.slots * z.stacked * z.body, bytes_accessed=10 * rows * width, transcendentals=0
        ),
        name="place_master",
    )(rep, *got)
    others = [shifted(half, "replica", k, copies) for k in range(1, copies)]

    new_one = pl.pallas_call(
        functools.partial(one_kernel, z),
        out_shape=jax.ShapeDtypeStruct((rows, width), F32),
        in_specs=[vmem] * peers,
        out_specs=hbm,
        scratch_shapes=[pltpu.VMEM((rows, width), F32), dma((z.blocks,))],
        compiler_params=compiler_params,
        cost_estimate=pl.CostEstimate(
            flops=2 * z.slots * z.stacked * z.body, bytes_accessed=8 * rows * width, transcendentals=0
        ),
        name="place_one",
    )(*got)

    params, new_two, checksum = pl.pallas_call(
        functools.partial(two_kernel, z),
        out_shape=(
            jax.ShapeDtypeStruct((rows, width * copies), BF16),
            jax.ShapeDtypeStruct((rows, width), F32),
            jax.ShapeDtypeStruct((1, rows), F32),
        ),
        in_specs=[smem] + [vmem] * (copies + peers) + [hbm],
        out_specs=(hbm, hbm, vmem),
        scratch_shapes=[pltpu.VMEM((rows, width), F32), dma((z.blocks,)), dma((max(1, copies - 1),))],
        input_output_aliases={copies + peers + 1: 0},
        compiler_params=compiler_params,
        cost_estimate=pl.CostEstimate(
            flops=2 * z.slots * z.stacked * z.body, bytes_accessed=12 * rows * width, transcendentals=0
        ),
        name="place_two",
    )(rep, half, *others, *got, params)
    return (new_master, new_one, new_two, params, checksum.reshape(rows))


def solution(mesh):
    return jax.shard_map(
        shards,
        mesh=mesh,
        in_specs=(
            P("fsdp", "replica"),
            P("fsdp", "replica"),
            P("fsdp", "replica"),
            P("replica", "fsdp", None),
            P("fsdp"),
        ),
        out_specs=(
            P("fsdp", "replica"),
            P("fsdp", "replica"),
            P("fsdp", "replica"),
            P("fsdp", None),
            P("fsdp"),
        ),
        check_vma=False,
    )
```

```python
import functools
import math

import jax
import jax.numpy as jnp
from jax import lax
from jax.experimental import pallas as pl
from jax.experimental.pallas import tpu as pltpu
from jax.sharding import PartitionSpec as P

LANES = 128
TILE_ROWS = 16
MIB = 1024 * 1024
VMEM_BYTES = 48 * MIB
MOST_SHIFT_PEERS = 16
GROUP = 7
DIGIT = 4
F32 = jnp.float32
BF16 = jnp.bfloat16


def iota(shape, axis):
    return lax.broadcasted_iota(jnp.int32, shape, axis)


class Sizes:
    def __init__(self, rows, width, peers, copies):
        self.rows, self.width, self.peers, self.copies = rows, width, peers, copies
        self.cap = max(2, 2 * rows // peers)
        self.split = max(1, TILE_ROWS // self.cap)
        self.lines = self.cap * self.split
        self.slots = peers * self.lines
        self.stacked = self.split * rows
        self.body = width // self.split
        self.cb = math.gcd(self.body, 512)
        self.blocks = self.body // self.cb
        self.span = self.split * self.cb
        self.sub = math.gcd(self.cb, 256)
        self.payload = 3 * self.body + LANES


def prepare_kernel(z, rep_ref, origin_ref, new_row_hbm, full_hbm, pick_ref, info_ref, mask_ref, *refs):
    parts, (full_buf, line_buf, sems, line_sem) = refs[: z.copies - 1], refs[z.copies - 1 :]
    step = z.width // z.blocks
    line_copy = pltpu.make_async_copy(new_row_hbm, line_buf, line_sem)
    line_copy.start()
    copies = []
    for k in range(1, z.copies):
        other = lax.rem(rep_ref[0] + k, z.copies)
        for j in range(z.blocks):
            there = pl.ds(pl.multiple_of(other * z.width + j * step, LANES), step)
            copies.append(
                pltpu.make_async_copy(
                    full_hbm.at[:, there], full_buf.at[k - 1, :, pl.ds(j * step, step)], sems.at[k - 1, j]
                )
            )
            copies[-1].start()
    line_copy.wait()
    line = line_buf[...]
    at_row, at_lane = iota((z.rows, z.rows), 0), iota((z.rows, z.rows), 1)
    column = jnp.sum(jnp.where(at_row == at_lane, line.astype(F32), 0.0), axis=1, keepdims=True).astype(jnp.int32)
    target, target_column = line // z.rows, column // z.rows
    earlier = (target_column == target) & (at_row < at_lane)
    rank = jnp.sum(jnp.where(earlier, 1.0, 0.0), axis=0, keepdims=True).astype(jnp.int32)
    shift = lax.rem(target - origin_ref[0] + z.peers, z.peers)
    shift_column = lax.rem(target_column - origin_ref[0] + z.peers, z.peers)
    for h in range(z.split):
        slot = shift * z.lines + h * z.cap + rank
        pick_ref[h] = jnp.where(iota((z.slots, z.rows), 0) == slot, 1.0, 0.0).astype(BF16)
    lane = iota((z.rows, LANES), 1)
    info_ref[...] = jnp.where(lane == 0, (column - target_column * z.rows + 1).astype(F32), 0.0)
    used = jnp.where(lane == shift_column, 1.0, 0.0)
    mask_ref[...] = jnp.max(used, axis=0, keepdims=True).astype(jnp.int32)
    for k in range(1, z.copies):
        for j in range(z.blocks):
            copies[(k - 1) * z.blocks + j].wait()
            at = slice(j * step, (j + 1) * step)
            parts[k - 1][:, at] = full_buf[k - 1, :, at].astype(BF16)


def agree_kernel(left, right, _, out):
    out[...] = jnp.maximum(left[...], right[...])


def choose_kernel(digits, left, right, *outs):
    total = jnp.maximum(left[...], right[...])
    lane = iota(total.shape, 1)
    for digit, out in zip(digits, outs):
        value = jnp.zeros(total.shape, jnp.int32)
        for i, s in enumerate(digit):
            value = value + jnp.where(lane == s, total << i, 0)
        out[0] = jnp.sum(value.astype(F32)).astype(jnp.int32)


def load_kernel(z, rep_ref, info_ref, master_hbm, one_hbm, two_hbm, full_hbm, master, one, two, own, meta_ref, sems):
    base = rep_ref[0] * z.width
    step = z.width // z.blocks
    copies = []
    for j in range(z.blocks):
        at = pl.ds(j * step, step)
        mine = pl.ds(pl.multiple_of(base + j * step, LANES), step)
        copies.append(
            [
                pltpu.make_async_copy(master_hbm.at[:, at], master.at[:, at], sems.at[0, j]),
                pltpu.make_async_copy(one_hbm.at[:, at], one.at[:, at], sems.at[1, j]),
                pltpu.make_async_copy(two_hbm.at[:, at], two.at[:, at], sems.at[2, j]),
                pltpu.make_async_copy(full_hbm.at[:, mine], own.at[:, at], sems.at[3, j]),
            ]
        )
    for i in range(4):
        for j in range(z.blocks):
            copies[j][i].start()
    part = jnp.zeros((z.rows, LANES), F32)
    for j in range(z.blocks):
        copies[j][0].wait()
        for at in range(j * step, (j + 1) * step, LANES):
            weights = 1.0 + ((iota((1, LANES), 1) + (base + at)) % 7).astype(F32) / 7.0
            part = part + master[:, at : at + LANES] * weights
    total = jnp.sum(part, axis=1, keepdims=True) * (1.0 / math.sqrt(z.width * z.copies))
    high = total.astype(BF16).astype(F32)
    middle = (total - high).astype(BF16).astype(F32)
    low = total - high - middle
    lane = iota((z.rows, LANES), 1)
    meta = jnp.where(lane == 1, high, jnp.where(lane == 2, middle, jnp.where(lane == 3, low, info_ref[...])))
    meta_ref[...] = meta.astype(BF16)
    for j in range(z.blocks):
        for i in range(1, 4):
            copies[j][i].wait()


def update_kernel(z, pick_ref, meta_ref, master, one, two, own, *refs):
    received, refs = refs[: z.copies - 1], refs[z.copies :]
    outs, rows_buf = refs[: z.peers], refs[z.peers]
    pick = jnp.concatenate([pick_ref[h] for h in range(z.split)], axis=1)
    for j in range(z.blocks):
        for h in range(z.split):
            for c in range(0, z.cb, z.sub):
                at = j * z.span + h * z.cb + c
                cols = slice(at, at + z.sub)
                summed = own[:, cols]
                for other in received:
                    summed = summed + other[:, cols].astype(F32)
                moved = master[:, cols]
                new_one = 0.9 * one[:, cols] + 0.1 * summed
                new_two = 0.95 * two[:, cols] + 0.05 * summed * summed
                update = new_one * (1.0 / (1.0 - 0.9**10)) / (jnp.sqrt(new_two * (1.0 / (1.0 - 0.95**10))) + 1e-08)
                new_master = moved - 0.05 * (update + 0.1 * moved)
                for i, value in enumerate((new_master, new_one, new_two)):
                    to = i * z.body + j * z.cb + c
                    rows_buf[h * z.rows : (h + 1) * z.rows, to : to + z.sub] = value.astype(BF16)
        for i in range(3):
            at = i * z.body + j * z.cb
            packed = jnp.dot(pick, rows_buf[:, at : at + z.cb], preferred_element_type=F32).astype(BF16)
            for s, out in enumerate(outs):
                out[:, at : at + z.cb] = packed[s * z.lines : (s + 1) * z.lines]
    meta = jnp.concatenate([meta_ref[...]] * z.split, axis=0)
    packed = jnp.dot(pick, meta, preferred_element_type=F32).astype(BF16)
    for s, out in enumerate(outs):
        out[:, 3 * z.body :] = packed[s * z.lines : (s + 1) * z.lines]


def gathered(refs, cols):
    return jnp.concatenate([ref[:, cols] for ref in refs], axis=0)


def placing(z, meta):
    offset = meta[:, :1].astype(F32).astype(jnp.int32)
    piece = lax.rem(iota((z.slots, 1), 0), z.lines) // z.cap
    wanted = jnp.where(offset > 0, offset - 1 + piece * z.rows, -1)
    return jnp.where(iota((z.slots, z.stacked), 1) == wanted, 1.0, 0.0).astype(BF16)


def placed(place, values):
    return lax.dot_general(place, values, (((0,), (0,)), ((), ())), preferred_element_type=F32)


def master_kernel(z, rep_ref, *refs):
    got, (new_master, params, half, place_out, master_buf, sems) = refs[: z.peers], refs[z.peers :]
    meta = gathered(got, slice(3 * z.body, 3 * z.body + LANES))
    place = placing(z, meta)
    place_out[...] = place
    copies = []
    for j in range(z.blocks):
        rows_out = placed(place, gathered(got, slice(j * z.cb, (j + 1) * z.cb)))
        for h in range(z.split):
            values = rows_out[h * z.rows : (h + 1) * z.rows]
            at = j * z.span + h * z.cb
            master_buf[:, at : at + z.cb] = values
            half[:, at : at + z.cb] = values.astype(BF16)
        at = pl.ds(j * z.span, z.span)
        there = pl.ds(pl.multiple_of(rep_ref[0] * z.width + j * z.span, LANES), z.span)
        copies.append(pltpu.make_async_copy(master_buf.at[:, at], new_master.at[:, at], sems.at[0, j]))
        copies.append(pltpu.make_async_copy(half.at[:, at], params.at[:, there], sems.at[1, j]))
        copies[-2].start()
        copies[-1].start()
    half[:, z.width :] = placed(place, meta)[: z.rows].astype(BF16)
    for copy in copies:
        copy.wait()


def place_one(z, i, place, got, out, buf, sems):
    copies = []
    for j in range(z.blocks):
        at = i * z.body + j * z.cb
        rows_out = placed(place, gathered(got, slice(at, at + z.cb)))
        for h in range(z.split):
            col = j * z.span + h * z.cb
            buf[:, col : col + z.cb] = rows_out[h * z.rows : (h + 1) * z.rows]
        cols = pl.ds(j * z.span, z.span)
        copies.append(pltpu.make_async_copy(buf.at[:, cols], out.at[:, cols], sems.at[j]))
        copies[-1].start()
    return copies


def one_kernel(z, place, *refs):
    got, (one_out, buf, sems) = refs[: z.peers], refs[z.peers :]
    for copy in place_one(z, 1, place[...], got, one_out, buf, sems):
        copy.wait()


def two_kernel(z, rep_ref, place, half, *refs):
    others, refs = refs[: z.copies - 1], refs[z.copies - 1 :]
    got, (_, params, two_out, checksum, buf, sems, param_sems) = refs[: z.peers], refs[z.peers :]
    copies = []
    for k, other in enumerate(others):
        replica = lax.rem(rep_ref[0] + z.copies - (k + 1), z.copies)
        there = pl.ds(pl.multiple_of(replica * z.width, LANES), z.width)
        copies.append(pltpu.make_async_copy(other.at[:, : z.width], params.at[:, there], param_sems.at[k]))
        copies[-1].start()
    copies += place_one(z, 2, place[...], got, two_out, buf, sems)
    sums = half[:, z.width :].astype(F32)
    for other in others:
        sums = sums + other[:, z.width :].astype(F32)
    lane = iota((z.rows, LANES), 1)
    column = jnp.sum(jnp.where((lane >= 1) & (lane <= 3), sums, 0.0), axis=1, keepdims=True)
    diagonal = iota((z.rows, z.rows), 0) == iota((z.rows, z.rows), 1)
    checksum[...] = jnp.sum(jnp.where(diagonal, column, 0.0), axis=0, keepdims=True)
    for copy in copies:
        copy.wait()


def shifted(value, axis, k, count):
    return lax.ppermute(value, axis, [(i, (i + k) % count) for i in range(count)])


def always_sent(peers):
    return sorted({peers // 2, peers - 1})


def shift_groups(peers):
    rest = [s for s in range(1, peers) if s not in always_sent(peers)]
    groups = -(-len(rest) // GROUP)
    return [rest[g::groups] for g in range(groups)]


def agree(used, stride, peers, after, compiler_params):
    vmem = pl.BlockSpec(memory_space=pltpu.VMEM)
    other = lax.ppermute(used, "fsdp", [(i, i ^ stride) for i in range(peers)])
    return pl.pallas_call(
        agree_kernel,
        out_shape=jax.ShapeDtypeStruct((1, LANES), jnp.int32),
        in_specs=[vmem, vmem, pl.BlockSpec(memory_space=pl.ANY)],
        out_specs=vmem,
        compiler_params=compiler_params,
        name="agree",
    )(used, other, after)


def digits_of(group):
    count = -(-len(group) // DIGIT)
    size = -(-len(group) // count)
    return [group[i : i + size] for i in range(0, len(group), size)]


def choose_branches(used, after, peers, compiler_params):
    vmem = pl.BlockSpec(memory_space=pltpu.VMEM)
    smem = pl.BlockSpec(memory_space=pltpu.SMEM)
    digits = [digit for group in shift_groups(peers) for digit in digits_of(group)]
    stride = 2
    while 2 * stride < peers:
        used = agree(used, stride, peers, after, compiler_params)
        stride *= 2
    other = lax.ppermute(used, "fsdp", [(i, i ^ stride) for i in range(peers)])
    return pl.pallas_call(
        functools.partial(choose_kernel, digits),
        out_shape=[pltpu.SMEM((1,), jnp.int32)] * len(digits),
        in_specs=[vmem, vmem],
        out_specs=[smem] * len(digits),
        compiler_params=compiler_params,
        name="choose",
    )(used, other)


def send_tree(peers, digits, numbers, sent, values):
    if not digits:
        return tuple(shifted(value, "fsdp", s, peers) if on else value for s, on, value in zip(*sent, values))

    def branch(used):
        on = [bool(used >> i & 1) for i in range(len(digits[0]))]

        def run(rest, operands):
            return send_tree(peers, digits[1:], rest, (sent[0], sent[1] + on), operands)

        return run

    branches = [branch(used) for used in range(1 << len(digits[0]))]
    return lax.switch(numbers[0], branches, numbers[1:], values)


def move(z, chunks, chosen):
    if chosen is None:
        got = lax.all_to_all(jnp.concatenate(chunks, axis=0), "fsdp", split_axis=0, concat_axis=0, tiled=True)
        return [got[s * z.lines : (s + 1) * z.lines] for s in range(z.peers)]
    got = list(chunks)
    always = always_sent(z.peers)
    for s in always:
        got[s] = shifted(chunks[s], "fsdp", s, z.peers)
    barred = lax.optimization_barrier((*chosen, *[got[s] for s in always]))
    chosen, moved = barred[: len(chosen)], barred[len(chosen) :]
    for s, value in zip(always, moved):
        got[s] = value
    numbers = [number[0] for number in chosen]
    for group in shift_groups(z.peers):
        digits = digits_of(group)
        mine, numbers = tuple(numbers[: len(digits)]), numbers[len(digits) :]
        values = send_tree(z.peers, digits, mine, (group, []), tuple(chunks[s] for s in group))
        for s, value in zip(group, values):
            got[s] = value
    return got


def shards(master, moment_one, moment_two, gradients, new_row):
    rows, width = master.shape
    peers, copies = lax.axis_size("fsdp"), lax.axis_size("replica")
    z = Sizes(rows, width, peers, copies)
    compiler_params = pltpu.CompilerParams(vmem_limit_bytes=VMEM_BYTES)
    smem = pl.BlockSpec(memory_space=pltpu.SMEM)
    vmem = pl.BlockSpec(memory_space=pltpu.VMEM)
    hbm = pl.BlockSpec(memory_space=pl.ANY)
    dma = pltpu.SemaphoreType.DMA

    replica = lax.axis_index("replica").astype(jnp.int32)
    rep = replica.reshape(1)
    by_shift = peers <= MOST_SHIFT_PEERS and peers & (peers - 1) == 0
    origin = (lax.axis_index("fsdp").astype(jnp.int32) if by_shift else jnp.int32(0)).reshape(1)
    state_in = [pltpu.with_memory_space_constraint(x, pltpu.HBM) for x in (master, moment_one, moment_two)]
    full = pltpu.with_memory_space_constraint(gradients[0], pltpu.HBM)

    part = jax.ShapeDtypeStruct((rows, width), BF16)
    pick, info, used, *parts = pl.pallas_call(
        functools.partial(prepare_kernel, z),
        out_shape=[
            jax.ShapeDtypeStruct((z.split, z.slots, rows), BF16),
            jax.ShapeDtypeStruct((rows, LANES), F32),
            jax.ShapeDtypeStruct((1, LANES), jnp.int32),
        ]
        + [part] * (copies - 1),
        in_specs=[smem, smem, hbm, hbm],
        out_specs=[vmem] * (copies + 2),
        scratch_shapes=[
            pltpu.VMEM((copies - 1, rows, width), F32),
            pltpu.VMEM((1, rows), jnp.int32),
            dma((copies - 1, z.blocks)),
            dma,
        ],
        compiler_params=compiler_params,
        cost_estimate=pl.CostEstimate(flops=1 << 30, bytes_accessed=1, transcendentals=0),
        name="prepare",
    )(rep, origin, pltpu.with_memory_space_constraint(new_row.reshape(1, rows), pltpu.HBM), full)
    received = [shifted(value, "replica", k + 1, copies) for k, value in enumerate(parts)]

    loaded = jax.ShapeDtypeStruct((rows, width), F32)
    *state, meta = pl.pallas_call(
        functools.partial(load_kernel, z),
        out_shape=[loaded, loaded, loaded, loaded, jax.ShapeDtypeStruct((rows, LANES), BF16)],
        in_specs=[smem, vmem, hbm, hbm, hbm, hbm],
        out_specs=[vmem] * 5,
        scratch_shapes=[dma((4, z.blocks))],
        compiler_params=compiler_params,
        cost_estimate=pl.CostEstimate(flops=1 << 30, bytes_accessed=1, transcendentals=0),
        name="load",
    )(rep, info, *state_in, full)

    if by_shift:
        used = agree(used, 1, peers, meta, compiler_params)
    chunks = pl.pallas_call(
        functools.partial(update_kernel, z),
        out_shape=[jax.ShapeDtypeStruct((z.lines, z.payload), BF16)] * peers,
        in_specs=[vmem] * (5 + copies) + [hbm],
        out_specs=[vmem] * peers,
        scratch_shapes=[pltpu.VMEM((z.stacked, 3 * z.body), BF16)],
        compiler_params=compiler_params,
        cost_estimate=pl.CostEstimate(
            flops=6 * z.slots * z.stacked * z.body, bytes_accessed=24 * rows * width, transcendentals=rows * width
        ),
        name="update",
    )(pick, meta, *state, *received, used)

    chosen = choose_branches(used, chunks[0], peers, compiler_params) if by_shift else None
    got = move(z, chunks, chosen)

    new_master, params, half, place = pl.pallas_call(
        functools.partial(master_kernel, z),
        out_shape=(
            jax.ShapeDtypeStruct((rows, width), F32),
            jax.ShapeDtypeStruct((rows, width * copies), BF16),
            jax.ShapeDtypeStruct((rows, width + LANES), BF16),
            jax.ShapeDtypeStruct((z.slots, z.stacked), BF16),
        ),
        in_specs=[smem] + [vmem] * peers,
        out_specs=(hbm, hbm, vmem, vmem),
        scratch_shapes=[pltpu.VMEM((rows, width), F32), dma((2, z.blocks))],
        compiler_params=compiler_params,
        cost_estimate=pl.CostEstimate(
            flops=2 * z.slots * z.stacked * z.body, bytes_accessed=10 * rows * width, transcendentals=0
        ),
        name="place_master",
    )(rep, *got)
    others = [shifted(half, "replica", k, copies) for k in range(1, copies)]

    new_one = pl.pallas_call(
        functools.partial(one_kernel, z),
        out_shape=jax.ShapeDtypeStruct((rows, width), F32),
        in_specs=[vmem] * (peers + 1),
        out_specs=hbm,
        scratch_shapes=[pltpu.VMEM((rows, width), F32), dma((z.blocks,))],
        compiler_params=compiler_params,
        cost_estimate=pl.CostEstimate(
            flops=2 * z.slots * z.stacked * z.body, bytes_accessed=8 * rows * width, transcendentals=0
        ),
        name="place_one",
    )(place, *got)

    params, new_two, checksum = pl.pallas_call(
        functools.partial(two_kernel, z),
        out_shape=(
            jax.ShapeDtypeStruct((rows, width * copies), BF16),
            jax.ShapeDtypeStruct((rows, width), F32),
            jax.ShapeDtypeStruct((1, rows), F32),
        ),
        in_specs=[smem] + [vmem] * (copies + peers + 1) + [hbm],
        out_specs=(hbm, hbm, vmem),
        scratch_shapes=[pltpu.VMEM((rows, width), F32), dma((z.blocks,)), dma((max(1, copies - 1),))],
        input_output_aliases={copies + peers + 2: 0},
        compiler_params=compiler_params,
        cost_estimate=pl.CostEstimate(
            flops=2 * z.slots * z.stacked * z.body, bytes_accessed=12 * rows * width, transcendentals=0
        ),
        name="place_two",
    )(rep, place, half, *others, *got, params)
    return (new_master, new_one, new_two, params, checksum.reshape(rows))


def solution(mesh):
    return jax.shard_map(
        shards,
        mesh=mesh,
        in_specs=(
            P("fsdp", "replica"),
            P("fsdp", "replica"),
            P("fsdp", "replica"),
            P("replica", "fsdp", None),
            P("fsdp"),
        ),
        out_specs=(
            P("fsdp", "replica"),
            P("fsdp", "replica"),
            P("fsdp", "replica"),
            P("fsdp", None),
            P("fsdp"),
        ),
        check_vma=False,
    )
```

```python
import functools
import math

import jax
import jax.numpy as jnp
from jax import lax
from jax.experimental import pallas as pl
from jax.experimental.pallas import tpu as pltpu
from jax.sharding import PartitionSpec as P

LANES = 128
TILE_ROWS = 16
MIB = 1024 * 1024
VMEM_BYTES = 48 * MIB
MOST_SHIFT_PEERS = 16
GROUP = 3
DIGIT = 3
F32 = jnp.float32
BF16 = jnp.bfloat16


def iota(shape, axis):
    return lax.broadcasted_iota(jnp.int32, shape, axis)


class Sizes:
    def __init__(self, rows, width, peers, copies):
        self.rows, self.width, self.peers, self.copies = rows, width, peers, copies
        self.cap = max(2, 2 * rows // peers)
        self.split = max(1, TILE_ROWS // self.cap)
        self.lines = self.cap * self.split
        self.slots = peers * self.lines
        self.stacked = self.split * rows
        self.body = width // self.split
        self.cb = math.gcd(self.body, 512)
        self.blocks = self.body // self.cb
        self.span = self.split * self.cb
        self.sub = math.gcd(self.cb, 256)
        self.payload = 3 * self.body + LANES


def prepare_kernel(z, rep_ref, origin_ref, new_row_hbm, full_hbm, pick_ref, info_ref, mask_ref, *refs):
    parts, (full_buf, line_buf, sems, line_sem) = refs[: z.copies - 1], refs[z.copies - 1 :]
    step = z.width // z.blocks
    line_copy = pltpu.make_async_copy(new_row_hbm, line_buf, line_sem)
    line_copy.start()
    copies = []
    for k in range(1, z.copies):
        other = lax.rem(rep_ref[0] + k, z.copies)
        for j in range(z.blocks):
            there = pl.ds(pl.multiple_of(other * z.width + j * step, LANES), step)
            copies.append(
                pltpu.make_async_copy(
                    full_hbm.at[:, there], full_buf.at[k - 1, :, pl.ds(j * step, step)], sems.at[k - 1, j]
                )
            )
            copies[-1].start()
    line_copy.wait()
    line = line_buf[...]
    at_row, at_lane = iota((z.rows, z.rows), 0), iota((z.rows, z.rows), 1)
    column = jnp.sum(jnp.where(at_row == at_lane, line.astype(F32), 0.0), axis=1, keepdims=True).astype(jnp.int32)
    target, target_column = line // z.rows, column // z.rows
    earlier = (target_column == target) & (at_row < at_lane)
    rank = jnp.sum(jnp.where(earlier, 1.0, 0.0), axis=0, keepdims=True).astype(jnp.int32)
    shift = lax.rem(target - origin_ref[0] + z.peers, z.peers)
    shift_column = lax.rem(target_column - origin_ref[0] + z.peers, z.peers)
    for h in range(z.split):
        slot = shift * z.lines + h * z.cap + rank
        pick_ref[h] = jnp.where(iota((z.slots, z.rows), 0) == slot, 1.0, 0.0).astype(BF16)
    lane = iota((z.rows, LANES), 1)
    info_ref[...] = jnp.where(lane == 0, (column - target_column * z.rows + 1).astype(F32), 0.0)
    used = jnp.where(lane == shift_column, 1.0, 0.0)
    mask_ref[...] = jnp.max(used, axis=0, keepdims=True).astype(jnp.int32)
    for k in range(1, z.copies):
        for j in range(z.blocks):
            copies[(k - 1) * z.blocks + j].wait()
            at = slice(j * step, (j + 1) * step)
            parts[k - 1][:, at] = full_buf[k - 1, :, at].astype(BF16)


def agree_kernel(left, right, _, out):
    out[...] = jnp.maximum(left[...], right[...])


def choose_kernel(digits, left, right, *outs):
    total = jnp.maximum(left[...], right[...])
    lane = iota(total.shape, 1)
    for digit, out in zip(digits, outs):
        value = jnp.zeros(total.shape, jnp.int32)
        for i, s in enumerate(digit):
            value = value + jnp.where(lane == s, total << i, 0)
        out[0] = jnp.sum(value.astype(F32)).astype(jnp.int32)


def load_kernel(z, rep_ref, info_ref, master_hbm, one_hbm, two_hbm, full_hbm, master, one, two, own, meta_ref, sems):
    base = rep_ref[0] * z.width
    step = z.width // z.blocks
    copies = []
    for j in range(z.blocks):
        at = pl.ds(j * step, step)
        mine = pl.ds(pl.multiple_of(base + j * step, LANES), step)
        copies.append(
            [
                pltpu.make_async_copy(master_hbm.at[:, at], master.at[:, at], sems.at[0, j]),
                pltpu.make_async_copy(one_hbm.at[:, at], one.at[:, at], sems.at[1, j]),
                pltpu.make_async_copy(two_hbm.at[:, at], two.at[:, at], sems.at[2, j]),
                pltpu.make_async_copy(full_hbm.at[:, mine], own.at[:, at], sems.at[3, j]),
            ]
        )
    for i in range(4):
        for j in range(z.blocks):
            copies[j][i].start()
    part = jnp.zeros((z.rows, LANES), F32)
    for j in range(z.blocks):
        copies[j][0].wait()
        for at in range(j * step, (j + 1) * step, LANES):
            weights = 1.0 + ((iota((1, LANES), 1) + (base + at)) % 7).astype(F32) / 7.0
            part = part + master[:, at : at + LANES] * weights
    total = jnp.sum(part, axis=1, keepdims=True) * (1.0 / math.sqrt(z.width * z.copies))
    high = total.astype(BF16).astype(F32)
    middle = (total - high).astype(BF16).astype(F32)
    low = total - high - middle
    lane = iota((z.rows, LANES), 1)
    meta = jnp.where(lane == 1, high, jnp.where(lane == 2, middle, jnp.where(lane == 3, low, info_ref[...])))
    meta_ref[...] = meta.astype(BF16)
    for j in range(z.blocks):
        for i in range(1, 4):
            copies[j][i].wait()


def update_kernel(z, pick_ref, meta_ref, master, one, two, own, *refs):
    received, refs = refs[: z.copies - 1], refs[z.copies :]
    outs, rows_buf = refs[: z.peers], refs[z.peers]
    pick = jnp.concatenate([pick_ref[h] for h in range(z.split)], axis=1)
    for j in range(z.blocks):
        for h in range(z.split):
            for c in range(0, z.cb, z.sub):
                at = j * z.span + h * z.cb + c
                cols = slice(at, at + z.sub)
                summed = own[:, cols]
                for other in received:
                    summed = summed + other[:, cols].astype(F32)
                moved = master[:, cols]
                new_one = 0.9 * one[:, cols] + 0.1 * summed
                new_two = 0.95 * two[:, cols] + 0.05 * summed * summed
                update = new_one * (1.0 / (1.0 - 0.9**10)) / (jnp.sqrt(new_two * (1.0 / (1.0 - 0.95**10))) + 1e-08)
                new_master = moved - 0.05 * (update + 0.1 * moved)
                for i, value in enumerate((new_master, new_one, new_two)):
                    to = i * z.body + j * z.cb + c
                    rows_buf[h * z.rows : (h + 1) * z.rows, to : to + z.sub] = value.astype(BF16)
        for i in range(3):
            at = i * z.body + j * z.cb
            packed = jnp.dot(pick, rows_buf[:, at : at + z.cb], preferred_element_type=F32).astype(BF16)
            for s, out in enumerate(outs):
                out[:, at : at + z.cb] = packed[s * z.lines : (s + 1) * z.lines]
    meta = jnp.concatenate([meta_ref[...]] * z.split, axis=0)
    packed = jnp.dot(pick, meta, preferred_element_type=F32).astype(BF16)
    for s, out in enumerate(outs):
        out[:, 3 * z.body :] = packed[s * z.lines : (s + 1) * z.lines]


def gathered(refs, cols):
    return jnp.concatenate([ref[:, cols] for ref in refs], axis=0)


def placing(z, meta):
    offset = meta[:, :1].astype(F32).astype(jnp.int32)
    piece = lax.rem(iota((z.slots, 1), 0), z.lines) // z.cap
    wanted = jnp.where(offset > 0, offset - 1 + piece * z.rows, -1)
    return jnp.where(iota((z.slots, z.stacked), 1) == wanted, 1.0, 0.0).astype(BF16)


def placed(place, values):
    return lax.dot_general(place, values, (((0,), (0,)), ((), ())), preferred_element_type=F32)


def master_kernel(z, rep_ref, *refs):
    got, (new_master, params, half, place_out, master_buf, sems) = refs[: z.peers], refs[z.peers :]
    meta = gathered(got, slice(3 * z.body, 3 * z.body + LANES))
    place = placing(z, meta)
    place_out[...] = place
    copies = []
    for j in range(z.blocks):
        rows_out = placed(place, gathered(got, slice(j * z.cb, (j + 1) * z.cb)))
        for h in range(z.split):
            values = rows_out[h * z.rows : (h + 1) * z.rows]
            at = j * z.span + h * z.cb
            master_buf[:, at : at + z.cb] = values
            half[:, at : at + z.cb] = values.astype(BF16)
        at = pl.ds(j * z.span, z.span)
        there = pl.ds(pl.multiple_of(rep_ref[0] * z.width + j * z.span, LANES), z.span)
        copies.append(pltpu.make_async_copy(master_buf.at[:, at], new_master.at[:, at], sems.at[0, j]))
        copies.append(pltpu.make_async_copy(half.at[:, at], params.at[:, there], sems.at[1, j]))
        copies[-2].start()
        copies[-1].start()
    half[:, z.width :] = placed(place, meta)[: z.rows].astype(BF16)
    for copy in copies:
        copy.wait()


def place_one(z, i, place, got, out, buf, sems):
    copies = []
    for j in range(z.blocks):
        at = i * z.body + j * z.cb
        rows_out = placed(place, gathered(got, slice(at, at + z.cb)))
        for h in range(z.split):
            col = j * z.span + h * z.cb
            buf[:, col : col + z.cb] = rows_out[h * z.rows : (h + 1) * z.rows]
        cols = pl.ds(j * z.span, z.span)
        copies.append(pltpu.make_async_copy(buf.at[:, cols], out.at[:, cols], sems.at[j]))
        copies[-1].start()
    return copies


def one_kernel(z, place, *refs):
    got, (one_out, buf, sems) = refs[: z.peers], refs[z.peers :]
    for copy in place_one(z, 1, place[...], got, one_out, buf, sems):
        copy.wait()


def two_kernel(z, rep_ref, place, half, *refs):
    others, refs = refs[: z.copies - 1], refs[z.copies - 1 :]
    got, (_, params, two_out, checksum, buf, sems, param_sems) = refs[: z.peers], refs[z.peers :]
    copies = []
    for k, other in enumerate(others):
        replica = lax.rem(rep_ref[0] + z.copies - (k + 1), z.copies)
        there = pl.ds(pl.multiple_of(replica * z.width, LANES), z.width)
        copies.append(pltpu.make_async_copy(other.at[:, : z.width], params.at[:, there], param_sems.at[k]))
        copies[-1].start()
    copies += place_one(z, 2, place[...], got, two_out, buf, sems)
    sums = half[:, z.width :].astype(F32)
    for other in others:
        sums = sums + other[:, z.width :].astype(F32)
    lane = iota((z.rows, LANES), 1)
    column = jnp.sum(jnp.where((lane >= 1) & (lane <= 3), sums, 0.0), axis=1, keepdims=True)
    diagonal = iota((z.rows, z.rows), 0) == iota((z.rows, z.rows), 1)
    checksum[...] = jnp.sum(jnp.where(diagonal, column, 0.0), axis=0, keepdims=True)
    for copy in copies:
        copy.wait()


def shifted(value, axis, k, count):
    return lax.ppermute(value, axis, [(i, (i + k) % count) for i in range(count)])


def always_sent(peers):
    return sorted({min(3, peers - 1), peers // 2, peers - 1})


def shift_groups(peers):
    rest = [s for s in range(1, peers) if s not in always_sent(peers)]
    groups = -(-len(rest) // GROUP)
    return [rest[g::groups] for g in range(groups)]


def agree(used, stride, peers, after, compiler_params):
    vmem = pl.BlockSpec(memory_space=pltpu.VMEM)
    other = lax.ppermute(used, "fsdp", [(i, i ^ stride) for i in range(peers)])
    return pl.pallas_call(
        agree_kernel,
        out_shape=jax.ShapeDtypeStruct((1, LANES), jnp.int32),
        in_specs=[vmem, vmem, pl.BlockSpec(memory_space=pl.ANY)],
        out_specs=vmem,
        compiler_params=compiler_params,
        name="agree",
    )(used, other, after)


def digits_of(group):
    count = -(-len(group) // DIGIT)
    size = -(-len(group) // count)
    return [group[i : i + size] for i in range(0, len(group), size)]


def choose_branches(used, after, peers, compiler_params):
    vmem = pl.BlockSpec(memory_space=pltpu.VMEM)
    smem = pl.BlockSpec(memory_space=pltpu.SMEM)
    digits = [digit for group in shift_groups(peers) for digit in digits_of(group)]
    stride = 2
    while 2 * stride < peers:
        used = agree(used, stride, peers, after, compiler_params)
        stride *= 2
    other = lax.ppermute(used, "fsdp", [(i, i ^ stride) for i in range(peers)])
    return pl.pallas_call(
        functools.partial(choose_kernel, digits),
        out_shape=[pltpu.SMEM((1,), jnp.int32)] * len(digits),
        in_specs=[vmem, vmem],
        out_specs=[smem] * len(digits),
        compiler_params=compiler_params,
        name="choose",
    )(used, other)


def send_tree(peers, digits, numbers, sent, values):
    if not digits:
        return tuple(shifted(value, "fsdp", s, peers) if on else value for s, on, value in zip(*sent, values))

    def branch(used):
        on = [bool(used >> i & 1) for i in range(len(digits[0]))]

        def run(rest, operands):
            return send_tree(peers, digits[1:], rest, (sent[0], sent[1] + on), operands)

        return run

    branches = [branch(used) for used in range(1 << len(digits[0]))]
    return lax.switch(numbers[0], branches, numbers[1:], values)


def move(z, chunks, chosen):
    if chosen is None:
        got = lax.all_to_all(jnp.concatenate(chunks, axis=0), "fsdp", split_axis=0, concat_axis=0, tiled=True)
        return [got[s * z.lines : (s + 1) * z.lines] for s in range(z.peers)]
    got = list(chunks)
    always = always_sent(z.peers)
    for s in always:
        got[s] = shifted(chunks[s], "fsdp", s, z.peers)
    barred = lax.optimization_barrier((*chosen, *[got[s] for s in always]))
    chosen, moved = barred[: len(chosen)], barred[len(chosen) :]
    for s, value in zip(always, moved):
        got[s] = value
    numbers = [number[0] for number in chosen]
    for group in shift_groups(z.peers):
        digits = digits_of(group)
        mine, numbers = tuple(numbers[: len(digits)]), numbers[len(digits) :]
        values = send_tree(z.peers, digits, mine, (group, []), tuple(chunks[s] for s in group))
        for s, value in zip(group, values):
            got[s] = value
    return got


def shards(master, moment_one, moment_two, gradients, new_row):
    rows, width = master.shape
    peers, copies = lax.axis_size("fsdp"), lax.axis_size("replica")
    z = Sizes(rows, width, peers, copies)
    compiler_params = pltpu.CompilerParams(vmem_limit_bytes=VMEM_BYTES)
    smem = pl.BlockSpec(memory_space=pltpu.SMEM)
    vmem = pl.BlockSpec(memory_space=pltpu.VMEM)
    hbm = pl.BlockSpec(memory_space=pl.ANY)
    dma = pltpu.SemaphoreType.DMA

    replica = lax.axis_index("replica").astype(jnp.int32)
    rep = replica.reshape(1)
    by_shift = peers <= MOST_SHIFT_PEERS and peers & (peers - 1) == 0
    origin = (lax.axis_index("fsdp").astype(jnp.int32) if by_shift else jnp.int32(0)).reshape(1)
    state_in = [pltpu.with_memory_space_constraint(x, pltpu.HBM) for x in (master, moment_one, moment_two)]
    full = pltpu.with_memory_space_constraint(gradients[0], pltpu.HBM)

    part = jax.ShapeDtypeStruct((rows, width), BF16)
    pick, info, used, *parts = pl.pallas_call(
        functools.partial(prepare_kernel, z),
        out_shape=[
            jax.ShapeDtypeStruct((z.split, z.slots, rows), BF16),
            jax.ShapeDtypeStruct((rows, LANES), F32),
            jax.ShapeDtypeStruct((1, LANES), jnp.int32),
        ]
        + [part] * (copies - 1),
        in_specs=[smem, smem, hbm, hbm],
        out_specs=[vmem] * (copies + 2),
        scratch_shapes=[
            pltpu.VMEM((copies - 1, rows, width), F32),
            pltpu.VMEM((1, rows), jnp.int32),
            dma((copies - 1, z.blocks)),
            dma,
        ],
        compiler_params=compiler_params,
        cost_estimate=pl.CostEstimate(flops=1 << 30, bytes_accessed=1, transcendentals=0),
        name="prepare",
    )(rep, origin, pltpu.with_memory_space_constraint(new_row.reshape(1, rows), pltpu.HBM), full)
    received = [shifted(value, "replica", k + 1, copies) for k, value in enumerate(parts)]

    loaded = jax.ShapeDtypeStruct((rows, width), F32)
    *state, meta = pl.pallas_call(
        functools.partial(load_kernel, z),
        out_shape=[loaded, loaded, loaded, loaded, jax.ShapeDtypeStruct((rows, LANES), BF16)],
        in_specs=[smem, vmem, hbm, hbm, hbm, hbm],
        out_specs=[vmem] * 5,
        scratch_shapes=[dma((4, z.blocks))],
        compiler_params=compiler_params,
        cost_estimate=pl.CostEstimate(flops=1 << 30, bytes_accessed=1, transcendentals=0),
        name="load",
    )(rep, info, *state_in, full)

    if by_shift:
        used = agree(used, 1, peers, meta, compiler_params)
    chunks = pl.pallas_call(
        functools.partial(update_kernel, z),
        out_shape=[jax.ShapeDtypeStruct((z.lines, z.payload), BF16)] * peers,
        in_specs=[vmem] * (5 + copies) + [hbm],
        out_specs=[vmem] * peers,
        scratch_shapes=[pltpu.VMEM((z.stacked, 3 * z.body), BF16)],
        compiler_params=compiler_params,
        cost_estimate=pl.CostEstimate(
            flops=6 * z.slots * z.stacked * z.body, bytes_accessed=24 * rows * width, transcendentals=rows * width
        ),
        name="update",
    )(pick, meta, *state, *received, used)

    chosen = choose_branches(used, chunks[0], peers, compiler_params) if by_shift else None
    got = move(z, chunks, chosen)

    new_master, params, half, place = pl.pallas_call(
        functools.partial(master_kernel, z),
        out_shape=(
            jax.ShapeDtypeStruct((rows, width), F32),
            jax.ShapeDtypeStruct((rows, width * copies), BF16),
            jax.ShapeDtypeStruct((rows, width + LANES), BF16),
            jax.ShapeDtypeStruct((z.slots, z.stacked), BF16),
        ),
        in_specs=[smem] + [vmem] * peers,
        out_specs=(hbm, hbm, vmem, vmem),
        scratch_shapes=[pltpu.VMEM((rows, width), F32), dma((2, z.blocks))],
        compiler_params=compiler_params,
        cost_estimate=pl.CostEstimate(
            flops=2 * z.slots * z.stacked * z.body, bytes_accessed=10 * rows * width, transcendentals=0
        ),
        name="place_master",
    )(rep, *got)
    others = [shifted(half, "replica", k, copies) for k in range(1, copies)]

    new_one = pl.pallas_call(
        functools.partial(one_kernel, z),
        out_shape=jax.ShapeDtypeStruct((rows, width), F32),
        in_specs=[vmem] * (peers + 1),
        out_specs=hbm,
        scratch_shapes=[pltpu.VMEM((rows, width), F32), dma((z.blocks,))],
        compiler_params=compiler_params,
        cost_estimate=pl.CostEstimate(
            flops=2 * z.slots * z.stacked * z.body, bytes_accessed=8 * rows * width, transcendentals=0
        ),
        name="place_one",
    )(place, *got)

    params, new_two, checksum = pl.pallas_call(
        functools.partial(two_kernel, z),
        out_shape=(
            jax.ShapeDtypeStruct((rows, width * copies), BF16),
            jax.ShapeDtypeStruct((rows, width), F32),
            jax.ShapeDtypeStruct((1, rows), F32),
        ),
        in_specs=[smem] + [vmem] * (copies + peers + 1) + [hbm],
        out_specs=(hbm, hbm, vmem),
        scratch_shapes=[pltpu.VMEM((rows, width), F32), dma((z.blocks,)), dma((max(1, copies - 1),))],
        input_output_aliases={copies + peers + 2: 0},
        compiler_params=compiler_params,
        cost_estimate=pl.CostEstimate(
            flops=2 * z.slots * z.stacked * z.body, bytes_accessed=12 * rows * width, transcendentals=0
        ),
        name="place_two",
    )(rep, place, half, *others, *got, params)
    return (new_master, new_one, new_two, params, checksum.reshape(rows))


def solution(mesh):
    return jax.shard_map(
        shards,
        mesh=mesh,
        in_specs=(
            P("fsdp", "replica"),
            P("fsdp", "replica"),
            P("fsdp", "replica"),
            P("replica", "fsdp", None),
            P("fsdp"),
        ),
        out_specs=(
            P("fsdp", "replica"),
            P("fsdp", "replica"),
            P("fsdp", "replica"),
            P("fsdp", None),
            P("fsdp"),
        ),
        check_vma=False,
    )
```

```python
import functools
import math

import jax
import jax.numpy as jnp
from jax import lax
from jax.experimental import pallas as pl
from jax.experimental.pallas import tpu as pltpu
from jax.sharding import PartitionSpec as P

LANES = 128
TILE_ROWS = 16
MIB = 1024 * 1024
VMEM_BYTES = 48 * MIB
MOST_SHIFT_PEERS = 16
GROUP = 3
DIGIT = 3
F32 = jnp.float32
BF16 = jnp.bfloat16


def iota(shape, axis):
    return lax.broadcasted_iota(jnp.int32, shape, axis)


class Sizes:
    def __init__(self, rows, width, peers, copies):
        self.rows, self.width, self.peers, self.copies = rows, width, peers, copies
        self.cap = max(2, 2 * rows // peers)
        self.split = max(1, TILE_ROWS // self.cap)
        self.lines = self.cap * self.split
        self.slots = peers * self.lines
        self.stacked = self.split * rows
        self.body = width // self.split
        self.cb = math.gcd(self.body, 512)
        self.blocks = self.body // self.cb
        self.span = self.split * self.cb
        self.sub = math.gcd(self.cb, 256)
        self.payload = 3 * self.body + LANES


def prepare_kernel(z, rep_ref, origin_ref, new_row_hbm, full_hbm, pick_ref, info_ref, mask_ref, *refs):
    parts, (full_buf, line_buf, sems, line_sem) = refs[: z.copies - 1], refs[z.copies - 1 :]
    step = z.width // z.blocks
    line_copy = pltpu.make_async_copy(new_row_hbm, line_buf, line_sem)
    line_copy.start()
    copies = []
    for k in range(1, z.copies):
        other = lax.rem(rep_ref[0] + k, z.copies)
        for j in range(z.blocks):
            there = pl.ds(pl.multiple_of(other * z.width + j * step, LANES), step)
            copies.append(
                pltpu.make_async_copy(
                    full_hbm.at[:, there], full_buf.at[k - 1, :, pl.ds(j * step, step)], sems.at[k - 1, j]
                )
            )
            copies[-1].start()
    line_copy.wait()
    line = line_buf[...]
    at_row, at_lane = iota((z.rows, z.rows), 0), iota((z.rows, z.rows), 1)
    column = jnp.sum(jnp.where(at_row == at_lane, line.astype(F32), 0.0), axis=1, keepdims=True).astype(jnp.int32)
    target, target_column = line // z.rows, column // z.rows
    earlier = (target_column == target) & (at_row < at_lane)
    rank = jnp.sum(jnp.where(earlier, 1.0, 0.0), axis=0, keepdims=True).astype(jnp.int32)
    shift = lax.rem(target - origin_ref[0] + z.peers, z.peers)
    shift_column = lax.rem(target_column - origin_ref[0] + z.peers, z.peers)
    for h in range(z.split):
        slot = shift * z.lines + h * z.cap + rank
        pick_ref[h] = jnp.where(iota((z.slots, z.rows), 0) == slot, 1.0, 0.0).astype(BF16)
    lane = iota((z.rows, LANES), 1)
    info_ref[...] = jnp.where(lane == 0, (column - target_column * z.rows + 1).astype(F32), 0.0)
    used = jnp.where(lane == shift_column, 1.0, 0.0)
    mask_ref[...] = jnp.max(used, axis=0, keepdims=True).astype(jnp.int32)
    for k in range(1, z.copies):
        for j in range(z.blocks):
            copies[(k - 1) * z.blocks + j].wait()
            at = slice(j * step, (j + 1) * step)
            parts[k - 1][:, at] = full_buf[k - 1, :, at].astype(BF16)


def agree_kernel(left, right, _, out):
    out[...] = jnp.maximum(left[...], right[...])


def choose_kernel(digits, left, right, *outs):
    total = jnp.maximum(left[...], right[...])
    lane = iota(total.shape, 1)
    for digit, out in zip(digits, outs):
        value = jnp.zeros(total.shape, jnp.int32)
        for i, s in enumerate(digit):
            value = value + jnp.where(lane == s, total << i, 0)
        out[0] = jnp.sum(value.astype(F32)).astype(jnp.int32)


def load_kernel(z, rep_ref, info_ref, master_hbm, one_hbm, two_hbm, full_hbm, master, one, two, own, meta_ref, sems):
    base = rep_ref[0] * z.width
    step = z.width // z.blocks
    copies = []
    for j in range(z.blocks):
        at = pl.ds(j * step, step)
        mine = pl.ds(pl.multiple_of(base + j * step, LANES), step)
        copies.append(
            [
                pltpu.make_async_copy(master_hbm.at[:, at], master.at[:, at], sems.at[0, j]),
                pltpu.make_async_copy(one_hbm.at[:, at], one.at[:, at], sems.at[1, j]),
                pltpu.make_async_copy(two_hbm.at[:, at], two.at[:, at], sems.at[2, j]),
                pltpu.make_async_copy(full_hbm.at[:, mine], own.at[:, at], sems.at[3, j]),
            ]
        )
    for i in range(4):
        for j in range(z.blocks):
            copies[j][i].start()
    part = jnp.zeros((z.rows, LANES), F32)
    for j in range(z.blocks):
        copies[j][0].wait()
        for at in range(j * step, (j + 1) * step, LANES):
            weights = 1.0 + ((iota((1, LANES), 1) + (base + at)) % 7).astype(F32) / 7.0
            part = part + master[:, at : at + LANES] * weights
    total = jnp.sum(part, axis=1, keepdims=True) * (1.0 / math.sqrt(z.width * z.copies))
    high = total.astype(BF16).astype(F32)
    middle = (total - high).astype(BF16).astype(F32)
    low = total - high - middle
    lane = iota((z.rows, LANES), 1)
    meta = jnp.where(lane == 1, high, jnp.where(lane == 2, middle, jnp.where(lane == 3, low, info_ref[...])))
    meta_ref[...] = meta.astype(BF16)
    for j in range(z.blocks):
        for i in range(1, 4):
            copies[j][i].wait()


def update_kernel(z, pick_ref, meta_ref, master, one, two, own, *refs):
    received, refs = refs[: z.copies - 1], refs[z.copies :]
    outs, rows_buf = refs[: z.peers], refs[z.peers]
    pick = jnp.concatenate([pick_ref[h] for h in range(z.split)], axis=1)
    for j in range(z.blocks):
        for h in range(z.split):
            for c in range(0, z.cb, z.sub):
                at = j * z.span + h * z.cb + c
                cols = slice(at, at + z.sub)
                summed = own[:, cols]
                for other in received:
                    summed = summed + other[:, cols].astype(F32)
                moved = master[:, cols]
                new_one = 0.9 * one[:, cols] + 0.1 * summed
                new_two = 0.95 * two[:, cols] + 0.05 * summed * summed
                update = new_one * (1.0 / (1.0 - 0.9**10)) / (jnp.sqrt(new_two * (1.0 / (1.0 - 0.95**10))) + 1e-08)
                new_master = moved - 0.05 * (update + 0.1 * moved)
                for i, value in enumerate((new_master, new_one, new_two)):
                    to = i * z.body + j * z.cb + c
                    rows_buf[h * z.rows : (h + 1) * z.rows, to : to + z.sub] = value.astype(BF16)
        for i in range(3):
            at = i * z.body + j * z.cb
            packed = jnp.dot(pick, rows_buf[:, at : at + z.cb], preferred_element_type=F32).astype(BF16)
            for s, out in enumerate(outs):
                out[:, at : at + z.cb] = packed[s * z.lines : (s + 1) * z.lines]
    meta = jnp.concatenate([meta_ref[...]] * z.split, axis=0)
    packed = jnp.dot(pick, meta, preferred_element_type=F32).astype(BF16)
    for s, out in enumerate(outs):
        out[:, 3 * z.body :] = packed[s * z.lines : (s + 1) * z.lines]


def gathered(refs, cols):
    return jnp.concatenate([ref[:, cols] for ref in refs], axis=0)


def placing(z, meta):
    offset = meta[:, :1].astype(F32).astype(jnp.int32)
    piece = lax.rem(iota((z.slots, 1), 0), z.lines) // z.cap
    wanted = jnp.where(offset > 0, offset - 1 + piece * z.rows, -1)
    return jnp.where(iota((z.slots, z.stacked), 1) == wanted, 1.0, 0.0).astype(BF16)


def placed(place, values):
    return lax.dot_general(place, values, (((0,), (0,)), ((), ())), preferred_element_type=F32)


def half_kernel(z, *refs):
    got, (half, place_out) = refs[: z.peers], refs[z.peers :]
    meta = gathered(got, slice(3 * z.body, 3 * z.body + LANES))
    place = placing(z, meta)
    place_out[...] = place
    for j in range(z.blocks):
        rows_out = placed(place, gathered(got, slice(j * z.cb, (j + 1) * z.cb))).astype(BF16)
        for h in range(z.split):
            at = j * z.span + h * z.cb
            half[:, at : at + z.cb] = rows_out[h * z.rows : (h + 1) * z.rows]
    half[:, z.width :] = placed(place, meta)[: z.rows].astype(BF16)


def place_moment(z, i, place, got, out, buf, sems):
    copies = []
    for j in range(z.blocks):
        at = i * z.body + j * z.cb
        rows_out = placed(place, gathered(got, slice(at, at + z.cb)))
        for h in range(z.split):
            col = j * z.span + h * z.cb
            buf[:, col : col + z.cb] = rows_out[h * z.rows : (h + 1) * z.rows]
        cols = pl.ds(j * z.span, z.span)
        copies.append(pltpu.make_async_copy(buf.at[:, cols], out.at[:, cols], sems.at[j]))
        copies[-1].start()
    return copies


def one_kernel(z, rep_ref, half, place, *refs):
    got, (new_master, params, one_out, master_buf, one_buf, sems) = refs[: z.peers], refs[z.peers :]
    there = pl.ds(pl.multiple_of(rep_ref[0] * z.width, LANES), z.width)
    copies = [pltpu.make_async_copy(half.at[:, : z.width], params.at[:, there], sems.at[0, 0])]
    copies[0].start()
    for j in range(z.blocks):
        at = slice(j * z.span, (j + 1) * z.span)
        master_buf[:, at] = half[:, at].astype(F32)
        cols = pl.ds(j * z.span, z.span)
        copies.append(pltpu.make_async_copy(master_buf.at[:, cols], new_master.at[:, cols], sems.at[1, j]))
        copies[-1].start()
    copies += place_moment(z, 1, place[...], got, one_out, one_buf, sems.at[2])
    for copy in copies:
        copy.wait()


def two_kernel(z, rep_ref, half, place, *refs):
    others, refs = refs[: z.copies - 1], refs[z.copies - 1 :]
    got, (_, params, two_out, checksum, buf, sems, param_sems) = refs[: z.peers], refs[z.peers :]
    copies = []
    for k, other in enumerate(others):
        replica = lax.rem(rep_ref[0] + z.copies - (k + 1), z.copies)
        there = pl.ds(pl.multiple_of(replica * z.width, LANES), z.width)
        copies.append(pltpu.make_async_copy(other.at[:, : z.width], params.at[:, there], param_sems.at[k]))
        copies[-1].start()
    copies += place_moment(z, 2, place[...], got, two_out, buf, sems)
    sums = half[:, z.width :].astype(F32)
    for other in others:
        sums = sums + other[:, z.width :].astype(F32)
    lane = iota((z.rows, LANES), 1)
    column = jnp.sum(jnp.where((lane >= 1) & (lane <= 3), sums, 0.0), axis=1, keepdims=True)
    diagonal = iota((z.rows, z.rows), 0) == iota((z.rows, z.rows), 1)
    checksum[...] = jnp.sum(jnp.where(diagonal, column, 0.0), axis=0, keepdims=True)
    for copy in copies:
        copy.wait()


def shifted(value, axis, k, count):
    return lax.ppermute(value, axis, [(i, (i + k) % count) for i in range(count)])


def always_sent(peers):
    return sorted({min(3, peers - 1), peers // 2, peers - 1})


def shift_groups(peers):
    rest = [s for s in range(1, peers) if s not in always_sent(peers)]
    groups = -(-len(rest) // GROUP)
    return [rest[g::groups] for g in range(groups)]


def agree(used, stride, peers, after, compiler_params):
    vmem = pl.BlockSpec(memory_space=pltpu.VMEM)
    other = lax.ppermute(used, "fsdp", [(i, i ^ stride) for i in range(peers)])
    return pl.pallas_call(
        agree_kernel,
        out_shape=jax.ShapeDtypeStruct((1, LANES), jnp.int32),
        in_specs=[vmem, vmem, pl.BlockSpec(memory_space=pl.ANY)],
        out_specs=vmem,
        compiler_params=compiler_params,
        name="agree",
    )(used, other, after)


def digits_of(group):
    count = -(-len(group) // DIGIT)
    size = -(-len(group) // count)
    return [group[i : i + size] for i in range(0, len(group), size)]


def choose_branches(used, after, peers, compiler_params):
    vmem = pl.BlockSpec(memory_space=pltpu.VMEM)
    smem = pl.BlockSpec(memory_space=pltpu.SMEM)
    digits = [digit for group in shift_groups(peers) for digit in digits_of(group)]
    stride = peers // 4
    while stride > 1:
        used = agree(used, stride, peers, after, compiler_params)
        stride //= 2
    other = lax.ppermute(used, "fsdp", [(i, i ^ stride) for i in range(peers)])
    return pl.pallas_call(
        functools.partial(choose_kernel, digits),
        out_shape=[pltpu.SMEM((1,), jnp.int32)] * len(digits),
        in_specs=[vmem, vmem],
        out_specs=[smem] * len(digits),
        compiler_params=compiler_params,
        name="choose",
    )(used, other)


def send_tree(peers, digits, numbers, sent, values):
    if not digits:
        return tuple(shifted(value, "fsdp", s, peers) if on else value for s, on, value in zip(*sent, values))

    def branch(used):
        on = [bool(used >> i & 1) for i in range(len(digits[0]))]

        def run(rest, operands):
            return send_tree(peers, digits[1:], rest, (sent[0], sent[1] + on), operands)

        return run

    branches = [branch(used) for used in range(1 << len(digits[0]))]
    return lax.switch(numbers[0], branches, numbers[1:], values)


def move(z, chunks, chosen):
    if chosen is None:
        got = lax.all_to_all(jnp.concatenate(chunks, axis=0), "fsdp", split_axis=0, concat_axis=0, tiled=True)
        return [got[s * z.lines : (s + 1) * z.lines] for s in range(z.peers)]
    got = list(chunks)
    always = always_sent(z.peers)
    for s in always:
        got[s] = shifted(chunks[s], "fsdp", s, z.peers)
    barred = lax.optimization_barrier((*chosen, *[got[s] for s in always]))
    chosen, moved = barred[: len(chosen)], barred[len(chosen) :]
    for s, value in zip(always, moved):
        got[s] = value
    numbers = [number[0] for number in chosen]
    for group in shift_groups(z.peers):
        digits = digits_of(group)
        mine, numbers = tuple(numbers[: len(digits)]), numbers[len(digits) :]
        values = send_tree(z.peers, digits, mine, (group, []), tuple(chunks[s] for s in group))
        for s, value in zip(group, values):
            got[s] = value
    return got


def shards(master, moment_one, moment_two, gradients, new_row):
    rows, width = master.shape
    peers, copies = lax.axis_size("fsdp"), lax.axis_size("replica")
    z = Sizes(rows, width, peers, copies)
    compiler_params = pltpu.CompilerParams(vmem_limit_bytes=VMEM_BYTES)
    smem = pl.BlockSpec(memory_space=pltpu.SMEM)
    vmem = pl.BlockSpec(memory_space=pltpu.VMEM)
    hbm = pl.BlockSpec(memory_space=pl.ANY)
    dma = pltpu.SemaphoreType.DMA

    replica = lax.axis_index("replica").astype(jnp.int32)
    rep = replica.reshape(1)
    by_shift = peers <= MOST_SHIFT_PEERS and peers & (peers - 1) == 0
    origin = (lax.axis_index("fsdp").astype(jnp.int32) if by_shift else jnp.int32(0)).reshape(1)
    state_in = [pltpu.with_memory_space_constraint(x, pltpu.HBM) for x in (master, moment_one, moment_two)]
    full = pltpu.with_memory_space_constraint(gradients[0], pltpu.HBM)

    part = jax.ShapeDtypeStruct((rows, width), BF16)
    pick, info, used, *parts = pl.pallas_call(
        functools.partial(prepare_kernel, z),
        out_shape=[
            jax.ShapeDtypeStruct((z.split, z.slots, rows), BF16),
            jax.ShapeDtypeStruct((rows, LANES), F32),
            jax.ShapeDtypeStruct((1, LANES), jnp.int32),
        ]
        + [part] * (copies - 1),
        in_specs=[smem, smem, hbm, hbm],
        out_specs=[vmem] * (copies + 2),
        scratch_shapes=[
            pltpu.VMEM((copies - 1, rows, width), F32),
            pltpu.VMEM((1, rows), jnp.int32),
            dma((copies - 1, z.blocks)),
            dma,
        ],
        compiler_params=compiler_params,
        cost_estimate=pl.CostEstimate(flops=1 << 30, bytes_accessed=1, transcendentals=0),
        name="prepare",
    )(rep, origin, pltpu.with_memory_space_constraint(new_row.reshape(1, rows), pltpu.HBM), full)
    received = [shifted(value, "replica", k + 1, copies) for k, value in enumerate(parts)]

    loaded = jax.ShapeDtypeStruct((rows, width), F32)
    *state, meta = pl.pallas_call(
        functools.partial(load_kernel, z),
        out_shape=[loaded, loaded, loaded, loaded, jax.ShapeDtypeStruct((rows, LANES), BF16)],
        in_specs=[smem, vmem, hbm, hbm, hbm, hbm],
        out_specs=[vmem] * 5,
        scratch_shapes=[dma((4, z.blocks))],
        compiler_params=compiler_params,
        cost_estimate=pl.CostEstimate(flops=1 << 30, bytes_accessed=1, transcendentals=0),
        name="load",
    )(rep, info, *state_in, full)

    if by_shift:
        used = agree(used, peers // 2, peers, meta, compiler_params)
    chunks = pl.pallas_call(
        functools.partial(update_kernel, z),
        out_shape=[jax.ShapeDtypeStruct((z.lines, z.payload), BF16)] * peers,
        in_specs=[vmem] * (5 + copies) + [hbm],
        out_specs=[vmem] * peers,
        scratch_shapes=[pltpu.VMEM((z.stacked, 3 * z.body), BF16)],
        compiler_params=compiler_params,
        cost_estimate=pl.CostEstimate(
            flops=6 * z.slots * z.stacked * z.body, bytes_accessed=24 * rows * width, transcendentals=rows * width
        ),
        name="update",
    )(pick, meta, *state, *received, used)

    chosen = choose_branches(used, chunks[0], peers, compiler_params) if by_shift else None
    got = move(z, chunks, chosen)

    wide = jax.ShapeDtypeStruct((rows, width), F32)
    full_params = jax.ShapeDtypeStruct((rows, width * copies), BF16)
    half, place = pl.pallas_call(
        functools.partial(half_kernel, z),
        out_shape=(
            jax.ShapeDtypeStruct((rows, width + LANES), BF16),
            jax.ShapeDtypeStruct((z.slots, z.stacked), BF16),
        ),
        in_specs=[vmem] * peers,
        out_specs=(vmem, vmem),
        compiler_params=compiler_params,
        name="place_half",
    )(*got)
    others = [shifted(half, "replica", k, copies) for k in range(1, copies)]

    new_master, params, new_one = pl.pallas_call(
        functools.partial(one_kernel, z),
        out_shape=(wide, full_params, wide),
        in_specs=[smem] + [vmem] * (peers + 2),
        out_specs=(hbm, hbm, hbm),
        scratch_shapes=[pltpu.VMEM((rows, width), F32)] * 2 + [dma((3, z.blocks))],
        compiler_params=compiler_params,
        cost_estimate=pl.CostEstimate(
            flops=2 * z.slots * z.stacked * z.body, bytes_accessed=12 * rows * width, transcendentals=0
        ),
        name="place_one",
    )(rep, half, place, *got)

    params, new_two, checksum = pl.pallas_call(
        functools.partial(two_kernel, z),
        out_shape=(full_params, wide, jax.ShapeDtypeStruct((1, rows), F32)),
        in_specs=[smem] + [vmem] * (copies + peers + 1) + [hbm],
        out_specs=(hbm, hbm, vmem),
        scratch_shapes=[pltpu.VMEM((rows, width), F32), dma((z.blocks,)), dma((max(1, copies - 1),))],
        input_output_aliases={copies + peers + 2: 0},
        compiler_params=compiler_params,
        cost_estimate=pl.CostEstimate(
            flops=2 * z.slots * z.stacked * z.body, bytes_accessed=12 * rows * width, transcendentals=0
        ),
        name="place_two",
    )(rep, half, place, *others, *got, params)
    return (new_master, new_one, new_two, params, checksum.reshape(rows))


def solution(mesh):
    return jax.shard_map(
        shards,
        mesh=mesh,
        in_specs=(
            P("fsdp", "replica"),
            P("fsdp", "replica"),
            P("fsdp", "replica"),
            P("replica", "fsdp", None),
            P("fsdp"),
        ),
        out_specs=(
            P("fsdp", "replica"),
            P("fsdp", "replica"),
            P("fsdp", "replica"),
            P("fsdp", None),
            P("fsdp"),
        ),
        check_vma=False,
    )
```

```python
import functools
import math

import jax
import jax.numpy as jnp
from jax import lax
from jax.experimental import pallas as pl
from jax.experimental.pallas import tpu as pltpu
from jax.sharding import PartitionSpec as P

LANES = 128
TILE_ROWS = 16
MIB = 1024 * 1024
VMEM_BYTES = 48 * MIB
MOST_SHIFT_PEERS = 16
GROUP = 3
DIGIT = 3
F32 = jnp.float32
BF16 = jnp.bfloat16


def iota(shape, axis):
    return lax.broadcasted_iota(jnp.int32, shape, axis)


class Sizes:
    def __init__(self, rows, width, peers, copies):
        self.rows, self.width, self.peers, self.copies = rows, width, peers, copies
        self.cap = max(2, 2 * rows // peers)
        self.split = max(1, TILE_ROWS // self.cap)
        self.lines = self.cap * self.split
        self.slots = peers * self.lines
        self.stacked = self.split * rows
        self.body = width // self.split
        self.cb = math.gcd(self.body, 512)
        self.blocks = self.body // self.cb
        self.span = self.split * self.cb
        self.sub = math.gcd(self.cb, 256)
        self.payload = 3 * self.body + LANES


def prepare_kernel(z, rep_ref, origin_ref, new_row_hbm, full_hbm, pick_ref, info_ref, mask_ref, *refs):
    parts, (full_buf, line_buf, sems, line_sem) = refs[: z.copies - 1], refs[z.copies - 1 :]
    step = z.width // z.blocks
    line_copy = pltpu.make_async_copy(new_row_hbm, line_buf, line_sem)
    line_copy.start()
    copies = []
    for k in range(1, z.copies):
        other = lax.rem(rep_ref[0] + k, z.copies)
        for j in range(z.blocks):
            there = pl.ds(pl.multiple_of(other * z.width + j * step, LANES), step)
            copies.append(
                pltpu.make_async_copy(
                    full_hbm.at[:, there], full_buf.at[k - 1, :, pl.ds(j * step, step)], sems.at[k - 1, j]
                )
            )
            copies[-1].start()
    line_copy.wait()
    line = line_buf[...]
    at_row, at_lane = iota((z.rows, z.rows), 0), iota((z.rows, z.rows), 1)
    column = jnp.sum(jnp.where(at_row == at_lane, line.astype(F32), 0.0), axis=1, keepdims=True).astype(jnp.int32)
    target, target_column = line // z.rows, column // z.rows
    earlier = (target_column == target) & (at_row < at_lane)
    rank = jnp.sum(jnp.where(earlier, 1.0, 0.0), axis=0, keepdims=True).astype(jnp.int32)
    shift = lax.rem(target - origin_ref[0] + z.peers, z.peers)
    shift_column = lax.rem(target_column - origin_ref[0] + z.peers, z.peers)
    for h in range(z.split):
        slot = shift * z.lines + h * z.cap + rank
        pick_ref[h] = jnp.where(iota((z.slots, z.rows), 0) == slot, 1.0, 0.0).astype(BF16)
    lane = iota((z.rows, LANES), 1)
    info_ref[...] = jnp.where(lane == 0, (column - target_column * z.rows + 1).astype(F32), 0.0)
    used = jnp.where(lane == shift_column, 1.0, 0.0)
    mask_ref[...] = jnp.max(used, axis=0, keepdims=True).astype(jnp.int32)
    for k in range(1, z.copies):
        for j in range(z.blocks):
            copies[(k - 1) * z.blocks + j].wait()
            at = slice(j * step, (j + 1) * step)
            parts[k - 1][:, at] = full_buf[k - 1, :, at].astype(BF16)


def agree_kernel(left, right, _, out):
    out[...] = jnp.maximum(left[...], right[...])


def choose_kernel(digits, left, right, *outs):
    total = jnp.maximum(left[...], right[...])
    lane = iota(total.shape, 1)
    for digit, out in zip(digits, outs):
        value = jnp.zeros(total.shape, jnp.int32)
        for i, s in enumerate(digit):
            value = value + jnp.where(lane == s, total << i, 0)
        out[0] = jnp.sum(value.astype(F32)).astype(jnp.int32)


def load_kernel(z, rep_ref, info_ref, master_hbm, one_hbm, two_hbm, full_hbm, master, one, two, own, meta_ref, sems):
    base = rep_ref[0] * z.width
    step = z.width // z.blocks
    copies = []
    for j in range(z.blocks):
        at = pl.ds(j * step, step)
        mine = pl.ds(pl.multiple_of(base + j * step, LANES), step)
        copies.append(
            [
                pltpu.make_async_copy(master_hbm.at[:, at], master.at[:, at], sems.at[0, j]),
                pltpu.make_async_copy(one_hbm.at[:, at], one.at[:, at], sems.at[1, j]),
                pltpu.make_async_copy(two_hbm.at[:, at], two.at[:, at], sems.at[2, j]),
                pltpu.make_async_copy(full_hbm.at[:, mine], own.at[:, at], sems.at[3, j]),
            ]
        )
    for i in range(4):
        for j in range(z.blocks):
            copies[j][i].start()
    part = jnp.zeros((z.rows, LANES), F32)
    for j in range(z.blocks):
        copies[j][0].wait()
        for at in range(j * step, (j + 1) * step, LANES):
            weights = 1.0 + ((iota((1, LANES), 1) + (base + at)) % 7).astype(F32) / 7.0
            part = part + master[:, at : at + LANES] * weights
    total = jnp.sum(part, axis=1, keepdims=True) * (1.0 / math.sqrt(z.width * z.copies))
    high = total.astype(BF16).astype(F32)
    middle = (total - high).astype(BF16).astype(F32)
    low = total - high - middle
    lane = iota((z.rows, LANES), 1)
    meta = jnp.where(lane == 1, high, jnp.where(lane == 2, middle, jnp.where(lane == 3, low, info_ref[...])))
    meta_ref[...] = meta.astype(BF16)
    for j in range(z.blocks):
        for i in range(1, 4):
            copies[j][i].wait()


def update_kernel(z, pick_ref, meta_ref, master, one, two, own, *refs):
    received, refs = refs[: z.copies - 1], refs[z.copies :]
    outs, rows_buf = refs[: z.peers], refs[z.peers]
    pick = jnp.concatenate([pick_ref[h] for h in range(z.split)], axis=1)
    for j in range(z.blocks):
        for h in range(z.split):
            for c in range(0, z.cb, z.sub):
                at = j * z.span + h * z.cb + c
                cols = slice(at, at + z.sub)
                summed = own[:, cols]
                for other in received:
                    summed = summed + other[:, cols].astype(F32)
                moved = master[:, cols]
                new_one = 0.9 * one[:, cols] + 0.1 * summed
                new_two = 0.95 * two[:, cols] + 0.05 * summed * summed
                update = new_one * (1.0 / (1.0 - 0.9**10)) / (jnp.sqrt(new_two * (1.0 / (1.0 - 0.95**10))) + 1e-08)
                new_master = moved - 0.05 * (update + 0.1 * moved)
                for i, value in enumerate((new_master, new_one, new_two)):
                    to = i * z.body + j * z.cb + c
                    rows_buf[h * z.rows : (h + 1) * z.rows, to : to + z.sub] = value.astype(BF16)
        for i in range(3):
            at = i * z.body + j * z.cb
            packed = jnp.dot(pick, rows_buf[:, at : at + z.cb], preferred_element_type=F32).astype(BF16)
            for s, out in enumerate(outs):
                out[:, at : at + z.cb] = packed[s * z.lines : (s + 1) * z.lines]
    meta = jnp.concatenate([meta_ref[...]] * z.split, axis=0)
    packed = jnp.dot(pick, meta, preferred_element_type=F32).astype(BF16)
    for s, out in enumerate(outs):
        out[:, 3 * z.body :] = packed[s * z.lines : (s + 1) * z.lines]


def gathered(refs, cols):
    return jnp.concatenate([ref[:, cols] for ref in refs], axis=0)


def placing(z, meta):
    offset = meta[:, :1].astype(F32).astype(jnp.int32)
    piece = lax.rem(iota((z.slots, 1), 0), z.lines) // z.cap
    wanted = jnp.where(offset > 0, offset - 1 + piece * z.rows, -1)
    return jnp.where(iota((z.slots, z.stacked), 1) == wanted, 1.0, 0.0).astype(BF16)


def placed(place, values):
    return lax.dot_general(place, values, (((0,), (0,)), ((), ())), preferred_element_type=F32)


def half_kernel(z, *refs):
    got, (half, place_out) = refs[: z.peers], refs[z.peers :]
    meta = gathered(got, slice(3 * z.body, 3 * z.body + LANES))
    place = placing(z, meta)
    place_out[...] = place
    for j in range(z.blocks):
        rows_out = placed(place, gathered(got, slice(j * z.cb, (j + 1) * z.cb))).astype(BF16)
        for h in range(z.split):
            at = j * z.span + h * z.cb
            half[:, at : at + z.cb] = rows_out[h * z.rows : (h + 1) * z.rows]
    half[:, z.width :] = placed(place, meta)[: z.rows].astype(BF16)


def place_moment(z, i, place, got, out, buf, sems):
    copies = []
    for j in range(z.blocks):
        at = i * z.body + j * z.cb
        rows_out = placed(place, gathered(got, slice(at, at + z.cb)))
        for h in range(z.split):
            col = j * z.span + h * z.cb
            buf[:, col : col + z.cb] = rows_out[h * z.rows : (h + 1) * z.rows]
        cols = pl.ds(j * z.span, z.span)
        copies.append(pltpu.make_async_copy(buf.at[:, cols], out.at[:, cols], sems.at[j]))
        copies[-1].start()
    return copies


def one_kernel(z, rep_ref, half, place, *refs):
    got, (new_master, params, one_out, master_buf, one_buf, sems) = refs[: z.peers], refs[z.peers :]
    there = pl.ds(pl.multiple_of(rep_ref[0] * z.width, LANES), z.width)
    copies = [pltpu.make_async_copy(half.at[:, : z.width], params.at[:, there], sems.at[0, 0])]
    copies[0].start()
    for j in range(z.blocks):
        at = slice(j * z.span, (j + 1) * z.span)
        master_buf[:, at] = half[:, at].astype(F32)
        cols = pl.ds(j * z.span, z.span)
        copies.append(pltpu.make_async_copy(master_buf.at[:, cols], new_master.at[:, cols], sems.at[1, j]))
        copies[-1].start()
    copies += place_moment(z, 1, place[...], got, one_out, one_buf, sems.at[2])
    for copy in copies:
        copy.wait()


def two_kernel(z, rep_ref, half, place, *refs):
    others, refs = refs[: z.copies - 1], refs[z.copies - 1 :]
    got, (_, params, two_out, checksum, buf, sems, param_sems) = refs[: z.peers], refs[z.peers :]
    copies = []
    for k, other in enumerate(others):
        replica = lax.rem(rep_ref[0] + z.copies - (k + 1), z.copies)
        there = pl.ds(pl.multiple_of(replica * z.width, LANES), z.width)
        copies.append(pltpu.make_async_copy(other.at[:, : z.width], params.at[:, there], param_sems.at[k]))
        copies[-1].start()
    copies += place_moment(z, 2, place[...], got, two_out, buf, sems)
    sums = half[:, z.width :].astype(F32)
    for other in others:
        sums = sums + other[:, z.width :].astype(F32)
    lane = iota((z.rows, LANES), 1)
    column = jnp.sum(jnp.where((lane >= 1) & (lane <= 3), sums, 0.0), axis=1, keepdims=True)
    diagonal = iota((z.rows, z.rows), 0) == iota((z.rows, z.rows), 1)
    checksum[...] = jnp.sum(jnp.where(diagonal, column, 0.0), axis=0, keepdims=True)
    for copy in copies:
        copy.wait()


def shifted(value, axis, k, count):
    return lax.ppermute(value, axis, [(i, (i + k) % count) for i in range(count)])


def always_sent(peers):
    near = [s for s in range(1, peers) if min(s, peers - s) < peers // 4]
    return [peers // 2] + near


def shift_groups(peers):
    rest = [s for s in range(1, peers) if s not in always_sent(peers)]
    groups = -(-len(rest) // GROUP)
    return [rest[g::groups] for g in range(groups)]


def agree(used, stride, peers, after, compiler_params):
    vmem = pl.BlockSpec(memory_space=pltpu.VMEM)
    other = lax.ppermute(used, "fsdp", [(i, i ^ stride) for i in range(peers)])
    return pl.pallas_call(
        agree_kernel,
        out_shape=jax.ShapeDtypeStruct((1, LANES), jnp.int32),
        in_specs=[vmem, vmem, pl.BlockSpec(memory_space=pl.ANY)],
        out_specs=vmem,
        compiler_params=compiler_params,
        name="agree",
    )(used, other, after)


def digits_of(group):
    count = -(-len(group) // DIGIT)
    size = -(-len(group) // count)
    return [group[i : i + size] for i in range(0, len(group), size)]


def choose_branches(used, after, peers, compiler_params):
    vmem = pl.BlockSpec(memory_space=pltpu.VMEM)
    smem = pl.BlockSpec(memory_space=pltpu.SMEM)
    digits = [digit for group in shift_groups(peers) for digit in digits_of(group)]
    stride = 2
    while 2 * stride < peers:
        used = agree(used, stride, peers, after, compiler_params)
        stride *= 2
    other = lax.ppermute(used, "fsdp", [(i, i ^ stride) for i in range(peers)])
    return pl.pallas_call(
        functools.partial(choose_kernel, digits),
        out_shape=[pltpu.SMEM((1,), jnp.int32)] * len(digits),
        in_specs=[vmem, vmem],
        out_specs=[smem] * len(digits),
        compiler_params=compiler_params,
        name="choose",
    )(used, other)


def send_tree(peers, digits, numbers, sent, values):
    if not digits:
        return tuple(shifted(value, "fsdp", s, peers) if on else value for s, on, value in zip(*sent, values))

    def branch(used):
        on = [bool(used >> i & 1) for i in range(len(digits[0]))]

        def run(rest, operands):
            return send_tree(peers, digits[1:], rest, (sent[0], sent[1] + on), operands)

        return run

    branches = [branch(used) for used in range(1 << len(digits[0]))]
    return lax.switch(numbers[0], branches, numbers[1:], values)


def move(z, chunks, chosen):
    if chosen is None:
        got = lax.all_to_all(jnp.concatenate(chunks, axis=0), "fsdp", split_axis=0, concat_axis=0, tiled=True)
        return [got[s * z.lines : (s + 1) * z.lines] for s in range(z.peers)]
    got = list(chunks)
    always = always_sent(z.peers)
    for s in always:
        got[s] = shifted(chunks[s], "fsdp", s, z.peers)
    barred = lax.optimization_barrier((*chosen, *[got[s] for s in always]))
    chosen, moved = barred[: len(chosen)], barred[len(chosen) :]
    for s, value in zip(always, moved):
        got[s] = value
    numbers = [number[0] for number in chosen]
    for group in shift_groups(z.peers):
        digits = digits_of(group)
        mine, numbers = tuple(numbers[: len(digits)]), numbers[len(digits) :]
        values = send_tree(z.peers, digits, mine, (group, []), tuple(chunks[s] for s in group))
        for s, value in zip(group, values):
            got[s] = value
    return got


def shards(master, moment_one, moment_two, gradients, new_row):
    rows, width = master.shape
    peers, copies = lax.axis_size("fsdp"), lax.axis_size("replica")
    z = Sizes(rows, width, peers, copies)
    compiler_params = pltpu.CompilerParams(vmem_limit_bytes=VMEM_BYTES)
    smem = pl.BlockSpec(memory_space=pltpu.SMEM)
    vmem = pl.BlockSpec(memory_space=pltpu.VMEM)
    hbm = pl.BlockSpec(memory_space=pl.ANY)
    dma = pltpu.SemaphoreType.DMA

    replica = lax.axis_index("replica").astype(jnp.int32)
    rep = replica.reshape(1)
    by_shift = peers <= MOST_SHIFT_PEERS and peers & (peers - 1) == 0
    origin = (lax.axis_index("fsdp").astype(jnp.int32) if by_shift else jnp.int32(0)).reshape(1)
    state_in = [pltpu.with_memory_space_constraint(x, pltpu.HBM) for x in (master, moment_one, moment_two)]
    full = pltpu.with_memory_space_constraint(gradients[0], pltpu.HBM)

    part = jax.ShapeDtypeStruct((rows, width), BF16)
    pick, info, used, *parts = pl.pallas_call(
        functools.partial(prepare_kernel, z),
        out_shape=[
            jax.ShapeDtypeStruct((z.split, z.slots, rows), BF16),
            jax.ShapeDtypeStruct((rows, LANES), F32),
            jax.ShapeDtypeStruct((1, LANES), jnp.int32),
        ]
        + [part] * (copies - 1),
        in_specs=[smem, smem, hbm, hbm],
        out_specs=[vmem] * (copies + 2),
        scratch_shapes=[
            pltpu.VMEM((copies - 1, rows, width), F32),
            pltpu.VMEM((1, rows), jnp.int32),
            dma((copies - 1, z.blocks)),
            dma,
        ],
        compiler_params=compiler_params,
        cost_estimate=pl.CostEstimate(flops=1 << 30, bytes_accessed=1, transcendentals=0),
        name="prepare",
    )(rep, origin, pltpu.with_memory_space_constraint(new_row.reshape(1, rows), pltpu.HBM), full)
    received = [shifted(value, "replica", k + 1, copies) for k, value in enumerate(parts)]

    loaded = jax.ShapeDtypeStruct((rows, width), F32)
    *state, meta = pl.pallas_call(
        functools.partial(load_kernel, z),
        out_shape=[loaded, loaded, loaded, loaded, jax.ShapeDtypeStruct((rows, LANES), BF16)],
        in_specs=[smem, vmem, hbm, hbm, hbm, hbm],
        out_specs=[vmem] * 5,
        scratch_shapes=[dma((4, z.blocks))],
        compiler_params=compiler_params,
        cost_estimate=pl.CostEstimate(flops=1 << 30, bytes_accessed=1, transcendentals=0),
        name="load",
    )(rep, info, *state_in, full)

    if by_shift:
        used = agree(used, 1, peers, meta, compiler_params)
    chunks = pl.pallas_call(
        functools.partial(update_kernel, z),
        out_shape=[jax.ShapeDtypeStruct((z.lines, z.payload), BF16)] * peers,
        in_specs=[vmem] * (5 + copies) + [hbm],
        out_specs=[vmem] * peers,
        scratch_shapes=[pltpu.VMEM((z.stacked, 3 * z.body), BF16)],
        compiler_params=compiler_params,
        cost_estimate=pl.CostEstimate(
            flops=6 * z.slots * z.stacked * z.body, bytes_accessed=24 * rows * width, transcendentals=rows * width
        ),
        name="update",
    )(pick, meta, *state, *received, used)

    chosen = choose_branches(used, chunks[0], peers, compiler_params) if by_shift else None
    got = move(z, chunks, chosen)

    wide = jax.ShapeDtypeStruct((rows, width), F32)
    full_params = jax.ShapeDtypeStruct((rows, width * copies), BF16)
    half, place = pl.pallas_call(
        functools.partial(half_kernel, z),
        out_shape=(
            jax.ShapeDtypeStruct((rows, width + LANES), BF16),
            jax.ShapeDtypeStruct((z.slots, z.stacked), BF16),
        ),
        in_specs=[vmem] * peers,
        out_specs=(vmem, vmem),
        compiler_params=compiler_params,
        name="place_half",
    )(*got)
    others = [shifted(half, "replica", k, copies) for k in range(1, copies)]

    new_master, params, new_one = pl.pallas_call(
        functools.partial(one_kernel, z),
        out_shape=(wide, full_params, wide),
        in_specs=[smem] + [vmem] * (peers + 2),
        out_specs=(hbm, hbm, hbm),
        scratch_shapes=[pltpu.VMEM((rows, width), F32)] * 2 + [dma((3, z.blocks))],
        compiler_params=compiler_params,
        cost_estimate=pl.CostEstimate(
            flops=2 * z.slots * z.stacked * z.body, bytes_accessed=12 * rows * width, transcendentals=0
        ),
        name="place_one",
    )(rep, half, place, *got)

    params, new_two, checksum = pl.pallas_call(
        functools.partial(two_kernel, z),
        out_shape=(full_params, wide, jax.ShapeDtypeStruct((1, rows), F32)),
        in_specs=[smem] + [vmem] * (copies + peers + 1) + [hbm],
        out_specs=(hbm, hbm, vmem),
        scratch_shapes=[pltpu.VMEM((rows, width), F32), dma((z.blocks,)), dma((max(1, copies - 1),))],
        input_output_aliases={copies + peers + 2: 0},
        compiler_params=compiler_params,
        cost_estimate=pl.CostEstimate(
            flops=2 * z.slots * z.stacked * z.body, bytes_accessed=12 * rows * width, transcendentals=0
        ),
        name="place_two",
    )(rep, half, place, *others, *got, params)
    return (new_master, new_one, new_two, params, checksum.reshape(rows))


def solution(mesh):
    return jax.shard_map(
        shards,
        mesh=mesh,
        in_specs=(
            P("fsdp", "replica"),
            P("fsdp", "replica"),
            P("fsdp", "replica"),
            P("replica", "fsdp", None),
            P("fsdp"),
        ),
        out_specs=(
            P("fsdp", "replica"),
            P("fsdp", "replica"),
            P("fsdp", "replica"),
            P("fsdp", None),
            P("fsdp"),
        ),
        check_vma=False,
    )
```

```python
import functools
import math

import jax
import jax.numpy as jnp
from jax import lax
from jax.experimental import pallas as pl
from jax.experimental.pallas import tpu as pltpu
from jax.sharding import PartitionSpec as P

LANES = 128
TILE_ROWS = 16
MIB = 1024 * 1024
VMEM_BYTES = 48 * MIB
MOST_SHIFT_PEERS = 16
GROUP = 3
DIGIT = 3
F32 = jnp.float32
BF16 = jnp.bfloat16


def iota(shape, axis):
    return lax.broadcasted_iota(jnp.int32, shape, axis)


class Sizes:
    def __init__(self, rows, width, peers, copies):
        self.rows, self.width, self.peers, self.copies = rows, width, peers, copies
        self.cap = max(2, 2 * rows // peers)
        self.split = max(1, TILE_ROWS // self.cap)
        self.lines = self.cap * self.split
        self.slots = peers * self.lines
        self.stacked = self.split * rows
        self.body = width // self.split
        self.cb = math.gcd(self.body, 512)
        self.blocks = self.body // self.cb
        self.span = self.split * self.cb
        self.sub = math.gcd(self.cb, 256)
        self.payload = 3 * self.body + LANES


def prepare_kernel(z, rep_ref, origin_ref, new_row_hbm, full_hbm, pick_ref, info_ref, mask_ref, *refs):
    parts, (full_buf, line_buf, sems, line_sem) = refs[: z.copies - 1], refs[z.copies - 1 :]
    step = z.width // z.blocks
    line_copy = pltpu.make_async_copy(new_row_hbm, line_buf, line_sem)
    line_copy.start()
    copies = []
    for k in range(1, z.copies):
        other = lax.rem(rep_ref[0] + k, z.copies)
        for j in range(z.blocks):
            there = pl.ds(pl.multiple_of(other * z.width + j * step, LANES), step)
            copies.append(
                pltpu.make_async_copy(
                    full_hbm.at[:, there], full_buf.at[k - 1, :, pl.ds(j * step, step)], sems.at[k - 1, j]
                )
            )
            copies[-1].start()
    line_copy.wait()
    line = line_buf[...]
    at_row, at_lane = iota((z.rows, z.rows), 0), iota((z.rows, z.rows), 1)
    column = jnp.sum(jnp.where(at_row == at_lane, line.astype(F32), 0.0), axis=1, keepdims=True).astype(jnp.int32)
    target, target_column = line // z.rows, column // z.rows
    earlier = (target_column == target) & (at_row < at_lane)
    rank = jnp.sum(jnp.where(earlier, 1.0, 0.0), axis=0, keepdims=True).astype(jnp.int32)
    shift = lax.rem(target - origin_ref[0] + z.peers, z.peers)
    shift_column = lax.rem(target_column - origin_ref[0] + z.peers, z.peers)
    for h in range(z.split):
        slot = shift * z.lines + h * z.cap + rank
        pick_ref[h] = jnp.where(iota((z.slots, z.rows), 0) == slot, 1.0, 0.0).astype(BF16)
    lane = iota((z.rows, LANES), 1)
    info_ref[...] = jnp.where(lane == 0, (column - target_column * z.rows + 1).astype(F32), 0.0)
    used = jnp.where(lane == shift_column, 1.0, 0.0)
    mask_ref[...] = jnp.max(used, axis=0, keepdims=True).astype(jnp.int32)
    for k in range(1, z.copies):
        for j in range(z.blocks):
            copies[(k - 1) * z.blocks + j].wait()
            at = slice(j * step, (j + 1) * step)
            parts[k - 1][:, at] = full_buf[k - 1, :, at].astype(BF16)


def agree_kernel(left, right, _, out):
    out[...] = jnp.maximum(left[...], right[...])


def choose_kernel(digits, left, right, *outs):
    total = jnp.maximum(left[...], right[...])
    lane = iota(total.shape, 1)
    for digit, out in zip(digits, outs):
        value = jnp.zeros(total.shape, jnp.int32)
        for i, s in enumerate(digit):
            value = value + jnp.where(lane == s, total << i, 0)
        out[0] = jnp.sum(value.astype(F32)).astype(jnp.int32)


def load_state_kernel(z, rep_ref, info_ref, master_hbm, one_hbm, master, one, meta_ref, sems):
    pieces = sems.shape[1]
    step = z.width // pieces
    copies = []
    for i, (src, dst) in enumerate(((master_hbm, master), (one_hbm, one))):
        for j in range(pieces):
            at = pl.ds(j * step, step)
            copies.append(pltpu.make_async_copy(src.at[:, at], dst.at[:, at], sems.at[i, j]))
            copies[-1].start()
    part = jnp.zeros((z.rows, LANES), F32)
    for j in range(pieces):
        copies[j].wait()
        for at in range(j * step, (j + 1) * step, LANES):
            weights = 1.0 + ((iota((1, LANES), 1) + (rep_ref[0] * z.width + at)) % 7).astype(F32) / 7.0
            part = part + master[:, at : at + LANES] * weights
    total = jnp.sum(part, axis=1, keepdims=True) * (1.0 / math.sqrt(z.width * z.copies))
    high = total.astype(BF16).astype(F32)
    middle = (total - high).astype(BF16).astype(F32)
    low = total - high - middle
    lane = iota((z.rows, LANES), 1)
    meta = jnp.where(lane == 1, high, jnp.where(lane == 2, middle, jnp.where(lane == 3, low, info_ref[...])))
    meta_ref[...] = meta.astype(BF16)
    for copy in copies[pieces:]:
        copy.wait()


def load_rest_kernel(z, rep_ref, two_hbm, full_hbm, _, two, own, sems):
    pieces = sems.shape[1]
    step = z.width // pieces
    copies = []
    for j in range(pieces):
        at = pl.ds(j * step, step)
        mine = pl.ds(pl.multiple_of(rep_ref[0] * z.width + j * step, LANES), step)
        copies.append(pltpu.make_async_copy(two_hbm.at[:, at], two.at[:, at], sems.at[0, j]))
        copies.append(pltpu.make_async_copy(full_hbm.at[:, mine], own.at[:, at], sems.at[1, j]))
    for copy in copies:
        copy.start()
    for copy in copies:
        copy.wait()


def update_kernel(z, pick_ref, meta_ref, master, one, two, own, *refs):
    received, refs = refs[: z.copies - 1], refs[z.copies :]
    outs, rows_buf = refs[: z.peers], refs[z.peers]
    pick = jnp.concatenate([pick_ref[h] for h in range(z.split)], axis=1)
    for j in range(z.blocks):
        for h in range(z.split):
            for c in range(0, z.cb, z.sub):
                at = j * z.span + h * z.cb + c
                cols = slice(at, at + z.sub)
                summed = own[:, cols]
                for other in received:
                    summed = summed + other[:, cols].astype(F32)
                moved = master[:, cols]
                new_one = 0.9 * one[:, cols] + 0.1 * summed
                new_two = 0.95 * two[:, cols] + 0.05 * summed * summed
                update = new_one * (1.0 / (1.0 - 0.9**10)) / (jnp.sqrt(new_two * (1.0 / (1.0 - 0.95**10))) + 1e-08)
                new_master = moved - 0.05 * (update + 0.1 * moved)
                for i, value in enumerate((new_master, new_one, new_two)):
                    to = i * z.body + j * z.cb + c
                    rows_buf[h * z.rows : (h + 1) * z.rows, to : to + z.sub] = value.astype(BF16)
        for i in range(3):
            at = i * z.body + j * z.cb
            packed = jnp.dot(pick, rows_buf[:, at : at + z.cb], preferred_element_type=F32).astype(BF16)
            for s, out in enumerate(outs):
                out[:, at : at + z.cb] = packed[s * z.lines : (s + 1) * z.lines]
    meta = jnp.concatenate([meta_ref[...]] * z.split, axis=0)
    packed = jnp.dot(pick, meta, preferred_element_type=F32).astype(BF16)
    for s, out in enumerate(outs):
        out[:, 3 * z.body :] = packed[s * z.lines : (s + 1) * z.lines]


def gathered(refs, cols):
    return jnp.concatenate([ref[:, cols] for ref in refs], axis=0)


def placing(z, meta):
    offset = meta[:, :1].astype(F32).astype(jnp.int32)
    piece = lax.rem(iota((z.slots, 1), 0), z.lines) // z.cap
    wanted = jnp.where(offset > 0, offset - 1 + piece * z.rows, -1)
    return jnp.where(iota((z.slots, z.stacked), 1) == wanted, 1.0, 0.0).T.astype(BF16)


def placed(place, values):
    return jnp.dot(place, values, preferred_element_type=F32)


def half_kernel(z, *refs):
    got, (half, place_out) = refs[: z.peers], refs[z.peers :]
    meta = gathered(got, slice(3 * z.body, 3 * z.body + LANES))
    place = placing(z, meta)
    place_out[...] = place
    for j in range(z.blocks):
        rows_out = placed(place, gathered(got, slice(j * z.cb, (j + 1) * z.cb))).astype(BF16)
        for h in range(z.split):
            at = j * z.span + h * z.cb
            half[:, at : at + z.cb] = rows_out[h * z.rows : (h + 1) * z.rows]
    half[:, z.width :] = placed(place, meta)[: z.rows].astype(BF16)


def place_moment(z, i, place, got, out, buf, sems):
    copies = []
    for j in range(z.blocks):
        at = i * z.body + j * z.cb
        rows_out = placed(place, gathered(got, slice(at, at + z.cb)))
        for h in range(z.split):
            col = j * z.span + h * z.cb
            buf[:, col : col + z.cb] = rows_out[h * z.rows : (h + 1) * z.rows]
        cols = pl.ds(j * z.span, z.span)
        copies.append(pltpu.make_async_copy(buf.at[:, cols], out.at[:, cols], sems.at[j]))
        copies[-1].start()
    return copies


def one_kernel(z, rep_ref, half, place, *refs):
    got, (new_master, params, one_out, master_buf, one_buf, sems) = refs[: z.peers], refs[z.peers :]
    there = pl.ds(pl.multiple_of(rep_ref[0] * z.width, LANES), z.width)
    copies = [pltpu.make_async_copy(half.at[:, : z.width], params.at[:, there], sems.at[0, 0])]
    copies[0].start()
    for j in range(z.blocks):
        at = slice(j * z.span, (j + 1) * z.span)
        master_buf[:, at] = half[:, at].astype(F32)
        cols = pl.ds(j * z.span, z.span)
        copies.append(pltpu.make_async_copy(master_buf.at[:, cols], new_master.at[:, cols], sems.at[1, j]))
        copies[-1].start()
    copies += place_moment(z, 1, place[...], got, one_out, one_buf, sems.at[2])
    for copy in copies:
        copy.wait()


def two_kernel(z, rep_ref, half, place, *refs):
    others, refs = refs[: z.copies - 1], refs[z.copies - 1 :]
    got, (_, params, two_out, checksum, buf, sems, param_sems) = refs[: z.peers], refs[z.peers :]
    copies = []
    for k, other in enumerate(others):
        replica = lax.rem(rep_ref[0] + z.copies - (k + 1), z.copies)
        there = pl.ds(pl.multiple_of(replica * z.width, LANES), z.width)
        copies.append(pltpu.make_async_copy(other.at[:, : z.width], params.at[:, there], param_sems.at[k]))
        copies[-1].start()
    copies += place_moment(z, 2, place[...], got, two_out, buf, sems)
    sums = half[:, z.width :].astype(F32)
    for other in others:
        sums = sums + other[:, z.width :].astype(F32)
    lane = iota((z.rows, LANES), 1)
    column = jnp.sum(jnp.where((lane >= 1) & (lane <= 3), sums, 0.0), axis=1, keepdims=True)
    diagonal = iota((z.rows, z.rows), 0) == iota((z.rows, z.rows), 1)
    checksum[...] = jnp.sum(jnp.where(diagonal, column, 0.0), axis=0, keepdims=True)
    for copy in copies:
        copy.wait()


def shifted(value, axis, k, count):
    return lax.ppermute(value, axis, [(i, (i + k) % count) for i in range(count)])


def always_sent(peers):
    return sorted({min(3, peers - 1), peers // 2, peers - 1})


def shift_groups(peers):
    rest = [s for s in range(1, peers) if s not in always_sent(peers)]
    groups = -(-len(rest) // GROUP)
    return [rest[g::groups] for g in range(groups)]


def agree(used, stride, peers, after, compiler_params):
    vmem = pl.BlockSpec(memory_space=pltpu.VMEM)
    other = lax.ppermute(used, "fsdp", [(i, i ^ stride) for i in range(peers)])
    return pl.pallas_call(
        agree_kernel,
        out_shape=jax.ShapeDtypeStruct((1, LANES), jnp.int32),
        in_specs=[vmem, vmem, pl.BlockSpec(memory_space=pl.ANY)],
        out_specs=vmem,
        compiler_params=compiler_params,
        name="agree",
    )(used, other, after)


def digits_of(group):
    count = -(-len(group) // DIGIT)
    size = -(-len(group) // count)
    return [group[i : i + size] for i in range(0, len(group), size)]


def choose_branches(used, after, peers, compiler_params):
    vmem = pl.BlockSpec(memory_space=pltpu.VMEM)
    smem = pl.BlockSpec(memory_space=pltpu.SMEM)
    digits = [digit for group in shift_groups(peers) for digit in digits_of(group)]
    stride = 4
    while 2 * stride < peers:
        used = agree(used, stride, peers, after, compiler_params)
        stride *= 2
    other = lax.ppermute(used, "fsdp", [(i, i ^ stride) for i in range(peers)])
    return pl.pallas_call(
        functools.partial(choose_kernel, digits),
        out_shape=[pltpu.SMEM((1,), jnp.int32)] * len(digits),
        in_specs=[vmem, vmem],
        out_specs=[smem] * len(digits),
        compiler_params=compiler_params,
        name="choose",
    )(used, other)


def send_tree(peers, digits, numbers, sent, values):
    if not digits:
        return tuple(shifted(value, "fsdp", s, peers) if on else value for s, on, value in zip(*sent, values))

    def branch(used):
        on = [bool(used >> i & 1) for i in range(len(digits[0]))]

        def run(rest, operands):
            return send_tree(peers, digits[1:], rest, (sent[0], sent[1] + on), operands)

        return run

    branches = [branch(used) for used in range(1 << len(digits[0]))]
    return lax.switch(numbers[0], branches, numbers[1:], values)


def move(z, chunks, chosen):
    if chosen is None:
        got = lax.all_to_all(jnp.concatenate(chunks, axis=0), "fsdp", split_axis=0, concat_axis=0, tiled=True)
        return [got[s * z.lines : (s + 1) * z.lines] for s in range(z.peers)]
    got = list(chunks)
    always = always_sent(z.peers)
    for s in always:
        got[s] = shifted(chunks[s], "fsdp", s, z.peers)
    barred = lax.optimization_barrier((*chosen, *[got[s] for s in always]))
    chosen, moved = barred[: len(chosen)], barred[len(chosen) :]
    for s, value in zip(always, moved):
        got[s] = value
    numbers = [number[0] for number in chosen]
    for group in shift_groups(z.peers):
        digits = digits_of(group)
        mine, numbers = tuple(numbers[: len(digits)]), numbers[len(digits) :]
        values = send_tree(z.peers, digits, mine, (group, []), tuple(chunks[s] for s in group))
        for s, value in zip(group, values):
            got[s] = value
    return got


def shards(master, moment_one, moment_two, gradients, new_row):
    rows, width = master.shape
    peers, copies = lax.axis_size("fsdp"), lax.axis_size("replica")
    z = Sizes(rows, width, peers, copies)
    compiler_params = pltpu.CompilerParams(vmem_limit_bytes=VMEM_BYTES)
    smem = pl.BlockSpec(memory_space=pltpu.SMEM)
    vmem = pl.BlockSpec(memory_space=pltpu.VMEM)
    hbm = pl.BlockSpec(memory_space=pl.ANY)
    dma = pltpu.SemaphoreType.DMA

    replica = lax.axis_index("replica").astype(jnp.int32)
    rep = replica.reshape(1)
    by_shift = 8 <= peers <= MOST_SHIFT_PEERS and peers & (peers - 1) == 0
    origin = (lax.axis_index("fsdp").astype(jnp.int32) if by_shift else jnp.int32(0)).reshape(1)
    state_in = [pltpu.with_memory_space_constraint(x, pltpu.HBM) for x in (master, moment_one, moment_two)]
    full = pltpu.with_memory_space_constraint(gradients[0], pltpu.HBM)

    part = jax.ShapeDtypeStruct((rows, width), BF16)
    pick, info, used, *parts = pl.pallas_call(
        functools.partial(prepare_kernel, z),
        out_shape=[
            jax.ShapeDtypeStruct((z.split, z.slots, rows), BF16),
            jax.ShapeDtypeStruct((rows, LANES), F32),
            jax.ShapeDtypeStruct((1, LANES), jnp.int32),
        ]
        + [part] * (copies - 1),
        in_specs=[smem, smem, hbm, hbm],
        out_specs=[vmem] * (copies + 2),
        scratch_shapes=[
            pltpu.VMEM((copies - 1, rows, width), F32),
            pltpu.VMEM((1, rows), jnp.int32),
            dma((copies - 1, z.blocks)),
            dma,
        ],
        compiler_params=compiler_params,
        cost_estimate=pl.CostEstimate(flops=1 << 30, bytes_accessed=1, transcendentals=0),
        name="prepare",
    )(rep, origin, pltpu.with_memory_space_constraint(new_row.reshape(1, rows), pltpu.HBM), full)
    received = [shifted(value, "replica", k + 1, copies) for k, value in enumerate(parts)]

    loaded = jax.ShapeDtypeStruct((rows, width), F32)
    load_cost = pl.CostEstimate(flops=1 << 30, bytes_accessed=1, transcendentals=0)
    load_sems = dma((2, math.gcd(4, z.blocks)))
    master_here, one_here, meta = pl.pallas_call(
        functools.partial(load_state_kernel, z),
        out_shape=(loaded, loaded, jax.ShapeDtypeStruct((rows, LANES), BF16)),
        in_specs=[smem, vmem, hbm, hbm],
        out_specs=(vmem, vmem, vmem),
        scratch_shapes=[load_sems],
        compiler_params=compiler_params,
        cost_estimate=load_cost,
        name="load_state",
    )(rep, info, state_in[0], state_in[1])
    if by_shift:
        used = agree(used, 1, peers, meta, compiler_params)
    two_here, own_here = pl.pallas_call(
        functools.partial(load_rest_kernel, z),
        out_shape=(loaded, loaded),
        in_specs=[smem, hbm, hbm, hbm],
        out_specs=(vmem, vmem),
        scratch_shapes=[load_sems],
        compiler_params=compiler_params,
        cost_estimate=load_cost,
        name="load_rest",
    )(rep, state_in[2], full, used)
    if by_shift:
        used = agree(used, 2, peers, own_here, compiler_params)
    chunks = pl.pallas_call(
        functools.partial(update_kernel, z),
        out_shape=[jax.ShapeDtypeStruct((z.lines, z.payload), BF16)] * peers,
        in_specs=[vmem] * (5 + copies) + [hbm],
        out_specs=[vmem] * peers,
        scratch_shapes=[pltpu.VMEM((z.stacked, 3 * z.body), BF16)],
        compiler_params=compiler_params,
        cost_estimate=pl.CostEstimate(
            flops=6 * z.slots * z.stacked * z.body, bytes_accessed=24 * rows * width, transcendentals=rows * width
        ),
        name="update",
    )(pick, meta, master_here, one_here, two_here, own_here, *received, used)

    chosen = choose_branches(used, chunks[0], peers, compiler_params) if by_shift else None
    got = move(z, chunks, chosen)

    wide = jax.ShapeDtypeStruct((rows, width), F32)
    full_params = jax.ShapeDtypeStruct((rows, width * copies), BF16)
    half, place = pl.pallas_call(
        functools.partial(half_kernel, z),
        out_shape=(
            jax.ShapeDtypeStruct((rows, width + LANES), BF16),
            jax.ShapeDtypeStruct((z.stacked, z.slots), BF16),
        ),
        in_specs=[vmem] * peers,
        out_specs=(vmem, vmem),
        compiler_params=compiler_params,
        name="place_half",
    )(*got)
    others = [shifted(half, "replica", k, copies) for k in range(1, copies)]

    new_master, params, new_one = pl.pallas_call(
        functools.partial(one_kernel, z),
        out_shape=(wide, full_params, wide),
        in_specs=[smem] + [vmem] * (peers + 2),
        out_specs=(hbm, hbm, hbm),
        scratch_shapes=[pltpu.VMEM((rows, width), F32)] * 2 + [dma((3, z.blocks))],
        compiler_params=compiler_params,
        cost_estimate=pl.CostEstimate(
            flops=2 * z.slots * z.stacked * z.body, bytes_accessed=12 * rows * width, transcendentals=0
        ),
        name="place_one",
    )(rep, half, place, *got)

    params, new_two, checksum = pl.pallas_call(
        functools.partial(two_kernel, z),
        out_shape=(full_params, wide, jax.ShapeDtypeStruct((1, rows), F32)),
        in_specs=[smem] + [vmem] * (copies + peers + 1) + [hbm],
        out_specs=(hbm, hbm, vmem),
        scratch_shapes=[pltpu.VMEM((rows, width), F32), dma((z.blocks,)), dma((max(1, copies - 1),))],
        input_output_aliases={copies + peers + 2: 0},
        compiler_params=compiler_params,
        cost_estimate=pl.CostEstimate(
            flops=2 * z.slots * z.stacked * z.body, bytes_accessed=12 * rows * width, transcendentals=0
        ),
        name="place_two",
    )(rep, half, place, *others, *got, params)
    return (new_master, new_one, new_two, params, checksum.reshape(rows))


def solution(mesh):
    return jax.shard_map(
        shards,
        mesh=mesh,
        in_specs=(
            P("fsdp", "replica"),
            P("fsdp", "replica"),
            P("fsdp", "replica"),
            P("replica", "fsdp", None),
            P("fsdp"),
        ),
        out_specs=(
            P("fsdp", "replica"),
            P("fsdp", "replica"),
            P("fsdp", "replica"),
            P("fsdp", None),
            P("fsdp"),
        ),
        check_vma=False,
    )
```

```python
import functools
import math

import jax
import jax.numpy as jnp
from jax import lax
from jax.experimental import pallas as pl
from jax.experimental.pallas import tpu as pltpu
from jax.sharding import PartitionSpec as P

LANES = 128
TILE_ROWS = 16
MIB = 1024 * 1024
VMEM_BYTES = 48 * MIB
MOST_SHIFT_PEERS = 16
GROUP = 3
DIGIT = 3
F32 = jnp.float32
BF16 = jnp.bfloat16


def iota(shape, axis):
    return lax.broadcasted_iota(jnp.int32, shape, axis)


class Sizes:
    def __init__(self, rows, width, peers, copies):
        self.rows, self.width, self.peers, self.copies = rows, width, peers, copies
        self.cap = max(2, 2 * rows // peers)
        self.split = max(1, TILE_ROWS // self.cap)
        self.lines = self.cap * self.split
        self.slots = peers * self.lines
        self.stacked = self.split * rows
        self.body = width // self.split
        self.cb = math.gcd(self.body, 512)
        self.blocks = self.body // self.cb
        self.span = self.split * self.cb
        self.sub = math.gcd(self.cb, 256)
        self.payload = 3 * self.body + LANES


def prepare_kernel(z, rep_ref, origin_ref, new_row_hbm, full_hbm, pick_ref, info_ref, mask_ref, *refs):
    parts, (full_buf, line_buf, sems, line_sem) = refs[: z.copies - 1], refs[z.copies - 1 :]
    step = z.width // z.blocks
    line_copy = pltpu.make_async_copy(new_row_hbm, line_buf, line_sem)
    line_copy.start()
    copies = []
    for k in range(1, z.copies):
        other = lax.rem(rep_ref[0] + k, z.copies)
        for j in range(z.blocks):
            there = pl.ds(pl.multiple_of(other * z.width + j * step, LANES), step)
            copies.append(
                pltpu.make_async_copy(
                    full_hbm.at[:, there], full_buf.at[k - 1, :, pl.ds(j * step, step)], sems.at[k - 1, j]
                )
            )
            copies[-1].start()
    line_copy.wait()
    line = line_buf[...]
    at_row, at_lane = iota((z.rows, z.rows), 0), iota((z.rows, z.rows), 1)
    column = jnp.sum(jnp.where(at_row == at_lane, line.astype(F32), 0.0), axis=1, keepdims=True).astype(jnp.int32)
    target, target_column = line // z.rows, column // z.rows
    earlier = (target_column == target) & (at_row < at_lane)
    rank = jnp.sum(jnp.where(earlier, 1.0, 0.0), axis=0, keepdims=True).astype(jnp.int32)
    shift = lax.rem(target - origin_ref[0] + z.peers, z.peers)
    shift_column = lax.rem(target_column - origin_ref[0] + z.peers, z.peers)
    for h in range(z.split):
        slot = shift * z.lines + h * z.cap + rank
        pick_ref[h] = jnp.where(iota((z.slots, z.rows), 0) == slot, 1.0, 0.0).astype(BF16)
    lane = iota((z.rows, LANES), 1)
    info_ref[...] = jnp.where(lane == 0, (column - target_column * z.rows + 1).astype(F32), 0.0)
    used = jnp.where(lane == shift_column, 1.0, 0.0)
    mask_ref[...] = jnp.max(used, axis=0, keepdims=True).astype(jnp.int32)
    for k in range(1, z.copies):
        for j in range(z.blocks):
            copies[(k - 1) * z.blocks + j].wait()
            at = slice(j * step, (j + 1) * step)
            parts[k - 1][:, at] = full_buf[k - 1, :, at].astype(BF16)


def choose_kernel(digits, masks, *outs):
    total = jnp.max(masks[...].astype(F32), axis=0).astype(jnp.int32)
    lane = iota(total.shape, 1)
    for digit, out in zip(digits, outs):
        value = jnp.zeros(total.shape, jnp.int32)
        for i, s in enumerate(digit):
            value = value + jnp.where(lane == s, total << i, 0)
        out[0] = jnp.sum(value.astype(F32)).astype(jnp.int32)


def load_kernel(z, rep_ref, info_ref, master_hbm, one_hbm, two_hbm, full_hbm, master, one, two, own, meta_ref, sems):
    base = rep_ref[0] * z.width
    step = z.width // z.blocks
    copies = []
    for j in range(z.blocks):
        at = pl.ds(j * step, step)
        mine = pl.ds(pl.multiple_of(base + j * step, LANES), step)
        copies.append(
            [
                pltpu.make_async_copy(master_hbm.at[:, at], master.at[:, at], sems.at[0, j]),
                pltpu.make_async_copy(one_hbm.at[:, at], one.at[:, at], sems.at[1, j]),
                pltpu.make_async_copy(two_hbm.at[:, at], two.at[:, at], sems.at[2, j]),
                pltpu.make_async_copy(full_hbm.at[:, mine], own.at[:, at], sems.at[3, j]),
            ]
        )
    for i in range(4):
        for j in range(z.blocks):
            copies[j][i].start()
    part = jnp.zeros((z.rows, LANES), F32)
    for j in range(z.blocks):
        copies[j][0].wait()
        for at in range(j * step, (j + 1) * step, LANES):
            weights = 1.0 + ((iota((1, LANES), 1) + (base + at)) % 7).astype(F32) / 7.0
            part = part + master[:, at : at + LANES] * weights
    total = jnp.sum(part, axis=1, keepdims=True) * (1.0 / math.sqrt(z.width * z.copies))
    high = total.astype(BF16).astype(F32)
    middle = (total - high).astype(BF16).astype(F32)
    low = total - high - middle
    lane = iota((z.rows, LANES), 1)
    meta = jnp.where(lane == 1, high, jnp.where(lane == 2, middle, jnp.where(lane == 3, low, info_ref[...])))
    meta_ref[...] = meta.astype(BF16)
    for j in range(z.blocks):
        for i in range(1, 4):
            copies[j][i].wait()


def update_kernel(z, pick_ref, meta_ref, used_ref, master, one, two, own, *refs):
    received, refs = refs[: z.copies - 1], refs[z.copies - 1 :]
    outs, masks_out, rows_buf = refs[: z.peers], refs[z.peers], refs[z.peers + 1]
    masks_out[...] = jnp.broadcast_to(used_ref[...][None], masks_out.shape)
    pick = jnp.concatenate([pick_ref[h] for h in range(z.split)], axis=1)
    for j in range(z.blocks):
        for h in range(z.split):
            for c in range(0, z.cb, z.sub):
                at = j * z.span + h * z.cb + c
                cols = slice(at, at + z.sub)
                summed = own[:, cols]
                for other in received:
                    summed = summed + other[:, cols].astype(F32)
                moved = master[:, cols]
                new_one = 0.9 * one[:, cols] + 0.1 * summed
                new_two = 0.95 * two[:, cols] + 0.05 * summed * summed
                update = new_one * (1.0 / (1.0 - 0.9**10)) / (jnp.sqrt(new_two * (1.0 / (1.0 - 0.95**10))) + 1e-08)
                new_master = moved - 0.05 * (update + 0.1 * moved)
                for i, value in enumerate((new_master, new_one, new_two)):
                    to = i * z.body + j * z.cb + c
                    rows_buf[h * z.rows : (h + 1) * z.rows, to : to + z.sub] = value.astype(BF16)
        for i in range(3):
            at = i * z.body + j * z.cb
            packed = jnp.dot(pick, rows_buf[:, at : at + z.cb], preferred_element_type=F32).astype(BF16)
            for s, out in enumerate(outs):
                out[:, at : at + z.cb] = packed[s * z.lines : (s + 1) * z.lines]
    meta = jnp.concatenate([meta_ref[...]] * z.split, axis=0)
    packed = jnp.dot(pick, meta, preferred_element_type=F32).astype(BF16)
    for s, out in enumerate(outs):
        out[:, 3 * z.body :] = packed[s * z.lines : (s + 1) * z.lines]


def gathered(refs, cols):
    return jnp.concatenate([ref[:, cols] for ref in refs], axis=0)


def placing(z, meta):
    offset = meta[:, :1].astype(F32).astype(jnp.int32)
    piece = lax.rem(iota((z.slots, 1), 0), z.lines) // z.cap
    wanted = jnp.where(offset > 0, offset - 1 + piece * z.rows, -1)
    return jnp.where(iota((z.slots, z.stacked), 1) == wanted, 1.0, 0.0).T.astype(BF16)


def placed(place, values):
    return jnp.dot(place, values, preferred_element_type=F32)


def half_kernel(z, *refs):
    got, (half, place_out) = refs[: z.peers], refs[z.peers :]
    meta = gathered(got, slice(3 * z.body, 3 * z.body + LANES))
    place = placing(z, meta)
    place_out[...] = place
    for j in range(z.blocks):
        rows_out = placed(place, gathered(got, slice(j * z.cb, (j + 1) * z.cb))).astype(BF16)
        for h in range(z.split):
            at = j * z.span + h * z.cb
            half[:, at : at + z.cb] = rows_out[h * z.rows : (h + 1) * z.rows]
    half[:, z.width :] = placed(place, meta)[: z.rows].astype(BF16)


def place_moment(z, i, place, got, out, buf, sems):
    copies = []
    for j in range(z.blocks):
        at = i * z.body + j * z.cb
        rows_out = placed(place, gathered(got, slice(at, at + z.cb)))
        for h in range(z.split):
            col = j * z.span + h * z.cb
            buf[:, col : col + z.cb] = rows_out[h * z.rows : (h + 1) * z.rows]
        cols = pl.ds(j * z.span, z.span)
        copies.append(pltpu.make_async_copy(buf.at[:, cols], out.at[:, cols], sems.at[j]))
        copies[-1].start()
    return copies


def rows_kernel(z, rep_ref, half, place, *refs):
    got, (new_master, params, one_out, two_out, master_buf, one_buf, two_buf, sems) = refs[: z.peers], refs[z.peers :]
    there = pl.ds(pl.multiple_of(rep_ref[0] * z.width, LANES), z.width)
    copies = [pltpu.make_async_copy(half.at[:, : z.width], params.at[:, there], sems.at[0, 0])]
    copies[0].start()
    for j in range(z.blocks):
        at = slice(j * z.span, (j + 1) * z.span)
        master_buf[:, at] = half[:, at].astype(F32)
        cols = pl.ds(j * z.span, z.span)
        copies.append(pltpu.make_async_copy(master_buf.at[:, cols], new_master.at[:, cols], sems.at[1, j]))
        copies[-1].start()
    copies += place_moment(z, 1, place[...], got, one_out, one_buf, sems.at[2])
    copies += place_moment(z, 2, place[...], got, two_out, two_buf, sems.at[3])
    for copy in copies:
        copy.wait()


def finish_kernel(z, rep_ref, half, *refs):
    others, (_, params, checksum, sems) = refs[: z.copies - 1], refs[z.copies - 1 :]
    copies = []
    for k, other in enumerate(others):
        replica = lax.rem(rep_ref[0] + z.copies - (k + 1), z.copies)
        there = pl.ds(pl.multiple_of(replica * z.width, LANES), z.width)
        copies.append(pltpu.make_async_copy(other.at[:, : z.width], params.at[:, there], sems.at[k]))
        copies[-1].start()
    sums = half[:, z.width :].astype(F32)
    for other in others:
        sums = sums + other[:, z.width :].astype(F32)
    lane = iota((z.rows, LANES), 1)
    column = jnp.sum(jnp.where((lane >= 1) & (lane <= 3), sums, 0.0), axis=1, keepdims=True)
    diagonal = iota((z.rows, z.rows), 0) == iota((z.rows, z.rows), 1)
    checksum[...] = jnp.sum(jnp.where(diagonal, column, 0.0), axis=0, keepdims=True)
    for copy in copies:
        copy.wait()


def shifted(value, axis, k, count):
    return lax.ppermute(value, axis, [(i, (i + k) % count) for i in range(count)])


def always_sent(peers):
    return [peers // 2, 3, peers - 1]


def shift_groups(peers):
    rest = [s for s in range(1, peers) if s not in always_sent(peers)]
    groups = -(-len(rest) // GROUP)
    return [rest[g::groups] for g in range(groups)]


def digits_of(group):
    count = -(-len(group) // DIGIT)
    size = -(-len(group) // count)
    return [group[i : i + size] for i in range(0, len(group), size)]


def choose_branches(masks, peers, compiler_params):
    digits = [digit for group in shift_groups(peers) for digit in digits_of(group)]
    masks = lax.all_to_all(masks, "fsdp", split_axis=0, concat_axis=0, tiled=True)
    return pl.pallas_call(
        functools.partial(choose_kernel, digits),
        out_shape=[pltpu.SMEM((1,), jnp.int32)] * len(digits),
        in_specs=[pl.BlockSpec(memory_space=pltpu.VMEM)],
        out_specs=[pl.BlockSpec(memory_space=pltpu.SMEM)] * len(digits),
        compiler_params=compiler_params,
        name="choose",
    )(masks)


def send_tree(peers, digits, numbers, sent, values):
    if not digits:
        return tuple(shifted(value, "fsdp", s, peers) if on else value for s, on, value in zip(*sent, values))

    def branch(used):
        on = [bool(used >> i & 1) for i in range(len(digits[0]))]

        def run(rest, operands):
            return send_tree(peers, digits[1:], rest, (sent[0], sent[1] + on), operands)

        return run

    branches = [branch(used) for used in range(1 << len(digits[0]))]
    return lax.switch(numbers[0], branches, numbers[1:], values)


def move(z, chunks, chosen):
    if chosen is None:
        got = lax.all_to_all(jnp.concatenate(chunks, axis=0), "fsdp", split_axis=0, concat_axis=0, tiled=True)
        return [got[s * z.lines : (s + 1) * z.lines] for s in range(z.peers)]
    got = list(chunks)
    always = always_sent(z.peers)
    for s in always:
        got[s] = shifted(chunks[s], "fsdp", s, z.peers)
    barred = lax.optimization_barrier((*chosen, *[got[s] for s in always]))
    chosen, moved = barred[: len(chosen)], barred[len(chosen) :]
    for s, value in zip(always, moved):
        got[s] = value
    numbers = [number[0] for number in chosen]
    for group in shift_groups(z.peers):
        digits = digits_of(group)
        mine, numbers = tuple(numbers[: len(digits)]), numbers[len(digits) :]
        values = send_tree(z.peers, digits, mine, (group, []), tuple(chunks[s] for s in group))
        for s, value in zip(group, values):
            got[s] = value
    return got


def shards(master, moment_one, moment_two, gradients, new_row):
    rows, width = master.shape
    peers, copies = lax.axis_size("fsdp"), lax.axis_size("replica")
    z = Sizes(rows, width, peers, copies)
    compiler_params = pltpu.CompilerParams(vmem_limit_bytes=VMEM_BYTES)
    smem = pl.BlockSpec(memory_space=pltpu.SMEM)
    vmem = pl.BlockSpec(memory_space=pltpu.VMEM)
    hbm = pl.BlockSpec(memory_space=pl.ANY)
    dma = pltpu.SemaphoreType.DMA

    replica = lax.axis_index("replica").astype(jnp.int32)
    rep = replica.reshape(1)
    by_shift = 8 <= peers <= MOST_SHIFT_PEERS
    origin = (lax.axis_index("fsdp").astype(jnp.int32) if by_shift else jnp.int32(0)).reshape(1)
    state_in = [pltpu.with_memory_space_constraint(x, pltpu.HBM) for x in (master, moment_one, moment_two)]
    full = pltpu.with_memory_space_constraint(gradients[0], pltpu.HBM)

    part = jax.ShapeDtypeStruct((rows, width), BF16)
    pick, info, used, *parts = pl.pallas_call(
        functools.partial(prepare_kernel, z),
        out_shape=[
            jax.ShapeDtypeStruct((z.split, z.slots, rows), BF16),
            jax.ShapeDtypeStruct((rows, LANES), F32),
            jax.ShapeDtypeStruct((1, LANES), jnp.int32),
        ]
        + [part] * (copies - 1),
        in_specs=[smem, smem, hbm, hbm],
        out_specs=[vmem] * (copies + 2),
        scratch_shapes=[
            pltpu.VMEM((copies - 1, rows, width), F32),
            pltpu.VMEM((1, rows), jnp.int32),
            dma((copies - 1, z.blocks)),
            dma,
        ],
        compiler_params=compiler_params,
        cost_estimate=pl.CostEstimate(flops=1 << 30, bytes_accessed=1, transcendentals=0),
        name="prepare",
    )(rep, origin, pltpu.with_memory_space_constraint(new_row.reshape(1, rows), pltpu.HBM), full)
    received = [shifted(value, "replica", k + 1, copies) for k, value in enumerate(parts)]

    loaded = jax.ShapeDtypeStruct((rows, width), F32)
    *state, meta = pl.pallas_call(
        functools.partial(load_kernel, z),
        out_shape=[loaded, loaded, loaded, loaded, jax.ShapeDtypeStruct((rows, LANES), BF16)],
        in_specs=[smem, vmem, hbm, hbm, hbm, hbm],
        out_specs=[vmem] * 5,
        scratch_shapes=[dma((4, z.blocks))],
        compiler_params=compiler_params,
        cost_estimate=pl.CostEstimate(flops=1 << 30, bytes_accessed=1, transcendentals=0),
        name="load",
    )(rep, info, *state_in, full)

    *chunks, masks = pl.pallas_call(
        functools.partial(update_kernel, z),
        out_shape=[jax.ShapeDtypeStruct((z.lines, z.payload), BF16)] * peers
        + [jax.ShapeDtypeStruct((peers, 1, LANES), jnp.int32)],
        in_specs=[vmem] * (6 + copies),
        out_specs=[vmem] * (peers + 1),
        scratch_shapes=[pltpu.VMEM((z.stacked, 3 * z.body), BF16)],
        compiler_params=compiler_params,
        cost_estimate=pl.CostEstimate(
            flops=6 * z.slots * z.stacked * z.body, bytes_accessed=24 * rows * width, transcendentals=rows * width
        ),
        name="update",
    )(pick, meta, used, *state, *received)

    chosen = choose_branches(masks, peers, compiler_params) if by_shift else None
    got = move(z, chunks, chosen)

    wide = jax.ShapeDtypeStruct((rows, width), F32)
    full_params = jax.ShapeDtypeStruct((rows, width * copies), BF16)
    half, place = pl.pallas_call(
        functools.partial(half_kernel, z),
        out_shape=(
            jax.ShapeDtypeStruct((rows, width + LANES), BF16),
            jax.ShapeDtypeStruct((z.stacked, z.slots), BF16),
        ),
        in_specs=[vmem] * peers,
        out_specs=(vmem, vmem),
        compiler_params=compiler_params,
        name="place_half",
    )(*got)
    others = [shifted(half, "replica", k, copies) for k in range(1, copies)]

    new_master, params, new_one, new_two = pl.pallas_call(
        functools.partial(rows_kernel, z),
        out_shape=(wide, full_params, wide, wide),
        in_specs=[smem] + [vmem] * (peers + 2),
        out_specs=(hbm, hbm, hbm, hbm),
        scratch_shapes=[pltpu.VMEM((rows, width), F32)] * 3 + [dma((4, z.blocks))],
        compiler_params=compiler_params,
        cost_estimate=pl.CostEstimate(
            flops=4 * z.slots * z.stacked * z.body, bytes_accessed=18 * rows * width, transcendentals=0
        ),
        name="place_rows",
    )(rep, half, place, *got)

    params, checksum = pl.pallas_call(
        functools.partial(finish_kernel, z),
        out_shape=(full_params, jax.ShapeDtypeStruct((1, rows), F32)),
        in_specs=[smem] + [vmem] * copies + [hbm],
        out_specs=(hbm, vmem),
        scratch_shapes=[dma((max(1, copies - 1),))],
        input_output_aliases={copies + 1: 0},
        compiler_params=compiler_params,
        cost_estimate=pl.CostEstimate(flops=0, bytes_accessed=4 * rows * width, transcendentals=0),
        name="finish",
    )(rep, half, *others, params)
    return (new_master, new_one, new_two, params, checksum.reshape(rows))


def solution(mesh):
    return jax.shard_map(
        shards,
        mesh=mesh,
        in_specs=(
            P("fsdp", "replica"),
            P("fsdp", "replica"),
            P("fsdp", "replica"),
            P("replica", "fsdp", None),
            P("fsdp"),
        ),
        out_specs=(
            P("fsdp", "replica"),
            P("fsdp", "replica"),
            P("fsdp", "replica"),
            P("fsdp", None),
            P("fsdp"),
        ),
        check_vma=False,
    )
```

```python
import functools
import math

import jax
import jax.numpy as jnp
from jax import lax
from jax.experimental import pallas as pl
from jax.experimental.pallas import tpu as pltpu
from jax.sharding import PartitionSpec as P

LANES = 128
TILE_ROWS = 16
MIB = 1024 * 1024
VMEM_BYTES = 24 * MIB
MOST_SHIFT_PEERS = 16
F32 = jnp.float32
BF16 = jnp.bfloat16


def iota(shape, axis):
    return lax.broadcasted_iota(jnp.int32, shape, axis)


class Sizes:
    def __init__(self, rows, width, peers, copies):
        self.rows, self.width, self.peers, self.copies = rows, width, peers, copies
        self.cap = max(2, 2 * rows // peers)
        self.split = max(1, TILE_ROWS // self.cap)
        self.lines = self.cap * self.split
        self.slots = peers * self.lines
        self.stacked = self.split * rows
        self.body = width // self.split
        self.cb = math.gcd(self.body, 512)
        self.blocks = self.body // self.cb
        self.span = self.split * self.cb
        self.sub = math.gcd(self.cb, 256)
        self.payload = 3 * self.body + LANES


def prepare_kernel(z, rep_ref, origin_ref, new_row_hbm, full_hbm, pick_ref, info_ref, mask_ref, *refs):
    parts, (full_buf, line_buf, sems, line_sem) = refs[: z.copies - 1], refs[z.copies - 1 :]
    step = z.width // z.blocks
    line_copy = pltpu.make_async_copy(new_row_hbm, line_buf, line_sem)
    line_copy.start()
    copies = []
    for k in range(1, z.copies):
        other = lax.rem(rep_ref[0] + k, z.copies)
        for j in range(z.blocks):
            there = pl.ds(pl.multiple_of(other * z.width + j * step, LANES), step)
            copies.append(
                pltpu.make_async_copy(
                    full_hbm.at[:, there], full_buf.at[k - 1, :, pl.ds(j * step, step)], sems.at[k - 1, j]
                )
            )
            copies[-1].start()
    line_copy.wait()
    line = line_buf[...]
    at_row, at_lane = iota((z.rows, z.rows), 0), iota((z.rows, z.rows), 1)
    column = jnp.sum(jnp.where(at_row == at_lane, line.astype(F32), 0.0), axis=1, keepdims=True).astype(jnp.int32)
    target, target_column = line // z.rows, column // z.rows
    earlier = (target_column == target) & (at_row < at_lane)
    rank = jnp.sum(jnp.where(earlier, 1.0, 0.0), axis=0, keepdims=True).astype(jnp.int32)
    shift = lax.rem(target - origin_ref[0] + z.peers, z.peers)
    shift_column = lax.rem(target_column - origin_ref[0] + z.peers, z.peers)
    for h in range(z.split):
        slot = shift * z.lines + h * z.cap + rank
        pick_ref[h] = jnp.where(iota((z.slots, z.rows), 0) == slot, 1.0, 0.0).astype(BF16)
    lane = iota((z.rows, LANES), 1)
    info_ref[...] = jnp.where(lane == 0, (column - target_column * z.rows + 1).astype(F32), 0.0)
    used = jnp.where(lane == shift_column, 1.0, 0.0)
    mask_ref[...] = jnp.max(used, axis=0, keepdims=True).astype(jnp.int32)
    for k in range(1, z.copies):
        for j in range(z.blocks):
            copies[(k - 1) * z.blocks + j].wait()
            at = slice(j * step, (j + 1) * step)
            parts[k - 1][:, at] = full_buf[k - 1, :, at].astype(BF16)


def agree_kernel(left, right, _, out):
    out[...] = jnp.maximum(left[...], right[...])


def choose_kernel(digits, left, right, *outs):
    total = jnp.maximum(left[...], right[...])
    lane = iota(total.shape, 1)
    for digit, out in zip(digits, outs):
        value = jnp.zeros(total.shape, jnp.int32)
        for i, s in enumerate(digit):
            value = value + jnp.where(lane == s, total << i, 0)
        out[0] = jnp.sum(value.astype(F32)).astype(jnp.int32)


def load_kernel(z, rep_ref, info_ref, master_hbm, one_hbm, two_hbm, full_hbm, master, one, two, own, meta_ref, sems):
    base = rep_ref[0] * z.width
    step = z.width // z.blocks
    copies = []
    for j in range(z.blocks):
        at = pl.ds(j * step, step)
        mine = pl.ds(pl.multiple_of(base + j * step, LANES), step)
        copies.append(
            [
                pltpu.make_async_copy(master_hbm.at[:, at], master.at[:, at], sems.at[0, j]),
                pltpu.make_async_copy(one_hbm.at[:, at], one.at[:, at], sems.at[1, j]),
                pltpu.make_async_copy(two_hbm.at[:, at], two.at[:, at], sems.at[2, j]),
                pltpu.make_async_copy(full_hbm.at[:, mine], own.at[:, at], sems.at[3, j]),
            ]
        )
    for i in range(4):
        for j in range(z.blocks):
            copies[j][i].start()
    part = jnp.zeros((z.rows, LANES), F32)
    for j in range(z.blocks):
        copies[j][0].wait()
        for at in range(j * step, (j + 1) * step, LANES):
            weights = 1.0 + ((iota((1, LANES), 1) + (base + at)) % 7).astype(F32) / 7.0
            part = part + master[:, at : at + LANES] * weights
    total = jnp.sum(part, axis=1, keepdims=True) * (1.0 / math.sqrt(z.width * z.copies))
    high = total.astype(BF16).astype(F32)
    middle = (total - high).astype(BF16).astype(F32)
    low = total - high - middle
    lane = iota((z.rows, LANES), 1)
    meta = jnp.where(lane == 1, high, jnp.where(lane == 2, middle, jnp.where(lane == 3, low, info_ref[...])))
    meta_ref[...] = meta.astype(BF16)
    for j in range(z.blocks):
        for i in range(1, 4):
            copies[j][i].wait()


def update_kernel(z, pick_ref, meta_ref, master, one, two, own, *refs):
    received, refs = refs[: z.copies - 1], refs[z.copies :]
    outs, rows_buf = refs[: z.peers], refs[z.peers]
    pick = jnp.concatenate([pick_ref[h] for h in range(z.split)], axis=1)
    for j in range(z.blocks):
        for h in range(z.split):
            for c in range(0, z.cb, z.sub):
                at = j * z.span + h * z.cb + c
                cols = slice(at, at + z.sub)
                summed = own[:, cols]
                for other in received:
                    summed = summed + other[:, cols].astype(F32)
                moved = master[:, cols]
                new_one = 0.9 * one[:, cols] + 0.1 * summed
                new_two = 0.95 * two[:, cols] + 0.05 * summed * summed
                update = new_one * (1.0 / (1.0 - 0.9**10)) / (jnp.sqrt(new_two * (1.0 / (1.0 - 0.95**10))) + 1e-08)
                new_master = moved - 0.05 * (update + 0.1 * moved)
                for i, value in enumerate((new_master, new_one, new_two)):
                    to = i * z.body + j * z.cb + c
                    rows_buf[h * z.rows : (h + 1) * z.rows, to : to + z.sub] = value.astype(BF16)
        for i in range(3):
            at = i * z.body + j * z.cb
            packed = jnp.dot(pick, rows_buf[:, at : at + z.cb], preferred_element_type=F32).astype(BF16)
            for s, out in enumerate(outs):
                out[:, at : at + z.cb] = packed[s * z.lines : (s + 1) * z.lines]
    meta = jnp.concatenate([meta_ref[...]] * z.split, axis=0)
    packed = jnp.dot(pick, meta, preferred_element_type=F32).astype(BF16)
    for s, out in enumerate(outs):
        out[:, 3 * z.body :] = packed[s * z.lines : (s + 1) * z.lines]


def gathered(refs, cols):
    return jnp.concatenate([ref[:, cols] for ref in refs], axis=0)


def placing(z, meta):
    offset = meta[:, :1].astype(F32).astype(jnp.int32)
    piece = lax.rem(iota((z.slots, 1), 0), z.lines) // z.cap
    wanted = jnp.where(offset > 0, offset - 1 + piece * z.rows, -1)
    return jnp.where(iota((z.slots, z.stacked), 1) == wanted, 1.0, 0.0).T.astype(BF16)


def placed(place, values):
    return jnp.dot(place, values, preferred_element_type=F32)


def half_kernel(z, *refs):
    got, (half, place_out) = refs[: z.peers], refs[z.peers :]
    meta = gathered(got, slice(3 * z.body, 3 * z.body + LANES))
    place = placing(z, meta)
    place_out[...] = place
    for j in range(z.blocks):
        rows_out = placed(place, gathered(got, slice(j * z.cb, (j + 1) * z.cb))).astype(BF16)
        for h in range(z.split):
            at = j * z.span + h * z.cb
            half[:, at : at + z.cb] = rows_out[h * z.rows : (h + 1) * z.rows]
    half[:, z.width :] = placed(place, meta)[: z.rows].astype(BF16)


def place_moment(z, i, place, got, out, buf, sems):
    copies = []
    for j in range(z.blocks):
        at = i * z.body + j * z.cb
        rows_out = placed(place, gathered(got, slice(at, at + z.cb)))
        for h in range(z.split):
            col = j * z.span + h * z.cb
            buf[:, col : col + z.cb] = rows_out[h * z.rows : (h + 1) * z.rows]
        cols = pl.ds(j * z.span, z.span)
        copies.append(pltpu.make_async_copy(buf.at[:, cols], out.at[:, cols], sems.at[j]))
        copies[-1].start()
    return copies


def rows_kernel(z, rep_ref, half, place, *refs):
    got, (new_master, params, one_out, two_out, master_buf, one_buf, two_buf, sems) = refs[: z.peers], refs[z.peers :]
    there = pl.ds(pl.multiple_of(rep_ref[0] * z.width, LANES), z.width)
    copies = [pltpu.make_async_copy(half.at[:, : z.width], params.at[:, there], sems.at[0, 0])]
    copies[0].start()
    for j in range(z.blocks):
        at = slice(j * z.span, (j + 1) * z.span)
        master_buf[:, at] = half[:, at].astype(F32)
        cols = pl.ds(j * z.span, z.span)
        copies.append(pltpu.make_async_copy(master_buf.at[:, cols], new_master.at[:, cols], sems.at[1, j]))
        copies[-1].start()
    copies += place_moment(z, 1, place[...], got, one_out, one_buf, sems.at[2])
    copies += place_moment(z, 2, place[...], got, two_out, two_buf, sems.at[3])
    for copy in copies:
        copy.wait()


def finish_kernel(z, rep_ref, half, *refs):
    others, (_, params, checksum, sems) = refs[: z.copies - 1], refs[z.copies - 1 :]
    copies = []
    for k, other in enumerate(others):
        replica = lax.rem(rep_ref[0] + z.copies - (k + 1), z.copies)
        there = pl.ds(pl.multiple_of(replica * z.width, LANES), z.width)
        copies.append(pltpu.make_async_copy(other.at[:, : z.width], params.at[:, there], sems.at[k]))
        copies[-1].start()
    sums = half[:, z.width :].astype(F32)
    for other in others:
        sums = sums + other[:, z.width :].astype(F32)
    lane = iota((z.rows, LANES), 1)
    column = jnp.sum(jnp.where((lane >= 1) & (lane <= 3), sums, 0.0), axis=1, keepdims=True)
    diagonal = iota((z.rows, z.rows), 0) == iota((z.rows, z.rows), 1)
    checksum[...] = jnp.sum(jnp.where(diagonal, column, 0.0), axis=0, keepdims=True)
    for copy in copies:
        copy.wait()


def shifted(value, axis, k, count):
    return lax.ppermute(value, axis, [(i, (i + k) % count) for i in range(count)])


def shift_groups(peers):
    return [[s, s + peers // 2] for s in range(1, peers // 2)]


def agree(used, stride, peers, after, compiler_params):
    vmem = pl.BlockSpec(memory_space=pltpu.VMEM)
    other = lax.ppermute(used, "fsdp", [(i, i ^ stride) for i in range(peers)])
    return pl.pallas_call(
        agree_kernel,
        out_shape=jax.ShapeDtypeStruct((1, LANES), jnp.int32),
        in_specs=[vmem, vmem, pl.BlockSpec(memory_space=pl.ANY)],
        out_specs=vmem,
        compiler_params=compiler_params,
        name="agree",
    )(used, other, after)


def choose_branches(used, after, peers, compiler_params):
    vmem = pl.BlockSpec(memory_space=pltpu.VMEM)
    smem = pl.BlockSpec(memory_space=pltpu.SMEM)
    groups = shift_groups(peers)
    for stride in range(peers // 4):
        if stride and stride & (stride - 1) == 0:
            used = agree(used, stride, peers, after, compiler_params)
    other = lax.ppermute(used, "fsdp", [(i, i ^ (peers // 2)) for i in range(peers)])
    return pl.pallas_call(
        functools.partial(choose_kernel, groups),
        out_shape=[pltpu.SMEM((1,), jnp.int32)] * len(groups),
        in_specs=[vmem, vmem],
        out_specs=[smem] * len(groups),
        compiler_params=compiler_params,
        name="choose",
    )(used, other)


def send_used(peers, group, used, chunks):
    return tuple(
        shifted(chunk, "fsdp", s, peers) if used >> i & 1 else chunk for i, (s, chunk) in enumerate(zip(group, chunks))
    )


def move(z, chunks, chosen):
    if chosen is None:
        got = lax.all_to_all(jnp.concatenate(chunks, axis=0), "fsdp", split_axis=0, concat_axis=0, tiled=True)
        return [got[s * z.lines : (s + 1) * z.lines] for s in range(z.peers)]
    got = list(chunks)
    half = z.peers // 2
    got[half] = shifted(chunks[half], "fsdp", half, z.peers)
    *chosen, got[half] = lax.optimization_barrier((*chosen, got[half]))
    for group, number in zip(shift_groups(z.peers), chosen):
        branches = [
            lambda *values, group=group, used=used: send_used(z.peers, group, used, values)
            for used in range(1 << len(group))
        ]
        for s, value in zip(group, lax.switch(number[0], branches, *[chunks[s] for s in group])):
            got[s] = value
    return got


def shards(master, moment_one, moment_two, gradients, new_row):
    rows, width = master.shape
    peers, copies = lax.axis_size("fsdp"), lax.axis_size("replica")
    z = Sizes(rows, width, peers, copies)
    compiler_params = pltpu.CompilerParams(vmem_limit_bytes=VMEM_BYTES)
    smem = pl.BlockSpec(memory_space=pltpu.SMEM)
    vmem = pl.BlockSpec(memory_space=pltpu.VMEM)
    hbm = pl.BlockSpec(memory_space=pl.ANY)
    dma = pltpu.SemaphoreType.DMA

    replica = lax.axis_index("replica").astype(jnp.int32)
    rep = replica.reshape(1)
    by_shift = 8 <= peers <= MOST_SHIFT_PEERS and peers & (peers - 1) == 0
    origin = (lax.axis_index("fsdp").astype(jnp.int32) if by_shift else jnp.int32(0)).reshape(1)
    state_in = [pltpu.with_memory_space_constraint(x, pltpu.HBM) for x in (master, moment_one, moment_two)]
    full = pltpu.with_memory_space_constraint(gradients[0], pltpu.HBM)

    part = jax.ShapeDtypeStruct((rows, width), BF16)
    pick, info, used, *parts = pl.pallas_call(
        functools.partial(prepare_kernel, z),
        out_shape=[
            jax.ShapeDtypeStruct((z.split, z.slots, rows), BF16),
            jax.ShapeDtypeStruct((rows, LANES), F32),
            jax.ShapeDtypeStruct((1, LANES), jnp.int32),
        ]
        + [part] * (copies - 1),
        in_specs=[smem, smem, hbm, hbm],
        out_specs=[vmem] * (copies + 2),
        scratch_shapes=[
            pltpu.VMEM((copies - 1, rows, width), F32),
            pltpu.VMEM((1, rows), jnp.int32),
            dma((copies - 1, z.blocks)),
            dma,
        ],
        compiler_params=compiler_params,
        cost_estimate=pl.CostEstimate(flops=1 << 30, bytes_accessed=1, transcendentals=0),
        name="prepare",
    )(rep, origin, pltpu.with_memory_space_constraint(new_row.reshape(1, rows), pltpu.HBM), full)
    received = [shifted(value, "replica", k + 1, copies) for k, value in enumerate(parts)]

    loaded = jax.ShapeDtypeStruct((rows, width), F32)
    *state, meta = pl.pallas_call(
        functools.partial(load_kernel, z),
        out_shape=[loaded, loaded, loaded, loaded, jax.ShapeDtypeStruct((rows, LANES), BF16)],
        in_specs=[smem, vmem, hbm, hbm, hbm, hbm],
        out_specs=[vmem] * 5,
        scratch_shapes=[dma((4, z.blocks))],
        compiler_params=compiler_params,
        cost_estimate=pl.CostEstimate(flops=1 << 30, bytes_accessed=1, transcendentals=0),
        name="load",
    )(rep, info, *state_in, full)

    if by_shift:
        used = agree(used, peers // 4, peers, meta, compiler_params)
    chunks = pl.pallas_call(
        functools.partial(update_kernel, z),
        out_shape=[jax.ShapeDtypeStruct((z.lines, z.payload), BF16)] * peers,
        in_specs=[vmem] * (5 + copies) + [hbm],
        out_specs=[vmem] * peers,
        scratch_shapes=[pltpu.VMEM((z.stacked, 3 * z.body), BF16)],
        compiler_params=compiler_params,
        cost_estimate=pl.CostEstimate(
            flops=6 * z.slots * z.stacked * z.body, bytes_accessed=24 * rows * width, transcendentals=rows * width
        ),
        name="update",
    )(pick, meta, *state, *received, used)

    chosen = choose_branches(used, chunks[0], peers, compiler_params) if by_shift else None
    got = move(z, chunks, chosen)

    wide = jax.ShapeDtypeStruct((rows, width), F32)
    full_params = jax.ShapeDtypeStruct((rows, width * copies), BF16)
    half, place = pl.pallas_call(
        functools.partial(half_kernel, z),
        out_shape=(
            jax.ShapeDtypeStruct((rows, width + LANES), BF16),
            jax.ShapeDtypeStruct((z.stacked, z.slots), BF16),
        ),
        in_specs=[vmem] * peers,
        out_specs=(vmem, vmem),
        compiler_params=compiler_params,
        name="place_half",
    )(*got)
    others = [shifted(half, "replica", k, copies) for k in range(1, copies)]

    new_master, params, new_one, new_two = pl.pallas_call(
        functools.partial(rows_kernel, z),
        out_shape=(wide, full_params, wide, wide),
        in_specs=[smem] + [vmem] * (peers + 2),
        out_specs=(hbm, hbm, hbm, hbm),
        scratch_shapes=[pltpu.VMEM((rows, width), F32)] * 3 + [dma((4, z.blocks))],
        compiler_params=compiler_params,
        cost_estimate=pl.CostEstimate(
            flops=4 * z.slots * z.stacked * z.body, bytes_accessed=18 * rows * width, transcendentals=0
        ),
        name="place_rows",
    )(rep, half, place, *got)

    params, checksum = pl.pallas_call(
        functools.partial(finish_kernel, z),
        out_shape=(full_params, jax.ShapeDtypeStruct((1, rows), F32)),
        in_specs=[smem] + [vmem] * copies + [hbm],
        out_specs=(hbm, vmem),
        scratch_shapes=[dma((max(1, copies - 1),))],
        input_output_aliases={copies + 1: 0},
        compiler_params=compiler_params,
        cost_estimate=pl.CostEstimate(flops=0, bytes_accessed=4 * rows * width, transcendentals=0),
        name="finish",
    )(rep, half, *others, params)
    return (new_master, new_one, new_two, params, checksum.reshape(rows))


def solution(mesh):
    return jax.shard_map(
        shards,
        mesh=mesh,
        in_specs=(
            P("fsdp", "replica"),
            P("fsdp", "replica"),
            P("fsdp", "replica"),
            P("replica", "fsdp", None),
            P("fsdp"),
        ),
        out_specs=(
            P("fsdp", "replica"),
            P("fsdp", "replica"),
            P("fsdp", "replica"),
            P("fsdp", None),
            P("fsdp"),
        ),
        check_vma=False,
    )
```

```python
import functools
import math

import jax
import jax.numpy as jnp
from jax import lax
from jax.experimental import pallas as pl
from jax.experimental.pallas import tpu as pltpu
from jax.sharding import PartitionSpec as P

LANES = 128
TILE_ROWS = 16
MIB = 1024 * 1024
VMEM_BYTES = 24 * MIB
MOST_SHIFT_PEERS = 16
GROUP = 4
WINDOW = 4
F32 = jnp.float32
BF16 = jnp.bfloat16


def iota(shape, axis):
    return lax.broadcasted_iota(jnp.int32, shape, axis)


class Sizes:
    def __init__(self, rows, width, peers, copies):
        self.rows, self.width, self.peers, self.copies = rows, width, peers, copies
        self.cap = max(2, 2 * rows // peers)
        self.split = max(1, TILE_ROWS // self.cap)
        self.lines = self.cap * self.split
        self.slots = peers * self.lines
        self.stacked = self.split * rows
        self.body = width // self.split
        self.cb = math.gcd(self.body, 512)
        self.blocks = self.body // self.cb
        self.span = self.split * self.cb
        self.sub = math.gcd(self.cb, 256)
        self.payload = 3 * self.body + LANES


def prepare_kernel(z, rep_ref, origin_ref, new_row_hbm, full_hbm, pick_ref, info_ref, mask_ref, *refs):
    parts, (full_buf, line_buf, sems, line_sem) = refs[: z.copies - 1], refs[z.copies - 1 :]
    step = z.width // z.blocks
    line_copy = pltpu.make_async_copy(new_row_hbm, line_buf, line_sem)
    line_copy.start()
    copies = []
    for k in range(1, z.copies):
        other = lax.rem(rep_ref[0] + k, z.copies)
        for j in range(z.blocks):
            there = pl.ds(pl.multiple_of(other * z.width + j * step, LANES), step)
            copies.append(
                pltpu.make_async_copy(
                    full_hbm.at[:, there], full_buf.at[k - 1, :, pl.ds(j * step, step)], sems.at[k - 1, j]
                )
            )
            copies[-1].start()
    line_copy.wait()
    line = line_buf[...]
    at_row, at_lane = iota((z.rows, z.rows), 0), iota((z.rows, z.rows), 1)
    column = jnp.sum(jnp.where(at_row == at_lane, line.astype(F32), 0.0), axis=1, keepdims=True).astype(jnp.int32)
    target, target_column = line // z.rows, column // z.rows
    earlier = (target_column == target) & (at_row < at_lane)
    rank = jnp.sum(jnp.where(earlier, 1.0, 0.0), axis=0, keepdims=True).astype(jnp.int32)
    shift = lax.rem(target - origin_ref[0] + z.peers, z.peers)
    shift_column = lax.rem(target_column - origin_ref[0] + z.peers, z.peers)
    for h in range(z.split):
        slot = shift * z.lines + h * z.cap + rank
        pick_ref[h] = jnp.where(iota((z.slots, z.rows), 0) == slot, 1.0, 0.0).astype(BF16)
    lane = iota((z.rows, LANES), 1)
    info_ref[...] = jnp.where(lane == 0, (column - target_column * z.rows + 1).astype(F32), 0.0)
    used = jnp.where(lane == shift_column, 1.0, 0.0)
    mask_ref[...] = jnp.max(used, axis=0, keepdims=True).astype(jnp.int32)
    for k in range(1, z.copies):
        for j in range(z.blocks):
            copies[(k - 1) * z.blocks + j].wait()
            at = slice(j * step, (j + 1) * step)
            parts[k - 1][:, at] = full_buf[k - 1, :, at].astype(BF16)


def agree_kernel(left, right, _, out):
    out[...] = jnp.maximum(left[...], right[...])


def choose_kernel(digits, left, right, *outs):
    total = jnp.maximum(left[...], right[...])
    lane = iota(total.shape, 1)
    for digit, out in zip(digits, outs):
        value = jnp.zeros(total.shape, jnp.int32)
        for i, s in enumerate(digit):
            value = value + jnp.where(lane == s, total << i, 0)
        out[0] = jnp.sum(value.astype(F32)).astype(jnp.int32)


def load_kernel(z, rep_ref, info_ref, master_hbm, one_hbm, two_hbm, full_hbm, master, one, two, own, meta_ref, sems):
    base = rep_ref[0] * z.width
    step = z.width // z.blocks
    copies = []
    for j in range(z.blocks):
        at = pl.ds(j * step, step)
        mine = pl.ds(pl.multiple_of(base + j * step, LANES), step)
        copies.append(
            [
                pltpu.make_async_copy(master_hbm.at[:, at], master.at[:, at], sems.at[0, j]),
                pltpu.make_async_copy(one_hbm.at[:, at], one.at[:, at], sems.at[1, j]),
                pltpu.make_async_copy(two_hbm.at[:, at], two.at[:, at], sems.at[2, j]),
                pltpu.make_async_copy(full_hbm.at[:, mine], own.at[:, at], sems.at[3, j]),
            ]
        )
    for i in range(4):
        for j in range(z.blocks):
            copies[j][i].start()
    part = jnp.zeros((z.rows, LANES), F32)
    for j in range(z.blocks):
        copies[j][0].wait()
        for at in range(j * step, (j + 1) * step, LANES):
            weights = 1.0 + ((iota((1, LANES), 1) + (base + at)) % 7).astype(F32) / 7.0
            part = part + master[:, at : at + LANES] * weights
    total = jnp.sum(part, axis=1, keepdims=True) * (1.0 / math.sqrt(z.width * z.copies))
    high = total.astype(BF16).astype(F32)
    middle = (total - high).astype(BF16).astype(F32)
    low = total - high - middle
    lane = iota((z.rows, LANES), 1)
    meta = jnp.where(lane == 1, high, jnp.where(lane == 2, middle, jnp.where(lane == 3, low, info_ref[...])))
    meta_ref[...] = meta.astype(BF16)
    for j in range(z.blocks):
        for i in range(1, 4):
            copies[j][i].wait()


def update_kernel(z, pick_ref, meta_ref, master, one, two, own, *refs):
    received, refs = refs[: z.copies - 1], refs[z.copies :]
    outs, rows_buf = refs[: z.peers], refs[z.peers]
    pick = jnp.concatenate([pick_ref[h] for h in range(z.split)], axis=1)
    for j in range(z.blocks):
        for h in range(z.split):
            for c in range(0, z.cb, z.sub):
                at = j * z.span + h * z.cb + c
                cols = slice(at, at + z.sub)
                summed = own[:, cols]
                for other in received:
                    summed = summed + other[:, cols].astype(F32)
                moved = master[:, cols]
                new_one = 0.9 * one[:, cols] + 0.1 * summed
                new_two = 0.95 * two[:, cols] + 0.05 * summed * summed
                update = new_one * (1.0 / (1.0 - 0.9**10)) / (jnp.sqrt(new_two * (1.0 / (1.0 - 0.95**10))) + 1e-08)
                new_master = moved - 0.05 * (update + 0.1 * moved)
                for i, value in enumerate((new_master, new_one, new_two)):
                    to = i * z.body + j * z.cb + c
                    rows_buf[h * z.rows : (h + 1) * z.rows, to : to + z.sub] = value.astype(BF16)
        for i in range(3):
            at = i * z.body + j * z.cb
            packed = jnp.dot(pick, rows_buf[:, at : at + z.cb], preferred_element_type=F32).astype(BF16)
            for s, out in enumerate(outs):
                out[:, at : at + z.cb] = packed[s * z.lines : (s + 1) * z.lines]
    meta = jnp.concatenate([meta_ref[...]] * z.split, axis=0)
    packed = jnp.dot(pick, meta, preferred_element_type=F32).astype(BF16)
    for s, out in enumerate(outs):
        out[:, 3 * z.body :] = packed[s * z.lines : (s + 1) * z.lines]


def gathered(refs, cols):
    return jnp.concatenate([ref[:, cols] for ref in refs], axis=0)


def placing(z, meta):
    offset = meta[:, :1].astype(F32).astype(jnp.int32)
    piece = lax.rem(iota((z.slots, 1), 0), z.lines) // z.cap
    wanted = jnp.where(offset > 0, offset - 1 + piece * z.rows, -1)
    return jnp.where(iota((z.slots, z.stacked), 1) == wanted, 1.0, 0.0).T.astype(BF16)


def placed(place, values):
    return jnp.dot(place, values, preferred_element_type=F32)


def half_kernel(z, *refs):
    got, (half, place_out) = refs[: z.peers], refs[z.peers :]
    meta = gathered(got, slice(3 * z.body, 3 * z.body + LANES))
    place = placing(z, meta)
    place_out[...] = place
    for j in range(z.blocks):
        rows_out = placed(place, gathered(got, slice(j * z.cb, (j + 1) * z.cb))).astype(BF16)
        for h in range(z.split):
            at = j * z.span + h * z.cb
            half[:, at : at + z.cb] = rows_out[h * z.rows : (h + 1) * z.rows]
    half[:, z.width :] = placed(place, meta)[: z.rows].astype(BF16)


def place_moment(z, i, place, got, out, buf, sems):
    copies = []
    for j in range(z.blocks):
        at = i * z.body + j * z.cb
        rows_out = placed(place, gathered(got, slice(at, at + z.cb)))
        for h in range(z.split):
            col = j * z.span + h * z.cb
            buf[:, col : col + z.cb] = rows_out[h * z.rows : (h + 1) * z.rows]
        cols = pl.ds(j * z.span, z.span)
        copies.append(pltpu.make_async_copy(buf.at[:, cols], out.at[:, cols], sems.at[j]))
        copies[-1].start()
    return copies


def rows_kernel(z, rep_ref, half, place, *refs):
    got, (new_master, params, one_out, two_out, master_buf, one_buf, two_buf, sems) = refs[: z.peers], refs[z.peers :]
    there = pl.ds(pl.multiple_of(rep_ref[0] * z.width, LANES), z.width)
    copies = [pltpu.make_async_copy(half.at[:, : z.width], params.at[:, there], sems.at[0, 0])]
    copies[0].start()
    for j in range(z.blocks):
        at = slice(j * z.span, (j + 1) * z.span)
        master_buf[:, at] = half[:, at].astype(F32)
        cols = pl.ds(j * z.span, z.span)
        copies.append(pltpu.make_async_copy(master_buf.at[:, cols], new_master.at[:, cols], sems.at[1, j]))
        copies[-1].start()
    copies += place_moment(z, 1, place[...], got, one_out, one_buf, sems.at[2])
    copies += place_moment(z, 2, place[...], got, two_out, two_buf, sems.at[3])
    for copy in copies:
        copy.wait()


def finish_kernel(z, rep_ref, half, *refs):
    others, (_, params, checksum, sems) = refs[: z.copies - 1], refs[z.copies - 1 :]
    copies = []
    for k, other in enumerate(others):
        replica = lax.rem(rep_ref[0] + z.copies - (k + 1), z.copies)
        there = pl.ds(pl.multiple_of(replica * z.width, LANES), z.width)
        copies.append(pltpu.make_async_copy(other.at[:, : z.width], params.at[:, there], sems.at[k]))
        copies[-1].start()
    sums = half[:, z.width :].astype(F32)
    for other in others:
        sums = sums + other[:, z.width :].astype(F32)
    lane = iota((z.rows, LANES), 1)
    column = jnp.sum(jnp.where((lane >= 1) & (lane <= 3), sums, 0.0), axis=1, keepdims=True)
    diagonal = iota((z.rows, z.rows), 0) == iota((z.rows, z.rows), 1)
    checksum[...] = jnp.sum(jnp.where(diagonal, column, 0.0), axis=0, keepdims=True)
    for copy in copies:
        copy.wait()


def shifted(value, axis, k, count):
    return lax.ppermute(value, axis, [(i, (i + k) % count) for i in range(count)])


def always_sent(peers):
    near = [s for s in range(1, peers) if min(s, peers - s) < peers // 4]
    return [peers // 2] + sorted(near, key=lambda s: (peers // 4 - s) % (peers // 4))


def shift_groups(peers):
    rest = [s for s in range(1, peers) if s not in always_sent(peers)]
    groups = -(-len(rest) // GROUP)
    return [rest[g::groups] for g in range(groups)]


def agree(used, stride, peers, after, compiler_params):
    vmem = pl.BlockSpec(memory_space=pltpu.VMEM)
    other = lax.ppermute(used, "fsdp", [(i, i ^ stride) for i in range(peers)])
    return pl.pallas_call(
        agree_kernel,
        out_shape=jax.ShapeDtypeStruct((1, LANES), jnp.int32),
        in_specs=[vmem, vmem, pl.BlockSpec(memory_space=pl.ANY)],
        out_specs=vmem,
        compiler_params=compiler_params,
        name="agree",
    )(used, other, after)


def choose_branches(used, peers, compiler_params):
    vmem = pl.BlockSpec(memory_space=pltpu.VMEM)
    smem = pl.BlockSpec(memory_space=pltpu.SMEM)
    groups = shift_groups(peers)
    other = lax.ppermute(used, "fsdp", [(i, i ^ (peers // 2)) for i in range(peers)])
    return pl.pallas_call(
        functools.partial(choose_kernel, groups),
        out_shape=[pltpu.SMEM((1,), jnp.int32)] * len(groups),
        in_specs=[vmem, vmem],
        out_specs=[smem] * len(groups),
        compiler_params=compiler_params,
        name="choose",
    )(used, other)


def send_used(peers, group, used, chunks):
    return tuple(
        shifted(chunk, "fsdp", s, peers) if used >> i & 1 else chunk for i, (s, chunk) in enumerate(zip(group, chunks))
    )


def move(z, chunks, used, by_shift, compiler_params):
    if not by_shift:
        got = lax.all_to_all(jnp.concatenate(chunks, axis=0), "fsdp", split_axis=0, concat_axis=0, tiled=True)
        return [got[s * z.lines : (s + 1) * z.lines] for s in range(z.peers)]
    got = list(chunks)
    always = always_sent(z.peers)
    for s in always[:WINDOW]:
        got[s] = shifted(chunks[s], "fsdp", s, z.peers)
    first, early = always[0], always[2:]
    for stride, s in zip([stride for stride in range(1, z.peers // 4) if stride & (stride - 1) == 0], early):
        used = agree(used, stride, z.peers, got[s], compiler_params)
    for s, after in zip(always[WINDOW:], always):
        ready = (got[first], used) if after == first else (got[after],)
        value = lax.optimization_barrier((chunks[s], *ready))[0]
        got[s] = shifted(value, "fsdp", s, z.peers)
    chosen = choose_branches(used, z.peers, compiler_params)
    barred = lax.optimization_barrier((*chosen, *[got[s] for s in always]))
    chosen = barred[: len(chosen)]
    for s, value in zip(always, barred[len(chosen) :]):
        got[s] = value
    for group, number in zip(shift_groups(z.peers), chosen):
        branches = [
            lambda *values, group=group, used=used: send_used(z.peers, group, used, values)
            for used in range(1 << len(group))
        ]
        for s, value in zip(group, lax.switch(number[0], branches, *[chunks[s] for s in group])):
            got[s] = value
    return got


def shards(master, moment_one, moment_two, gradients, new_row):
    rows, width = master.shape
    peers, copies = lax.axis_size("fsdp"), lax.axis_size("replica")
    z = Sizes(rows, width, peers, copies)
    compiler_params = pltpu.CompilerParams(vmem_limit_bytes=VMEM_BYTES)
    smem = pl.BlockSpec(memory_space=pltpu.SMEM)
    vmem = pl.BlockSpec(memory_space=pltpu.VMEM)
    hbm = pl.BlockSpec(memory_space=pl.ANY)
    dma = pltpu.SemaphoreType.DMA

    replica = lax.axis_index("replica").astype(jnp.int32)
    rep = replica.reshape(1)
    by_shift = 8 <= peers <= MOST_SHIFT_PEERS and peers & (peers - 1) == 0
    origin = (lax.axis_index("fsdp").astype(jnp.int32) if by_shift else jnp.int32(0)).reshape(1)
    state_in = [pltpu.with_memory_space_constraint(x, pltpu.HBM) for x in (master, moment_one, moment_two)]
    full = pltpu.with_memory_space_constraint(gradients[0], pltpu.HBM)

    part = jax.ShapeDtypeStruct((rows, width), BF16)
    pick, info, used, *parts = pl.pallas_call(
        functools.partial(prepare_kernel, z),
        out_shape=[
            jax.ShapeDtypeStruct((z.split, z.slots, rows), BF16),
            jax.ShapeDtypeStruct((rows, LANES), F32),
            jax.ShapeDtypeStruct((1, LANES), jnp.int32),
        ]
        + [part] * (copies - 1),
        in_specs=[smem, smem, hbm, hbm],
        out_specs=[vmem] * (copies + 2),
        scratch_shapes=[
            pltpu.VMEM((copies - 1, rows, width), F32),
            pltpu.VMEM((1, rows), jnp.int32),
            dma((copies - 1, z.blocks)),
            dma,
        ],
        compiler_params=compiler_params,
        cost_estimate=pl.CostEstimate(flops=1 << 30, bytes_accessed=1, transcendentals=0),
        name="prepare",
    )(rep, origin, pltpu.with_memory_space_constraint(new_row.reshape(1, rows), pltpu.HBM), full)
    received = [shifted(value, "replica", k + 1, copies) for k, value in enumerate(parts)]

    loaded = jax.ShapeDtypeStruct((rows, width), F32)
    *state, meta = pl.pallas_call(
        functools.partial(load_kernel, z),
        out_shape=[loaded, loaded, loaded, loaded, jax.ShapeDtypeStruct((rows, LANES), BF16)],
        in_specs=[smem, vmem, hbm, hbm, hbm, hbm],
        out_specs=[vmem] * 5,
        scratch_shapes=[dma((4, z.blocks))],
        compiler_params=compiler_params,
        cost_estimate=pl.CostEstimate(flops=1 << 30, bytes_accessed=1, transcendentals=0),
        name="load",
    )(rep, info, *state_in, full)

    if by_shift:
        used = agree(used, peers // 4, peers, meta, compiler_params)
    chunks = pl.pallas_call(
        functools.partial(update_kernel, z),
        out_shape=[jax.ShapeDtypeStruct((z.lines, z.payload), BF16)] * peers,
        in_specs=[vmem] * (5 + copies) + [hbm],
        out_specs=[vmem] * peers,
        scratch_shapes=[pltpu.VMEM((z.stacked, 3 * z.body), BF16)],
        compiler_params=compiler_params,
        cost_estimate=pl.CostEstimate(
            flops=6 * z.slots * z.stacked * z.body, bytes_accessed=24 * rows * width, transcendentals=rows * width
        ),
        name="update",
    )(pick, meta, *state, *received, used)

    got = move(z, chunks, used, by_shift, compiler_params)

    wide = jax.ShapeDtypeStruct((rows, width), F32)
    full_params = jax.ShapeDtypeStruct((rows, width * copies), BF16)
    half, place = pl.pallas_call(
        functools.partial(half_kernel, z),
        out_shape=(
            jax.ShapeDtypeStruct((rows, width + LANES), BF16),
            jax.ShapeDtypeStruct((z.stacked, z.slots), BF16),
        ),
        in_specs=[vmem] * peers,
        out_specs=(vmem, vmem),
        compiler_params=compiler_params,
        name="place_half",
    )(*got)
    others = [shifted(half, "replica", k, copies) for k in range(1, copies)]

    new_master, params, new_one, new_two = pl.pallas_call(
        functools.partial(rows_kernel, z),
        out_shape=(wide, full_params, wide, wide),
        in_specs=[smem] + [vmem] * (peers + 2),
        out_specs=(hbm, hbm, hbm, hbm),
        scratch_shapes=[pltpu.VMEM((rows, width), F32)] * 3 + [dma((4, z.blocks))],
        compiler_params=compiler_params,
        cost_estimate=pl.CostEstimate(
            flops=4 * z.slots * z.stacked * z.body, bytes_accessed=18 * rows * width, transcendentals=0
        ),
        name="place_rows",
    )(rep, half, place, *got)

    params, checksum = pl.pallas_call(
        functools.partial(finish_kernel, z),
        out_shape=(full_params, jax.ShapeDtypeStruct((1, rows), F32)),
        in_specs=[smem] + [vmem] * copies + [hbm],
        out_specs=(hbm, vmem),
        scratch_shapes=[dma((max(1, copies - 1),))],
        input_output_aliases={copies + 1: 0},
        compiler_params=compiler_params,
        cost_estimate=pl.CostEstimate(flops=0, bytes_accessed=4 * rows * width, transcendentals=0),
        name="finish",
    )(rep, half, *others, params)
    return (new_master, new_one, new_two, params, checksum.reshape(rows))


def solution(mesh):
    return jax.shard_map(
        shards,
        mesh=mesh,
        in_specs=(
            P("fsdp", "replica"),
            P("fsdp", "replica"),
            P("fsdp", "replica"),
            P("replica", "fsdp", None),
            P("fsdp"),
        ),
        out_specs=(
            P("fsdp", "replica"),
            P("fsdp", "replica"),
            P("fsdp", "replica"),
            P("fsdp", None),
            P("fsdp"),
        ),
        check_vma=False,
    )
```

```python
import functools
import math

import jax
import jax.numpy as jnp
from jax import lax
from jax.experimental import pallas as pl
from jax.experimental.pallas import tpu as pltpu
from jax.sharding import PartitionSpec as P

LANES = 128
TILE_ROWS = 16
MIB = 1024 * 1024
VMEM_BYTES = 24 * MIB
SHIFT_PEERS = 16
GROUP = 4
WINDOW = 4
F32 = jnp.float32
BF16 = jnp.bfloat16


def iota(shape, axis):
    return lax.broadcasted_iota(jnp.int32, shape, axis)


class Sizes:
    def __init__(self, rows, width, peers, copies):
        self.rows, self.width, self.peers, self.copies = rows, width, peers, copies
        self.cap = max(2, 2 * rows // peers)
        self.split = max(1, TILE_ROWS // self.cap)
        self.lines = self.cap * self.split
        self.slots = peers * self.lines
        self.stacked = self.split * rows
        self.body = width // self.split
        self.cb = math.gcd(self.body, 512)
        self.blocks = self.body // self.cb
        self.span = self.split * self.cb
        self.sub = math.gcd(self.cb, 256)
        self.payload = 3 * self.body + LANES


def prepare_kernel(z, rep_ref, origin_ref, new_row_hbm, full_hbm, pick_ref, info_ref, mask_ref, *refs):
    parts, (full_buf, line_buf, sems, line_sem) = refs[: z.copies - 1], refs[z.copies - 1 :]
    step = z.width // z.blocks
    line_copy = pltpu.make_async_copy(new_row_hbm, line_buf, line_sem)
    line_copy.start()
    copies = []
    for k in range(1, z.copies):
        other = lax.rem(rep_ref[0] + k, z.copies)
        for j in range(z.blocks):
            there = pl.ds(pl.multiple_of(other * z.width + j * step, LANES), step)
            copies.append(
                pltpu.make_async_copy(
                    full_hbm.at[:, there], full_buf.at[k - 1, :, pl.ds(j * step, step)], sems.at[k - 1, j]
                )
            )
            copies[-1].start()
    line_copy.wait()
    line = line_buf[...]
    at_row, at_lane = iota((z.rows, z.rows), 0), iota((z.rows, z.rows), 1)
    column = jnp.sum(jnp.where(at_row == at_lane, line.astype(F32), 0.0), axis=1, keepdims=True).astype(jnp.int32)
    target, target_column = line // z.rows, column // z.rows
    earlier = (target_column == target) & (at_row < at_lane)
    rank = jnp.sum(jnp.where(earlier, 1.0, 0.0), axis=0, keepdims=True).astype(jnp.int32)
    shift = lax.rem(target - origin_ref[0] + z.peers, z.peers)
    shift_column = lax.rem(target_column - origin_ref[0] + z.peers, z.peers)
    for h in range(z.split):
        slot = shift * z.lines + h * z.cap + rank
        pick_ref[h] = jnp.where(iota((z.slots, z.rows), 0) == slot, 1.0, 0.0).astype(BF16)
    lane = iota((z.rows, LANES), 1)
    info_ref[...] = jnp.where(lane == 0, (column - target_column * z.rows + 1).astype(F32), 0.0)
    used = jnp.where(lane == shift_column, 1.0, 0.0)
    mask_ref[...] = jnp.max(used, axis=0, keepdims=True).astype(jnp.int32)
    for k in range(1, z.copies):
        for j in range(z.blocks):
            copies[(k - 1) * z.blocks + j].wait()
            at = slice(j * step, (j + 1) * step)
            parts[k - 1][:, at] = full_buf[k - 1, :, at].astype(BF16)


def agree_kernel(left, right, _, out):
    out[...] = jnp.maximum(left[...], right[...])


def choose_kernel(digits, left, right, *outs):
    total = jnp.maximum(left[...], right[...])
    lane = iota(total.shape, 1)
    for digit, out in zip(digits, outs):
        value = jnp.zeros(total.shape, jnp.int32)
        for i, s in enumerate(digit):
            value = value + jnp.where(lane == s, total << i, 0)
        out[0] = jnp.sum(value.astype(F32)).astype(jnp.int32)


def load_kernel(z, rep_ref, info_ref, master_hbm, one_hbm, two_hbm, full_hbm, master, one, two, own, meta_ref, sems):
    base = rep_ref[0] * z.width
    step = z.width // z.blocks
    copies = []
    for j in range(z.blocks):
        at = pl.ds(j * step, step)
        mine = pl.ds(pl.multiple_of(base + j * step, LANES), step)
        copies.append(
            [
                pltpu.make_async_copy(master_hbm.at[:, at], master.at[:, at], sems.at[0, j]),
                pltpu.make_async_copy(one_hbm.at[:, at], one.at[:, at], sems.at[1, j]),
                pltpu.make_async_copy(two_hbm.at[:, at], two.at[:, at], sems.at[2, j]),
                pltpu.make_async_copy(full_hbm.at[:, mine], own.at[:, at], sems.at[3, j]),
            ]
        )
    for i in range(4):
        for j in range(z.blocks):
            copies[j][i].start()
    part = jnp.zeros((z.rows, LANES), F32)
    for j in range(z.blocks):
        copies[j][0].wait()
        for at in range(j * step, (j + 1) * step, LANES):
            weights = 1.0 + ((iota((1, LANES), 1) + (base + at)) % 7).astype(F32) / 7.0
            part = part + master[:, at : at + LANES] * weights
    total = jnp.sum(part, axis=1, keepdims=True) * (1.0 / math.sqrt(z.width * z.copies))
    high = total.astype(BF16).astype(F32)
    middle = (total - high).astype(BF16).astype(F32)
    low = total - high - middle
    lane = iota((z.rows, LANES), 1)
    meta = jnp.where(lane == 1, high, jnp.where(lane == 2, middle, jnp.where(lane == 3, low, info_ref[...])))
    meta_ref[...] = meta.astype(BF16)
    for j in range(z.blocks):
        for i in range(1, 4):
            copies[j][i].wait()


def update_kernel(z, pick_ref, meta_ref, master, one, two, own, *refs):
    received, refs = refs[: z.copies - 1], refs[z.copies :]
    outs, rows_buf = refs[: z.peers], refs[z.peers]
    pick = jnp.concatenate([pick_ref[h] for h in range(z.split)], axis=1)
    for j in range(z.blocks):
        for h in range(z.split):
            for c in range(0, z.cb, z.sub):
                at = j * z.span + h * z.cb + c
                cols = slice(at, at + z.sub)
                summed = own[:, cols]
                for other in received:
                    summed = summed + other[:, cols].astype(F32)
                moved = master[:, cols]
                new_one = 0.9 * one[:, cols] + 0.1 * summed
                new_two = 0.95 * two[:, cols] + 0.05 * summed * summed
                update = new_one * (1.0 / (1.0 - 0.9**10)) / (jnp.sqrt(new_two * (1.0 / (1.0 - 0.95**10))) + 1e-08)
                new_master = moved - 0.05 * (update + 0.1 * moved)
                for i, value in enumerate((new_master, new_one, new_two)):
                    to = i * z.body + j * z.cb + c
                    rows_buf[h * z.rows : (h + 1) * z.rows, to : to + z.sub] = value.astype(BF16)
        for i in range(3):
            at = i * z.body + j * z.cb
            packed = jnp.dot(pick, rows_buf[:, at : at + z.cb], preferred_element_type=F32).astype(BF16)
            for s, out in enumerate(outs):
                out[:, at : at + z.cb] = packed[s * z.lines : (s + 1) * z.lines]
    meta = jnp.concatenate([meta_ref[...]] * z.split, axis=0)
    packed = jnp.dot(pick, meta, preferred_element_type=F32).astype(BF16)
    for s, out in enumerate(outs):
        out[:, 3 * z.body :] = packed[s * z.lines : (s + 1) * z.lines]


def gathered(refs, cols):
    return jnp.concatenate([ref[:, cols] for ref in refs], axis=0)


def placing(z, meta):
    offset = meta[:, :1].astype(F32).astype(jnp.int32)
    piece = lax.rem(iota((z.slots, 1), 0), z.lines) // z.cap
    wanted = jnp.where(offset > 0, offset - 1 + piece * z.rows, -1)
    return jnp.where(iota((z.slots, z.stacked), 1) == wanted, 1.0, 0.0).T.astype(BF16)


def placed(place, values):
    return jnp.dot(place, values, preferred_element_type=F32)


def half_kernel(z, *refs):
    got, (half, place_out) = refs[: z.peers], refs[z.peers :]
    meta = gathered(got, slice(3 * z.body, 3 * z.body + LANES))
    place = placing(z, meta)
    place_out[...] = place
    for j in range(z.blocks):
        rows_out = placed(place, gathered(got, slice(j * z.cb, (j + 1) * z.cb))).astype(BF16)
        for h in range(z.split):
            at = j * z.span + h * z.cb
            half[:, at : at + z.cb] = rows_out[h * z.rows : (h + 1) * z.rows]
    half[:, z.width :] = placed(place, meta)[: z.rows].astype(BF16)


def place_moment(z, i, place, got, out, buf, sems):
    copies = []
    for j in range(z.blocks):
        at = i * z.body + j * z.cb
        rows_out = placed(place, gathered(got, slice(at, at + z.cb)))
        for h in range(z.split):
            col = j * z.span + h * z.cb
            buf[:, col : col + z.cb] = rows_out[h * z.rows : (h + 1) * z.rows]
        cols = pl.ds(j * z.span, z.span)
        copies.append(pltpu.make_async_copy(buf.at[:, cols], out.at[:, cols], sems.at[j]))
        copies[-1].start()
    return copies


def rows_kernel(z, rep_ref, half, place, *refs):
    got, (new_master, params, one_out, two_out, master_buf, one_buf, two_buf, sems) = refs[: z.peers], refs[z.peers :]
    there = pl.ds(pl.multiple_of(rep_ref[0] * z.width, LANES), z.width)
    copies = [pltpu.make_async_copy(half.at[:, : z.width], params.at[:, there], sems.at[0, 0])]
    copies[0].start()
    for j in range(z.blocks):
        at = slice(j * z.span, (j + 1) * z.span)
        master_buf[:, at] = half[:, at].astype(F32)
        cols = pl.ds(j * z.span, z.span)
        copies.append(pltpu.make_async_copy(master_buf.at[:, cols], new_master.at[:, cols], sems.at[1, j]))
        copies[-1].start()
    copies += place_moment(z, 1, place[...], got, one_out, one_buf, sems.at[2])
    copies += place_moment(z, 2, place[...], got, two_out, two_buf, sems.at[3])
    for copy in copies:
        copy.wait()


def finish_kernel(z, rep_ref, half, *refs):
    others, (_, params, checksum, sems) = refs[: z.copies - 1], refs[z.copies - 1 :]
    copies = []
    for k, other in enumerate(others):
        replica = lax.rem(rep_ref[0] + z.copies - (k + 1), z.copies)
        there = pl.ds(pl.multiple_of(replica * z.width, LANES), z.width)
        copies.append(pltpu.make_async_copy(other.at[:, : z.width], params.at[:, there], sems.at[k]))
        copies[-1].start()
    sums = half[:, z.width :].astype(F32)
    for other in others:
        sums = sums + other[:, z.width :].astype(F32)
    lane = iota((z.rows, LANES), 1)
    column = jnp.sum(jnp.where((lane >= 1) & (lane <= 3), sums, 0.0), axis=1, keepdims=True)
    diagonal = iota((z.rows, z.rows), 0) == iota((z.rows, z.rows), 1)
    checksum[...] = jnp.sum(jnp.where(diagonal, column, 0.0), axis=0, keepdims=True)
    for copy in copies:
        copy.wait()


def shifted(value, axis, k, count):
    return lax.ppermute(value, axis, [(i, (i + k) % count) for i in range(count)])


def always_sent(peers):
    near = [s for s in range(1, peers) if min(s, peers - s) < peers // 4]
    return [peers // 2] + sorted(near, key=lambda s: (peers // 4 - s) % (peers // 4))


def shift_groups(peers):
    rest = [s for s in range(1, peers) if s not in always_sent(peers)]
    groups = -(-len(rest) // GROUP)
    return [rest[g::groups] for g in range(groups)]


def agree(used, stride, peers, after, compiler_params):
    vmem = pl.BlockSpec(memory_space=pltpu.VMEM)
    other = lax.ppermute(used, "fsdp", [(i, i ^ stride) for i in range(peers)])
    return pl.pallas_call(
        agree_kernel,
        out_shape=jax.ShapeDtypeStruct((1, LANES), jnp.int32),
        in_specs=[vmem, vmem, pl.BlockSpec(memory_space=pl.ANY)],
        out_specs=vmem,
        compiler_params=compiler_params,
        name="agree",
    )(used, other, after)


def choose_branches(used, peers, compiler_params):
    vmem = pl.BlockSpec(memory_space=pltpu.VMEM)
    smem = pl.BlockSpec(memory_space=pltpu.SMEM)
    groups = shift_groups(peers)
    other = lax.ppermute(used, "fsdp", [(i, i ^ (peers // 2)) for i in range(peers)])
    return pl.pallas_call(
        functools.partial(choose_kernel, groups),
        out_shape=[pltpu.SMEM((1,), jnp.int32)] * len(groups),
        in_specs=[vmem, vmem],
        out_specs=[smem] * len(groups),
        compiler_params=compiler_params,
        name="choose",
    )(used, other)


def send_used(peers, group, used, chunks):
    return tuple(
        shifted(chunk, "fsdp", s, peers) if used >> i & 1 else chunk for i, (s, chunk) in enumerate(zip(group, chunks))
    )


def move(z, chunks, used, by_shift, compiler_params):
    if not by_shift:
        got = lax.all_to_all(jnp.concatenate(chunks, axis=0), "fsdp", split_axis=0, concat_axis=0, tiled=True)
        return [got[s * z.lines : (s + 1) * z.lines] for s in range(z.peers)]
    got = list(chunks)
    always = always_sent(z.peers)
    for s in always[:WINDOW]:
        got[s] = shifted(chunks[s], "fsdp", s, z.peers)
    early = always[1:WINDOW]
    agreed = agree(used, 1, z.peers, got[early[-1]], compiler_params)
    used = agree(agreed, 2, z.peers, got[early[1]], compiler_params)
    for s, after in zip(always[WINDOW:], early):
        ready = (got[after], agreed) if after == early[0] else (got[after],)
        value = lax.optimization_barrier((chunks[s], *ready))[0]
        got[s] = shifted(value, "fsdp", s, z.peers)
    chosen = choose_branches(used, z.peers, compiler_params)
    barred = lax.optimization_barrier((*chosen, *[got[s] for s in always]))
    chosen = barred[: len(chosen)]
    for s, value in zip(always, barred[len(chosen) :]):
        got[s] = value
    for group, number in zip(shift_groups(z.peers), chosen):
        branches = [
            lambda *values, group=group, used=used: send_used(z.peers, group, used, values)
            for used in range(1 << len(group))
        ]
        for s, value in zip(group, lax.switch(number[0], branches, *[chunks[s] for s in group])):
            got[s] = value
    return got


def shards(master, moment_one, moment_two, gradients, new_row):
    rows, width = master.shape
    peers, copies = lax.axis_size("fsdp"), lax.axis_size("replica")
    z = Sizes(rows, width, peers, copies)
    compiler_params = pltpu.CompilerParams(vmem_limit_bytes=VMEM_BYTES)
    smem = pl.BlockSpec(memory_space=pltpu.SMEM)
    vmem = pl.BlockSpec(memory_space=pltpu.VMEM)
    hbm = pl.BlockSpec(memory_space=pl.ANY)
    dma = pltpu.SemaphoreType.DMA

    replica = lax.axis_index("replica").astype(jnp.int32)
    rep = replica.reshape(1)
    by_shift = peers == SHIFT_PEERS
    origin = (lax.axis_index("fsdp").astype(jnp.int32) if by_shift else jnp.int32(0)).reshape(1)
    state_in = [pltpu.with_memory_space_constraint(x, pltpu.HBM) for x in (master, moment_one, moment_two)]
    full = pltpu.with_memory_space_constraint(gradients[0], pltpu.HBM)

    part = jax.ShapeDtypeStruct((rows, width), BF16)
    pick, info, used, *parts = pl.pallas_call(
        functools.partial(prepare_kernel, z),
        out_shape=[
            jax.ShapeDtypeStruct((z.split, z.slots, rows), BF16),
            jax.ShapeDtypeStruct((rows, LANES), F32),
            jax.ShapeDtypeStruct((1, LANES), jnp.int32),
        ]
        + [part] * (copies - 1),
        in_specs=[smem, smem, hbm, hbm],
        out_specs=[vmem] * (copies + 2),
        scratch_shapes=[
            pltpu.VMEM((copies - 1, rows, width), F32),
            pltpu.VMEM((1, rows), jnp.int32),
            dma((copies - 1, z.blocks)),
            dma,
        ],
        compiler_params=compiler_params,
        cost_estimate=pl.CostEstimate(flops=1 << 30, bytes_accessed=1, transcendentals=0),
        name="prepare",
    )(rep, origin, pltpu.with_memory_space_constraint(new_row.reshape(1, rows), pltpu.HBM), full)
    received = [shifted(value, "replica", k + 1, copies) for k, value in enumerate(parts)]

    loaded = jax.ShapeDtypeStruct((rows, width), F32)
    *state, meta = pl.pallas_call(
        functools.partial(load_kernel, z),
        out_shape=[loaded, loaded, loaded, loaded, jax.ShapeDtypeStruct((rows, LANES), BF16)],
        in_specs=[smem, vmem, hbm, hbm, hbm, hbm],
        out_specs=[vmem] * 5,
        scratch_shapes=[dma((4, z.blocks))],
        compiler_params=compiler_params,
        cost_estimate=pl.CostEstimate(flops=1 << 30, bytes_accessed=1, transcendentals=0),
        name="load",
    )(rep, info, *state_in, full)

    if by_shift:
        used = agree(used, peers // 4, peers, meta, compiler_params)
    chunks = pl.pallas_call(
        functools.partial(update_kernel, z),
        out_shape=[jax.ShapeDtypeStruct((z.lines, z.payload), BF16)] * peers,
        in_specs=[vmem] * (5 + copies) + [hbm],
        out_specs=[vmem] * peers,
        scratch_shapes=[pltpu.VMEM((z.stacked, 3 * z.body), BF16)],
        compiler_params=compiler_params,
        cost_estimate=pl.CostEstimate(
            flops=6 * z.slots * z.stacked * z.body, bytes_accessed=24 * rows * width, transcendentals=rows * width
        ),
        name="update",
    )(pick, meta, *state, *received, used)

    got = move(z, chunks, used, by_shift, compiler_params)

    wide = jax.ShapeDtypeStruct((rows, width), F32)
    full_params = jax.ShapeDtypeStruct((rows, width * copies), BF16)
    half, place = pl.pallas_call(
        functools.partial(half_kernel, z),
        out_shape=(
            jax.ShapeDtypeStruct((rows, width + LANES), BF16),
            jax.ShapeDtypeStruct((z.stacked, z.slots), BF16),
        ),
        in_specs=[vmem] * peers,
        out_specs=(vmem, vmem),
        compiler_params=compiler_params,
        name="place_half",
    )(*got)
    others = [shifted(half, "replica", k, copies) for k in range(1, copies)]

    new_master, params, new_one, new_two = pl.pallas_call(
        functools.partial(rows_kernel, z),
        out_shape=(wide, full_params, wide, wide),
        in_specs=[smem] + [vmem] * (peers + 2),
        out_specs=(hbm, hbm, hbm, hbm),
        scratch_shapes=[pltpu.VMEM((rows, width), F32)] * 3 + [dma((4, z.blocks))],
        compiler_params=compiler_params,
        cost_estimate=pl.CostEstimate(
            flops=4 * z.slots * z.stacked * z.body, bytes_accessed=18 * rows * width, transcendentals=0
        ),
        name="place_rows",
    )(rep, half, place, *got)

    params, checksum = pl.pallas_call(
        functools.partial(finish_kernel, z),
        out_shape=(full_params, jax.ShapeDtypeStruct((1, rows), F32)),
        in_specs=[smem] + [vmem] * copies + [hbm],
        out_specs=(hbm, vmem),
        scratch_shapes=[dma((max(1, copies - 1),))],
        input_output_aliases={copies + 1: 0},
        compiler_params=compiler_params,
        cost_estimate=pl.CostEstimate(flops=0, bytes_accessed=4 * rows * width, transcendentals=0),
        name="finish",
    )(rep, half, *others, params)
    return (new_master, new_one, new_two, params, checksum.reshape(rows))


def solution(mesh):
    return jax.shard_map(
        shards,
        mesh=mesh,
        in_specs=(
            P("fsdp", "replica"),
            P("fsdp", "replica"),
            P("fsdp", "replica"),
            P("replica", "fsdp", None),
            P("fsdp"),
        ),
        out_specs=(
            P("fsdp", "replica"),
            P("fsdp", "replica"),
            P("fsdp", "replica"),
            P("fsdp", None),
            P("fsdp"),
        ),
        check_vma=False,
    )
```

```python
import functools
import math

import jax
import jax.numpy as jnp
from jax import lax
from jax.experimental import pallas as pl
from jax.experimental.pallas import tpu as pltpu
from jax.sharding import PartitionSpec as P

LANES = 128
TILE_ROWS = 16
MIB = 1024 * 1024
VMEM_BYTES = 24 * MIB
SHIFT_PEERS = 16
GROUP = 4
F32 = jnp.float32
BF16 = jnp.bfloat16


def iota(shape, axis):
    return lax.broadcasted_iota(jnp.int32, shape, axis)


class Sizes:
    def __init__(self, rows, width, peers, copies):
        self.rows, self.width, self.peers, self.copies = rows, width, peers, copies
        self.cap = max(2, 2 * rows // peers)
        self.split = max(1, TILE_ROWS // self.cap)
        self.lines = self.cap * self.split
        self.slots = peers * self.lines
        self.stacked = self.split * rows
        self.body = width // self.split
        self.cb = math.gcd(self.body, 512)
        self.blocks = self.body // self.cb
        self.span = self.split * self.cb
        self.sub = math.gcd(self.cb, 256)
        self.payload = 3 * self.body + LANES


def prepare_kernel(z, rep_ref, origin_ref, new_row_hbm, full_hbm, pick_ref, info_ref, mask_ref, *refs):
    parts, (full_buf, line_buf, sems, line_sem) = refs[: z.copies - 1], refs[z.copies - 1 :]
    step = z.width // z.blocks
    line_copy = pltpu.make_async_copy(new_row_hbm, line_buf, line_sem)
    line_copy.start()
    copies = []
    for k in range(1, z.copies):
        other = lax.rem(rep_ref[0] + k, z.copies)
        for j in range(z.blocks):
            there = pl.ds(pl.multiple_of(other * z.width + j * step, LANES), step)
            copies.append(
                pltpu.make_async_copy(
                    full_hbm.at[:, there], full_buf.at[k - 1, :, pl.ds(j * step, step)], sems.at[k - 1, j]
                )
            )
            copies[-1].start()
    line_copy.wait()
    line = line_buf[...]
    at_row, at_lane = iota((z.rows, z.rows), 0), iota((z.rows, z.rows), 1)
    column = jnp.sum(jnp.where(at_row == at_lane, line.astype(F32), 0.0), axis=1, keepdims=True).astype(jnp.int32)
    target, target_column = line // z.rows, column // z.rows
    earlier = (target_column == target) & (at_row < at_lane)
    rank = jnp.sum(jnp.where(earlier, 1.0, 0.0), axis=0, keepdims=True).astype(jnp.int32)
    shift = lax.rem(target - origin_ref[0] + z.peers, z.peers)
    shift_column = lax.rem(target_column - origin_ref[0] + z.peers, z.peers)
    for h in range(z.split):
        slot = shift * z.lines + h * z.cap + rank
        pick_ref[h] = jnp.where(iota((z.slots, z.rows), 0) == slot, 1.0, 0.0).astype(BF16)
    lane = iota((z.rows, LANES), 1)
    info_ref[...] = jnp.where(lane == 0, (column - target_column * z.rows + 1).astype(F32), 0.0)
    used = jnp.where(lane == shift_column, 1.0, 0.0)
    mask_ref[...] = jnp.max(used, axis=0, keepdims=True).astype(jnp.int32)
    for k in range(1, z.copies):
        for j in range(z.blocks):
            copies[(k - 1) * z.blocks + j].wait()
            at = slice(j * step, (j + 1) * step)
            parts[k - 1][:, at] = full_buf[k - 1, :, at].astype(BF16)


def agree_kernel(left, right, _, out):
    out[...] = jnp.maximum(left[...], right[...])


def choose_kernel(digits, left, right, *outs):
    total = jnp.maximum(left[...], right[...])
    lane = iota(total.shape, 1)
    for digit, out in zip(digits, outs):
        value = jnp.zeros(total.shape, jnp.int32)
        for i, s in enumerate(digit):
            value = value + jnp.where(lane == s, total << i, 0)
        out[0] = jnp.sum(value.astype(F32)).astype(jnp.int32)


def load_kernel(z, rep_ref, info_ref, master_hbm, one_hbm, two_hbm, full_hbm, master, one, two, own, meta_ref, sems):
    base = rep_ref[0] * z.width
    step = z.width // z.blocks
    copies = []
    for j in range(z.blocks):
        at = pl.ds(j * step, step)
        mine = pl.ds(pl.multiple_of(base + j * step, LANES), step)
        copies.append(
            [
                pltpu.make_async_copy(master_hbm.at[:, at], master.at[:, at], sems.at[0, j]),
                pltpu.make_async_copy(one_hbm.at[:, at], one.at[:, at], sems.at[1, j]),
                pltpu.make_async_copy(two_hbm.at[:, at], two.at[:, at], sems.at[2, j]),
                pltpu.make_async_copy(full_hbm.at[:, mine], own.at[:, at], sems.at[3, j]),
            ]
        )
    for i in range(4):
        for j in range(z.blocks):
            copies[j][i].start()
    part = jnp.zeros((z.rows, LANES), F32)
    for j in range(z.blocks):
        copies[j][0].wait()
        for at in range(j * step, (j + 1) * step, LANES):
            weights = 1.0 + ((iota((1, LANES), 1) + (base + at)) % 7).astype(F32) / 7.0
            part = part + master[:, at : at + LANES] * weights
    total = jnp.sum(part, axis=1, keepdims=True) * (1.0 / math.sqrt(z.width * z.copies))
    high = total.astype(BF16).astype(F32)
    middle = (total - high).astype(BF16).astype(F32)
    low = total - high - middle
    lane = iota((z.rows, LANES), 1)
    meta = jnp.where(lane == 1, high, jnp.where(lane == 2, middle, jnp.where(lane == 3, low, info_ref[...])))
    meta_ref[...] = meta.astype(BF16)
    for j in range(z.blocks):
        for i in range(1, 4):
            copies[j][i].wait()


def update_kernel(z, pick_ref, meta_ref, master, one, two, own, *refs):
    received, refs = refs[: z.copies - 1], refs[z.copies :]
    outs, rows_buf = refs[: z.peers], refs[z.peers]
    pick = jnp.concatenate([pick_ref[h] for h in range(z.split)], axis=1)
    for j in range(z.blocks):
        for h in range(z.split):
            for c in range(0, z.cb, z.sub):
                at = j * z.span + h * z.cb + c
                cols = slice(at, at + z.sub)
                summed = own[:, cols]
                for other in received:
                    summed = summed + other[:, cols].astype(F32)
                moved = master[:, cols]
                new_one = 0.9 * one[:, cols] + 0.1 * summed
                new_two = 0.95 * two[:, cols] + 0.05 * summed * summed
                update = new_one * (1.0 / (1.0 - 0.9**10)) / (jnp.sqrt(new_two * (1.0 / (1.0 - 0.95**10))) + 1e-08)
                new_master = moved - 0.05 * (update + 0.1 * moved)
                for i, value in enumerate((new_master, new_one, new_two)):
                    to = i * z.body + j * z.cb + c
                    rows_buf[h * z.rows : (h + 1) * z.rows, to : to + z.sub] = value.astype(BF16)
        for i in range(3):
            at = i * z.body + j * z.cb
            packed = jnp.dot(pick, rows_buf[:, at : at + z.cb], preferred_element_type=F32).astype(BF16)
            for s, out in enumerate(outs):
                out[:, at : at + z.cb] = packed[s * z.lines : (s + 1) * z.lines]
    meta = jnp.concatenate([meta_ref[...]] * z.split, axis=0)
    packed = jnp.dot(pick, meta, preferred_element_type=F32).astype(BF16)
    for s, out in enumerate(outs):
        out[:, 3 * z.body :] = packed[s * z.lines : (s + 1) * z.lines]


def gathered(refs, cols):
    return jnp.concatenate([ref[:, cols] for ref in refs], axis=0)


def placing(z, meta):
    offset = meta[:, :1].astype(F32).astype(jnp.int32)
    piece = lax.rem(iota((z.slots, 1), 0), z.lines) // z.cap
    wanted = jnp.where(offset > 0, offset - 1 + piece * z.rows, -1)
    return jnp.where(iota((z.slots, z.stacked), 1) == wanted, 1.0, 0.0).T.astype(BF16)


def placed(place, values):
    return jnp.dot(place, values, preferred_element_type=F32)


def half_kernel(z, *refs):
    got, (half, place_out) = refs[: z.peers], refs[z.peers :]
    meta = gathered(got, slice(3 * z.body, 3 * z.body + LANES))
    place = placing(z, meta)
    place_out[...] = place
    for j in range(z.blocks):
        rows_out = placed(place, gathered(got, slice(j * z.cb, (j + 1) * z.cb))).astype(BF16)
        for h in range(z.split):
            at = j * z.span + h * z.cb
            half[:, at : at + z.cb] = rows_out[h * z.rows : (h + 1) * z.rows]
    half[:, z.width :] = placed(place, meta)[: z.rows].astype(BF16)


def place_moment(z, i, place, got, out, buf, sems):
    copies = []
    for j in range(z.blocks):
        at = i * z.body + j * z.cb
        rows_out = placed(place, gathered(got, slice(at, at + z.cb)))
        for h in range(z.split):
            col = j * z.span + h * z.cb
            buf[:, col : col + z.cb] = rows_out[h * z.rows : (h + 1) * z.rows]
        cols = pl.ds(j * z.span, z.span)
        copies.append(pltpu.make_async_copy(buf.at[:, cols], out.at[:, cols], sems.at[j]))
        copies[-1].start()
    return copies


def rows_kernel(z, rep_ref, half, place, *refs):
    got, (new_master, params, one_out, two_out, master_buf, one_buf, two_buf, sems) = refs[: z.peers], refs[z.peers :]
    there = pl.ds(pl.multiple_of(rep_ref[0] * z.width, LANES), z.width)
    copies = [pltpu.make_async_copy(half.at[:, : z.width], params.at[:, there], sems.at[0, 0])]
    copies[0].start()
    for j in range(z.blocks):
        at = slice(j * z.span, (j + 1) * z.span)
        master_buf[:, at] = half[:, at].astype(F32)
        cols = pl.ds(j * z.span, z.span)
        copies.append(pltpu.make_async_copy(master_buf.at[:, cols], new_master.at[:, cols], sems.at[1, j]))
        copies[-1].start()
    copies += place_moment(z, 1, place[...], got, one_out, one_buf, sems.at[2])
    copies += place_moment(z, 2, place[...], got, two_out, two_buf, sems.at[3])
    for copy in copies:
        copy.wait()


def finish_kernel(z, rep_ref, half, *refs):
    others, (_, params, checksum, sems) = refs[: z.copies - 1], refs[z.copies - 1 :]
    copies = []
    for k, other in enumerate(others):
        replica = lax.rem(rep_ref[0] + z.copies - (k + 1), z.copies)
        there = pl.ds(pl.multiple_of(replica * z.width, LANES), z.width)
        copies.append(pltpu.make_async_copy(other.at[:, : z.width], params.at[:, there], sems.at[k]))
        copies[-1].start()
    sums = half[:, z.width :].astype(F32)
    for other in others:
        sums = sums + other[:, z.width :].astype(F32)
    lane = iota((z.rows, LANES), 1)
    column = jnp.sum(jnp.where((lane >= 1) & (lane <= 3), sums, 0.0), axis=1, keepdims=True)
    diagonal = iota((z.rows, z.rows), 0) == iota((z.rows, z.rows), 1)
    checksum[...] = jnp.sum(jnp.where(diagonal, column, 0.0), axis=0, keepdims=True)
    for copy in copies:
        copy.wait()


def shifted(value, axis, k, count):
    return lax.ppermute(value, axis, [(i, (i + k) % count) for i in range(count)])


def always_sent(peers):
    return [peers // 2, peers // 4 - 1, peers - 1]


def shift_groups(peers):
    rest = [s for s in range(1, peers) if s not in always_sent(peers)]
    groups = -(-len(rest) // GROUP)
    return [rest[g::groups] for g in range(groups)]


def agree(used, stride, peers, after, compiler_params):
    vmem = pl.BlockSpec(memory_space=pltpu.VMEM)
    other = lax.ppermute(used, "fsdp", [(i, i ^ stride) for i in range(peers)])
    return pl.pallas_call(
        agree_kernel,
        out_shape=jax.ShapeDtypeStruct((1, LANES), jnp.int32),
        in_specs=[vmem, vmem, pl.BlockSpec(memory_space=pl.ANY)],
        out_specs=vmem,
        compiler_params=compiler_params,
        name="agree",
    )(used, other, after)


def choose_branches(used, peers, compiler_params):
    vmem = pl.BlockSpec(memory_space=pltpu.VMEM)
    smem = pl.BlockSpec(memory_space=pltpu.SMEM)
    groups = shift_groups(peers)
    other = lax.ppermute(used, "fsdp", [(i, i ^ (peers // 2)) for i in range(peers)])
    return pl.pallas_call(
        functools.partial(choose_kernel, groups),
        out_shape=[pltpu.SMEM((1,), jnp.int32)] * len(groups),
        in_specs=[vmem, vmem],
        out_specs=[smem] * len(groups),
        compiler_params=compiler_params,
        name="choose",
    )(used, other)


def send_used(peers, group, used, chunks):
    return tuple(
        shifted(chunk, "fsdp", s, peers) if used >> i & 1 else chunk for i, (s, chunk) in enumerate(zip(group, chunks))
    )


def move(z, chunks, used, by_shift, compiler_params):
    if not by_shift:
        got = lax.all_to_all(jnp.concatenate(chunks, axis=0), "fsdp", split_axis=0, concat_axis=0, tiled=True)
        return [got[s * z.lines : (s + 1) * z.lines] for s in range(z.peers)]
    got = list(chunks)
    always = always_sent(z.peers)
    first = always[0]
    got[first] = shifted(chunks[first], "fsdp", first, z.peers)
    used = agree(used, 1, z.peers, chunks[first], compiler_params)
    for s in always[1:]:
        value, _ = lax.optimization_barrier((chunks[s], used))
        got[s] = shifted(value, "fsdp", s, z.peers)
    used = agree(used, 2, z.peers, chunks[first], compiler_params)
    chosen = choose_branches(used, z.peers, compiler_params)
    barred = lax.optimization_barrier((*chosen, *[got[s] for s in always]))
    chosen = barred[: len(chosen)]
    for s, value in zip(always, barred[len(chosen) :]):
        got[s] = value
    for group, number in zip(shift_groups(z.peers), chosen):
        branches = [
            lambda *values, group=group, used=used: send_used(z.peers, group, used, values)
            for used in range(1 << len(group))
        ]
        for s, value in zip(group, lax.switch(number[0], branches, *[chunks[s] for s in group])):
            got[s] = value
    return got


def shards(master, moment_one, moment_two, gradients, new_row):
    rows, width = master.shape
    peers, copies = lax.axis_size("fsdp"), lax.axis_size("replica")
    z = Sizes(rows, width, peers, copies)
    compiler_params = pltpu.CompilerParams(vmem_limit_bytes=VMEM_BYTES)
    smem = pl.BlockSpec(memory_space=pltpu.SMEM)
    vmem = pl.BlockSpec(memory_space=pltpu.VMEM)
    hbm = pl.BlockSpec(memory_space=pl.ANY)
    dma = pltpu.SemaphoreType.DMA

    replica = lax.axis_index("replica").astype(jnp.int32)
    rep = replica.reshape(1)
    by_shift = peers == SHIFT_PEERS
    origin = (lax.axis_index("fsdp").astype(jnp.int32) if by_shift else jnp.int32(0)).reshape(1)
    state_in = [pltpu.with_memory_space_constraint(x, pltpu.HBM) for x in (master, moment_one, moment_two)]
    full = pltpu.with_memory_space_constraint(gradients[0], pltpu.HBM)

    part = jax.ShapeDtypeStruct((rows, width), BF16)
    pick, info, used, *parts = pl.pallas_call(
        functools.partial(prepare_kernel, z),
        out_shape=[
            jax.ShapeDtypeStruct((z.split, z.slots, rows), BF16),
            jax.ShapeDtypeStruct((rows, LANES), F32),
            jax.ShapeDtypeStruct((1, LANES), jnp.int32),
        ]
        + [part] * (copies - 1),
        in_specs=[smem, smem, hbm, hbm],
        out_specs=[vmem] * (copies + 2),
        scratch_shapes=[
            pltpu.VMEM((copies - 1, rows, width), F32),
            pltpu.VMEM((1, rows), jnp.int32),
            dma((copies - 1, z.blocks)),
            dma,
        ],
        compiler_params=compiler_params,
        cost_estimate=pl.CostEstimate(flops=1 << 30, bytes_accessed=1, transcendentals=0),
        name="prepare",
    )(rep, origin, pltpu.with_memory_space_constraint(new_row.reshape(1, rows), pltpu.HBM), full)
    received = [shifted(value, "replica", k + 1, copies) for k, value in enumerate(parts)]

    loaded = jax.ShapeDtypeStruct((rows, width), F32)
    *state, meta = pl.pallas_call(
        functools.partial(load_kernel, z),
        out_shape=[loaded, loaded, loaded, loaded, jax.ShapeDtypeStruct((rows, LANES), BF16)],
        in_specs=[smem, vmem, hbm, hbm, hbm, hbm],
        out_specs=[vmem] * 5,
        scratch_shapes=[dma((4, z.blocks))],
        compiler_params=compiler_params,
        cost_estimate=pl.CostEstimate(flops=1 << 30, bytes_accessed=1, transcendentals=0),
        name="load",
    )(rep, info, *state_in, full)

    if by_shift:
        used = agree(used, peers // 4, peers, meta, compiler_params)
    chunks = pl.pallas_call(
        functools.partial(update_kernel, z),
        out_shape=[jax.ShapeDtypeStruct((z.lines, z.payload), BF16)] * peers,
        in_specs=[vmem] * (5 + copies) + [hbm],
        out_specs=[vmem] * peers,
        scratch_shapes=[pltpu.VMEM((z.stacked, 3 * z.body), BF16)],
        compiler_params=compiler_params,
        cost_estimate=pl.CostEstimate(
            flops=6 * z.slots * z.stacked * z.body, bytes_accessed=24 * rows * width, transcendentals=rows * width
        ),
        name="update",
    )(pick, meta, *state, *received, used)

    got = move(z, chunks, used, by_shift, compiler_params)

    wide = jax.ShapeDtypeStruct((rows, width), F32)
    full_params = jax.ShapeDtypeStruct((rows, width * copies), BF16)
    half, place = pl.pallas_call(
        functools.partial(half_kernel, z),
        out_shape=(
            jax.ShapeDtypeStruct((rows, width + LANES), BF16),
            jax.ShapeDtypeStruct((z.stacked, z.slots), BF16),
        ),
        in_specs=[vmem] * peers,
        out_specs=(vmem, vmem),
        compiler_params=compiler_params,
        name="place_half",
    )(*got)
    others = [shifted(half, "replica", k, copies) for k in range(1, copies)]

    new_master, params, new_one, new_two = pl.pallas_call(
        functools.partial(rows_kernel, z),
        out_shape=(wide, full_params, wide, wide),
        in_specs=[smem] + [vmem] * (peers + 2),
        out_specs=(hbm, hbm, hbm, hbm),
        scratch_shapes=[pltpu.VMEM((rows, width), F32)] * 3 + [dma((4, z.blocks))],
        compiler_params=compiler_params,
        cost_estimate=pl.CostEstimate(
            flops=4 * z.slots * z.stacked * z.body, bytes_accessed=18 * rows * width, transcendentals=0
        ),
        name="place_rows",
    )(rep, half, place, *got)

    params, checksum = pl.pallas_call(
        functools.partial(finish_kernel, z),
        out_shape=(full_params, jax.ShapeDtypeStruct((1, rows), F32)),
        in_specs=[smem] + [vmem] * copies + [hbm],
        out_specs=(hbm, vmem),
        scratch_shapes=[dma((max(1, copies - 1),))],
        input_output_aliases={copies + 1: 0},
        compiler_params=compiler_params,
        cost_estimate=pl.CostEstimate(flops=0, bytes_accessed=4 * rows * width, transcendentals=0),
        name="finish",
    )(rep, half, *others, params)
    return (new_master, new_one, new_two, params, checksum.reshape(rows))


def solution(mesh):
    return jax.shard_map(
        shards,
        mesh=mesh,
        in_specs=(
            P("fsdp", "replica"),
            P("fsdp", "replica"),
            P("fsdp", "replica"),
            P("replica", "fsdp", None),
            P("fsdp"),
        ),
        out_specs=(
            P("fsdp", "replica"),
            P("fsdp", "replica"),
            P("fsdp", "replica"),
            P("fsdp", None),
            P("fsdp"),
        ),
        check_vma=False,
    )
```

```python
import functools
import math

import jax
import jax.numpy as jnp
from jax import lax
from jax.experimental import pallas as pl
from jax.experimental.pallas import tpu as pltpu
from jax.sharding import PartitionSpec as P

LANES = 128
TILE_ROWS = 16
MIB = 1024 * 1024
VMEM_BYTES = 24 * MIB
SHIFT_PEERS = 16
GROUP = 5
F32 = jnp.float32
BF16 = jnp.bfloat16


def iota(shape, axis):
    return lax.broadcasted_iota(jnp.int32, shape, axis)


class Sizes:
    def __init__(self, rows, width, peers, copies):
        self.rows, self.width, self.peers, self.copies = rows, width, peers, copies
        self.cap = max(2, 2 * rows // peers)
        self.split = max(1, TILE_ROWS // self.cap)
        self.lines = self.cap * self.split
        self.slots = peers * self.lines
        self.stacked = self.split * rows
        self.body = width // self.split
        self.cb = math.gcd(self.body, 512)
        self.blocks = self.body // self.cb
        self.span = self.split * self.cb
        self.sub = math.gcd(self.cb, 256)
        self.payload = 3 * self.body + LANES


def prepare_kernel(z, rep_ref, origin_ref, new_row_hbm, full_hbm, pick_ref, info_ref, mask_ref, *refs):
    parts, (full_buf, line_buf, sems, line_sem) = refs[: z.copies - 1], refs[z.copies - 1 :]
    step = z.width // z.blocks
    line_copy = pltpu.make_async_copy(new_row_hbm, line_buf, line_sem)
    line_copy.start()
    copies = []
    for k in range(1, z.copies):
        other = lax.rem(rep_ref[0] + k, z.copies)
        for j in range(z.blocks):
            there = pl.ds(pl.multiple_of(other * z.width + j * step, LANES), step)
            copies.append(
                pltpu.make_async_copy(
                    full_hbm.at[:, there], full_buf.at[k - 1, :, pl.ds(j * step, step)], sems.at[k - 1, j]
                )
            )
            copies[-1].start()
    line_copy.wait()
    line = line_buf[...]
    at_row, at_lane = iota((z.rows, z.rows), 0), iota((z.rows, z.rows), 1)
    column = jnp.sum(jnp.where(at_row == at_lane, line.astype(F32), 0.0), axis=1, keepdims=True).astype(jnp.int32)
    target, target_column = line // z.rows, column // z.rows
    earlier = (target_column == target) & (at_row < at_lane)
    rank = jnp.sum(jnp.where(earlier, 1.0, 0.0), axis=0, keepdims=True).astype(jnp.int32)
    shift = lax.rem(target - origin_ref[0] + z.peers, z.peers)
    shift_column = lax.rem(target_column - origin_ref[0] + z.peers, z.peers)
    for h in range(z.split):
        slot = shift * z.lines + h * z.cap + rank
        pick_ref[h] = jnp.where(iota((z.slots, z.rows), 0) == slot, 1.0, 0.0).astype(BF16)
    lane = iota((z.rows, LANES), 1)
    info_ref[...] = jnp.where(lane == 0, (column - target_column * z.rows + 1).astype(F32), 0.0)
    used = jnp.where(lane == shift_column, 1.0, 0.0)
    mask_ref[...] = jnp.max(used, axis=0, keepdims=True).astype(jnp.int32)
    for k in range(1, z.copies):
        for j in range(z.blocks):
            copies[(k - 1) * z.blocks + j].wait()
            at = slice(j * step, (j + 1) * step)
            parts[k - 1][:, at] = full_buf[k - 1, :, at].astype(BF16)


def agree_kernel(left, right, _, out):
    out[...] = jnp.maximum(left[...], right[...])


def choose_kernel(digits, left, right, *outs):
    total = jnp.maximum(left[...], right[...])
    lane = iota(total.shape, 1)
    for digit, out in zip(digits, outs):
        value = jnp.zeros(total.shape, jnp.int32)
        for i, s in enumerate(digit):
            value = value + jnp.where(lane == s, total << i, 0)
        out[0] = jnp.sum(value.astype(F32)).astype(jnp.int32)


def load_kernel(z, rep_ref, info_ref, master_hbm, one_hbm, two_hbm, full_hbm, master, one, two, own, meta_ref, sems):
    base = rep_ref[0] * z.width
    step = z.width // z.blocks
    copies = []
    for j in range(z.blocks):
        at = pl.ds(j * step, step)
        mine = pl.ds(pl.multiple_of(base + j * step, LANES), step)
        copies.append(
            [
                pltpu.make_async_copy(master_hbm.at[:, at], master.at[:, at], sems.at[0, j]),
                pltpu.make_async_copy(one_hbm.at[:, at], one.at[:, at], sems.at[1, j]),
                pltpu.make_async_copy(two_hbm.at[:, at], two.at[:, at], sems.at[2, j]),
                pltpu.make_async_copy(full_hbm.at[:, mine], own.at[:, at], sems.at[3, j]),
            ]
        )
    for i in range(4):
        for j in range(z.blocks):
            copies[j][i].start()
    part = jnp.zeros((z.rows, LANES), F32)
    for j in range(z.blocks):
        copies[j][0].wait()
        for at in range(j * step, (j + 1) * step, LANES):
            weights = 1.0 + ((iota((1, LANES), 1) + (base + at)) % 7).astype(F32) / 7.0
            part = part + master[:, at : at + LANES] * weights
    total = jnp.sum(part, axis=1, keepdims=True) * (1.0 / math.sqrt(z.width * z.copies))
    high = total.astype(BF16).astype(F32)
    middle = (total - high).astype(BF16).astype(F32)
    low = total - high - middle
    lane = iota((z.rows, LANES), 1)
    meta = jnp.where(lane == 1, high, jnp.where(lane == 2, middle, jnp.where(lane == 3, low, info_ref[...])))
    meta_ref[...] = meta.astype(BF16)
    for j in range(z.blocks):
        for i in range(1, 4):
            copies[j][i].wait()


def update_kernel(z, pick_ref, meta_ref, master, one, two, own, *refs):
    received, refs = refs[: z.copies - 1], refs[z.copies :]
    outs, rows_buf = refs[: z.peers], refs[z.peers]
    pick = jnp.concatenate([pick_ref[h] for h in range(z.split)], axis=1)
    for j in range(z.blocks):
        for h in range(z.split):
            for c in range(0, z.cb, z.sub):
                at = j * z.span + h * z.cb + c
                cols = slice(at, at + z.sub)
                summed = own[:, cols]
                for other in received:
                    summed = summed + other[:, cols].astype(F32)
                moved = master[:, cols]
                new_one = 0.9 * one[:, cols] + 0.1 * summed
                new_two = 0.95 * two[:, cols] + 0.05 * summed * summed
                update = new_one * (1.0 / (1.0 - 0.9**10)) / (jnp.sqrt(new_two * (1.0 / (1.0 - 0.95**10))) + 1e-08)
                new_master = moved - 0.05 * (update + 0.1 * moved)
                for i, value in enumerate((new_master, new_one, new_two)):
                    to = i * z.body + j * z.cb + c
                    rows_buf[h * z.rows : (h + 1) * z.rows, to : to + z.sub] = value.astype(BF16)
        for i in range(3):
            at = i * z.body + j * z.cb
            packed = jnp.dot(pick, rows_buf[:, at : at + z.cb], preferred_element_type=F32).astype(BF16)
            for s, out in enumerate(outs):
                out[:, at : at + z.cb] = packed[s * z.lines : (s + 1) * z.lines]
    meta = jnp.concatenate([meta_ref[...]] * z.split, axis=0)
    packed = jnp.dot(pick, meta, preferred_element_type=F32).astype(BF16)
    for s, out in enumerate(outs):
        out[:, 3 * z.body :] = packed[s * z.lines : (s + 1) * z.lines]


def gathered(refs, cols):
    return jnp.concatenate([ref[:, cols] for ref in refs], axis=0)


def placing(z, meta):
    offset = meta[:, :1].astype(F32).astype(jnp.int32)
    piece = lax.rem(iota((z.slots, 1), 0), z.lines) // z.cap
    wanted = jnp.where(offset > 0, offset - 1 + piece * z.rows, -1)
    return jnp.where(iota((z.slots, z.stacked), 1) == wanted, 1.0, 0.0).T.astype(BF16)


def placed(place, values):
    return jnp.dot(place, values, preferred_element_type=F32)


def half_kernel(z, *refs):
    got, (half, place_out) = refs[: z.peers], refs[z.peers :]
    meta = gathered(got, slice(3 * z.body, 3 * z.body + LANES))
    place = placing(z, meta)
    place_out[...] = place
    for j in range(z.blocks):
        rows_out = placed(place, gathered(got, slice(j * z.cb, (j + 1) * z.cb))).astype(BF16)
        for h in range(z.split):
            at = j * z.span + h * z.cb
            half[:, at : at + z.cb] = rows_out[h * z.rows : (h + 1) * z.rows]
    half[:, z.width :] = placed(place, meta)[: z.rows].astype(BF16)


def place_moment(z, i, place, got, out, buf, sems):
    copies = []
    for j in range(z.blocks):
        at = i * z.body + j * z.cb
        rows_out = placed(place, gathered(got, slice(at, at + z.cb)))
        for h in range(z.split):
            col = j * z.span + h * z.cb
            buf[:, col : col + z.cb] = rows_out[h * z.rows : (h + 1) * z.rows]
        cols = pl.ds(j * z.span, z.span)
        copies.append(pltpu.make_async_copy(buf.at[:, cols], out.at[:, cols], sems.at[j]))
        copies[-1].start()
    return copies


def rows_kernel(z, rep_ref, half, place, *refs):
    got, (new_master, params, one_out, two_out, master_buf, one_buf, two_buf, sems) = refs[: z.peers], refs[z.peers :]
    there = pl.ds(pl.multiple_of(rep_ref[0] * z.width, LANES), z.width)
    copies = [pltpu.make_async_copy(half.at[:, : z.width], params.at[:, there], sems.at[0, 0])]
    copies[0].start()
    for j in range(z.blocks):
        at = slice(j * z.span, (j + 1) * z.span)
        master_buf[:, at] = half[:, at].astype(F32)
        cols = pl.ds(j * z.span, z.span)
        copies.append(pltpu.make_async_copy(master_buf.at[:, cols], new_master.at[:, cols], sems.at[1, j]))
        copies[-1].start()
    copies += place_moment(z, 1, place[...], got, one_out, one_buf, sems.at[2])
    copies += place_moment(z, 2, place[...], got, two_out, two_buf, sems.at[3])
    for copy in copies:
        copy.wait()


def finish_kernel(z, rep_ref, half, *refs):
    others, (_, params, checksum, sems) = refs[: z.copies - 1], refs[z.copies - 1 :]
    copies = []
    for k, other in enumerate(others):
        replica = lax.rem(rep_ref[0] + z.copies - (k + 1), z.copies)
        there = pl.ds(pl.multiple_of(replica * z.width, LANES), z.width)
        copies.append(pltpu.make_async_copy(other.at[:, : z.width], params.at[:, there], sems.at[k]))
        copies[-1].start()
    sums = half[:, z.width :].astype(F32)
    for other in others:
        sums = sums + other[:, z.width :].astype(F32)
    lane = iota((z.rows, LANES), 1)
    column = jnp.sum(jnp.where((lane >= 1) & (lane <= 3), sums, 0.0), axis=1, keepdims=True)
    diagonal = iota((z.rows, z.rows), 0) == iota((z.rows, z.rows), 1)
    checksum[...] = jnp.sum(jnp.where(diagonal, column, 0.0), axis=0, keepdims=True)
    for copy in copies:
        copy.wait()


def shifted(value, axis, k, count):
    return lax.ppermute(value, axis, [(i, (i + k) % count) for i in range(count)])


def always_sent(peers):
    near = peers // 4 - 1
    return [peers // 2, near, peers - 1, 1, peers - near]


def shift_groups(peers):
    rest = [s for s in range(1, peers) if s not in always_sent(peers)]
    groups = -(-len(rest) // GROUP)
    return [rest[g::groups] for g in range(groups)]


def agree(used, stride, peers, after, compiler_params):
    vmem = pl.BlockSpec(memory_space=pltpu.VMEM)
    other = lax.ppermute(used, "fsdp", [(i, i ^ stride) for i in range(peers)])
    return pl.pallas_call(
        agree_kernel,
        out_shape=jax.ShapeDtypeStruct((1, LANES), jnp.int32),
        in_specs=[vmem, vmem, pl.BlockSpec(memory_space=pl.ANY)],
        out_specs=vmem,
        compiler_params=compiler_params,
        name="agree",
    )(used, other, after)


def choose_branches(used, peers, compiler_params):
    vmem = pl.BlockSpec(memory_space=pltpu.VMEM)
    smem = pl.BlockSpec(memory_space=pltpu.SMEM)
    groups = shift_groups(peers)
    other = lax.ppermute(used, "fsdp", [(i, i ^ (peers // 2)) for i in range(peers)])
    return pl.pallas_call(
        functools.partial(choose_kernel, groups),
        out_shape=[pltpu.SMEM((1,), jnp.int32)] * len(groups),
        in_specs=[vmem, vmem],
        out_specs=[smem] * len(groups),
        compiler_params=compiler_params,
        name="choose",
    )(used, other)


def send_used(peers, group, used, chunks):
    return tuple(
        shifted(chunk, "fsdp", s, peers) if used >> i & 1 else chunk for i, (s, chunk) in enumerate(zip(group, chunks))
    )


def move(z, chunks, used, by_shift, compiler_params):
    if not by_shift:
        got = lax.all_to_all(jnp.concatenate(chunks, axis=0), "fsdp", split_axis=0, concat_axis=0, tiled=True)
        return [got[s * z.lines : (s + 1) * z.lines] for s in range(z.peers)]
    got = list(chunks)
    always = always_sent(z.peers)
    first = always[0]
    got[first] = shifted(chunks[first], "fsdp", first, z.peers)
    used = agree(used, 1, z.peers, chunks[first], compiler_params)
    for s in always[1:-1]:
        value, _ = lax.optimization_barrier((chunks[s], used))
        got[s] = shifted(value, "fsdp", s, z.peers)
    used = agree(used, 2, z.peers, chunks[first], compiler_params)
    last = always[-1]
    value, *_ = lax.optimization_barrier((chunks[last], used, got[always[2]]))
    got[last] = shifted(value, "fsdp", last, z.peers)
    chosen = choose_branches(used, z.peers, compiler_params)
    barred = lax.optimization_barrier((*chosen, *[got[s] for s in always]))
    chosen = barred[: len(chosen)]
    for s, value in zip(always, barred[len(chosen) :]):
        got[s] = value
    for group, number in zip(shift_groups(z.peers), chosen):
        branches = [
            lambda *values, group=group, used=used: send_used(z.peers, group, used, values)
            for used in range(1 << len(group))
        ]
        for s, value in zip(group, lax.switch(number[0], branches, *[chunks[s] for s in group])):
            got[s] = value
    return got


def shards(master, moment_one, moment_two, gradients, new_row):
    rows, width = master.shape
    peers, copies = lax.axis_size("fsdp"), lax.axis_size("replica")
    z = Sizes(rows, width, peers, copies)
    compiler_params = pltpu.CompilerParams(vmem_limit_bytes=VMEM_BYTES)
    smem = pl.BlockSpec(memory_space=pltpu.SMEM)
    vmem = pl.BlockSpec(memory_space=pltpu.VMEM)
    hbm = pl.BlockSpec(memory_space=pl.ANY)
    dma = pltpu.SemaphoreType.DMA

    replica = lax.axis_index("replica").astype(jnp.int32)
    rep = replica.reshape(1)
    by_shift = peers == SHIFT_PEERS
    origin = (lax.axis_index("fsdp").astype(jnp.int32) if by_shift else jnp.int32(0)).reshape(1)
    state_in = [pltpu.with_memory_space_constraint(x, pltpu.HBM) for x in (master, moment_one, moment_two)]
    full = pltpu.with_memory_space_constraint(gradients[0], pltpu.HBM)

    part = jax.ShapeDtypeStruct((rows, width), BF16)
    pick, info, used, *parts = pl.pallas_call(
        functools.partial(prepare_kernel, z),
        out_shape=[
            jax.ShapeDtypeStruct((z.split, z.slots, rows), BF16),
            jax.ShapeDtypeStruct((rows, LANES), F32),
            jax.ShapeDtypeStruct((1, LANES), jnp.int32),
        ]
        + [part] * (copies - 1),
        in_specs=[smem, smem, hbm, hbm],
        out_specs=[vmem] * (copies + 2),
        scratch_shapes=[
            pltpu.VMEM((copies - 1, rows, width), F32),
            pltpu.VMEM((1, rows), jnp.int32),
            dma((copies - 1, z.blocks)),
            dma,
        ],
        compiler_params=compiler_params,
        cost_estimate=pl.CostEstimate(flops=1 << 30, bytes_accessed=1, transcendentals=0),
        name="prepare",
    )(rep, origin, pltpu.with_memory_space_constraint(new_row.reshape(1, rows), pltpu.HBM), full)
    received = [shifted(value, "replica", k + 1, copies) for k, value in enumerate(parts)]

    loaded = jax.ShapeDtypeStruct((rows, width), F32)
    *state, meta = pl.pallas_call(
        functools.partial(load_kernel, z),
        out_shape=[loaded, loaded, loaded, loaded, jax.ShapeDtypeStruct((rows, LANES), BF16)],
        in_specs=[smem, vmem, hbm, hbm, hbm, hbm],
        out_specs=[vmem] * 5,
        scratch_shapes=[dma((4, z.blocks))],
        compiler_params=compiler_params,
        cost_estimate=pl.CostEstimate(flops=1 << 30, bytes_accessed=1, transcendentals=0),
        name="load",
    )(rep, info, *state_in, full)

    if by_shift:
        used = agree(used, peers // 4, peers, meta, compiler_params)
    chunks = pl.pallas_call(
        functools.partial(update_kernel, z),
        out_shape=[jax.ShapeDtypeStruct((z.lines, z.payload), BF16)] * peers,
        in_specs=[vmem] * (5 + copies) + [hbm],
        out_specs=[vmem] * peers,
        scratch_shapes=[pltpu.VMEM((z.stacked, 3 * z.body), BF16)],
        compiler_params=compiler_params,
        cost_estimate=pl.CostEstimate(
            flops=6 * z.slots * z.stacked * z.body, bytes_accessed=24 * rows * width, transcendentals=rows * width
        ),
        name="update",
    )(pick, meta, *state, *received, used)

    got = move(z, chunks, used, by_shift, compiler_params)

    wide = jax.ShapeDtypeStruct((rows, width), F32)
    full_params = jax.ShapeDtypeStruct((rows, width * copies), BF16)
    half, place = pl.pallas_call(
        functools.partial(half_kernel, z),
        out_shape=(
            jax.ShapeDtypeStruct((rows, width + LANES), BF16),
            jax.ShapeDtypeStruct((z.stacked, z.slots), BF16),
        ),
        in_specs=[vmem] * peers,
        out_specs=(vmem, vmem),
        compiler_params=compiler_params,
        name="place_half",
    )(*got)
    others = [shifted(half, "replica", k, copies) for k in range(1, copies)]

    new_master, params, new_one, new_two = pl.pallas_call(
        functools.partial(rows_kernel, z),
        out_shape=(wide, full_params, wide, wide),
        in_specs=[smem] + [vmem] * (peers + 2),
        out_specs=(hbm, hbm, hbm, hbm),
        scratch_shapes=[pltpu.VMEM((rows, width), F32)] * 3 + [dma((4, z.blocks))],
        compiler_params=compiler_params,
        cost_estimate=pl.CostEstimate(
            flops=4 * z.slots * z.stacked * z.body, bytes_accessed=18 * rows * width, transcendentals=0
        ),
        name="place_rows",
    )(rep, half, place, *got)

    params, checksum = pl.pallas_call(
        functools.partial(finish_kernel, z),
        out_shape=(full_params, jax.ShapeDtypeStruct((1, rows), F32)),
        in_specs=[smem] + [vmem] * copies + [hbm],
        out_specs=(hbm, vmem),
        scratch_shapes=[dma((max(1, copies - 1),))],
        input_output_aliases={copies + 1: 0},
        compiler_params=compiler_params,
        cost_estimate=pl.CostEstimate(flops=0, bytes_accessed=4 * rows * width, transcendentals=0),
        name="finish",
    )(rep, half, *others, params)
    return (new_master, new_one, new_two, params, checksum.reshape(rows))


def solution(mesh):
    return jax.shard_map(
        shards,
        mesh=mesh,
        in_specs=(
            P("fsdp", "replica"),
            P("fsdp", "replica"),
            P("fsdp", "replica"),
            P("replica", "fsdp", None),
            P("fsdp"),
        ),
        out_specs=(
            P("fsdp", "replica"),
            P("fsdp", "replica"),
            P("fsdp", "replica"),
            P("fsdp", None),
            P("fsdp"),
        ),
        check_vma=False,
    )
```

```python
import functools
import math

import jax
import jax.numpy as jnp
from jax import lax
from jax.experimental import pallas as pl
from jax.experimental.pallas import tpu as pltpu
from jax.sharding import PartitionSpec as P

LANES = 128
TILE_ROWS = 16
MIB = 1024 * 1024
VMEM_BYTES = 24 * MIB
SHIFT_PEERS = 16
GROUP = 4
F32 = jnp.float32
BF16 = jnp.bfloat16


def iota(shape, axis):
    return lax.broadcasted_iota(jnp.int32, shape, axis)


class Sizes:
    def __init__(self, rows, width, peers, copies):
        self.rows, self.width, self.peers, self.copies = rows, width, peers, copies
        self.cap = max(2, 2 * rows // peers)
        self.split = max(1, TILE_ROWS // self.cap)
        self.lines = self.cap * self.split
        self.slots = peers * self.lines
        self.stacked = self.split * rows
        self.body = width // self.split
        self.cb = math.gcd(self.body, 512)
        self.blocks = self.body // self.cb
        self.span = self.split * self.cb
        self.sub = math.gcd(self.cb, 256)
        self.payload = 3 * self.body + LANES


def prepare_kernel(z, rep_ref, origin_ref, new_row_hbm, full_hbm, pick_ref, info_ref, mask_ref, *refs):
    parts, (full_buf, line_buf, sems, line_sem) = refs[: z.copies - 1], refs[z.copies - 1 :]
    step = z.width // z.blocks
    line_copy = pltpu.make_async_copy(new_row_hbm, line_buf, line_sem)
    line_copy.start()
    copies = []
    for k in range(1, z.copies):
        other = lax.rem(rep_ref[0] + k, z.copies)
        for j in range(z.blocks):
            there = pl.ds(pl.multiple_of(other * z.width + j * step, LANES), step)
            copies.append(
                pltpu.make_async_copy(
                    full_hbm.at[:, there], full_buf.at[k - 1, :, pl.ds(j * step, step)], sems.at[k - 1, j]
                )
            )
            copies[-1].start()
    line_copy.wait()
    line = line_buf[...]
    at_row, at_lane = iota((z.rows, z.rows), 0), iota((z.rows, z.rows), 1)
    column = jnp.sum(jnp.where(at_row == at_lane, line.astype(F32), 0.0), axis=1, keepdims=True).astype(jnp.int32)
    target, target_column = line // z.rows, column // z.rows
    earlier = (target_column == target) & (at_row < at_lane)
    rank = jnp.sum(jnp.where(earlier, 1.0, 0.0), axis=0, keepdims=True).astype(jnp.int32)
    shift = lax.rem(target - origin_ref[0] + z.peers, z.peers)
    shift_column = lax.rem(target_column - origin_ref[0] + z.peers, z.peers)
    for h in range(z.split):
        slot = shift * z.lines + h * z.cap + rank
        pick_ref[h] = jnp.where(iota((z.slots, z.rows), 0) == slot, 1.0, 0.0).astype(BF16)
    lane = iota((z.rows, LANES), 1)
    info_ref[...] = jnp.where(lane == 0, (column - target_column * z.rows + 1).astype(F32), 0.0)
    used = jnp.where(lane == shift_column, 1.0, 0.0)
    mask_ref[...] = jnp.max(used, axis=0, keepdims=True).astype(jnp.int32)
    for k in range(1, z.copies):
        for j in range(z.blocks):
            copies[(k - 1) * z.blocks + j].wait()
            at = slice(j * step, (j + 1) * step)
            parts[k - 1][:, at] = full_buf[k - 1, :, at].astype(BF16)


def agree_kernel(left, right, _, out):
    out[...] = jnp.maximum(left[...], right[...])


def choose_kernel(digits, left, right, *outs):
    total = jnp.maximum(left[...], right[...])
    lane = iota(total.shape, 1)
    for digit, out in zip(digits, outs):
        value = jnp.zeros(total.shape, jnp.int32)
        for i, s in enumerate(digit):
            value = value + jnp.where(lane == s, total << i, 0)
        out[0] = jnp.sum(value.astype(F32)).astype(jnp.int32)


def load_kernel(z, rep_ref, info_ref, master_hbm, one_hbm, two_hbm, full_hbm, master, one, two, own, meta_ref, sems):
    base = rep_ref[0] * z.width
    step = z.width // z.blocks
    copies = []
    for j in range(z.blocks):
        at = pl.ds(j * step, step)
        mine = pl.ds(pl.multiple_of(base + j * step, LANES), step)
        copies.append(
            [
                pltpu.make_async_copy(master_hbm.at[:, at], master.at[:, at], sems.at[0, j]),
                pltpu.make_async_copy(one_hbm.at[:, at], one.at[:, at], sems.at[1, j]),
                pltpu.make_async_copy(two_hbm.at[:, at], two.at[:, at], sems.at[2, j]),
                pltpu.make_async_copy(full_hbm.at[:, mine], own.at[:, at], sems.at[3, j]),
            ]
        )
    for i in range(4):
        for j in range(z.blocks):
            copies[j][i].start()
    part = jnp.zeros((z.rows, LANES), F32)
    for j in range(z.blocks):
        copies[j][0].wait()
        for at in range(j * step, (j + 1) * step, LANES):
            weights = 1.0 + ((iota((1, LANES), 1) + (base + at)) % 7).astype(F32) / 7.0
            part = part + master[:, at : at + LANES] * weights
    total = jnp.sum(part, axis=1, keepdims=True) * (1.0 / math.sqrt(z.width * z.copies))
    high = total.astype(BF16).astype(F32)
    middle = (total - high).astype(BF16).astype(F32)
    low = total - high - middle
    lane = iota((z.rows, LANES), 1)
    meta = jnp.where(lane == 1, high, jnp.where(lane == 2, middle, jnp.where(lane == 3, low, info_ref[...])))
    meta_ref[...] = meta.astype(BF16)
    for j in range(z.blocks):
        for i in range(1, 4):
            copies[j][i].wait()


def update_kernel(z, pick_ref, meta_ref, master, one, two, own, *refs):
    received, refs = refs[: z.copies - 1], refs[z.copies :]
    outs, rows_buf = refs[: z.peers], refs[z.peers]
    pick = jnp.concatenate([pick_ref[h] for h in range(z.split)], axis=1)
    for j in range(z.blocks):
        for h in range(z.split):
            for c in range(0, z.cb, z.sub):
                at = j * z.span + h * z.cb + c
                cols = slice(at, at + z.sub)
                summed = own[:, cols]
                for other in received:
                    summed = summed + other[:, cols].astype(F32)
                moved = master[:, cols]
                new_one = 0.9 * one[:, cols] + 0.1 * summed
                new_two = 0.95 * two[:, cols] + 0.05 * summed * summed
                update = new_one * (1.0 / (1.0 - 0.9**10)) / (jnp.sqrt(new_two * (1.0 / (1.0 - 0.95**10))) + 1e-08)
                new_master = moved - 0.05 * (update + 0.1 * moved)
                for i, value in enumerate((new_master, new_one, new_two)):
                    to = i * z.body + j * z.cb + c
                    rows_buf[h * z.rows : (h + 1) * z.rows, to : to + z.sub] = value.astype(BF16)
        for i in range(3):
            at = i * z.body + j * z.cb
            packed = jnp.dot(pick, rows_buf[:, at : at + z.cb], preferred_element_type=F32).astype(BF16)
            for s, out in enumerate(outs):
                out[:, at : at + z.cb] = packed[s * z.lines : (s + 1) * z.lines]
    meta = jnp.concatenate([meta_ref[...]] * z.split, axis=0)
    packed = jnp.dot(pick, meta, preferred_element_type=F32).astype(BF16)
    for s, out in enumerate(outs):
        out[:, 3 * z.body :] = packed[s * z.lines : (s + 1) * z.lines]


def gathered(refs, cols):
    return jnp.concatenate([ref[:, cols] for ref in refs], axis=0)


def placing(z, meta):
    offset = meta[:, :1].astype(F32).astype(jnp.int32)
    piece = lax.rem(iota((z.slots, 1), 0), z.lines) // z.cap
    wanted = jnp.where(offset > 0, offset - 1 + piece * z.rows, -1)
    return jnp.where(iota((z.slots, z.stacked), 1) == wanted, 1.0, 0.0).T.astype(BF16)


def placed(place, values):
    return jnp.dot(place, values, preferred_element_type=F32)


def half_kernel(z, *refs):
    got, (half, place_out) = refs[: z.peers], refs[z.peers :]
    meta = gathered(got, slice(3 * z.body, 3 * z.body + LANES))
    place = placing(z, meta)
    place_out[...] = place
    for j in range(z.blocks):
        rows_out = placed(place, gathered(got, slice(j * z.cb, (j + 1) * z.cb))).astype(BF16)
        for h in range(z.split):
            at = j * z.span + h * z.cb
            half[:, at : at + z.cb] = rows_out[h * z.rows : (h + 1) * z.rows]
    half[:, z.width :] = placed(place, meta)[: z.rows].astype(BF16)


def place_moment(z, i, place, got, out, buf, sems):
    copies = []
    for j in range(z.blocks):
        at = i * z.body + j * z.cb
        rows_out = placed(place, gathered(got, slice(at, at + z.cb)))
        for h in range(z.split):
            col = j * z.span + h * z.cb
            buf[:, col : col + z.cb] = rows_out[h * z.rows : (h + 1) * z.rows]
        cols = pl.ds(j * z.span, z.span)
        copies.append(pltpu.make_async_copy(buf.at[:, cols], out.at[:, cols], sems.at[j]))
        copies[-1].start()
    return copies


def rows_kernel(z, rep_ref, half, place, *refs):
    got, (new_master, params, one_out, two_out, master_buf, one_buf, two_buf, sems) = refs[: z.peers], refs[z.peers :]
    there = pl.ds(pl.multiple_of(rep_ref[0] * z.width, LANES), z.width)
    copies = [pltpu.make_async_copy(half.at[:, : z.width], params.at[:, there], sems.at[0, 0])]
    copies[0].start()
    for j in range(z.blocks):
        at = slice(j * z.span, (j + 1) * z.span)
        master_buf[:, at] = half[:, at].astype(F32)
        cols = pl.ds(j * z.span, z.span)
        copies.append(pltpu.make_async_copy(master_buf.at[:, cols], new_master.at[:, cols], sems.at[1, j]))
        copies[-1].start()
    copies += place_moment(z, 1, place[...], got, one_out, one_buf, sems.at[2])
    copies += place_moment(z, 2, place[...], got, two_out, two_buf, sems.at[3])
    for copy in copies:
        copy.wait()


def finish_kernel(z, rep_ref, half, *refs):
    others, (_, params, checksum, sems) = refs[: z.copies - 1], refs[z.copies - 1 :]
    copies = []
    for k, other in enumerate(others):
        replica = lax.rem(rep_ref[0] + z.copies - (k + 1), z.copies)
        there = pl.ds(pl.multiple_of(replica * z.width, LANES), z.width)
        copies.append(pltpu.make_async_copy(other.at[:, : z.width], params.at[:, there], sems.at[k]))
        copies[-1].start()
    sums = half[:, z.width :].astype(F32)
    for other in others:
        sums = sums + other[:, z.width :].astype(F32)
    lane = iota((z.rows, LANES), 1)
    column = jnp.sum(jnp.where((lane >= 1) & (lane <= 3), sums, 0.0), axis=1, keepdims=True)
    diagonal = iota((z.rows, z.rows), 0) == iota((z.rows, z.rows), 1)
    checksum[...] = jnp.sum(jnp.where(diagonal, column, 0.0), axis=0, keepdims=True)
    for copy in copies:
        copy.wait()


def shifted(value, axis, k, count):
    return lax.ppermute(value, axis, [(i, (i + k) % count) for i in range(count)])


def always_sent(peers):
    return [peers // 2, peers // 4 - 1, peers - 1]


def shift_groups(peers):
    rest = [s for s in range(1, peers) if s not in always_sent(peers)]
    groups = -(-len(rest) // GROUP)
    return [rest[g::groups] for g in range(groups)]


def agree(used, stride, peers, after, compiler_params):
    vmem = pl.BlockSpec(memory_space=pltpu.VMEM)
    other = lax.ppermute(used, "fsdp", [(i, i ^ stride) for i in range(peers)])
    return pl.pallas_call(
        agree_kernel,
        out_shape=jax.ShapeDtypeStruct((1, LANES), jnp.int32),
        in_specs=[vmem, vmem, pl.BlockSpec(memory_space=pl.ANY)],
        out_specs=vmem,
        compiler_params=compiler_params,
        name="agree",
    )(used, other, after)


def choose_branches(used, peers, compiler_params):
    vmem = pl.BlockSpec(memory_space=pltpu.VMEM)
    smem = pl.BlockSpec(memory_space=pltpu.SMEM)
    groups = shift_groups(peers)
    other = lax.ppermute(used, "fsdp", [(i, i ^ (peers // 2)) for i in range(peers)])
    return pl.pallas_call(
        functools.partial(choose_kernel, groups),
        out_shape=[pltpu.SMEM((1,), jnp.int32)] * len(groups),
        in_specs=[vmem, vmem],
        out_specs=[smem] * len(groups),
        compiler_params=compiler_params,
        name="choose",
    )(used, other)


def send_used(peers, group, used, chunks):
    return tuple(
        shifted(chunk, "fsdp", s, peers) if used >> i & 1 else chunk for i, (s, chunk) in enumerate(zip(group, chunks))
    )


def move(z, chunks, used, by_shift, compiler_params):
    if not by_shift:
        got = lax.all_to_all(jnp.concatenate(chunks, axis=0), "fsdp", split_axis=0, concat_axis=0, tiled=True)
        return [got[s * z.lines : (s + 1) * z.lines] for s in range(z.peers)]
    got = list(chunks)
    always = always_sent(z.peers)
    for s in always:
        got[s] = shifted(chunks[s], "fsdp", s, z.peers)
    for stride in (1, 2):
        used = agree(used, stride, z.peers, chunks[0], compiler_params)
    chosen = choose_branches(used, z.peers, compiler_params)
    barred = lax.optimization_barrier((*chosen, *[got[s] for s in always]))
    chosen = barred[: len(chosen)]
    for s, value in zip(always, barred[len(chosen) :]):
        got[s] = value
    for group, number in zip(shift_groups(z.peers), chosen):
        branches = [
            lambda *values, group=group, used=used: send_used(z.peers, group, used, values)
            for used in range(1 << len(group))
        ]
        for s, value in zip(group, lax.switch(number[0], branches, *[chunks[s] for s in group])):
            got[s] = value
    return got


def shards(master, moment_one, moment_two, gradients, new_row):
    rows, width = master.shape
    peers, copies = lax.axis_size("fsdp"), lax.axis_size("replica")
    z = Sizes(rows, width, peers, copies)
    compiler_params = pltpu.CompilerParams(vmem_limit_bytes=VMEM_BYTES)
    smem = pl.BlockSpec(memory_space=pltpu.SMEM)
    vmem = pl.BlockSpec(memory_space=pltpu.VMEM)
    hbm = pl.BlockSpec(memory_space=pl.ANY)
    dma = pltpu.SemaphoreType.DMA

    replica = lax.axis_index("replica").astype(jnp.int32)
    rep = replica.reshape(1)
    by_shift = peers == SHIFT_PEERS
    origin = (lax.axis_index("fsdp").astype(jnp.int32) if by_shift else jnp.int32(0)).reshape(1)
    state_in = [pltpu.with_memory_space_constraint(x, pltpu.HBM) for x in (master, moment_one, moment_two)]
    full = pltpu.with_memory_space_constraint(gradients[0], pltpu.HBM)

    part = jax.ShapeDtypeStruct((rows, width), BF16)
    pick, info, used, *parts = pl.pallas_call(
        functools.partial(prepare_kernel, z),
        out_shape=[
            jax.ShapeDtypeStruct((z.split, z.slots, rows), BF16),
            jax.ShapeDtypeStruct((rows, LANES), F32),
            jax.ShapeDtypeStruct((1, LANES), jnp.int32),
        ]
        + [part] * (copies - 1),
        in_specs=[smem, smem, hbm, hbm],
        out_specs=[vmem] * (copies + 2),
        scratch_shapes=[
            pltpu.VMEM((copies - 1, rows, width), F32),
            pltpu.VMEM((1, rows), jnp.int32),
            dma((copies - 1, z.blocks)),
            dma,
        ],
        compiler_params=compiler_params,
        cost_estimate=pl.CostEstimate(flops=1 << 30, bytes_accessed=1, transcendentals=0),
        name="prepare",
    )(rep, origin, pltpu.with_memory_space_constraint(new_row.reshape(1, rows), pltpu.HBM), full)
    received = [shifted(value, "replica", k + 1, copies) for k, value in enumerate(parts)]

    loaded = jax.ShapeDtypeStruct((rows, width), F32)
    *state, meta = pl.pallas_call(
        functools.partial(load_kernel, z),
        out_shape=[loaded, loaded, loaded, loaded, jax.ShapeDtypeStruct((rows, LANES), BF16)],
        in_specs=[smem, vmem, hbm, hbm, hbm, hbm],
        out_specs=[vmem] * 5,
        scratch_shapes=[dma((4, z.blocks))],
        compiler_params=compiler_params,
        cost_estimate=pl.CostEstimate(flops=1 << 30, bytes_accessed=1, transcendentals=0),
        name="load",
    )(rep, info, *state_in, full)

    if by_shift:
        used = agree(used, peers // 4, peers, meta, compiler_params)
    chunks = pl.pallas_call(
        functools.partial(update_kernel, z),
        out_shape=[jax.ShapeDtypeStruct((z.lines, z.payload), BF16)] * peers,
        in_specs=[vmem] * (5 + copies) + [hbm],
        out_specs=[vmem] * peers,
        scratch_shapes=[pltpu.VMEM((z.stacked, 3 * z.body), BF16)],
        compiler_params=compiler_params,
        cost_estimate=pl.CostEstimate(
            flops=6 * z.slots * z.stacked * z.body, bytes_accessed=24 * rows * width, transcendentals=rows * width
        ),
        name="update",
    )(pick, meta, *state, *received, used)

    got = move(z, chunks, used, by_shift, compiler_params)

    wide = jax.ShapeDtypeStruct((rows, width), F32)
    full_params = jax.ShapeDtypeStruct((rows, width * copies), BF16)
    half, place = pl.pallas_call(
        functools.partial(half_kernel, z),
        out_shape=(
            jax.ShapeDtypeStruct((rows, width + LANES), BF16),
            jax.ShapeDtypeStruct((z.stacked, z.slots), BF16),
        ),
        in_specs=[vmem] * peers,
        out_specs=(vmem, vmem),
        compiler_params=compiler_params,
        name="place_half",
    )(*got)
    others = [shifted(half, "replica", k, copies) for k in range(1, copies)]

    new_master, params, new_one, new_two = pl.pallas_call(
        functools.partial(rows_kernel, z),
        out_shape=(wide, full_params, wide, wide),
        in_specs=[smem] + [vmem] * (peers + 2),
        out_specs=(hbm, hbm, hbm, hbm),
        scratch_shapes=[pltpu.VMEM((rows, width), F32)] * 3 + [dma((4, z.blocks))],
        compiler_params=compiler_params,
        cost_estimate=pl.CostEstimate(
            flops=4 * z.slots * z.stacked * z.body, bytes_accessed=18 * rows * width, transcendentals=0
        ),
        name="place_rows",
    )(rep, half, place, *got)

    params, checksum = pl.pallas_call(
        functools.partial(finish_kernel, z),
        out_shape=(full_params, jax.ShapeDtypeStruct((1, rows), F32)),
        in_specs=[smem] + [vmem] * copies + [hbm],
        out_specs=(hbm, vmem),
        scratch_shapes=[dma((max(1, copies - 1),))],
        input_output_aliases={copies + 1: 0},
        compiler_params=compiler_params,
        cost_estimate=pl.CostEstimate(flops=0, bytes_accessed=4 * rows * width, transcendentals=0),
        name="finish",
    )(rep, half, *others, params)
    return (new_master, new_one, new_two, params, checksum.reshape(rows))


def solution(mesh):
    return jax.shard_map(
        shards,
        mesh=mesh,
        in_specs=(
            P("fsdp", "replica"),
            P("fsdp", "replica"),
            P("fsdp", "replica"),
            P("replica", "fsdp", None),
            P("fsdp"),
        ),
        out_specs=(
            P("fsdp", "replica"),
            P("fsdp", "replica"),
            P("fsdp", "replica"),
            P("fsdp", None),
            P("fsdp"),
        ),
        check_vma=False,
    )
```

```python
import functools
import math

import jax
import jax.numpy as jnp
from jax import lax
from jax.experimental import pallas as pl
from jax.experimental.pallas import tpu as pltpu
from jax.sharding import PartitionSpec as P

LANES = 128
TILE_ROWS = 16
MIB = 1024 * 1024
VMEM_BYTES = 24 * MIB
SHIFT_PEERS = 16
GROUP = 4
F32 = jnp.float32
BF16 = jnp.bfloat16


def iota(shape, axis):
    return lax.broadcasted_iota(jnp.int32, shape, axis)


class Sizes:
    def __init__(self, rows, width, peers, copies):
        self.rows, self.width, self.peers, self.copies = rows, width, peers, copies
        self.cap = max(2, 2 * rows // peers)
        self.split = max(1, TILE_ROWS // self.cap)
        self.lines = self.cap * self.split
        self.slots = peers * self.lines
        self.stacked = self.split * rows
        self.body = width // self.split
        self.cb = math.gcd(self.body, 512)
        self.blocks = self.body // self.cb
        self.span = self.split * self.cb
        self.sub = math.gcd(self.cb, 256)
        self.payload = 3 * self.body + LANES


def prepare_kernel(z, rep_ref, origin_ref, new_row_hbm, full_hbm, pick_ref, info_ref, mask_ref, *refs):
    parts, (full_buf, line_buf, sems, line_sem) = refs[: z.copies - 1], refs[z.copies - 1 :]
    step = z.width // z.blocks
    line_copy = pltpu.make_async_copy(new_row_hbm, line_buf, line_sem)
    line_copy.start()
    copies = []
    for k in range(1, z.copies):
        other = lax.rem(rep_ref[0] + k, z.copies)
        for j in range(z.blocks):
            there = pl.ds(pl.multiple_of(other * z.width + j * step, LANES), step)
            copies.append(
                pltpu.make_async_copy(
                    full_hbm.at[:, there], full_buf.at[k - 1, :, pl.ds(j * step, step)], sems.at[k - 1, j]
                )
            )
            copies[-1].start()
    line_copy.wait()
    line = line_buf[...]
    at_row, at_lane = iota((z.rows, z.rows), 0), iota((z.rows, z.rows), 1)
    column = jnp.sum(jnp.where(at_row == at_lane, line.astype(F32), 0.0), axis=1, keepdims=True).astype(jnp.int32)
    target, target_column = line // z.rows, column // z.rows
    earlier = (target_column == target) & (at_row < at_lane)
    rank = jnp.sum(jnp.where(earlier, 1.0, 0.0), axis=0, keepdims=True).astype(jnp.int32)
    shift = lax.rem(target - origin_ref[0] + z.peers, z.peers)
    shift_column = lax.rem(target_column - origin_ref[0] + z.peers, z.peers)
    for h in range(z.split):
        slot = shift * z.lines + h * z.cap + rank
        pick_ref[h] = jnp.where(iota((z.slots, z.rows), 0) == slot, 1.0, 0.0).astype(BF16)
    lane = iota((z.rows, LANES), 1)
    info_ref[...] = jnp.where(lane == 0, (column - target_column * z.rows + 1).astype(F32), 0.0)
    used = jnp.where(lane == shift_column, 1.0, 0.0)
    mask_ref[...] = jnp.max(used, axis=0, keepdims=True).astype(jnp.int32)
    for k in range(1, z.copies):
        for j in range(z.blocks):
            copies[(k - 1) * z.blocks + j].wait()
            at = slice(j * step, (j + 1) * step)
            parts[k - 1][:, at] = full_buf[k - 1, :, at].astype(BF16)


def agree_kernel(left, right, _, out):
    out[...] = jnp.maximum(left[...], right[...])


def choose_kernel(digits, left, right, *outs):
    total = jnp.maximum(left[...], right[...])
    lane = iota(total.shape, 1)
    for digit, out in zip(digits, outs):
        value = jnp.zeros(total.shape, jnp.int32)
        for i, s in enumerate(digit):
            value = value + jnp.where(lane == s, total << i, 0)
        out[0] = jnp.sum(value.astype(F32)).astype(jnp.int32)


def load_kernel(z, rep_ref, info_ref, master_hbm, one_hbm, two_hbm, full_hbm, master, one, two, own, meta_ref, sems):
    base = rep_ref[0] * z.width
    step = z.width // z.blocks
    copies = []
    for j in range(z.blocks):
        at = pl.ds(j * step, step)
        mine = pl.ds(pl.multiple_of(base + j * step, LANES), step)
        copies.append(
            [
                pltpu.make_async_copy(master_hbm.at[:, at], master.at[:, at], sems.at[0, j]),
                pltpu.make_async_copy(one_hbm.at[:, at], one.at[:, at], sems.at[1, j]),
                pltpu.make_async_copy(two_hbm.at[:, at], two.at[:, at], sems.at[2, j]),
                pltpu.make_async_copy(full_hbm.at[:, mine], own.at[:, at], sems.at[3, j]),
            ]
        )
    for i in range(4):
        for j in range(z.blocks):
            copies[j][i].start()
    part = jnp.zeros((z.rows, LANES), F32)
    for j in range(z.blocks):
        copies[j][0].wait()
        for at in range(j * step, (j + 1) * step, LANES):
            weights = 1.0 + ((iota((1, LANES), 1) + (base + at)) % 7).astype(F32) / 7.0
            part = part + master[:, at : at + LANES] * weights
    total = jnp.sum(part, axis=1, keepdims=True) * (1.0 / math.sqrt(z.width * z.copies))
    high = total.astype(BF16).astype(F32)
    middle = (total - high).astype(BF16).astype(F32)
    low = total - high - middle
    lane = iota((z.rows, LANES), 1)
    meta = jnp.where(lane == 1, high, jnp.where(lane == 2, middle, jnp.where(lane == 3, low, info_ref[...])))
    meta_ref[...] = meta.astype(BF16)
    for j in range(z.blocks):
        for i in range(1, 4):
            copies[j][i].wait()


def update_kernel(z, pick_ref, meta_ref, master, one, two, own, *refs):
    received, refs = refs[: z.copies - 1], refs[z.copies :]
    outs, rows_buf = refs[: z.peers], refs[z.peers]
    pick = jnp.concatenate([pick_ref[h] for h in range(z.split)], axis=1)
    for j in range(z.blocks):
        for h in range(z.split):
            for c in range(0, z.cb, z.sub):
                at = j * z.span + h * z.cb + c
                cols = slice(at, at + z.sub)
                summed = own[:, cols]
                for other in received:
                    summed = summed + other[:, cols].astype(F32)
                moved = master[:, cols]
                new_one = 0.9 * one[:, cols] + 0.1 * summed
                new_two = 0.95 * two[:, cols] + 0.05 * summed * summed
                update = new_one * (1.0 / (1.0 - 0.9**10)) / (jnp.sqrt(new_two * (1.0 / (1.0 - 0.95**10))) + 1e-08)
                new_master = moved - 0.05 * (update + 0.1 * moved)
                for i, value in enumerate((new_master, new_one, new_two)):
                    to = i * z.body + j * z.cb + c
                    rows_buf[h * z.rows : (h + 1) * z.rows, to : to + z.sub] = value.astype(BF16)
        for i in range(3):
            at = i * z.body + j * z.cb
            packed = jnp.dot(pick, rows_buf[:, at : at + z.cb], preferred_element_type=F32).astype(BF16)
            for s, out in enumerate(outs):
                out[:, at : at + z.cb] = packed[s * z.lines : (s + 1) * z.lines]
    meta = jnp.concatenate([meta_ref[...]] * z.split, axis=0)
    packed = jnp.dot(pick, meta, preferred_element_type=F32).astype(BF16)
    for s, out in enumerate(outs):
        out[:, 3 * z.body :] = packed[s * z.lines : (s + 1) * z.lines]


def gathered(refs, cols):
    return jnp.concatenate([ref[:, cols] for ref in refs], axis=0)


def placing(z, meta):
    offset = meta[:, :1].astype(F32).astype(jnp.int32)
    piece = lax.rem(iota((z.slots, 1), 0), z.lines) // z.cap
    wanted = jnp.where(offset > 0, offset - 1 + piece * z.rows, -1)
    return jnp.where(iota((z.slots, z.stacked), 1) == wanted, 1.0, 0.0).T.astype(BF16)


def placed(place, values):
    return jnp.dot(place, values, preferred_element_type=F32)


def half_kernel(z, *refs):
    got, (half, place_out) = refs[: z.peers], refs[z.peers :]
    meta = gathered(got, slice(3 * z.body, 3 * z.body + LANES))
    place = placing(z, meta)
    place_out[...] = place
    for j in range(z.blocks):
        rows_out = placed(place, gathered(got, slice(j * z.cb, (j + 1) * z.cb))).astype(BF16)
        for h in range(z.split):
            at = j * z.span + h * z.cb
            half[:, at : at + z.cb] = rows_out[h * z.rows : (h + 1) * z.rows]
    half[:, z.width :] = placed(place, meta)[: z.rows].astype(BF16)


def place_moment(z, i, place, got, out, buf, sems):
    copies = []
    for j in range(z.blocks):
        at = i * z.body + j * z.cb
        rows_out = placed(place, gathered(got, slice(at, at + z.cb)))
        for h in range(z.split):
            col = j * z.span + h * z.cb
            buf[:, col : col + z.cb] = rows_out[h * z.rows : (h + 1) * z.rows]
        cols = pl.ds(j * z.span, z.span)
        copies.append(pltpu.make_async_copy(buf.at[:, cols], out.at[:, cols], sems.at[j]))
        copies[-1].start()
    return copies


def rows_kernel(z, rep_ref, half, place, *refs):
    got, (new_master, params, one_out, two_out, master_buf, one_buf, two_buf, sems) = refs[: z.peers], refs[z.peers :]
    there = pl.ds(pl.multiple_of(rep_ref[0] * z.width, LANES), z.width)
    copies = [pltpu.make_async_copy(half.at[:, : z.width], params.at[:, there], sems.at[0, 0])]
    copies[0].start()
    for j in range(z.blocks):
        at = slice(j * z.span, (j + 1) * z.span)
        master_buf[:, at] = half[:, at].astype(F32)
        cols = pl.ds(j * z.span, z.span)
        copies.append(pltpu.make_async_copy(master_buf.at[:, cols], new_master.at[:, cols], sems.at[1, j]))
        copies[-1].start()
    copies += place_moment(z, 1, place[...], got, one_out, one_buf, sems.at[2])
    copies += place_moment(z, 2, place[...], got, two_out, two_buf, sems.at[3])
    for copy in copies:
        copy.wait()


def finish_kernel(z, rep_ref, half, *refs):
    others, (_, params, checksum, sems) = refs[: z.copies - 1], refs[z.copies - 1 :]
    copies = []
    for k, other in enumerate(others):
        replica = lax.rem(rep_ref[0] + z.copies - (k + 1), z.copies)
        there = pl.ds(pl.multiple_of(replica * z.width, LANES), z.width)
        copies.append(pltpu.make_async_copy(other.at[:, : z.width], params.at[:, there], sems.at[k]))
        copies[-1].start()
    sums = half[:, z.width :].astype(F32)
    for other in others:
        sums = sums + other[:, z.width :].astype(F32)
    lane = iota((z.rows, LANES), 1)
    column = jnp.sum(jnp.where((lane >= 1) & (lane <= 3), sums, 0.0), axis=1, keepdims=True)
    diagonal = iota((z.rows, z.rows), 0) == iota((z.rows, z.rows), 1)
    checksum[...] = jnp.sum(jnp.where(diagonal, column, 0.0), axis=0, keepdims=True)
    for copy in copies:
        copy.wait()


def shifted(value, axis, k, count):
    return lax.ppermute(value, axis, [(i, (i + k) % count) for i in range(count)])


def always_sent(peers):
    return [peers // 4 - 1, peers // 2, peers - 1]


def shift_groups(peers):
    rest = [s for s in range(1, peers) if s not in always_sent(peers)]
    groups = -(-len(rest) // GROUP)
    return [rest[g::groups] for g in range(groups)]


def agree(used, stride, peers, after, compiler_params):
    vmem = pl.BlockSpec(memory_space=pltpu.VMEM)
    other = lax.ppermute(used, "fsdp", [(i, i ^ stride) for i in range(peers)])
    return pl.pallas_call(
        agree_kernel,
        out_shape=jax.ShapeDtypeStruct((1, LANES), jnp.int32),
        in_specs=[vmem, vmem, pl.BlockSpec(memory_space=pl.ANY)],
        out_specs=vmem,
        compiler_params=compiler_params,
        name="agree",
    )(used, other, after)


def choose_branches(used, peers, compiler_params):
    vmem = pl.BlockSpec(memory_space=pltpu.VMEM)
    smem = pl.BlockSpec(memory_space=pltpu.SMEM)
    groups = shift_groups(peers)
    other = lax.ppermute(used, "fsdp", [(i, i ^ (peers // 2)) for i in range(peers)])
    return pl.pallas_call(
        functools.partial(choose_kernel, groups),
        out_shape=[pltpu.SMEM((1,), jnp.int32)] * len(groups),
        in_specs=[vmem, vmem],
        out_specs=[smem] * len(groups),
        compiler_params=compiler_params,
        name="choose",
    )(used, other)


def send_used(peers, group, used, chunks):
    return tuple(
        shifted(chunk, "fsdp", s, peers) if used >> i & 1 else chunk for i, (s, chunk) in enumerate(zip(group, chunks))
    )


def move(z, chunks, used, by_shift, compiler_params):
    if not by_shift:
        got = lax.all_to_all(jnp.concatenate(chunks, axis=0), "fsdp", split_axis=0, concat_axis=0, tiled=True)
        return [got[s * z.lines : (s + 1) * z.lines] for s in range(z.peers)]
    got = list(chunks)
    always = always_sent(z.peers)
    for s in always:
        got[s] = shifted(chunks[s], "fsdp", s, z.peers)
    for stride in (2, 4):
        used = agree(used, stride, z.peers, chunks[0], compiler_params)
    chosen = choose_branches(used, z.peers, compiler_params)
    barred = lax.optimization_barrier((*chosen, *[got[s] for s in always]))
    chosen = barred[: len(chosen)]
    for s, value in zip(always, barred[len(chosen) :]):
        got[s] = value
    for group, number in zip(shift_groups(z.peers), chosen):
        branches = [
            lambda *values, group=group, used=used: send_used(z.peers, group, used, values)
            for used in range(1 << len(group))
        ]
        for s, value in zip(group, lax.switch(number[0], branches, *[chunks[s] for s in group])):
            got[s] = value
    return got


def shards(master, moment_one, moment_two, gradients, new_row):
    rows, width = master.shape
    peers, copies = lax.axis_size("fsdp"), lax.axis_size("replica")
    z = Sizes(rows, width, peers, copies)
    compiler_params = pltpu.CompilerParams(vmem_limit_bytes=VMEM_BYTES)
    smem = pl.BlockSpec(memory_space=pltpu.SMEM)
    vmem = pl.BlockSpec(memory_space=pltpu.VMEM)
    hbm = pl.BlockSpec(memory_space=pl.ANY)
    dma = pltpu.SemaphoreType.DMA

    replica = lax.axis_index("replica").astype(jnp.int32)
    rep = replica.reshape(1)
    by_shift = peers == SHIFT_PEERS
    origin = (lax.axis_index("fsdp").astype(jnp.int32) if by_shift else jnp.int32(0)).reshape(1)
    state_in = [pltpu.with_memory_space_constraint(x, pltpu.HBM) for x in (master, moment_one, moment_two)]
    full = pltpu.with_memory_space_constraint(gradients[0], pltpu.HBM)

    part = jax.ShapeDtypeStruct((rows, width), BF16)
    pick, info, used, *parts = pl.pallas_call(
        functools.partial(prepare_kernel, z),
        out_shape=[
            jax.ShapeDtypeStruct((z.split, z.slots, rows), BF16),
            jax.ShapeDtypeStruct((rows, LANES), F32),
            jax.ShapeDtypeStruct((1, LANES), jnp.int32),
        ]
        + [part] * (copies - 1),
        in_specs=[smem, smem, hbm, hbm],
        out_specs=[vmem] * (copies + 2),
        scratch_shapes=[
            pltpu.VMEM((copies - 1, rows, width), F32),
            pltpu.VMEM((1, rows), jnp.int32),
            dma((copies - 1, z.blocks)),
            dma,
        ],
        compiler_params=compiler_params,
        cost_estimate=pl.CostEstimate(flops=1 << 30, bytes_accessed=1, transcendentals=0),
        name="prepare",
    )(rep, origin, pltpu.with_memory_space_constraint(new_row.reshape(1, rows), pltpu.HBM), full)
    received = [shifted(value, "replica", k + 1, copies) for k, value in enumerate(parts)]

    loaded = jax.ShapeDtypeStruct((rows, width), F32)
    *state, meta = pl.pallas_call(
        functools.partial(load_kernel, z),
        out_shape=[loaded, loaded, loaded, loaded, jax.ShapeDtypeStruct((rows, LANES), BF16)],
        in_specs=[smem, vmem, hbm, hbm, hbm, hbm],
        out_specs=[vmem] * 5,
        scratch_shapes=[dma((4, z.blocks))],
        compiler_params=compiler_params,
        cost_estimate=pl.CostEstimate(flops=1 << 30, bytes_accessed=1, transcendentals=0),
        name="load",
    )(rep, info, *state_in, full)

    if by_shift:
        used = agree(used, 1, peers, meta, compiler_params)
    chunks = pl.pallas_call(
        functools.partial(update_kernel, z),
        out_shape=[jax.ShapeDtypeStruct((z.lines, z.payload), BF16)] * peers,
        in_specs=[vmem] * (5 + copies) + [hbm],
        out_specs=[vmem] * peers,
        scratch_shapes=[pltpu.VMEM((z.stacked, 3 * z.body), BF16)],
        compiler_params=compiler_params,
        cost_estimate=pl.CostEstimate(
            flops=6 * z.slots * z.stacked * z.body, bytes_accessed=24 * rows * width, transcendentals=rows * width
        ),
        name="update",
    )(pick, meta, *state, *received, used)

    got = move(z, chunks, used, by_shift, compiler_params)

    wide = jax.ShapeDtypeStruct((rows, width), F32)
    full_params = jax.ShapeDtypeStruct((rows, width * copies), BF16)
    half, place = pl.pallas_call(
        functools.partial(half_kernel, z),
        out_shape=(
            jax.ShapeDtypeStruct((rows, width + LANES), BF16),
            jax.ShapeDtypeStruct((z.stacked, z.slots), BF16),
        ),
        in_specs=[vmem] * peers,
        out_specs=(vmem, vmem),
        compiler_params=compiler_params,
        name="place_half",
    )(*got)
    others = [shifted(half, "replica", k, copies) for k in range(1, copies)]

    new_master, params, new_one, new_two = pl.pallas_call(
        functools.partial(rows_kernel, z),
        out_shape=(wide, full_params, wide, wide),
        in_specs=[smem] + [vmem] * (peers + 2),
        out_specs=(hbm, hbm, hbm, hbm),
        scratch_shapes=[pltpu.VMEM((rows, width), F32)] * 3 + [dma((4, z.blocks))],
        compiler_params=compiler_params,
        cost_estimate=pl.CostEstimate(
            flops=4 * z.slots * z.stacked * z.body, bytes_accessed=18 * rows * width, transcendentals=0
        ),
        name="place_rows",
    )(rep, half, place, *got)

    params, checksum = pl.pallas_call(
        functools.partial(finish_kernel, z),
        out_shape=(full_params, jax.ShapeDtypeStruct((1, rows), F32)),
        in_specs=[smem] + [vmem] * copies + [hbm],
        out_specs=(hbm, vmem),
        scratch_shapes=[dma((max(1, copies - 1),))],
        input_output_aliases={copies + 1: 0},
        compiler_params=compiler_params,
        cost_estimate=pl.CostEstimate(flops=0, bytes_accessed=4 * rows * width, transcendentals=0),
        name="finish",
    )(rep, half, *others, params)
    return (new_master, new_one, new_two, params, checksum.reshape(rows))


def solution(mesh):
    return jax.shard_map(
        shards,
        mesh=mesh,
        in_specs=(
            P("fsdp", "replica"),
            P("fsdp", "replica"),
            P("fsdp", "replica"),
            P("replica", "fsdp", None),
            P("fsdp"),
        ),
        out_specs=(
            P("fsdp", "replica"),
            P("fsdp", "replica"),
            P("fsdp", "replica"),
            P("fsdp", None),
            P("fsdp"),
        ),
        check_vma=False,
    )
```

```python
import functools
import math

import jax
import jax.numpy as jnp
from jax import lax
from jax.experimental import pallas as pl
from jax.experimental.pallas import tpu as pltpu
from jax.sharding import PartitionSpec as P

LANES = 128
TILE_ROWS = 16
MIB = 1024 * 1024
VMEM_BYTES = 24 * MIB
SHIFT_PEERS = 16
GROUP = 4
F32 = jnp.float32
BF16 = jnp.bfloat16


def iota(shape, axis):
    return lax.broadcasted_iota(jnp.int32, shape, axis)


class Sizes:
    def __init__(self, rows, width, peers, copies):
        self.rows, self.width, self.peers, self.copies = rows, width, peers, copies
        self.cap = max(2, 2 * rows // peers)
        self.split = max(1, TILE_ROWS // self.cap)
        self.lines = self.cap * self.split
        self.slots = peers * self.lines
        self.stacked = self.split * rows
        self.body = width // self.split
        self.cb = math.gcd(self.body, 512)
        self.blocks = self.body // self.cb
        self.span = self.split * self.cb
        self.sub = math.gcd(self.cb, 256)
        self.payload = 3 * self.body + LANES


def prepare_kernel(z, rep_ref, origin_ref, new_row_hbm, full_hbm, pick_ref, info_ref, mask_ref, *refs):
    parts, (full_buf, line_buf, sems, line_sem) = refs[: z.copies - 1], refs[z.copies - 1 :]
    step = z.width // z.blocks
    line_copy = pltpu.make_async_copy(new_row_hbm, line_buf, line_sem)
    line_copy.start()
    copies = []
    for k in range(1, z.copies):
        other = lax.rem(rep_ref[0] + k, z.copies)
        for j in range(z.blocks):
            there = pl.ds(pl.multiple_of(other * z.width + j * step, LANES), step)
            copies.append(
                pltpu.make_async_copy(
                    full_hbm.at[:, there], full_buf.at[k - 1, :, pl.ds(j * step, step)], sems.at[k - 1, j]
                )
            )
            copies[-1].start()
    line_copy.wait()
    line = line_buf[...]
    at_row, at_lane = iota((z.rows, z.rows), 0), iota((z.rows, z.rows), 1)
    column = jnp.sum(jnp.where(at_row == at_lane, line.astype(F32), 0.0), axis=1, keepdims=True).astype(jnp.int32)
    target, target_column = line // z.rows, column // z.rows
    earlier = (target_column == target) & (at_row < at_lane)
    rank = jnp.sum(jnp.where(earlier, 1.0, 0.0), axis=0, keepdims=True).astype(jnp.int32)
    shift = lax.rem(target - origin_ref[0] + z.peers, z.peers)
    shift_column = lax.rem(target_column - origin_ref[0] + z.peers, z.peers)
    for h in range(z.split):
        slot = shift * z.lines + h * z.cap + rank
        pick_ref[h] = jnp.where(iota((z.slots, z.rows), 0) == slot, 1.0, 0.0).astype(BF16)
    lane = iota((z.rows, LANES), 1)
    info_ref[...] = jnp.where(lane == 0, (column - target_column * z.rows + 1).astype(F32), 0.0)
    used = jnp.where(lane == shift_column, 1.0, 0.0)
    mask_ref[...] = jnp.max(used, axis=0, keepdims=True).astype(jnp.int32)
    for k in range(1, z.copies):
        for j in range(z.blocks):
            copies[(k - 1) * z.blocks + j].wait()
            at = slice(j * step, (j + 1) * step)
            parts[k - 1][:, at] = full_buf[k - 1, :, at].astype(BF16)


def agree_kernel(left, right, _, out):
    out[...] = jnp.maximum(left[...], right[...])


def choose_kernel(digits, left, right, *outs):
    total = jnp.maximum(left[...], right[...])
    lane = iota(total.shape, 1)
    for digit, out in zip(digits, outs):
        value = jnp.zeros(total.shape, jnp.int32)
        for i, s in enumerate(digit):
            value = value + jnp.where(lane == s, total << i, 0)
        out[0] = jnp.sum(value.astype(F32)).astype(jnp.int32)


def load_kernel(z, rep_ref, info_ref, master_hbm, one_hbm, two_hbm, full_hbm, master, one, two, own, meta_ref, sems):
    base = rep_ref[0] * z.width
    step = z.width // z.blocks
    copies = []
    for j in range(z.blocks):
        at = pl.ds(j * step, step)
        mine = pl.ds(pl.multiple_of(base + j * step, LANES), step)
        copies.append(
            [
                pltpu.make_async_copy(master_hbm.at[:, at], master.at[:, at], sems.at[0, j]),
                pltpu.make_async_copy(one_hbm.at[:, at], one.at[:, at], sems.at[1, j]),
                pltpu.make_async_copy(two_hbm.at[:, at], two.at[:, at], sems.at[2, j]),
                pltpu.make_async_copy(full_hbm.at[:, mine], own.at[:, at], sems.at[3, j]),
            ]
        )
    for i in range(4):
        for j in range(z.blocks):
            copies[j][i].start()
    part = jnp.zeros((z.rows, LANES), F32)
    for j in range(z.blocks):
        copies[j][0].wait()
        for at in range(j * step, (j + 1) * step, LANES):
            weights = 1.0 + ((iota((1, LANES), 1) + (base + at)) % 7).astype(F32) / 7.0
            part = part + master[:, at : at + LANES] * weights
    total = jnp.sum(part, axis=1, keepdims=True) * (1.0 / math.sqrt(z.width * z.copies))
    high = total.astype(BF16).astype(F32)
    middle = (total - high).astype(BF16).astype(F32)
    low = total - high - middle
    lane = iota((z.rows, LANES), 1)
    meta = jnp.where(lane == 1, high, jnp.where(lane == 2, middle, jnp.where(lane == 3, low, info_ref[...])))
    meta_ref[...] = meta.astype(BF16)
    for j in range(z.blocks):
        for i in range(1, 4):
            copies[j][i].wait()


def update_kernel(z, pick_ref, meta_ref, master, one, two, own, *refs):
    received, refs = refs[: z.copies - 1], refs[z.copies :]
    outs, rows_buf = refs[: z.peers], refs[z.peers]
    pick = jnp.concatenate([pick_ref[h] for h in range(z.split)], axis=1)
    for j in range(z.blocks):
        for h in range(z.split):
            for c in range(0, z.cb, z.sub):
                at = j * z.span + h * z.cb + c
                cols = slice(at, at + z.sub)
                summed = own[:, cols]
                for other in received:
                    summed = summed + other[:, cols].astype(F32)
                moved = master[:, cols]
                new_one = 0.9 * one[:, cols] + 0.1 * summed
                new_two = 0.95 * two[:, cols] + 0.05 * summed * summed
                update = new_one * (1.0 / (1.0 - 0.9**10)) / (jnp.sqrt(new_two * (1.0 / (1.0 - 0.95**10))) + 1e-08)
                new_master = moved - 0.05 * (update + 0.1 * moved)
                for i, value in enumerate((new_master, new_one, new_two)):
                    to = i * z.body + j * z.cb + c
                    rows_buf[h * z.rows : (h + 1) * z.rows, to : to + z.sub] = value.astype(BF16)
        for i in range(3):
            at = i * z.body + j * z.cb
            packed = jnp.dot(pick, rows_buf[:, at : at + z.cb], preferred_element_type=F32).astype(BF16)
            for s, out in enumerate(outs):
                out[:, at : at + z.cb] = packed[s * z.lines : (s + 1) * z.lines]
    meta = jnp.concatenate([meta_ref[...]] * z.split, axis=0)
    packed = jnp.dot(pick, meta, preferred_element_type=F32).astype(BF16)
    for s, out in enumerate(outs):
        out[:, 3 * z.body :] = packed[s * z.lines : (s + 1) * z.lines]


def gathered(refs, cols):
    return jnp.concatenate([ref[:, cols] for ref in refs], axis=0)


def placing(z, meta):
    offset = meta[:, :1].astype(F32).astype(jnp.int32)
    piece = lax.rem(iota((z.slots, 1), 0), z.lines) // z.cap
    wanted = jnp.where(offset > 0, offset - 1 + piece * z.rows, -1)
    return jnp.where(iota((z.slots, z.stacked), 1) == wanted, 1.0, 0.0).T.astype(BF16)


def placed(place, values):
    return jnp.dot(place, values, preferred_element_type=F32)


def half_kernel(z, *refs):
    got, (half, place_out) = refs[: z.peers], refs[z.peers :]
    meta = gathered(got, slice(3 * z.body, 3 * z.body + LANES))
    place = placing(z, meta)
    place_out[...] = place
    for j in range(z.blocks):
        rows_out = placed(place, gathered(got, slice(j * z.cb, (j + 1) * z.cb))).astype(BF16)
        for h in range(z.split):
            at = j * z.span + h * z.cb
            half[:, at : at + z.cb] = rows_out[h * z.rows : (h + 1) * z.rows]
    half[:, z.width :] = placed(place, meta)[: z.rows].astype(BF16)


def place_moment(z, i, place, got, out, buf, sems):
    copies = []
    for j in range(z.blocks):
        at = i * z.body + j * z.cb
        rows_out = placed(place, gathered(got, slice(at, at + z.cb)))
        for h in range(z.split):
            col = j * z.span + h * z.cb
            buf[:, col : col + z.cb] = rows_out[h * z.rows : (h + 1) * z.rows]
        cols = pl.ds(j * z.span, z.span)
        copies.append(pltpu.make_async_copy(buf.at[:, cols], out.at[:, cols], sems.at[j]))
        copies[-1].start()
    return copies


def rows_kernel(z, rep_ref, half, place, *refs):
    got, (new_master, params, one_out, two_out, master_buf, one_buf, two_buf, sems) = refs[: z.peers], refs[z.peers :]
    there = pl.ds(pl.multiple_of(rep_ref[0] * z.width, LANES), z.width)
    copies = [pltpu.make_async_copy(half.at[:, : z.width], params.at[:, there], sems.at[0, 0])]
    copies[0].start()
    for j in range(z.blocks):
        at = slice(j * z.span, (j + 1) * z.span)
        master_buf[:, at] = half[:, at].astype(F32)
        cols = pl.ds(j * z.span, z.span)
        copies.append(pltpu.make_async_copy(master_buf.at[:, cols], new_master.at[:, cols], sems.at[1, j]))
        copies[-1].start()
    copies += place_moment(z, 1, place[...], got, one_out, one_buf, sems.at[2])
    copies += place_moment(z, 2, place[...], got, two_out, two_buf, sems.at[3])
    for copy in copies:
        copy.wait()


def finish_kernel(z, rep_ref, half, *refs):
    others, (_, params, checksum, sems) = refs[: z.copies - 1], refs[z.copies - 1 :]
    copies = []
    for k, other in enumerate(others):
        replica = lax.rem(rep_ref[0] + z.copies - (k + 1), z.copies)
        there = pl.ds(pl.multiple_of(replica * z.width, LANES), z.width)
        copies.append(pltpu.make_async_copy(other.at[:, : z.width], params.at[:, there], sems.at[k]))
        copies[-1].start()
    sums = half[:, z.width :].astype(F32)
    for other in others:
        sums = sums + other[:, z.width :].astype(F32)
    lane = iota((z.rows, LANES), 1)
    column = jnp.sum(jnp.where((lane >= 1) & (lane <= 3), sums, 0.0), axis=1, keepdims=True)
    diagonal = iota((z.rows, z.rows), 0) == iota((z.rows, z.rows), 1)
    checksum[...] = jnp.sum(jnp.where(diagonal, column, 0.0), axis=0, keepdims=True)
    for copy in copies:
        copy.wait()


def shifted(value, axis, k, count):
    return lax.ppermute(value, axis, [(i, (i + k) % count) for i in range(count)])


def always_sent(peers):
    return [peers // 4 - 1, peers // 2, peers - 1]


def shift_groups(peers):
    always, half = always_sent(peers), peers // 2
    rest = [s for s in range(1, peers) if s not in always]
    rest = sorted(rest, key=lambda s: ((s + half) % peers in always, s % half, s))
    return [rest[i : i + GROUP] for i in range(0, len(rest), GROUP)]


def agree(used, stride, peers, after, compiler_params):
    vmem = pl.BlockSpec(memory_space=pltpu.VMEM)
    other = lax.ppermute(used, "fsdp", [(i, i ^ stride) for i in range(peers)])
    return pl.pallas_call(
        agree_kernel,
        out_shape=jax.ShapeDtypeStruct((1, LANES), jnp.int32),
        in_specs=[vmem, vmem, pl.BlockSpec(memory_space=pl.ANY)],
        out_specs=vmem,
        compiler_params=compiler_params,
        name="agree",
    )(used, other, after)


def choose_branches(used, peers, compiler_params):
    vmem = pl.BlockSpec(memory_space=pltpu.VMEM)
    smem = pl.BlockSpec(memory_space=pltpu.SMEM)
    groups = shift_groups(peers)
    other = lax.ppermute(used, "fsdp", [(i, i ^ (peers // 2)) for i in range(peers)])
    return pl.pallas_call(
        functools.partial(choose_kernel, groups),
        out_shape=[pltpu.SMEM((1,), jnp.int32)] * len(groups),
        in_specs=[vmem, vmem],
        out_specs=[smem] * len(groups),
        compiler_params=compiler_params,
        name="choose",
    )(used, other)


def send_used(peers, group, used, chunks):
    return tuple(
        shifted(chunk, "fsdp", s, peers) if used >> i & 1 else chunk for i, (s, chunk) in enumerate(zip(group, chunks))
    )


def move(z, chunks, used, by_shift, compiler_params):
    if not by_shift:
        got = lax.all_to_all(jnp.concatenate(chunks, axis=0), "fsdp", split_axis=0, concat_axis=0, tiled=True)
        return [got[s * z.lines : (s + 1) * z.lines] for s in range(z.peers)]
    got = list(chunks)
    always = always_sent(z.peers)
    for s in always[:-1]:
        got[s] = shifted(chunks[s], "fsdp", s, z.peers)
    used, _ = lax.optimization_barrier((used, chunks[0]))
    used = agree(used, 2, z.peers, chunks[0], compiler_params)
    last = always[-1]
    value, _ = lax.optimization_barrier((chunks[last], used))
    got[last] = shifted(value, "fsdp", last, z.peers)
    used = agree(used, 4, z.peers, chunks[0], compiler_params)
    chosen = choose_branches(used, z.peers, compiler_params)
    barred = lax.optimization_barrier((*chosen, *[got[s] for s in always]))
    chosen = barred[: len(chosen)]
    for s, value in zip(always, barred[len(chosen) :]):
        got[s] = value
    for group, number in zip(shift_groups(z.peers), chosen):
        branches = [
            lambda *values, group=group, used=used: send_used(z.peers, group, used, values)
            for used in range(1 << len(group))
        ]
        for s, value in zip(group, lax.switch(number[0], branches, *[chunks[s] for s in group])):
            got[s] = value
    return got


def shards(master, moment_one, moment_two, gradients, new_row):
    rows, width = master.shape
    peers, copies = lax.axis_size("fsdp"), lax.axis_size("replica")
    z = Sizes(rows, width, peers, copies)
    compiler_params = pltpu.CompilerParams(vmem_limit_bytes=VMEM_BYTES)
    smem = pl.BlockSpec(memory_space=pltpu.SMEM)
    vmem = pl.BlockSpec(memory_space=pltpu.VMEM)
    hbm = pl.BlockSpec(memory_space=pl.ANY)
    dma = pltpu.SemaphoreType.DMA

    replica = lax.axis_index("replica").astype(jnp.int32)
    rep = replica.reshape(1)
    by_shift = peers == SHIFT_PEERS
    origin = (lax.axis_index("fsdp").astype(jnp.int32) if by_shift else jnp.int32(0)).reshape(1)
    state_in = [pltpu.with_memory_space_constraint(x, pltpu.HBM) for x in (master, moment_one, moment_two)]
    full = pltpu.with_memory_space_constraint(gradients[0], pltpu.HBM)

    part = jax.ShapeDtypeStruct((rows, width), BF16)
    pick, info, used, *parts = pl.pallas_call(
        functools.partial(prepare_kernel, z),
        out_shape=[
            jax.ShapeDtypeStruct((z.split, z.slots, rows), BF16),
            jax.ShapeDtypeStruct((rows, LANES), F32),
            jax.ShapeDtypeStruct((1, LANES), jnp.int32),
        ]
        + [part] * (copies - 1),
        in_specs=[smem, smem, hbm, hbm],
        out_specs=[vmem] * (copies + 2),
        scratch_shapes=[
            pltpu.VMEM((copies - 1, rows, width), F32),
            pltpu.VMEM((1, rows), jnp.int32),
            dma((copies - 1, z.blocks)),
            dma,
        ],
        compiler_params=compiler_params,
        cost_estimate=pl.CostEstimate(flops=1 << 30, bytes_accessed=1, transcendentals=0),
        name="prepare",
    )(rep, origin, pltpu.with_memory_space_constraint(new_row.reshape(1, rows), pltpu.HBM), full)
    received = [shifted(value, "replica", k + 1, copies) for k, value in enumerate(parts)]

    loaded = jax.ShapeDtypeStruct((rows, width), F32)
    *state, meta = pl.pallas_call(
        functools.partial(load_kernel, z),
        out_shape=[loaded, loaded, loaded, loaded, jax.ShapeDtypeStruct((rows, LANES), BF16)],
        in_specs=[smem, vmem, hbm, hbm, hbm, hbm],
        out_specs=[vmem] * 5,
        scratch_shapes=[dma((4, z.blocks))],
        compiler_params=compiler_params,
        cost_estimate=pl.CostEstimate(flops=1 << 30, bytes_accessed=1, transcendentals=0),
        name="load",
    )(rep, info, *state_in, full)

    if by_shift:
        used = agree(used, 1, peers, meta, compiler_params)
    chunks = pl.pallas_call(
        functools.partial(update_kernel, z),
        out_shape=[jax.ShapeDtypeStruct((z.lines, z.payload), BF16)] * peers,
        in_specs=[vmem] * (5 + copies) + [hbm],
        out_specs=[vmem] * peers,
        scratch_shapes=[pltpu.VMEM((z.stacked, 3 * z.body), BF16)],
        compiler_params=compiler_params,
        cost_estimate=pl.CostEstimate(
            flops=6 * z.slots * z.stacked * z.body, bytes_accessed=24 * rows * width, transcendentals=rows * width
        ),
        name="update",
    )(pick, meta, *state, *received, used)

    got = move(z, chunks, used, by_shift, compiler_params)

    wide = jax.ShapeDtypeStruct((rows, width), F32)
    full_params = jax.ShapeDtypeStruct((rows, width * copies), BF16)
    half, place = pl.pallas_call(
        functools.partial(half_kernel, z),
        out_shape=(
            jax.ShapeDtypeStruct((rows, width + LANES), BF16),
            jax.ShapeDtypeStruct((z.stacked, z.slots), BF16),
        ),
        in_specs=[vmem] * peers,
        out_specs=(vmem, vmem),
        compiler_params=compiler_params,
        name="place_half",
    )(*got)
    others = [shifted(half, "replica", k, copies) for k in range(1, copies)]

    new_master, params, new_one, new_two = pl.pallas_call(
        functools.partial(rows_kernel, z),
        out_shape=(wide, full_params, wide, wide),
        in_specs=[smem] + [vmem] * (peers + 2),
        out_specs=(hbm, hbm, hbm, hbm),
        scratch_shapes=[pltpu.VMEM((rows, width), F32)] * 3 + [dma((4, z.blocks))],
        compiler_params=compiler_params,
        cost_estimate=pl.CostEstimate(
            flops=4 * z.slots * z.stacked * z.body, bytes_accessed=18 * rows * width, transcendentals=0
        ),
        name="place_rows",
    )(rep, half, place, *got)

    params, checksum = pl.pallas_call(
        functools.partial(finish_kernel, z),
        out_shape=(full_params, jax.ShapeDtypeStruct((1, rows), F32)),
        in_specs=[smem] + [vmem] * copies + [hbm],
        out_specs=(hbm, vmem),
        scratch_shapes=[dma((max(1, copies - 1),))],
        input_output_aliases={copies + 1: 0},
        compiler_params=compiler_params,
        cost_estimate=pl.CostEstimate(flops=0, bytes_accessed=4 * rows * width, transcendentals=0),
        name="finish",
    )(rep, half, *others, params)
    return (new_master, new_one, new_two, params, checksum.reshape(rows))


def solution(mesh):
    return jax.shard_map(
        shards,
        mesh=mesh,
        in_specs=(
            P("fsdp", "replica"),
            P("fsdp", "replica"),
            P("fsdp", "replica"),
            P("replica", "fsdp", None),
            P("fsdp"),
        ),
        out_specs=(
            P("fsdp", "replica"),
            P("fsdp", "replica"),
            P("fsdp", "replica"),
            P("fsdp", None),
            P("fsdp"),
        ),
        check_vma=False,
    )
```

```python
import functools
import math

import jax
import jax.numpy as jnp
from jax import lax
from jax.experimental import pallas as pl
from jax.experimental.pallas import tpu as pltpu
from jax.sharding import PartitionSpec as P

LANES = 128
TILE_ROWS = 16
MIB = 1024 * 1024
VMEM_BYTES = 24 * MIB
SHIFT_PEERS = 16
GROUP = 6
EXACT = 3
F32 = jnp.float32
BF16 = jnp.bfloat16


def iota(shape, axis):
    return lax.broadcasted_iota(jnp.int32, shape, axis)


class Sizes:
    def __init__(self, rows, width, peers, copies):
        self.rows, self.width, self.peers, self.copies = rows, width, peers, copies
        self.cap = max(2, 2 * rows // peers)
        self.split = max(1, TILE_ROWS // self.cap)
        self.lines = self.cap * self.split
        self.slots = peers * self.lines
        self.stacked = self.split * rows
        self.body = width // self.split
        self.cb = math.gcd(self.body, 512)
        self.blocks = self.body // self.cb
        self.span = self.split * self.cb
        self.sub = math.gcd(self.cb, 256)
        self.payload = 3 * self.body + LANES


def prepare_kernel(z, rep_ref, origin_ref, new_row_hbm, full_hbm, pick_ref, info_ref, mask_ref, *refs):
    parts, (full_buf, line_buf, sems, line_sem) = refs[: z.copies - 1], refs[z.copies - 1 :]
    step = z.width // z.blocks
    line_copy = pltpu.make_async_copy(new_row_hbm, line_buf, line_sem)
    line_copy.start()
    copies = []
    for k in range(1, z.copies):
        other = lax.rem(rep_ref[0] + k, z.copies)
        for j in range(z.blocks):
            there = pl.ds(pl.multiple_of(other * z.width + j * step, LANES), step)
            copies.append(
                pltpu.make_async_copy(
                    full_hbm.at[:, there], full_buf.at[k - 1, :, pl.ds(j * step, step)], sems.at[k - 1, j]
                )
            )
            copies[-1].start()
    line_copy.wait()
    line = line_buf[...]
    at_row, at_lane = iota((z.rows, z.rows), 0), iota((z.rows, z.rows), 1)
    column = jnp.sum(jnp.where(at_row == at_lane, line.astype(F32), 0.0), axis=1, keepdims=True).astype(jnp.int32)
    target, target_column = line // z.rows, column // z.rows
    earlier = (target_column == target) & (at_row < at_lane)
    rank = jnp.sum(jnp.where(earlier, 1.0, 0.0), axis=0, keepdims=True).astype(jnp.int32)
    shift = lax.rem(target - origin_ref[0] + z.peers, z.peers)
    shift_column = lax.rem(target_column - origin_ref[0] + z.peers, z.peers)
    for h in range(z.split):
        slot = shift * z.lines + h * z.cap + rank
        pick_ref[h] = jnp.where(iota((z.slots, z.rows), 0) == slot, 1.0, 0.0).astype(BF16)
    lane = iota((z.rows, LANES), 1)
    info_ref[...] = jnp.where(lane == 0, (column - target_column * z.rows + 1).astype(F32), 0.0)
    used = jnp.where(lane == shift_column, 1.0, 0.0)
    mask_ref[...] = jnp.max(used, axis=0, keepdims=True).astype(jnp.int32)
    for k in range(1, z.copies):
        for j in range(z.blocks):
            copies[(k - 1) * z.blocks + j].wait()
            at = slice(j * step, (j + 1) * step)
            parts[k - 1][:, at] = full_buf[k - 1, :, at].astype(BF16)


def agree_kernel(left, right, _, out):
    out[...] = jnp.maximum(left[...], right[...])


def choose_kernel(groups, left, right, table, *outs):
    total = jnp.maximum(left[...], right[...])
    lane = iota(total.shape, 1)
    for group, out in zip(groups, outs):
        value = jnp.zeros(total.shape, jnp.int32)
        for i, s in enumerate(group):
            value = value + jnp.where(lane == s, total << i, 0)
        out[0] = table[jnp.sum(value.astype(F32)).astype(jnp.int32)]


def load_kernel(z, rep_ref, info_ref, master_hbm, one_hbm, two_hbm, full_hbm, master, one, two, own, meta_ref, sems):
    base = rep_ref[0] * z.width
    step = z.width // z.blocks
    copies = []
    for j in range(z.blocks):
        at = pl.ds(j * step, step)
        mine = pl.ds(pl.multiple_of(base + j * step, LANES), step)
        copies.append(
            [
                pltpu.make_async_copy(master_hbm.at[:, at], master.at[:, at], sems.at[0, j]),
                pltpu.make_async_copy(one_hbm.at[:, at], one.at[:, at], sems.at[1, j]),
                pltpu.make_async_copy(two_hbm.at[:, at], two.at[:, at], sems.at[2, j]),
                pltpu.make_async_copy(full_hbm.at[:, mine], own.at[:, at], sems.at[3, j]),
            ]
        )
    for i in range(4):
        for j in range(z.blocks):
            copies[j][i].start()
    part = jnp.zeros((z.rows, LANES), F32)
    for j in range(z.blocks):
        copies[j][0].wait()
        for at in range(j * step, (j + 1) * step, LANES):
            weights = 1.0 + ((iota((1, LANES), 1) + (base + at)) % 7).astype(F32) / 7.0
            part = part + master[:, at : at + LANES] * weights
    total = jnp.sum(part, axis=1, keepdims=True) * (1.0 / math.sqrt(z.width * z.copies))
    high = total.astype(BF16).astype(F32)
    middle = (total - high).astype(BF16).astype(F32)
    low = total - high - middle
    lane = iota((z.rows, LANES), 1)
    meta = jnp.where(lane == 1, high, jnp.where(lane == 2, middle, jnp.where(lane == 3, low, info_ref[...])))
    meta_ref[...] = meta.astype(BF16)
    for j in range(z.blocks):
        for i in range(1, 4):
            copies[j][i].wait()


def update_kernel(z, pick_ref, meta_ref, master, one, two, own, *refs):
    received, refs = refs[: z.copies - 1], refs[z.copies :]
    outs, rows_buf = refs[: z.peers], refs[z.peers]
    pick = jnp.concatenate([pick_ref[h] for h in range(z.split)], axis=1)
    for j in range(z.blocks):
        for h in range(z.split):
            for c in range(0, z.cb, z.sub):
                at = j * z.span + h * z.cb + c
                cols = slice(at, at + z.sub)
                summed = own[:, cols]
                for other in received:
                    summed = summed + other[:, cols].astype(F32)
                moved = master[:, cols]
                new_one = 0.9 * one[:, cols] + 0.1 * summed
                new_two = 0.95 * two[:, cols] + 0.05 * summed * summed
                update = new_one * (1.0 / (1.0 - 0.9**10)) / (jnp.sqrt(new_two * (1.0 / (1.0 - 0.95**10))) + 1e-08)
                new_master = moved - 0.05 * (update + 0.1 * moved)
                for i, value in enumerate((new_master, new_one, new_two)):
                    to = i * z.body + j * z.cb + c
                    rows_buf[h * z.rows : (h + 1) * z.rows, to : to + z.sub] = value.astype(BF16)
        for i in range(3):
            at = i * z.body + j * z.cb
            packed = jnp.dot(pick, rows_buf[:, at : at + z.cb], preferred_element_type=F32).astype(BF16)
            for s, out in enumerate(outs):
                out[:, at : at + z.cb] = packed[s * z.lines : (s + 1) * z.lines]
    meta = jnp.concatenate([meta_ref[...]] * z.split, axis=0)
    packed = jnp.dot(pick, meta, preferred_element_type=F32).astype(BF16)
    for s, out in enumerate(outs):
        out[:, 3 * z.body :] = packed[s * z.lines : (s + 1) * z.lines]


def gathered(refs, cols):
    return jnp.concatenate([ref[:, cols] for ref in refs], axis=0)


def placing(z, meta):
    offset = meta[:, :1].astype(F32).astype(jnp.int32)
    piece = lax.rem(iota((z.slots, 1), 0), z.lines) // z.cap
    wanted = jnp.where(offset > 0, offset - 1 + piece * z.rows, -1)
    return jnp.where(iota((z.slots, z.stacked), 1) == wanted, 1.0, 0.0).T.astype(BF16)


def placed(place, values):
    return jnp.dot(place, values, preferred_element_type=F32)


def half_kernel(z, *refs):
    got, (half, place_out) = refs[: z.peers], refs[z.peers :]
    meta = gathered(got, slice(3 * z.body, 3 * z.body + LANES))
    place = placing(z, meta)
    place_out[...] = place
    for j in range(z.blocks):
        rows_out = placed(place, gathered(got, slice(j * z.cb, (j + 1) * z.cb))).astype(BF16)
        for h in range(z.split):
            at = j * z.span + h * z.cb
            half[:, at : at + z.cb] = rows_out[h * z.rows : (h + 1) * z.rows]
    half[:, z.width :] = placed(place, meta)[: z.rows].astype(BF16)


def place_moment(z, i, place, got, out, buf, sems):
    copies = []
    for j in range(z.blocks):
        at = i * z.body + j * z.cb
        rows_out = placed(place, gathered(got, slice(at, at + z.cb)))
        for h in range(z.split):
            col = j * z.span + h * z.cb
            buf[:, col : col + z.cb] = rows_out[h * z.rows : (h + 1) * z.rows]
        cols = pl.ds(j * z.span, z.span)
        copies.append(pltpu.make_async_copy(buf.at[:, cols], out.at[:, cols], sems.at[j]))
        copies[-1].start()
    return copies


def rows_kernel(z, rep_ref, half, place, *refs):
    got, (new_master, params, one_out, two_out, master_buf, one_buf, two_buf, sems) = refs[: z.peers], refs[z.peers :]
    there = pl.ds(pl.multiple_of(rep_ref[0] * z.width, LANES), z.width)
    copies = [pltpu.make_async_copy(half.at[:, : z.width], params.at[:, there], sems.at[0, 0])]
    copies[0].start()
    for j in range(z.blocks):
        at = slice(j * z.span, (j + 1) * z.span)
        master_buf[:, at] = half[:, at].astype(F32)
        cols = pl.ds(j * z.span, z.span)
        copies.append(pltpu.make_async_copy(master_buf.at[:, cols], new_master.at[:, cols], sems.at[1, j]))
        copies[-1].start()
    copies += place_moment(z, 1, place[...], got, one_out, one_buf, sems.at[2])
    copies += place_moment(z, 2, place[...], got, two_out, two_buf, sems.at[3])
    for copy in copies:
        copy.wait()


def finish_kernel(z, rep_ref, half, *refs):
    others, (_, params, checksum, sems) = refs[: z.copies - 1], refs[z.copies - 1 :]
    copies = []
    for k, other in enumerate(others):
        replica = lax.rem(rep_ref[0] + z.copies - (k + 1), z.copies)
        there = pl.ds(pl.multiple_of(replica * z.width, LANES), z.width)
        copies.append(pltpu.make_async_copy(other.at[:, : z.width], params.at[:, there], sems.at[k]))
        copies[-1].start()
    sums = half[:, z.width :].astype(F32)
    for other in others:
        sums = sums + other[:, z.width :].astype(F32)
    lane = iota((z.rows, LANES), 1)
    column = jnp.sum(jnp.where((lane >= 1) & (lane <= 3), sums, 0.0), axis=1, keepdims=True)
    diagonal = iota((z.rows, z.rows), 0) == iota((z.rows, z.rows), 1)
    checksum[...] = jnp.sum(jnp.where(diagonal, column, 0.0), axis=0, keepdims=True)
    for copy in copies:
        copy.wait()


def shifted(value, axis, k, count):
    return lax.ppermute(value, axis, [(i, (i + k) % count) for i in range(count)])


def always_sent(peers):
    return [peers // 4 - 1, peers // 2, peers - 1]


def shift_groups(peers):
    always, half = always_sent(peers), peers // 2
    rest = [s for s in range(1, peers) if s not in always]
    rest = sorted(rest, key=lambda s: ((s + half) % peers in always, s % half, s))
    return [rest[i : i + GROUP] for i in range(0, len(rest), GROUP)]


def leaves_of(count):
    by_size = [[] for _ in range(count + 1)]
    for used in range(1 << count):
        by_size[bin(used).count("1")].append(used)
    if count <= EXACT + 1:
        return list(range(1 << count))
    middle = by_size[EXACT]
    wide = [used for size in range(EXACT + 2, count, 2) for used in by_size[size]]
    small = [used for size in range(2, EXACT) for used in by_size[size]]
    cut = len(middle) // 2
    return by_size[1] + wide + middle[:cut] + small + middle[cut:] + by_size[count] + by_size[0]


def leaf_table(count):
    leaves = leaves_of(count)
    table = []
    for used in range(1 << count):
        holding = [i for i, leaf in enumerate(leaves) if leaf & used == used]
        table.append(min(holding, key=lambda i: bin(leaves[i]).count("1")))
    return jnp.array(table, jnp.int32)


def agree(used, stride, peers, after, compiler_params):
    vmem = pl.BlockSpec(memory_space=pltpu.VMEM)
    other = lax.ppermute(used, "fsdp", [(i, i ^ stride) for i in range(peers)])
    return pl.pallas_call(
        agree_kernel,
        out_shape=jax.ShapeDtypeStruct((1, LANES), jnp.int32),
        in_specs=[vmem, vmem, pl.BlockSpec(memory_space=pl.ANY)],
        out_specs=vmem,
        compiler_params=compiler_params,
        name="agree",
    )(used, other, after)


def choose_branches(used, peers, compiler_params):
    vmem = pl.BlockSpec(memory_space=pltpu.VMEM)
    smem = pl.BlockSpec(memory_space=pltpu.SMEM)
    groups = shift_groups(peers)
    other = lax.ppermute(used, "fsdp", [(i, i ^ (peers // 2)) for i in range(peers)])
    return pl.pallas_call(
        functools.partial(choose_kernel, groups),
        out_shape=[pltpu.SMEM((1,), jnp.int32)] * len(groups),
        in_specs=[vmem, vmem, smem],
        out_specs=[smem] * len(groups),
        compiler_params=compiler_params,
        name="choose",
    )(used, other, leaf_table(len(groups[0])))


def send_used(peers, group, used, chunks):
    return tuple(
        shifted(chunk, "fsdp", s, peers) if used >> i & 1 else chunk for i, (s, chunk) in enumerate(zip(group, chunks))
    )


def move(z, chunks, used, by_shift, compiler_params):
    if not by_shift:
        got = lax.all_to_all(jnp.concatenate(chunks, axis=0), "fsdp", split_axis=0, concat_axis=0, tiled=True)
        return [got[s * z.lines : (s + 1) * z.lines] for s in range(z.peers)]
    got = list(chunks)
    always = always_sent(z.peers)
    for s in always[:-1]:
        got[s] = shifted(chunks[s], "fsdp", s, z.peers)
    used, _ = lax.optimization_barrier((used, chunks[0]))
    used = agree(used, 2, z.peers, chunks[0], compiler_params)
    last = always[-1]
    value, _ = lax.optimization_barrier((chunks[last], used))
    got[last] = shifted(value, "fsdp", last, z.peers)
    used = agree(used, 4, z.peers, chunks[0], compiler_params)
    chosen = choose_branches(used, z.peers, compiler_params)
    barred = lax.optimization_barrier((*chosen, *[got[s] for s in always]))
    chosen = barred[: len(chosen)]
    for s, value in zip(always, barred[len(chosen) :]):
        got[s] = value
    for group, number in zip(shift_groups(z.peers), chosen):
        branches = [
            lambda *values, group=group, used=used: send_used(z.peers, group, used, values)
            for used in leaves_of(len(group))
        ]
        for s, value in zip(group, lax.switch(number[0], branches, *[chunks[s] for s in group])):
            got[s] = value
    return got


def shards(master, moment_one, moment_two, gradients, new_row):
    rows, width = master.shape
    peers, copies = lax.axis_size("fsdp"), lax.axis_size("replica")
    z = Sizes(rows, width, peers, copies)
    compiler_params = pltpu.CompilerParams(vmem_limit_bytes=VMEM_BYTES)
    smem = pl.BlockSpec(memory_space=pltpu.SMEM)
    vmem = pl.BlockSpec(memory_space=pltpu.VMEM)
    hbm = pl.BlockSpec(memory_space=pl.ANY)
    dma = pltpu.SemaphoreType.DMA

    replica = lax.axis_index("replica").astype(jnp.int32)
    rep = replica.reshape(1)
    by_shift = peers == SHIFT_PEERS
    origin = (lax.axis_index("fsdp").astype(jnp.int32) if by_shift else jnp.int32(0)).reshape(1)
    state_in = [pltpu.with_memory_space_constraint(x, pltpu.HBM) for x in (master, moment_one, moment_two)]
    full = pltpu.with_memory_space_constraint(gradients[0], pltpu.HBM)

    part = jax.ShapeDtypeStruct((rows, width), BF16)
    pick, info, used, *parts = pl.pallas_call(
        functools.partial(prepare_kernel, z),
        out_shape=[
            jax.ShapeDtypeStruct((z.split, z.slots, rows), BF16),
            jax.ShapeDtypeStruct((rows, LANES), F32),
            jax.ShapeDtypeStruct((1, LANES), jnp.int32),
        ]
        + [part] * (copies - 1),
        in_specs=[smem, smem, hbm, hbm],
        out_specs=[vmem] * (copies + 2),
        scratch_shapes=[
            pltpu.VMEM((copies - 1, rows, width), F32),
            pltpu.VMEM((1, rows), jnp.int32),
            dma((copies - 1, z.blocks)),
            dma,
        ],
        compiler_params=compiler_params,
        cost_estimate=pl.CostEstimate(flops=1 << 30, bytes_accessed=1, transcendentals=0),
        name="prepare",
    )(rep, origin, pltpu.with_memory_space_constraint(new_row.reshape(1, rows), pltpu.HBM), full)
    received = [shifted(value, "replica", k + 1, copies) for k, value in enumerate(parts)]

    loaded = jax.ShapeDtypeStruct((rows, width), F32)
    *state, meta = pl.pallas_call(
        functools.partial(load_kernel, z),
        out_shape=[loaded, loaded, loaded, loaded, jax.ShapeDtypeStruct((rows, LANES), BF16)],
        in_specs=[smem, vmem, hbm, hbm, hbm, hbm],
        out_specs=[vmem] * 5,
        scratch_shapes=[dma((4, z.blocks))],
        compiler_params=compiler_params,
        cost_estimate=pl.CostEstimate(flops=1 << 30, bytes_accessed=1, transcendentals=0),
        name="load",
    )(rep, info, *state_in, full)

    if by_shift:
        used = agree(used, 1, peers, meta, compiler_params)
    chunks = pl.pallas_call(
        functools.partial(update_kernel, z),
        out_shape=[jax.ShapeDtypeStruct((z.lines, z.payload), BF16)] * peers,
        in_specs=[vmem] * (5 + copies) + [hbm],
        out_specs=[vmem] * peers,
        scratch_shapes=[pltpu.VMEM((z.stacked, 3 * z.body), BF16)],
        compiler_params=compiler_params,
        cost_estimate=pl.CostEstimate(
            flops=6 * z.slots * z.stacked * z.body, bytes_accessed=24 * rows * width, transcendentals=rows * width
        ),
        name="update",
    )(pick, meta, *state, *received, used)

    got = move(z, chunks, used, by_shift, compiler_params)

    wide = jax.ShapeDtypeStruct((rows, width), F32)
    full_params = jax.ShapeDtypeStruct((rows, width * copies), BF16)
    half, place = pl.pallas_call(
        functools.partial(half_kernel, z),
        out_shape=(
            jax.ShapeDtypeStruct((rows, width + LANES), BF16),
            jax.ShapeDtypeStruct((z.stacked, z.slots), BF16),
        ),
        in_specs=[vmem] * peers,
        out_specs=(vmem, vmem),
        compiler_params=compiler_params,
        name="place_half",
    )(*got)
    others = [shifted(half, "replica", k, copies) for k in range(1, copies)]

    new_master, params, new_one, new_two = pl.pallas_call(
        functools.partial(rows_kernel, z),
        out_shape=(wide, full_params, wide, wide),
        in_specs=[smem] + [vmem] * (peers + 2),
        out_specs=(hbm, hbm, hbm, hbm),
        scratch_shapes=[pltpu.VMEM((rows, width), F32)] * 3 + [dma((4, z.blocks))],
        compiler_params=compiler_params,
        cost_estimate=pl.CostEstimate(
            flops=4 * z.slots * z.stacked * z.body, bytes_accessed=18 * rows * width, transcendentals=0
        ),
        name="place_rows",
    )(rep, half, place, *got)

    params, checksum = pl.pallas_call(
        functools.partial(finish_kernel, z),
        out_shape=(full_params, jax.ShapeDtypeStruct((1, rows), F32)),
        in_specs=[smem] + [vmem] * copies + [hbm],
        out_specs=(hbm, vmem),
        scratch_shapes=[dma((max(1, copies - 1),))],
        input_output_aliases={copies + 1: 0},
        compiler_params=compiler_params,
        cost_estimate=pl.CostEstimate(flops=0, bytes_accessed=4 * rows * width, transcendentals=0),
        name="finish",
    )(rep, half, *others, params)
    return (new_master, new_one, new_two, params, checksum.reshape(rows))


def solution(mesh):
    return jax.shard_map(
        shards,
        mesh=mesh,
        in_specs=(
            P("fsdp", "replica"),
            P("fsdp", "replica"),
            P("fsdp", "replica"),
            P("replica", "fsdp", None),
            P("fsdp"),
        ),
        out_specs=(
            P("fsdp", "replica"),
            P("fsdp", "replica"),
            P("fsdp", "replica"),
            P("fsdp", None),
            P("fsdp"),
        ),
        check_vma=False,
    )
```

```python
import functools
import math

import jax
import jax.numpy as jnp
from jax import lax
from jax.experimental import pallas as pl
from jax.experimental.pallas import tpu as pltpu
from jax.sharding import PartitionSpec as P

LANES = 128
TILE_ROWS = 16
MIB = 1024 * 1024
VMEM_BYTES = 24 * MIB
SHIFT_PEERS = 16
GROUP = 5
F32 = jnp.float32
BF16 = jnp.bfloat16


def iota(shape, axis):
    return lax.broadcasted_iota(jnp.int32, shape, axis)


class Sizes:
    def __init__(self, rows, width, peers, copies):
        self.rows, self.width, self.peers, self.copies = rows, width, peers, copies
        self.cap = max(2, 2 * rows // peers)
        self.split = max(1, TILE_ROWS // self.cap)
        self.lines = self.cap * self.split
        self.slots = peers * self.lines
        self.stacked = self.split * rows
        self.body = width // self.split
        self.cb = math.gcd(self.body, 512)
        self.blocks = self.body // self.cb
        self.span = self.split * self.cb
        self.sub = math.gcd(self.cb, 256)
        self.payload = 3 * self.body + LANES


def prepare_kernel(z, rep_ref, origin_ref, new_row_hbm, full_hbm, pick_ref, info_ref, mask_ref, *refs):
    parts, (full_buf, line_buf, sems, line_sem) = refs[: z.copies - 1], refs[z.copies - 1 :]
    step = z.width // z.blocks
    line_copy = pltpu.make_async_copy(new_row_hbm, line_buf, line_sem)
    line_copy.start()
    copies = []
    for k in range(1, z.copies):
        other = lax.rem(rep_ref[0] + k, z.copies)
        for j in range(z.blocks):
            there = pl.ds(pl.multiple_of(other * z.width + j * step, LANES), step)
            copies.append(
                pltpu.make_async_copy(
                    full_hbm.at[:, there], full_buf.at[k - 1, :, pl.ds(j * step, step)], sems.at[k - 1, j]
                )
            )
            copies[-1].start()
    line_copy.wait()
    line = line_buf[...]
    at_row, at_lane = iota((z.rows, z.rows), 0), iota((z.rows, z.rows), 1)
    column = jnp.sum(jnp.where(at_row == at_lane, line.astype(F32), 0.0), axis=1, keepdims=True).astype(jnp.int32)
    target, target_column = line // z.rows, column // z.rows
    earlier = (target_column == target) & (at_row < at_lane)
    rank = jnp.sum(jnp.where(earlier, 1.0, 0.0), axis=0, keepdims=True).astype(jnp.int32)
    shift = lax.rem(target - origin_ref[0] + z.peers, z.peers)
    shift_column = lax.rem(target_column - origin_ref[0] + z.peers, z.peers)
    for h in range(z.split):
        slot = shift * z.lines + h * z.cap + rank
        pick_ref[h] = jnp.where(iota((z.slots, z.rows), 0) == slot, 1.0, 0.0).astype(BF16)
    lane = iota((z.rows, LANES), 1)
    info_ref[...] = jnp.where(lane == 0, (column - target_column * z.rows + 1).astype(F32), 0.0)
    used = jnp.where(lane == shift_column, 1.0, 0.0)
    mask_ref[...] = jnp.max(used, axis=0, keepdims=True).astype(jnp.int32)
    for k in range(1, z.copies):
        for j in range(z.blocks):
            copies[(k - 1) * z.blocks + j].wait()
            at = slice(j * step, (j + 1) * step)
            parts[k - 1][:, at] = full_buf[k - 1, :, at].astype(BF16)


def agree_kernel(left, right, _, out):
    out[...] = jnp.maximum(left[...], right[...])


def choose_kernel(digits, left, right, *outs):
    total = jnp.maximum(left[...], right[...])
    lane = iota(total.shape, 1)
    for digit, out in zip(digits, outs):
        value = jnp.zeros(total.shape, jnp.int32)
        for i, s in enumerate(digit):
            value = value + jnp.where(lane == s, total << i, 0)
        out[0] = jnp.sum(value.astype(F32)).astype(jnp.int32)


def load_kernel(z, rep_ref, info_ref, master_hbm, one_hbm, two_hbm, full_hbm, master, one, two, own, meta_ref, sems):
    base = rep_ref[0] * z.width
    step = z.width // z.blocks
    copies = []
    for j in range(z.blocks):
        at = pl.ds(j * step, step)
        mine = pl.ds(pl.multiple_of(base + j * step, LANES), step)
        copies.append(
            [
                pltpu.make_async_copy(master_hbm.at[:, at], master.at[:, at], sems.at[0, j]),
                pltpu.make_async_copy(one_hbm.at[:, at], one.at[:, at], sems.at[1, j]),
                pltpu.make_async_copy(two_hbm.at[:, at], two.at[:, at], sems.at[2, j]),
                pltpu.make_async_copy(full_hbm.at[:, mine], own.at[:, at], sems.at[3, j]),
            ]
        )
    for i in range(4):
        for j in range(z.blocks):
            copies[j][i].start()
    part = jnp.zeros((z.rows, LANES), F32)
    for j in range(z.blocks):
        copies[j][0].wait()
        for at in range(j * step, (j + 1) * step, LANES):
            weights = 1.0 + ((iota((1, LANES), 1) + (base + at)) % 7).astype(F32) / 7.0
            part = part + master[:, at : at + LANES] * weights
    total = jnp.sum(part, axis=1, keepdims=True) * (1.0 / math.sqrt(z.width * z.copies))
    high = total.astype(BF16).astype(F32)
    middle = (total - high).astype(BF16).astype(F32)
    low = total - high - middle
    lane = iota((z.rows, LANES), 1)
    meta = jnp.where(lane == 1, high, jnp.where(lane == 2, middle, jnp.where(lane == 3, low, info_ref[...])))
    meta_ref[...] = meta.astype(BF16)
    for j in range(z.blocks):
        for i in range(1, 4):
            copies[j][i].wait()


def update_kernel(z, pick_ref, meta_ref, master, one, two, own, *refs):
    received, refs = refs[: z.copies - 1], refs[z.copies :]
    outs, rows_buf = refs[: z.peers], refs[z.peers]
    pick = jnp.concatenate([pick_ref[h] for h in range(z.split)], axis=1)
    for j in range(z.blocks):
        for h in range(z.split):
            for c in range(0, z.cb, z.sub):
                at = j * z.span + h * z.cb + c
                cols = slice(at, at + z.sub)
                summed = own[:, cols]
                for other in received:
                    summed = summed + other[:, cols].astype(F32)
                moved = master[:, cols]
                new_one = 0.9 * one[:, cols] + 0.1 * summed
                new_two = 0.95 * two[:, cols] + 0.05 * summed * summed
                update = new_one * (1.0 / (1.0 - 0.9**10)) / (jnp.sqrt(new_two * (1.0 / (1.0 - 0.95**10))) + 1e-08)
                new_master = moved - 0.05 * (update + 0.1 * moved)
                for i, value in enumerate((new_master, new_one, new_two)):
                    to = i * z.body + j * z.cb + c
                    rows_buf[h * z.rows : (h + 1) * z.rows, to : to + z.sub] = value.astype(BF16)
        for i in range(3):
            at = i * z.body + j * z.cb
            packed = jnp.dot(pick, rows_buf[:, at : at + z.cb], preferred_element_type=F32).astype(BF16)
            for s, out in enumerate(outs):
                out[:, at : at + z.cb] = packed[s * z.lines : (s + 1) * z.lines]
    meta = jnp.concatenate([meta_ref[...]] * z.split, axis=0)
    packed = jnp.dot(pick, meta, preferred_element_type=F32).astype(BF16)
    for s, out in enumerate(outs):
        out[:, 3 * z.body :] = packed[s * z.lines : (s + 1) * z.lines]


def gathered(refs, cols):
    return jnp.concatenate([ref[:, cols] for ref in refs], axis=0)


def placing(z, meta):
    offset = meta[:, :1].astype(F32).astype(jnp.int32)
    piece = lax.rem(iota((z.slots, 1), 0), z.lines) // z.cap
    wanted = jnp.where(offset > 0, offset - 1 + piece * z.rows, -1)
    return jnp.where(iota((z.slots, z.stacked), 1) == wanted, 1.0, 0.0).T.astype(BF16)


def placed(place, values):
    return jnp.dot(place, values, preferred_element_type=F32)


def half_kernel(z, *refs):
    got, (half, place_out) = refs[: z.peers], refs[z.peers :]
    meta = gathered(got, slice(3 * z.body, 3 * z.body + LANES))
    place = placing(z, meta)
    place_out[...] = place
    for j in range(z.blocks):
        rows_out = placed(place, gathered(got, slice(j * z.cb, (j + 1) * z.cb))).astype(BF16)
        for h in range(z.split):
            at = j * z.span + h * z.cb
            half[:, at : at + z.cb] = rows_out[h * z.rows : (h + 1) * z.rows]
    half[:, z.width :] = placed(place, meta)[: z.rows].astype(BF16)


def place_moment(z, i, place, got, out, buf, sems):
    copies = []
    for j in range(z.blocks):
        at = i * z.body + j * z.cb
        rows_out = placed(place, gathered(got, slice(at, at + z.cb)))
        for h in range(z.split):
            col = j * z.span + h * z.cb
            buf[:, col : col + z.cb] = rows_out[h * z.rows : (h + 1) * z.rows]
        cols = pl.ds(j * z.span, z.span)
        copies.append(pltpu.make_async_copy(buf.at[:, cols], out.at[:, cols], sems.at[j]))
        copies[-1].start()
    return copies


def rows_kernel(z, rep_ref, half, place, *refs):
    got, (new_master, params, one_out, two_out, master_buf, one_buf, two_buf, sems) = refs[: z.peers], refs[z.peers :]
    there = pl.ds(pl.multiple_of(rep_ref[0] * z.width, LANES), z.width)
    copies = [pltpu.make_async_copy(half.at[:, : z.width], params.at[:, there], sems.at[0, 0])]
    copies[0].start()
    for j in range(z.blocks):
        at = slice(j * z.span, (j + 1) * z.span)
        master_buf[:, at] = half[:, at].astype(F32)
        cols = pl.ds(j * z.span, z.span)
        copies.append(pltpu.make_async_copy(master_buf.at[:, cols], new_master.at[:, cols], sems.at[1, j]))
        copies[-1].start()
    copies += place_moment(z, 1, place[...], got, one_out, one_buf, sems.at[2])
    copies += place_moment(z, 2, place[...], got, two_out, two_buf, sems.at[3])
    for copy in copies:
        copy.wait()


def finish_kernel(z, rep_ref, half, *refs):
    others, (_, params, checksum, sems) = refs[: z.copies - 1], refs[z.copies - 1 :]
    copies = []
    for k, other in enumerate(others):
        replica = lax.rem(rep_ref[0] + z.copies - (k + 1), z.copies)
        there = pl.ds(pl.multiple_of(replica * z.width, LANES), z.width)
        copies.append(pltpu.make_async_copy(other.at[:, : z.width], params.at[:, there], sems.at[k]))
        copies[-1].start()
    sums = half[:, z.width :].astype(F32)
    for other in others:
        sums = sums + other[:, z.width :].astype(F32)
    lane = iota((z.rows, LANES), 1)
    column = jnp.sum(jnp.where((lane >= 1) & (lane <= 3), sums, 0.0), axis=1, keepdims=True)
    diagonal = iota((z.rows, z.rows), 0) == iota((z.rows, z.rows), 1)
    checksum[...] = jnp.sum(jnp.where(diagonal, column, 0.0), axis=0, keepdims=True)
    for copy in copies:
        copy.wait()


def shifted(value, axis, k, count):
    return lax.ppermute(value, axis, [(i, (i + k) % count) for i in range(count)])


def always_sent(peers):
    return [peers // 4 - 1, peers // 2, peers - 1]


def shift_groups(peers):
    always, half = always_sent(peers), peers // 2
    rest = [s for s in range(1, peers) if s not in always]
    rest = sorted(rest, key=lambda s: ((s + half) % peers in always, s % half, s))
    return [rest[i : i + GROUP] for i in range(0, len(rest), GROUP)]


def agree(used, stride, peers, after, compiler_params):
    vmem = pl.BlockSpec(memory_space=pltpu.VMEM)
    other = lax.ppermute(used, "fsdp", [(i, i ^ stride) for i in range(peers)])
    return pl.pallas_call(
        agree_kernel,
        out_shape=jax.ShapeDtypeStruct((1, LANES), jnp.int32),
        in_specs=[vmem, vmem, pl.BlockSpec(memory_space=pl.ANY)],
        out_specs=vmem,
        compiler_params=compiler_params,
        name="agree",
    )(used, other, after)


def choose_branches(used, peers, compiler_params):
    vmem = pl.BlockSpec(memory_space=pltpu.VMEM)
    smem = pl.BlockSpec(memory_space=pltpu.SMEM)
    groups = shift_groups(peers)
    other = lax.ppermute(used, "fsdp", [(i, i ^ (peers // 2)) for i in range(peers)])
    return pl.pallas_call(
        functools.partial(choose_kernel, groups),
        out_shape=[pltpu.SMEM((1,), jnp.int32)] * len(groups),
        in_specs=[vmem, vmem],
        out_specs=[smem] * len(groups),
        compiler_params=compiler_params,
        name="choose",
    )(used, other)


def send_used(peers, group, used, chunks):
    return tuple(
        shifted(chunk, "fsdp", s, peers) if used >> i & 1 else chunk for i, (s, chunk) in enumerate(zip(group, chunks))
    )


def move(z, chunks, used, by_shift, compiler_params):
    if not by_shift:
        got = lax.all_to_all(jnp.concatenate(chunks, axis=0), "fsdp", split_axis=0, concat_axis=0, tiled=True)
        return [got[s * z.lines : (s + 1) * z.lines] for s in range(z.peers)]
    got = list(chunks)
    always = always_sent(z.peers)
    for s in always:
        got[s] = shifted(chunks[s], "fsdp", s, z.peers)
    for stride in (2, 4):
        used = agree(used, stride, z.peers, chunks[0], compiler_params)
    chosen = choose_branches(used, z.peers, compiler_params)
    barred = lax.optimization_barrier((*chosen, *[got[s] for s in always]))
    chosen = barred[: len(chosen)]
    for s, value in zip(always, barred[len(chosen) :]):
        got[s] = value
    for group, number in zip(shift_groups(z.peers), chosen):
        branches = [
            lambda *values, group=group, used=used: send_used(z.peers, group, used, values)
            for used in range(1 << len(group))
        ]
        for s, value in zip(group, lax.switch(number[0], branches, *[chunks[s] for s in group])):
            got[s] = value
    return got


def shards(master, moment_one, moment_two, gradients, new_row):
    rows, width = master.shape
    peers, copies = lax.axis_size("fsdp"), lax.axis_size("replica")
    z = Sizes(rows, width, peers, copies)
    compiler_params = pltpu.CompilerParams(vmem_limit_bytes=VMEM_BYTES)
    smem = pl.BlockSpec(memory_space=pltpu.SMEM)
    vmem = pl.BlockSpec(memory_space=pltpu.VMEM)
    hbm = pl.BlockSpec(memory_space=pl.ANY)
    dma = pltpu.SemaphoreType.DMA

    replica = lax.axis_index("replica").astype(jnp.int32)
    rep = replica.reshape(1)
    by_shift = peers == SHIFT_PEERS
    origin = (lax.axis_index("fsdp").astype(jnp.int32) if by_shift else jnp.int32(0)).reshape(1)
    state_in = [pltpu.with_memory_space_constraint(x, pltpu.HBM) for x in (master, moment_one, moment_two)]
    full = pltpu.with_memory_space_constraint(gradients[0], pltpu.HBM)

    part = jax.ShapeDtypeStruct((rows, width), BF16)
    pick, info, used, *parts = pl.pallas_call(
        functools.partial(prepare_kernel, z),
        out_shape=[
            jax.ShapeDtypeStruct((z.split, z.slots, rows), BF16),
            jax.ShapeDtypeStruct((rows, LANES), F32),
            jax.ShapeDtypeStruct((1, LANES), jnp.int32),
        ]
        + [part] * (copies - 1),
        in_specs=[smem, smem, hbm, hbm],
        out_specs=[vmem] * (copies + 2),
        scratch_shapes=[
            pltpu.VMEM((copies - 1, rows, width), F32),
            pltpu.VMEM((1, rows), jnp.int32),
            dma((copies - 1, z.blocks)),
            dma,
        ],
        compiler_params=compiler_params,
        cost_estimate=pl.CostEstimate(flops=1 << 30, bytes_accessed=1, transcendentals=0),
        name="prepare",
    )(rep, origin, pltpu.with_memory_space_constraint(new_row.reshape(1, rows), pltpu.HBM), full)
    received = [shifted(value, "replica", k + 1, copies) for k, value in enumerate(parts)]

    loaded = jax.ShapeDtypeStruct((rows, width), F32)
    *state, meta = pl.pallas_call(
        functools.partial(load_kernel, z),
        out_shape=[loaded, loaded, loaded, loaded, jax.ShapeDtypeStruct((rows, LANES), BF16)],
        in_specs=[smem, vmem, hbm, hbm, hbm, hbm],
        out_specs=[vmem] * 5,
        scratch_shapes=[dma((4, z.blocks))],
        compiler_params=compiler_params,
        cost_estimate=pl.CostEstimate(flops=1 << 30, bytes_accessed=1, transcendentals=0),
        name="load",
    )(rep, info, *state_in, full)

    if by_shift:
        used = agree(used, 1, peers, meta, compiler_params)
    chunks = pl.pallas_call(
        functools.partial(update_kernel, z),
        out_shape=[jax.ShapeDtypeStruct((z.lines, z.payload), BF16)] * peers,
        in_specs=[vmem] * (5 + copies) + [hbm],
        out_specs=[vmem] * peers,
        scratch_shapes=[pltpu.VMEM((z.stacked, 3 * z.body), BF16)],
        compiler_params=compiler_params,
        cost_estimate=pl.CostEstimate(
            flops=6 * z.slots * z.stacked * z.body, bytes_accessed=24 * rows * width, transcendentals=rows * width
        ),
        name="update",
    )(pick, meta, *state, *received, used)

    got = move(z, chunks, used, by_shift, compiler_params)

    wide = jax.ShapeDtypeStruct((rows, width), F32)
    full_params = jax.ShapeDtypeStruct((rows, width * copies), BF16)
    half, place = pl.pallas_call(
        functools.partial(half_kernel, z),
        out_shape=(
            jax.ShapeDtypeStruct((rows, width + LANES), BF16),
            jax.ShapeDtypeStruct((z.stacked, z.slots), BF16),
        ),
        in_specs=[vmem] * peers,
        out_specs=(vmem, vmem),
        compiler_params=compiler_params,
        name="place_half",
    )(*got)
    others = [shifted(half, "replica", k, copies) for k in range(1, copies)]

    new_master, params, new_one, new_two = pl.pallas_call(
        functools.partial(rows_kernel, z),
        out_shape=(wide, full_params, wide, wide),
        in_specs=[smem] + [vmem] * (peers + 2),
        out_specs=(hbm, hbm, hbm, hbm),
        scratch_shapes=[pltpu.VMEM((rows, width), F32)] * 3 + [dma((4, z.blocks))],
        compiler_params=compiler_params,
        cost_estimate=pl.CostEstimate(
            flops=4 * z.slots * z.stacked * z.body, bytes_accessed=18 * rows * width, transcendentals=0
        ),
        name="place_rows",
    )(rep, half, place, *got)

    params, checksum = pl.pallas_call(
        functools.partial(finish_kernel, z),
        out_shape=(full_params, jax.ShapeDtypeStruct((1, rows), F32)),
        in_specs=[smem] + [vmem] * copies + [hbm],
        out_specs=(hbm, vmem),
        scratch_shapes=[dma((max(1, copies - 1),))],
        input_output_aliases={copies + 1: 0},
        compiler_params=compiler_params,
        cost_estimate=pl.CostEstimate(flops=0, bytes_accessed=4 * rows * width, transcendentals=0),
        name="finish",
    )(rep, half, *others, params)
    return (new_master, new_one, new_two, params, checksum.reshape(rows))


def solution(mesh):
    return jax.shard_map(
        shards,
        mesh=mesh,
        in_specs=(
            P("fsdp", "replica"),
            P("fsdp", "replica"),
            P("fsdp", "replica"),
            P("replica", "fsdp", None),
            P("fsdp"),
        ),
        out_specs=(
            P("fsdp", "replica"),
            P("fsdp", "replica"),
            P("fsdp", "replica"),
            P("fsdp", None),
            P("fsdp"),
        ),
        check_vma=False,
    )
```

```python
import functools
import math

import jax
import jax.numpy as jnp
from jax import lax
from jax.experimental import pallas as pl
from jax.experimental.pallas import tpu as pltpu
from jax.sharding import PartitionSpec as P

LANES = 128
TILE_ROWS = 16
MIB = 1024 * 1024
VMEM_BYTES = 24 * MIB
SHIFT_PEERS = 16
GROUP = 5
F32 = jnp.float32
BF16 = jnp.bfloat16


def iota(shape, axis):
    return lax.broadcasted_iota(jnp.int32, shape, axis)


class Sizes:
    def __init__(self, rows, width, peers, copies):
        self.rows, self.width, self.peers, self.copies = rows, width, peers, copies
        self.cap = max(2, 2 * rows // peers)
        self.split = max(1, TILE_ROWS // self.cap)
        self.lines = self.cap * self.split
        self.slots = peers * self.lines
        self.stacked = self.split * rows
        self.body = width // self.split
        self.cb = math.gcd(self.body, 512)
        self.blocks = self.body // self.cb
        self.span = self.split * self.cb
        self.sub = math.gcd(self.cb, 256)
        self.payload = 3 * self.body + LANES


def prepare_kernel(z, rep_ref, origin_ref, new_row_hbm, full_hbm, pick_ref, info_ref, mask_ref, *refs):
    parts, (full_buf, line_buf, sems, line_sem) = refs[: z.copies - 1], refs[z.copies - 1 :]
    step = z.width // z.blocks
    line_copy = pltpu.make_async_copy(new_row_hbm, line_buf, line_sem)
    line_copy.start()
    copies = []
    for k in range(1, z.copies):
        other = lax.rem(rep_ref[0] + k, z.copies)
        for j in range(z.blocks):
            there = pl.ds(pl.multiple_of(other * z.width + j * step, LANES), step)
            copies.append(
                pltpu.make_async_copy(
                    full_hbm.at[:, there], full_buf.at[k - 1, :, pl.ds(j * step, step)], sems.at[k - 1, j]
                )
            )
            copies[-1].start()
    line_copy.wait()
    line = line_buf[...]
    at_row, at_lane = iota((z.rows, z.rows), 0), iota((z.rows, z.rows), 1)
    column = jnp.sum(jnp.where(at_row == at_lane, line.astype(F32), 0.0), axis=1, keepdims=True).astype(jnp.int32)
    target, target_column = line // z.rows, column // z.rows
    earlier = (target_column == target) & (at_row < at_lane)
    rank = jnp.sum(jnp.where(earlier, 1.0, 0.0), axis=0, keepdims=True).astype(jnp.int32)
    shift = lax.rem(target - origin_ref[0] + z.peers, z.peers)
    shift_column = lax.rem(target_column - origin_ref[0] + z.peers, z.peers)
    for h in range(z.split):
        slot = shift * z.lines + h * z.cap + rank
        pick_ref[h] = jnp.where(iota((z.slots, z.rows), 0) == slot, 1.0, 0.0).astype(BF16)
    lane = iota((z.rows, LANES), 1)
    info_ref[...] = jnp.where(lane == 0, (column - target_column * z.rows + 1).astype(F32), 0.0)
    used = jnp.where(lane == shift_column, 1.0, 0.0)
    mask_ref[...] = jnp.max(used, axis=0, keepdims=True).astype(jnp.int32)
    for k in range(1, z.copies):
        for j in range(z.blocks):
            copies[(k - 1) * z.blocks + j].wait()
            at = slice(j * step, (j + 1) * step)
            parts[k - 1][:, at] = full_buf[k - 1, :, at].astype(BF16)


def agree_kernel(left, right, _, out):
    out[...] = jnp.maximum(left[...], right[...])


def choose_kernel(groups, *refs):
    masks, outs = refs[: -len(groups)], refs[-len(groups) :]
    total = masks[0][...]
    for mask in masks[1:]:
        total = jnp.maximum(total, mask[...])
    lane = iota(total.shape, 1)
    for group, out in zip(groups, outs):
        value = jnp.zeros(total.shape, jnp.int32)
        for i, s in enumerate(group):
            value = value + jnp.where(lane == s, total << i, 0)
        out[0] = jnp.sum(value.astype(F32)).astype(jnp.int32)


def load_kernel(z, rep_ref, info_ref, master_hbm, one_hbm, two_hbm, full_hbm, master, one, two, own, meta_ref, sems):
    base = rep_ref[0] * z.width
    step = z.width // z.blocks
    copies = []
    for j in range(z.blocks):
        at = pl.ds(j * step, step)
        mine = pl.ds(pl.multiple_of(base + j * step, LANES), step)
        copies.append(
            [
                pltpu.make_async_copy(master_hbm.at[:, at], master.at[:, at], sems.at[0, j]),
                pltpu.make_async_copy(one_hbm.at[:, at], one.at[:, at], sems.at[1, j]),
                pltpu.make_async_copy(two_hbm.at[:, at], two.at[:, at], sems.at[2, j]),
                pltpu.make_async_copy(full_hbm.at[:, mine], own.at[:, at], sems.at[3, j]),
            ]
        )
    for i in range(4):
        for j in range(z.blocks):
            copies[j][i].start()
    part = jnp.zeros((z.rows, LANES), F32)
    for j in range(z.blocks):
        copies[j][0].wait()
        for at in range(j * step, (j + 1) * step, LANES):
            weights = 1.0 + ((iota((1, LANES), 1) + (base + at)) % 7).astype(F32) / 7.0
            part = part + master[:, at : at + LANES] * weights
    total = jnp.sum(part, axis=1, keepdims=True) * (1.0 / math.sqrt(z.width * z.copies))
    high = total.astype(BF16).astype(F32)
    middle = (total - high).astype(BF16).astype(F32)
    low = total - high - middle
    lane = iota((z.rows, LANES), 1)
    meta = jnp.where(lane == 1, high, jnp.where(lane == 2, middle, jnp.where(lane == 3, low, info_ref[...])))
    meta_ref[...] = meta.astype(BF16)
    for j in range(z.blocks):
        for i in range(1, 4):
            copies[j][i].wait()


def update_kernel(z, pick_ref, meta_ref, master, one, two, own, *refs):
    received, refs = refs[: z.copies - 1], refs[z.copies :]
    outs, rows_buf = refs[: z.peers], refs[z.peers]
    pick = jnp.concatenate([pick_ref[h] for h in range(z.split)], axis=1)
    for j in range(z.blocks):
        for h in range(z.split):
            for c in range(0, z.cb, z.sub):
                at = j * z.span + h * z.cb + c
                cols = slice(at, at + z.sub)
                summed = own[:, cols]
                for other in received:
                    summed = summed + other[:, cols].astype(F32)
                moved = master[:, cols]
                new_one = 0.9 * one[:, cols] + 0.1 * summed
                new_two = 0.95 * two[:, cols] + 0.05 * summed * summed
                update = new_one * (1.0 / (1.0 - 0.9**10)) / (jnp.sqrt(new_two * (1.0 / (1.0 - 0.95**10))) + 1e-08)
                new_master = moved - 0.05 * (update + 0.1 * moved)
                for i, value in enumerate((new_master, new_one, new_two)):
                    to = i * z.body + j * z.cb + c
                    rows_buf[h * z.rows : (h + 1) * z.rows, to : to + z.sub] = value.astype(BF16)
        for i in range(3):
            at = i * z.body + j * z.cb
            packed = jnp.dot(pick, rows_buf[:, at : at + z.cb], preferred_element_type=F32).astype(BF16)
            for s, out in enumerate(outs):
                out[:, at : at + z.cb] = packed[s * z.lines : (s + 1) * z.lines]
    meta = jnp.concatenate([meta_ref[...]] * z.split, axis=0)
    packed = jnp.dot(pick, meta, preferred_element_type=F32).astype(BF16)
    for s, out in enumerate(outs):
        out[:, 3 * z.body :] = packed[s * z.lines : (s + 1) * z.lines]


def gathered(refs, cols):
    return jnp.concatenate([ref[:, cols] for ref in refs], axis=0)


def placing(z, meta):
    offset = meta[:, :1].astype(F32).astype(jnp.int32)
    piece = lax.rem(iota((z.slots, 1), 0), z.lines) // z.cap
    wanted = jnp.where(offset > 0, offset - 1 + piece * z.rows, -1)
    return jnp.where(iota((z.slots, z.stacked), 1) == wanted, 1.0, 0.0).T.astype(BF16)


def placed(place, values):
    return jnp.dot(place, values, preferred_element_type=F32)


def half_kernel(z, *refs):
    got, (half, place_out) = refs[: z.peers], refs[z.peers :]
    meta = gathered(got, slice(3 * z.body, 3 * z.body + LANES))
    place = placing(z, meta)
    place_out[...] = place
    for j in range(z.blocks):
        rows_out = placed(place, gathered(got, slice(j * z.cb, (j + 1) * z.cb))).astype(BF16)
        for h in range(z.split):
            at = j * z.span + h * z.cb
            half[:, at : at + z.cb] = rows_out[h * z.rows : (h + 1) * z.rows]
    half[:, z.width :] = placed(place, meta)[: z.rows].astype(BF16)


def place_moment(z, i, place, got, out, buf, sems):
    copies = []
    for j in range(z.blocks):
        at = i * z.body + j * z.cb
        rows_out = placed(place, gathered(got, slice(at, at + z.cb)))
        for h in range(z.split):
            col = j * z.span + h * z.cb
            buf[:, col : col + z.cb] = rows_out[h * z.rows : (h + 1) * z.rows]
        cols = pl.ds(j * z.span, z.span)
        copies.append(pltpu.make_async_copy(buf.at[:, cols], out.at[:, cols], sems.at[j]))
        copies[-1].start()
    return copies


def rows_kernel(z, rep_ref, half, place, *refs):
    got, (new_master, params, one_out, two_out, master_buf, one_buf, two_buf, sems) = refs[: z.peers], refs[z.peers :]
    there = pl.ds(pl.multiple_of(rep_ref[0] * z.width, LANES), z.width)
    copies = [pltpu.make_async_copy(half.at[:, : z.width], params.at[:, there], sems.at[0, 0])]
    copies[0].start()
    for j in range(z.blocks):
        at = slice(j * z.span, (j + 1) * z.span)
        master_buf[:, at] = half[:, at].astype(F32)
        cols = pl.ds(j * z.span, z.span)
        copies.append(pltpu.make_async_copy(master_buf.at[:, cols], new_master.at[:, cols], sems.at[1, j]))
        copies[-1].start()
    copies += place_moment(z, 1, place[...], got, one_out, one_buf, sems.at[2])
    copies += place_moment(z, 2, place[...], got, two_out, two_buf, sems.at[3])
    for copy in copies:
        copy.wait()


def finish_kernel(z, rep_ref, half, *refs):
    others, (_, params, checksum, sems) = refs[: z.copies - 1], refs[z.copies - 1 :]
    copies = []
    for k, other in enumerate(others):
        replica = lax.rem(rep_ref[0] + z.copies - (k + 1), z.copies)
        for j in range(z.blocks):
            here = pl.ds(j * z.span, z.span)
            there = pl.ds(pl.multiple_of(replica * z.width + j * z.span, LANES), z.span)
            copies.append(pltpu.make_async_copy(other.at[:, here], params.at[:, there], sems.at[k, j]))
            copies[-1].start()
    sums = half[:, z.width :].astype(F32)
    for other in others:
        sums = sums + other[:, z.width :].astype(F32)
    lane = iota((z.rows, LANES), 1)
    column = jnp.sum(jnp.where((lane >= 1) & (lane <= 3), sums, 0.0), axis=1, keepdims=True)
    diagonal = iota((z.rows, z.rows), 0) == iota((z.rows, z.rows), 1)
    checksum[...] = jnp.sum(jnp.where(diagonal, column, 0.0), axis=0, keepdims=True)
    for copy in copies:
        copy.wait()


def shifted(value, axis, k, count):
    return lax.ppermute(value, axis, [(i, (i + k) % count) for i in range(count)])


def always_sent(peers):
    return [peers // 4 - 1, peers // 2, peers - 1]


def shift_groups(peers):
    always, half = always_sent(peers), peers // 2
    rest = [s for s in range(1, peers) if s not in always]
    rest = sorted(rest, key=lambda s: ((s + half) % peers in always, s % half, s))
    return [rest[i : i + GROUP] for i in range(0, len(rest), GROUP)]


def agree(used, stride, peers, after, compiler_params):
    vmem = pl.BlockSpec(memory_space=pltpu.VMEM)
    other = lax.ppermute(used, "fsdp", [(i, i ^ stride) for i in range(peers)])
    return pl.pallas_call(
        agree_kernel,
        out_shape=jax.ShapeDtypeStruct((1, LANES), jnp.int32),
        in_specs=[vmem, vmem, pl.BlockSpec(memory_space=pl.ANY)],
        out_specs=vmem,
        compiler_params=compiler_params,
        name="agree",
    )(used, other, after)


def choose_branches(used, peers, compiler_params):
    vmem = pl.BlockSpec(memory_space=pltpu.VMEM)
    smem = pl.BlockSpec(memory_space=pltpu.SMEM)
    groups = shift_groups(peers)
    steps = range(peers // 4, peers, peers // 4)
    masks = [used] + [lax.ppermute(used, "fsdp", [(i, i ^ step) for i in range(peers)]) for step in steps]
    return pl.pallas_call(
        functools.partial(choose_kernel, groups),
        out_shape=[pltpu.SMEM((1,), jnp.int32)] * len(groups),
        in_specs=[vmem] * len(masks),
        out_specs=[smem] * len(groups),
        compiler_params=compiler_params,
        name="choose",
    )(*masks)


def send_used(peers, group, used, chunks):
    return tuple(
        shifted(chunk, "fsdp", s, peers) if used >> i & 1 else chunk for i, (s, chunk) in enumerate(zip(group, chunks))
    )


def move(z, chunks, used, by_shift, compiler_params):
    if not by_shift:
        got = lax.all_to_all(jnp.concatenate(chunks, axis=0), "fsdp", split_axis=0, concat_axis=0, tiled=True)
        return [got[s * z.lines : (s + 1) * z.lines] for s in range(z.peers)]
    got = list(chunks)
    always = always_sent(z.peers)
    for s in always:
        got[s] = shifted(chunks[s], "fsdp", s, z.peers)
    used = agree(used, 2, z.peers, chunks[0], compiler_params)
    chosen = choose_branches(used, z.peers, compiler_params)
    barred = lax.optimization_barrier((*chosen, *[got[s] for s in always]))
    chosen = barred[: len(chosen)]
    for s, value in zip(always, barred[len(chosen) :]):
        got[s] = value
    for group, number in zip(shift_groups(z.peers), chosen):
        branches = [
            lambda *values, group=group, used=used: send_used(z.peers, group, used, values)
            for used in range(1 << len(group))
        ]
        for s, value in zip(group, lax.switch(number[0], branches, *[chunks[s] for s in group])):
            got[s] = value
    return got


def shards(master, moment_one, moment_two, gradients, new_row):
    rows, width = master.shape
    peers, copies = lax.axis_size("fsdp"), lax.axis_size("replica")
    z = Sizes(rows, width, peers, copies)
    compiler_params = pltpu.CompilerParams(vmem_limit_bytes=VMEM_BYTES)
    smem = pl.BlockSpec(memory_space=pltpu.SMEM)
    vmem = pl.BlockSpec(memory_space=pltpu.VMEM)
    hbm = pl.BlockSpec(memory_space=pl.ANY)
    dma = pltpu.SemaphoreType.DMA

    replica = lax.axis_index("replica").astype(jnp.int32)
    rep = replica.reshape(1)
    by_shift = peers == SHIFT_PEERS
    origin = (lax.axis_index("fsdp").astype(jnp.int32) if by_shift else jnp.int32(0)).reshape(1)
    state_in = [pltpu.with_memory_space_constraint(x, pltpu.HBM) for x in (master, moment_one, moment_two)]
    full = pltpu.with_memory_space_constraint(gradients[0], pltpu.HBM)

    part = jax.ShapeDtypeStruct((rows, width), BF16)
    pick, info, used, *parts = pl.pallas_call(
        functools.partial(prepare_kernel, z),
        out_shape=[
            jax.ShapeDtypeStruct((z.split, z.slots, rows), BF16),
            jax.ShapeDtypeStruct((rows, LANES), F32),
            jax.ShapeDtypeStruct((1, LANES), jnp.int32),
        ]
        + [part] * (copies - 1),
        in_specs=[smem, smem, hbm, hbm],
        out_specs=[vmem] * (copies + 2),
        scratch_shapes=[
            pltpu.VMEM((copies - 1, rows, width), F32),
            pltpu.VMEM((1, rows), jnp.int32),
            dma((copies - 1, z.blocks)),
            dma,
        ],
        compiler_params=compiler_params,
        cost_estimate=pl.CostEstimate(flops=1 << 30, bytes_accessed=1, transcendentals=0),
        name="prepare",
    )(rep, origin, pltpu.with_memory_space_constraint(new_row.reshape(1, rows), pltpu.HBM), full)
    received = [shifted(value, "replica", k + 1, copies) for k, value in enumerate(parts)]

    loaded = jax.ShapeDtypeStruct((rows, width), F32)
    *state, meta = pl.pallas_call(
        functools.partial(load_kernel, z),
        out_shape=[loaded, loaded, loaded, loaded, jax.ShapeDtypeStruct((rows, LANES), BF16)],
        in_specs=[smem, vmem, hbm, hbm, hbm, hbm],
        out_specs=[vmem] * 5,
        scratch_shapes=[dma((4, z.blocks))],
        compiler_params=compiler_params,
        cost_estimate=pl.CostEstimate(flops=1 << 30, bytes_accessed=1, transcendentals=0),
        name="load",
    )(rep, info, *state_in, full)

    if by_shift:
        used = agree(used, 1, peers, meta, compiler_params)
    chunks = pl.pallas_call(
        functools.partial(update_kernel, z),
        out_shape=[jax.ShapeDtypeStruct((z.lines, z.payload), BF16)] * peers,
        in_specs=[vmem] * (5 + copies) + [hbm],
        out_specs=[vmem] * peers,
        scratch_shapes=[pltpu.VMEM((z.stacked, 3 * z.body), BF16)],
        compiler_params=compiler_params,
        cost_estimate=pl.CostEstimate(
            flops=6 * z.slots * z.stacked * z.body, bytes_accessed=24 * rows * width, transcendentals=rows * width
        ),
        name="update",
    )(pick, meta, *state, *received, used)

    got = move(z, chunks, used, by_shift, compiler_params)

    wide = jax.ShapeDtypeStruct((rows, width), F32)
    full_params = jax.ShapeDtypeStruct((rows, width * copies), BF16)
    half, place = pl.pallas_call(
        functools.partial(half_kernel, z),
        out_shape=(
            jax.ShapeDtypeStruct((rows, width + LANES), BF16),
            jax.ShapeDtypeStruct((z.stacked, z.slots), BF16),
        ),
        in_specs=[vmem] * peers,
        out_specs=(vmem, vmem),
        compiler_params=compiler_params,
        name="place_half",
    )(*got)
    others = [shifted(half, "replica", k, copies) for k in range(1, copies)]

    new_master, params, new_one, new_two = pl.pallas_call(
        functools.partial(rows_kernel, z),
        out_shape=(wide, full_params, wide, wide),
        in_specs=[smem] + [vmem] * (peers + 2),
        out_specs=(hbm, hbm, hbm, hbm),
        scratch_shapes=[pltpu.VMEM((rows, width), F32)] * 3 + [dma((4, z.blocks))],
        compiler_params=compiler_params,
        cost_estimate=pl.CostEstimate(
            flops=4 * z.slots * z.stacked * z.body, bytes_accessed=18 * rows * width, transcendentals=0
        ),
        name="place_rows",
    )(rep, half, place, *got)

    params, checksum = pl.pallas_call(
        functools.partial(finish_kernel, z),
        out_shape=(full_params, jax.ShapeDtypeStruct((1, rows), F32)),
        in_specs=[smem] + [vmem] * copies + [hbm],
        out_specs=(hbm, vmem),
        scratch_shapes=[dma((max(1, copies - 1), z.blocks))],
        input_output_aliases={copies + 1: 0},
        compiler_params=compiler_params,
        cost_estimate=pl.CostEstimate(flops=0, bytes_accessed=4 * rows * width, transcendentals=0),
        name="finish",
    )(rep, half, *others, params)
    return (new_master, new_one, new_two, params, checksum.reshape(rows))


def solution(mesh):
    return jax.shard_map(
        shards,
        mesh=mesh,
        in_specs=(
            P("fsdp", "replica"),
            P("fsdp", "replica"),
            P("fsdp", "replica"),
            P("replica", "fsdp", None),
            P("fsdp"),
        ),
        out_specs=(
            P("fsdp", "replica"),
            P("fsdp", "replica"),
            P("fsdp", "replica"),
            P("fsdp", None),
            P("fsdp"),
        ),
        check_vma=False,
    )
```

```python
import functools
import math

import jax
import jax.numpy as jnp
from jax import lax
from jax.experimental import pallas as pl
from jax.experimental.pallas import tpu as pltpu
from jax.sharding import PartitionSpec as P

LANES = 128
TILE_ROWS = 16
MIB = 1024 * 1024
VMEM_BYTES = 24 * MIB
SHIFT_PEERS = 16
GROUP = 5
F32 = jnp.float32
BF16 = jnp.bfloat16


def iota(shape, axis):
    return lax.broadcasted_iota(jnp.int32, shape, axis)


class Sizes:
    def __init__(self, rows, width, peers, copies):
        self.rows, self.width, self.peers, self.copies = rows, width, peers, copies
        self.cap = max(2, 2 * rows // peers)
        self.split = max(1, TILE_ROWS // self.cap)
        self.lines = self.cap * self.split
        self.slots = peers * self.lines
        self.stacked = self.split * rows
        self.body = width // self.split
        self.cb = math.gcd(self.body, 512)
        self.blocks = self.body // self.cb
        self.span = self.split * self.cb
        self.sub = math.gcd(self.cb, 256)
        self.payload = 3 * self.body + LANES


def prepare_kernel(z, rep_ref, origin_ref, new_row_hbm, full_hbm, pick_ref, info_ref, mask_ref, *refs):
    parts, (full_buf, line_buf, sems, line_sem) = refs[: z.copies - 1], refs[z.copies - 1 :]
    step = z.width // z.blocks
    line_copy = pltpu.make_async_copy(new_row_hbm, line_buf, line_sem)
    line_copy.start()
    copies = []
    for k in range(1, z.copies):
        other = lax.rem(rep_ref[0] + k, z.copies)
        for j in range(z.blocks):
            there = pl.ds(pl.multiple_of(other * z.width + j * step, LANES), step)
            copies.append(
                pltpu.make_async_copy(
                    full_hbm.at[:, there], full_buf.at[k - 1, :, pl.ds(j * step, step)], sems.at[k - 1, j]
                )
            )
            copies[-1].start()
    line_copy.wait()
    line = line_buf[...]
    at_row, at_lane = iota((z.rows, z.rows), 0), iota((z.rows, z.rows), 1)
    column = jnp.sum(jnp.where(at_row == at_lane, line.astype(F32), 0.0), axis=1, keepdims=True).astype(jnp.int32)
    target, target_column = line // z.rows, column // z.rows
    earlier = (target_column == target) & (at_row < at_lane)
    rank = jnp.sum(jnp.where(earlier, 1.0, 0.0), axis=0, keepdims=True).astype(jnp.int32)
    shift = lax.rem(target - origin_ref[0] + z.peers, z.peers)
    shift_column = lax.rem(target_column - origin_ref[0] + z.peers, z.peers)
    for h in range(z.split):
        slot = shift * z.lines + h * z.cap + rank
        pick_ref[h] = jnp.where(iota((z.slots, z.rows), 0) == slot, 1.0, 0.0).astype(BF16)
    lane = iota((z.rows, LANES), 1)
    info_ref[...] = jnp.where(lane == 0, (column - target_column * z.rows + 1).astype(F32), 0.0)
    used = jnp.where(lane == shift_column, 1.0, 0.0)
    mask_ref[...] = jnp.max(used, axis=0, keepdims=True).astype(jnp.int32)
    for k in range(1, z.copies):
        for j in range(z.blocks):
            copies[(k - 1) * z.blocks + j].wait()
            at = slice(j * step, (j + 1) * step)
            parts[k - 1][:, at] = full_buf[k - 1, :, at].astype(BF16)


def agree_kernel(left, right, _, out):
    out[...] = jnp.maximum(left[...], right[...])


def choose_kernel(digits, left, right, *outs):
    total = jnp.maximum(left[...], right[...])
    lane = iota(total.shape, 1)
    for digit, out in zip(digits, outs):
        value = jnp.zeros(total.shape, jnp.int32)
        for i, s in enumerate(digit):
            value = value + jnp.where(lane == s, total << i, 0)
        out[0] = jnp.sum(value.astype(F32)).astype(jnp.int32)


def load_kernel(z, rep_ref, info_ref, master_hbm, one_hbm, two_hbm, full_hbm, master, one, two, own, meta_ref, sems):
    base = rep_ref[0] * z.width
    step = z.width // z.blocks
    copies = []
    for j in range(z.blocks):
        at = pl.ds(j * step, step)
        mine = pl.ds(pl.multiple_of(base + j * step, LANES), step)
        copies.append(
            [
                pltpu.make_async_copy(master_hbm.at[:, at], master.at[:, at], sems.at[0, j]),
                pltpu.make_async_copy(one_hbm.at[:, at], one.at[:, at], sems.at[1, j]),
                pltpu.make_async_copy(two_hbm.at[:, at], two.at[:, at], sems.at[2, j]),
                pltpu.make_async_copy(full_hbm.at[:, mine], own.at[:, at], sems.at[3, j]),
            ]
        )
    for i in range(4):
        for j in range(z.blocks):
            copies[j][i].start()
    part = jnp.zeros((z.rows, LANES), F32)
    for j in range(z.blocks):
        copies[j][0].wait()
        for at in range(j * step, (j + 1) * step, LANES):
            weights = 1.0 + ((iota((1, LANES), 1) + (base + at)) % 7).astype(F32) / 7.0
            part = part + master[:, at : at + LANES] * weights
    total = jnp.sum(part, axis=1, keepdims=True) * (1.0 / math.sqrt(z.width * z.copies))
    high = total.astype(BF16).astype(F32)
    middle = (total - high).astype(BF16).astype(F32)
    low = total - high - middle
    lane = iota((z.rows, LANES), 1)
    meta = jnp.where(lane == 1, high, jnp.where(lane == 2, middle, jnp.where(lane == 3, low, info_ref[...])))
    meta_ref[...] = meta.astype(BF16)
    for j in range(z.blocks):
        for i in range(1, 4):
            copies[j][i].wait()


def update_kernel(z, pick_ref, meta_ref, master, one, two, own, *refs):
    received, refs = refs[: z.copies - 1], refs[z.copies :]
    outs, rows_buf = refs[: z.peers], refs[z.peers]
    pick = jnp.concatenate([pick_ref[h] for h in range(z.split)], axis=1)
    for j in range(z.blocks):
        for h in range(z.split):
            for c in range(0, z.cb, z.sub):
                at = j * z.span + h * z.cb + c
                cols = slice(at, at + z.sub)
                summed = own[:, cols]
                for other in received:
                    summed = summed + other[:, cols].astype(F32)
                moved = master[:, cols]
                new_one = 0.9 * one[:, cols] + 0.1 * summed
                new_two = 0.95 * two[:, cols] + 0.05 * summed * summed
                update = new_one * (1.0 / (1.0 - 0.9**10)) / (jnp.sqrt(new_two * (1.0 / (1.0 - 0.95**10))) + 1e-08)
                new_master = moved - 0.05 * (update + 0.1 * moved)
                for i, value in enumerate((new_master, new_one, new_two)):
                    to = i * z.body + j * z.cb + c
                    rows_buf[h * z.rows : (h + 1) * z.rows, to : to + z.sub] = value.astype(BF16)
        for i in range(3):
            at = i * z.body + j * z.cb
            packed = jnp.dot(pick, rows_buf[:, at : at + z.cb], preferred_element_type=F32).astype(BF16)
            for s, out in enumerate(outs):
                out[:, at : at + z.cb] = packed[s * z.lines : (s + 1) * z.lines]
    meta = jnp.concatenate([meta_ref[...]] * z.split, axis=0)
    packed = jnp.dot(pick, meta, preferred_element_type=F32).astype(BF16)
    for s, out in enumerate(outs):
        out[:, 3 * z.body :] = packed[s * z.lines : (s + 1) * z.lines]


def gathered(refs, cols):
    return jnp.concatenate([ref[:, cols] for ref in refs], axis=0)


def placing(z, meta):
    offset = meta[:, :1].astype(F32).astype(jnp.int32)
    piece = lax.rem(iota((z.slots, 1), 0), z.lines) // z.cap
    wanted = jnp.where(offset > 0, offset - 1 + piece * z.rows, -1)
    return jnp.where(iota((z.slots, z.stacked), 1) == wanted, 1.0, 0.0).T.astype(BF16)


def placed(place, values):
    return jnp.dot(place, values, preferred_element_type=F32)


def half_kernel(z, *refs):
    got, (half, place_out) = refs[: z.peers], refs[z.peers :]
    meta = gathered(got, slice(3 * z.body, 3 * z.body + LANES))
    place = placing(z, meta)
    place_out[...] = place
    for j in range(z.blocks):
        rows_out = placed(place, gathered(got, slice(j * z.cb, (j + 1) * z.cb))).astype(BF16)
        for h in range(z.split):
            at = j * z.span + h * z.cb
            half[:, at : at + z.cb] = rows_out[h * z.rows : (h + 1) * z.rows]
    half[:, z.width :] = placed(place, meta)[: z.rows].astype(BF16)


def place_moment(z, i, place, got, out, buf, sems):
    copies = []
    for j in range(z.blocks):
        at = i * z.body + j * z.cb
        rows_out = placed(place, gathered(got, slice(at, at + z.cb)))
        for h in range(z.split):
            col = j * z.span + h * z.cb
            buf[:, col : col + z.cb] = rows_out[h * z.rows : (h + 1) * z.rows]
        cols = pl.ds(j * z.span, z.span)
        copies.append(pltpu.make_async_copy(buf.at[:, cols], out.at[:, cols], sems.at[j]))
        copies[-1].start()
    return copies


def rows_kernel(z, rep_ref, half, place, *refs):
    got, (new_master, params, one_out, two_out, master_buf, one_buf, two_buf, sems) = refs[: z.peers], refs[z.peers :]
    there = pl.ds(pl.multiple_of(rep_ref[0] * z.width, LANES), z.width)
    copies = [pltpu.make_async_copy(half.at[:, : z.width], params.at[:, there], sems.at[0, 0])]
    copies[0].start()
    for j in range(z.blocks):
        at = slice(j * z.span, (j + 1) * z.span)
        master_buf[:, at] = half[:, at].astype(F32)
        cols = pl.ds(j * z.span, z.span)
        copies.append(pltpu.make_async_copy(master_buf.at[:, cols], new_master.at[:, cols], sems.at[1, j]))
        copies[-1].start()
    copies += place_moment(z, 1, place[...], got, one_out, one_buf, sems.at[2])
    copies += place_moment(z, 2, place[...], got, two_out, two_buf, sems.at[3])
    for copy in copies:
        copy.wait()


def finish_kernel(z, rep_ref, half, *refs):
    others, (_, params, checksum, sems) = refs[: z.copies - 1], refs[z.copies - 1 :]
    copies = []
    for k, other in enumerate(others):
        replica = lax.rem(rep_ref[0] + z.copies - (k + 1), z.copies)
        there = pl.ds(pl.multiple_of(replica * z.width, LANES), z.width)
        copies.append(pltpu.make_async_copy(other.at[:, : z.width], params.at[:, there], sems.at[k]))
        copies[-1].start()
    sums = half[:, z.width :].astype(F32)
    for other in others:
        sums = sums + other[:, z.width :].astype(F32)
    lane = iota((z.rows, LANES), 1)
    column = jnp.sum(jnp.where((lane >= 1) & (lane <= 3), sums, 0.0), axis=1, keepdims=True)
    diagonal = iota((z.rows, z.rows), 0) == iota((z.rows, z.rows), 1)
    checksum[...] = jnp.sum(jnp.where(diagonal, column, 0.0), axis=0, keepdims=True)
    for copy in copies:
        copy.wait()


def shifted(value, axis, k, count):
    return lax.ppermute(value, axis, [(i, (i + k) % count) for i in range(count)])


def always_sent(peers):
    return [peers // 2, peers // 4 - 1, peers - 1]


def shift_groups(peers):
    always, half = always_sent(peers), peers // 2
    rest = [s for s in range(1, peers) if s not in always]
    rest = sorted(rest, key=lambda s: ((s + half) % peers in always, s % half, s))
    return [rest[i : i + GROUP] for i in range(0, len(rest), GROUP)]


def agree(used, stride, peers, after, compiler_params):
    vmem = pl.BlockSpec(memory_space=pltpu.VMEM)
    other = lax.ppermute(used, "fsdp", [(i, i ^ stride) for i in range(peers)])
    return pl.pallas_call(
        agree_kernel,
        out_shape=jax.ShapeDtypeStruct((1, LANES), jnp.int32),
        in_specs=[vmem, vmem, pl.BlockSpec(memory_space=pl.ANY)],
        out_specs=vmem,
        compiler_params=compiler_params,
        name="agree",
    )(used, other, after)


def choose_branches(used, peers, compiler_params):
    vmem = pl.BlockSpec(memory_space=pltpu.VMEM)
    smem = pl.BlockSpec(memory_space=pltpu.SMEM)
    groups = shift_groups(peers)
    other = lax.ppermute(used, "fsdp", [(i, i ^ (peers // 2)) for i in range(peers)])
    return pl.pallas_call(
        functools.partial(choose_kernel, groups),
        out_shape=[pltpu.SMEM((1,), jnp.int32)] * len(groups),
        in_specs=[vmem, vmem],
        out_specs=[smem] * len(groups),
        compiler_params=compiler_params,
        name="choose",
    )(used, other)


def send_used(peers, group, used, chunks):
    return tuple(
        shifted(chunk, "fsdp", s, peers) if used >> i & 1 else chunk for i, (s, chunk) in enumerate(zip(group, chunks))
    )


def move(z, chunks, used, by_shift, compiler_params):
    if not by_shift:
        got = lax.all_to_all(jnp.concatenate(chunks, axis=0), "fsdp", split_axis=0, concat_axis=0, tiled=True)
        return [got[s * z.lines : (s + 1) * z.lines] for s in range(z.peers)]
    got = list(chunks)
    always = always_sent(z.peers)
    for s in always:
        got[s] = shifted(chunks[s], "fsdp", s, z.peers)
    for stride in (2, 4):
        used = agree(used, stride, z.peers, chunks[0], compiler_params)
    chosen = choose_branches(used, z.peers, compiler_params)
    barred = lax.optimization_barrier((*chosen, *[got[s] for s in always]))
    chosen = barred[: len(chosen)]
    for s, value in zip(always, barred[len(chosen) :]):
        got[s] = value
    for group, number in zip(shift_groups(z.peers), chosen):
        branches = [
            lambda *values, group=group, used=used: send_used(z.peers, group, used, values)
            for used in range(1 << len(group))
        ]
        for s, value in zip(group, lax.switch(number[0], branches, *[chunks[s] for s in group])):
            got[s] = value
    return got


def shards(master, moment_one, moment_two, gradients, new_row):
    rows, width = master.shape
    peers, copies = lax.axis_size("fsdp"), lax.axis_size("replica")
    z = Sizes(rows, width, peers, copies)
    compiler_params = pltpu.CompilerParams(vmem_limit_bytes=VMEM_BYTES)
    smem = pl.BlockSpec(memory_space=pltpu.SMEM)
    vmem = pl.BlockSpec(memory_space=pltpu.VMEM)
    hbm = pl.BlockSpec(memory_space=pl.ANY)
    dma = pltpu.SemaphoreType.DMA

    replica = lax.axis_index("replica").astype(jnp.int32)
    rep = replica.reshape(1)
    by_shift = peers == SHIFT_PEERS
    origin = (lax.axis_index("fsdp").astype(jnp.int32) if by_shift else jnp.int32(0)).reshape(1)
    state_in = [pltpu.with_memory_space_constraint(x, pltpu.HBM) for x in (master, moment_one, moment_two)]
    full = pltpu.with_memory_space_constraint(gradients[0], pltpu.HBM)

    part = jax.ShapeDtypeStruct((rows, width), BF16)
    pick, info, used, *parts = pl.pallas_call(
        functools.partial(prepare_kernel, z),
        out_shape=[
            jax.ShapeDtypeStruct((z.split, z.slots, rows), BF16),
            jax.ShapeDtypeStruct((rows, LANES), F32),
            jax.ShapeDtypeStruct((1, LANES), jnp.int32),
        ]
        + [part] * (copies - 1),
        in_specs=[smem, smem, hbm, hbm],
        out_specs=[vmem] * (copies + 2),
        scratch_shapes=[
            pltpu.VMEM((copies - 1, rows, width), F32),
            pltpu.VMEM((1, rows), jnp.int32),
            dma((copies - 1, z.blocks)),
            dma,
        ],
        compiler_params=compiler_params,
        cost_estimate=pl.CostEstimate(flops=1 << 30, bytes_accessed=1, transcendentals=0),
        name="prepare",
    )(rep, origin, pltpu.with_memory_space_constraint(new_row.reshape(1, rows), pltpu.HBM), full)
    received = [shifted(value, "replica", k + 1, copies) for k, value in enumerate(parts)]

    loaded = jax.ShapeDtypeStruct((rows, width), F32)
    *state, meta = pl.pallas_call(
        functools.partial(load_kernel, z),
        out_shape=[loaded, loaded, loaded, loaded, jax.ShapeDtypeStruct((rows, LANES), BF16)],
        in_specs=[smem, vmem, hbm, hbm, hbm, hbm],
        out_specs=[vmem] * 5,
        scratch_shapes=[dma((4, z.blocks))],
        compiler_params=compiler_params,
        cost_estimate=pl.CostEstimate(flops=1 << 30, bytes_accessed=1, transcendentals=0),
        name="load",
    )(rep, info, *state_in, full)

    if by_shift:
        used = agree(used, 1, peers, meta, compiler_params)
    chunks = pl.pallas_call(
        functools.partial(update_kernel, z),
        out_shape=[jax.ShapeDtypeStruct((z.lines, z.payload), BF16)] * peers,
        in_specs=[vmem] * (5 + copies) + [hbm],
        out_specs=[vmem] * peers,
        scratch_shapes=[pltpu.VMEM((z.stacked, 3 * z.body), BF16)],
        compiler_params=compiler_params,
        cost_estimate=pl.CostEstimate(
            flops=6 * z.slots * z.stacked * z.body, bytes_accessed=24 * rows * width, transcendentals=rows * width
        ),
        name="update",
    )(pick, meta, *state, *received, used)

    got = move(z, chunks, used, by_shift, compiler_params)

    wide = jax.ShapeDtypeStruct((rows, width), F32)
    full_params = jax.ShapeDtypeStruct((rows, width * copies), BF16)
    half, place = pl.pallas_call(
        functools.partial(half_kernel, z),
        out_shape=(
            jax.ShapeDtypeStruct((rows, width + LANES), BF16),
            jax.ShapeDtypeStruct((z.stacked, z.slots), BF16),
        ),
        in_specs=[vmem] * peers,
        out_specs=(vmem, vmem),
        compiler_params=compiler_params,
        name="place_half",
    )(*got)
    others = [shifted(half, "replica", k, copies) for k in range(1, copies)]

    new_master, params, new_one, new_two = pl.pallas_call(
        functools.partial(rows_kernel, z),
        out_shape=(wide, full_params, wide, wide),
        in_specs=[smem] + [vmem] * (peers + 2),
        out_specs=(hbm, hbm, hbm, hbm),
        scratch_shapes=[pltpu.VMEM((rows, width), F32)] * 3 + [dma((4, z.blocks))],
        compiler_params=compiler_params,
        cost_estimate=pl.CostEstimate(
            flops=4 * z.slots * z.stacked * z.body, bytes_accessed=18 * rows * width, transcendentals=0
        ),
        name="place_rows",
    )(rep, half, place, *got)

    params, checksum = pl.pallas_call(
        functools.partial(finish_kernel, z),
        out_shape=(full_params, jax.ShapeDtypeStruct((1, rows), F32)),
        in_specs=[smem] + [vmem] * copies + [hbm],
        out_specs=(hbm, vmem),
        scratch_shapes=[dma((max(1, copies - 1),))],
        input_output_aliases={copies + 1: 0},
        compiler_params=compiler_params,
        cost_estimate=pl.CostEstimate(flops=0, bytes_accessed=4 * rows * width, transcendentals=0),
        name="finish",
    )(rep, half, *others, params)
    return (new_master, new_one, new_two, params, checksum.reshape(rows))


def solution(mesh):
    return jax.shard_map(
        shards,
        mesh=mesh,
        in_specs=(
            P("fsdp", "replica"),
            P("fsdp", "replica"),
            P("fsdp", "replica"),
            P("replica", "fsdp", None),
            P("fsdp"),
        ),
        out_specs=(
            P("fsdp", "replica"),
            P("fsdp", "replica"),
            P("fsdp", "replica"),
            P("fsdp", None),
            P("fsdp"),
        ),
        check_vma=False,
    )
```

```python
import functools
import math

import jax
import jax.numpy as jnp
from jax import lax
from jax.experimental import pallas as pl
from jax.experimental.pallas import tpu as pltpu
from jax.sharding import PartitionSpec as P

LANES = 128
TILE_ROWS = 16
MIB = 1024 * 1024
VMEM_BYTES = 24 * MIB
SHIFT_PEERS = 16
F32 = jnp.float32
BF16 = jnp.bfloat16


def iota(shape, axis):
    return lax.broadcasted_iota(jnp.int32, shape, axis)


class Sizes:
    def __init__(self, rows, width, peers, copies):
        self.rows, self.width, self.peers, self.copies = rows, width, peers, copies
        self.cap = max(2, 2 * rows // peers)
        self.split = max(1, TILE_ROWS // self.cap)
        self.lines = self.cap * self.split
        self.slots = peers * self.lines
        self.stacked = self.split * rows
        self.body = width // self.split
        self.cb = math.gcd(self.body, 512)
        self.blocks = self.body // self.cb
        self.span = self.split * self.cb
        self.sub = math.gcd(self.cb, 256)
        self.payload = 3 * self.body + LANES


def prepare_kernel(z, rep_ref, origin_ref, new_row_hbm, full_hbm, pick_ref, info_ref, mask_ref, *refs):
    parts, (full_buf, line_buf, sems, line_sem) = refs[: z.copies - 1], refs[z.copies - 1 :]
    step = z.width // z.blocks
    line_copy = pltpu.make_async_copy(new_row_hbm, line_buf, line_sem)
    line_copy.start()
    copies = []
    for k in range(1, z.copies):
        other = lax.rem(rep_ref[0] + k, z.copies)
        for j in range(z.blocks):
            there = pl.ds(pl.multiple_of(other * z.width + j * step, LANES), step)
            copies.append(
                pltpu.make_async_copy(
                    full_hbm.at[:, there], full_buf.at[k - 1, :, pl.ds(j * step, step)], sems.at[k - 1, j]
                )
            )
            copies[-1].start()
    line_copy.wait()
    line = line_buf[...]
    at_row, at_lane = iota((z.rows, z.rows), 0), iota((z.rows, z.rows), 1)
    column = jnp.sum(jnp.where(at_row == at_lane, line.astype(F32), 0.0), axis=1, keepdims=True).astype(jnp.int32)
    target, target_column = line // z.rows, column // z.rows
    earlier = (target_column == target) & (at_row < at_lane)
    rank = jnp.sum(jnp.where(earlier, 1.0, 0.0), axis=0, keepdims=True).astype(jnp.int32)
    shift = lax.rem(target - origin_ref[0] + z.peers, z.peers)
    shift_column = lax.rem(target_column - origin_ref[0] + z.peers, z.peers)
    for h in range(z.split):
        slot = shift * z.lines + h * z.cap + rank
        pick_ref[h] = jnp.where(iota((z.slots, z.rows), 0) == slot, 1.0, 0.0).astype(BF16)
    lane = iota((z.rows, LANES), 1)
    info_ref[...] = jnp.where(lane == 0, (column - target_column * z.rows + 1).astype(F32), 0.0)
    used = jnp.where(lane == shift_column, 1.0, 0.0)
    mask_ref[...] = jnp.max(used, axis=0, keepdims=True).astype(jnp.int32)
    for k in range(1, z.copies):
        for j in range(z.blocks):
            copies[(k - 1) * z.blocks + j].wait()
            at = slice(j * step, (j + 1) * step)
            parts[k - 1][:, at] = full_buf[k - 1, :, at].astype(BF16)


def agree_kernel(left, right, _, out):
    out[...] = jnp.maximum(left[...], right[...])


def choose_kernel(digits, left, right, *outs):
    total = jnp.maximum(left[...], right[...])
    lane = iota(total.shape, 1)
    for digit, out in zip(digits, outs):
        value = jnp.zeros(total.shape, jnp.int32)
        for i, s in enumerate(digit):
            value = value + jnp.where(lane == s, total << i, 0)
        out[0] = jnp.sum(value.astype(F32)).astype(jnp.int32)


def load_kernel(z, rep_ref, info_ref, master_hbm, one_hbm, two_hbm, full_hbm, master, one, two, own, meta_ref, sems):
    base = rep_ref[0] * z.width
    step = z.width // z.blocks
    copies = []
    for j in range(z.blocks):
        at = pl.ds(j * step, step)
        mine = pl.ds(pl.multiple_of(base + j * step, LANES), step)
        copies.append(
            [
                pltpu.make_async_copy(master_hbm.at[:, at], master.at[:, at], sems.at[0, j]),
                pltpu.make_async_copy(one_hbm.at[:, at], one.at[:, at], sems.at[1, j]),
                pltpu.make_async_copy(two_hbm.at[:, at], two.at[:, at], sems.at[2, j]),
                pltpu.make_async_copy(full_hbm.at[:, mine], own.at[:, at], sems.at[3, j]),
            ]
        )
    for i in range(4):
        for j in range(z.blocks):
            copies[j][i].start()
    part = jnp.zeros((z.rows, LANES), F32)
    for j in range(z.blocks):
        copies[j][0].wait()
        for at in range(j * step, (j + 1) * step, LANES):
            weights = 1.0 + ((iota((1, LANES), 1) + (base + at)) % 7).astype(F32) / 7.0
            part = part + master[:, at : at + LANES] * weights
    total = jnp.sum(part, axis=1, keepdims=True) * (1.0 / math.sqrt(z.width * z.copies))
    high = total.astype(BF16).astype(F32)
    middle = (total - high).astype(BF16).astype(F32)
    low = total - high - middle
    lane = iota((z.rows, LANES), 1)
    meta = jnp.where(lane == 1, high, jnp.where(lane == 2, middle, jnp.where(lane == 3, low, info_ref[...])))
    meta_ref[...] = meta.astype(BF16)
    for j in range(z.blocks):
        for i in range(1, 4):
            copies[j][i].wait()


def update_kernel(z, pick_ref, meta_ref, master, one, two, own, *refs):
    received, refs = refs[: z.copies - 1], refs[z.copies :]
    outs, rows_buf = refs[: z.peers], refs[z.peers]
    pick = jnp.concatenate([pick_ref[h] for h in range(z.split)], axis=1)
    for j in range(z.blocks):
        for h in range(z.split):
            for c in range(0, z.cb, z.sub):
                at = j * z.span + h * z.cb + c
                cols = slice(at, at + z.sub)
                summed = own[:, cols]
                for other in received:
                    summed = summed + other[:, cols].astype(F32)
                moved = master[:, cols]
                new_one = 0.9 * one[:, cols] + 0.1 * summed
                new_two = 0.95 * two[:, cols] + 0.05 * summed * summed
                update = new_one * (1.0 / (1.0 - 0.9**10)) / (jnp.sqrt(new_two * (1.0 / (1.0 - 0.95**10))) + 1e-08)
                new_master = moved - 0.05 * (update + 0.1 * moved)
                for i, value in enumerate((new_master, new_one, new_two)):
                    to = i * z.body + j * z.cb + c
                    rows_buf[h * z.rows : (h + 1) * z.rows, to : to + z.sub] = value.astype(BF16)
        for i in range(3):
            at = i * z.body + j * z.cb
            packed = jnp.dot(pick, rows_buf[:, at : at + z.cb], preferred_element_type=F32).astype(BF16)
            for s, out in enumerate(outs):
                out[:, at : at + z.cb] = packed[s * z.lines : (s + 1) * z.lines]
    meta = jnp.concatenate([meta_ref[...]] * z.split, axis=0)
    packed = jnp.dot(pick, meta, preferred_element_type=F32).astype(BF16)
    for s, out in enumerate(outs):
        out[:, 3 * z.body :] = packed[s * z.lines : (s + 1) * z.lines]


def gathered(refs, cols):
    return jnp.concatenate([ref[:, cols] for ref in refs], axis=0)


def placing(z, meta):
    offset = meta[:, :1].astype(F32).astype(jnp.int32)
    piece = lax.rem(iota((z.slots, 1), 0), z.lines) // z.cap
    wanted = jnp.where(offset > 0, offset - 1 + piece * z.rows, -1)
    return jnp.where(iota((z.slots, z.stacked), 1) == wanted, 1.0, 0.0).T.astype(BF16)


def placed(place, values):
    return jnp.dot(place, values, preferred_element_type=F32)


def half_kernel(z, *refs):
    got, (half, place_out) = refs[: z.peers], refs[z.peers :]
    meta = gathered(got, slice(3 * z.body, 3 * z.body + LANES))
    place = placing(z, meta)
    place_out[...] = place
    for j in range(z.blocks):
        rows_out = placed(place, gathered(got, slice(j * z.cb, (j + 1) * z.cb))).astype(BF16)
        for h in range(z.split):
            at = j * z.span + h * z.cb
            half[:, at : at + z.cb] = rows_out[h * z.rows : (h + 1) * z.rows]
    half[:, z.width :] = placed(place, meta)[: z.rows].astype(BF16)


def place_moment(z, i, place, got, out, buf, sems):
    copies = []
    for j in range(z.blocks):
        at = i * z.body + j * z.cb
        rows_out = placed(place, gathered(got, slice(at, at + z.cb)))
        for h in range(z.split):
            col = j * z.span + h * z.cb
            buf[:, col : col + z.cb] = rows_out[h * z.rows : (h + 1) * z.rows]
        cols = pl.ds(j * z.span, z.span)
        copies.append(pltpu.make_async_copy(buf.at[:, cols], out.at[:, cols], sems.at[j]))
        copies[-1].start()
    return copies


def rows_kernel(z, rep_ref, half, place, *refs):
    got, (new_master, params, one_out, two_out, master_buf, one_buf, two_buf, sems) = refs[: z.peers], refs[z.peers :]
    there = pl.ds(pl.multiple_of(rep_ref[0] * z.width, LANES), z.width)
    copies = [pltpu.make_async_copy(half.at[:, : z.width], params.at[:, there], sems.at[0, 0])]
    copies[0].start()
    for j in range(z.blocks):
        at = slice(j * z.span, (j + 1) * z.span)
        master_buf[:, at] = half[:, at].astype(F32)
        cols = pl.ds(j * z.span, z.span)
        copies.append(pltpu.make_async_copy(master_buf.at[:, cols], new_master.at[:, cols], sems.at[1, j]))
        copies[-1].start()
    copies += place_moment(z, 1, place[...], got, one_out, one_buf, sems.at[2])
    copies += place_moment(z, 2, place[...], got, two_out, two_buf, sems.at[3])
    for copy in copies:
        copy.wait()


def finish_kernel(z, rep_ref, half, *refs):
    others, (_, params, checksum, sems) = refs[: z.copies - 1], refs[z.copies - 1 :]
    copies = []
    for k, other in enumerate(others):
        replica = lax.rem(rep_ref[0] + z.copies - (k + 1), z.copies)
        there = pl.ds(pl.multiple_of(replica * z.width, LANES), z.width)
        copies.append(pltpu.make_async_copy(other.at[:, : z.width], params.at[:, there], sems.at[k]))
        copies[-1].start()
    sums = half[:, z.width :].astype(F32)
    for other in others:
        sums = sums + other[:, z.width :].astype(F32)
    lane = iota((z.rows, LANES), 1)
    column = jnp.sum(jnp.where((lane >= 1) & (lane <= 3), sums, 0.0), axis=1, keepdims=True)
    diagonal = iota((z.rows, z.rows), 0) == iota((z.rows, z.rows), 1)
    checksum[...] = jnp.sum(jnp.where(diagonal, column, 0.0), axis=0, keepdims=True)
    for copy in copies:
        copy.wait()


def shifted(value, axis, k, count):
    return lax.ppermute(value, axis, [(i, (i + k) % count) for i in range(count)])


def always_sent(peers):
    return [peers // 2, peers // 4 - 1, peers - 1]


def shift_groups(peers):
    plane, half = peers // 4, peers // 2
    rest = [s for s in range(1, peers) if s not in always_sent(peers)]
    straight = [s for s in rest if s % plane == 0]
    first = [s for s in rest if s % plane == 1] + [half + 2]
    return [first, [s for s in rest if s not in first + straight], straight]


def agree(used, stride, peers, after, compiler_params):
    vmem = pl.BlockSpec(memory_space=pltpu.VMEM)
    other = lax.ppermute(used, "fsdp", [(i, i ^ stride) for i in range(peers)])
    return pl.pallas_call(
        agree_kernel,
        out_shape=jax.ShapeDtypeStruct((1, LANES), jnp.int32),
        in_specs=[vmem, vmem, pl.BlockSpec(memory_space=pl.ANY)],
        out_specs=vmem,
        compiler_params=compiler_params,
        name="agree",
    )(used, other, after)


def choose_branches(used, peers, compiler_params):
    vmem = pl.BlockSpec(memory_space=pltpu.VMEM)
    smem = pl.BlockSpec(memory_space=pltpu.SMEM)
    groups = shift_groups(peers)
    other = lax.ppermute(used, "fsdp", [(i, i ^ (peers // 2)) for i in range(peers)])
    return pl.pallas_call(
        functools.partial(choose_kernel, groups),
        out_shape=[pltpu.SMEM((1,), jnp.int32)] * len(groups),
        in_specs=[vmem, vmem],
        out_specs=[smem] * len(groups),
        compiler_params=compiler_params,
        name="choose",
    )(used, other)


def send_used(peers, group, used, chunks):
    return tuple(
        shifted(chunk, "fsdp", s, peers) if used >> i & 1 else chunk for i, (s, chunk) in enumerate(zip(group, chunks))
    )


def move(z, chunks, used, by_shift, compiler_params):
    if not by_shift:
        got = lax.all_to_all(jnp.concatenate(chunks, axis=0), "fsdp", split_axis=0, concat_axis=0, tiled=True)
        return [got[s * z.lines : (s + 1) * z.lines] for s in range(z.peers)]
    got = list(chunks)
    always = always_sent(z.peers)
    for s in always:
        got[s] = shifted(chunks[s], "fsdp", s, z.peers)
    for stride in (2, 4):
        used = agree(used, stride, z.peers, chunks[0], compiler_params)
    chosen = choose_branches(used, z.peers, compiler_params)
    barred = lax.optimization_barrier((*chosen, *[got[s] for s in always]))
    chosen = barred[: len(chosen)]
    for s, value in zip(always, barred[len(chosen) :]):
        got[s] = value
    for group, number in zip(shift_groups(z.peers), chosen):
        branches = [
            lambda *values, group=group, used=used: send_used(z.peers, group, used, values)
            for used in range(1 << len(group))
        ]
        for s, value in zip(group, lax.switch(number[0], branches, *[chunks[s] for s in group])):
            got[s] = value
    return got


def shards(master, moment_one, moment_two, gradients, new_row):
    rows, width = master.shape
    peers, copies = lax.axis_size("fsdp"), lax.axis_size("replica")
    z = Sizes(rows, width, peers, copies)
    compiler_params = pltpu.CompilerParams(vmem_limit_bytes=VMEM_BYTES)
    smem = pl.BlockSpec(memory_space=pltpu.SMEM)
    vmem = pl.BlockSpec(memory_space=pltpu.VMEM)
    hbm = pl.BlockSpec(memory_space=pl.ANY)
    dma = pltpu.SemaphoreType.DMA

    replica = lax.axis_index("replica").astype(jnp.int32)
    rep = replica.reshape(1)
    by_shift = peers == SHIFT_PEERS
    origin = (lax.axis_index("fsdp").astype(jnp.int32) if by_shift else jnp.int32(0)).reshape(1)
    state_in = [pltpu.with_memory_space_constraint(x, pltpu.HBM) for x in (master, moment_one, moment_two)]
    full = pltpu.with_memory_space_constraint(gradients[0], pltpu.HBM)

    part = jax.ShapeDtypeStruct((rows, width), BF16)
    pick, info, used, *parts = pl.pallas_call(
        functools.partial(prepare_kernel, z),
        out_shape=[
            jax.ShapeDtypeStruct((z.split, z.slots, rows), BF16),
            jax.ShapeDtypeStruct((rows, LANES), F32),
            jax.ShapeDtypeStruct((1, LANES), jnp.int32),
        ]
        + [part] * (copies - 1),
        in_specs=[smem, smem, hbm, hbm],
        out_specs=[vmem] * (copies + 2),
        scratch_shapes=[
            pltpu.VMEM((copies - 1, rows, width), F32),
            pltpu.VMEM((1, rows), jnp.int32),
            dma((copies - 1, z.blocks)),
            dma,
        ],
        compiler_params=compiler_params,
        cost_estimate=pl.CostEstimate(flops=1 << 30, bytes_accessed=1, transcendentals=0),
        name="prepare",
    )(rep, origin, pltpu.with_memory_space_constraint(new_row.reshape(1, rows), pltpu.HBM), full)
    received = [shifted(value, "replica", k + 1, copies) for k, value in enumerate(parts)]

    loaded = jax.ShapeDtypeStruct((rows, width), F32)
    *state, meta = pl.pallas_call(
        functools.partial(load_kernel, z),
        out_shape=[loaded, loaded, loaded, loaded, jax.ShapeDtypeStruct((rows, LANES), BF16)],
        in_specs=[smem, vmem, hbm, hbm, hbm, hbm],
        out_specs=[vmem] * 5,
        scratch_shapes=[dma((4, z.blocks))],
        compiler_params=compiler_params,
        cost_estimate=pl.CostEstimate(flops=1 << 30, bytes_accessed=1, transcendentals=0),
        name="load",
    )(rep, info, *state_in, full)

    if by_shift:
        used = agree(used, 1, peers, meta, compiler_params)
    chunks = pl.pallas_call(
        functools.partial(update_kernel, z),
        out_shape=[jax.ShapeDtypeStruct((z.lines, z.payload), BF16)] * peers,
        in_specs=[vmem] * (5 + copies) + [hbm],
        out_specs=[vmem] * peers,
        scratch_shapes=[pltpu.VMEM((z.stacked, 3 * z.body), BF16)],
        compiler_params=compiler_params,
        cost_estimate=pl.CostEstimate(
            flops=6 * z.slots * z.stacked * z.body, bytes_accessed=24 * rows * width, transcendentals=rows * width
        ),
        name="update",
    )(pick, meta, *state, *received, used)

    got = move(z, chunks, used, by_shift, compiler_params)

    wide = jax.ShapeDtypeStruct((rows, width), F32)
    full_params = jax.ShapeDtypeStruct((rows, width * copies), BF16)
    half, place = pl.pallas_call(
        functools.partial(half_kernel, z),
        out_shape=(
            jax.ShapeDtypeStruct((rows, width + LANES), BF16),
            jax.ShapeDtypeStruct((z.stacked, z.slots), BF16),
        ),
        in_specs=[vmem] * peers,
        out_specs=(vmem, vmem),
        compiler_params=compiler_params,
        name="place_half",
    )(*got)
    others = [shifted(half, "replica", k, copies) for k in range(1, copies)]

    new_master, params, new_one, new_two = pl.pallas_call(
        functools.partial(rows_kernel, z),
        out_shape=(wide, full_params, wide, wide),
        in_specs=[smem] + [vmem] * (peers + 2),
        out_specs=(hbm, hbm, hbm, hbm),
        scratch_shapes=[pltpu.VMEM((rows, width), F32)] * 3 + [dma((4, z.blocks))],
        compiler_params=compiler_params,
        cost_estimate=pl.CostEstimate(
            flops=4 * z.slots * z.stacked * z.body, bytes_accessed=18 * rows * width, transcendentals=0
        ),
        name="place_rows",
    )(rep, half, place, *got)

    params, checksum = pl.pallas_call(
        functools.partial(finish_kernel, z),
        out_shape=(full_params, jax.ShapeDtypeStruct((1, rows), F32)),
        in_specs=[smem] + [vmem] * copies + [hbm],
        out_specs=(hbm, vmem),
        scratch_shapes=[dma((max(1, copies - 1),))],
        input_output_aliases={copies + 1: 0},
        compiler_params=compiler_params,
        cost_estimate=pl.CostEstimate(flops=0, bytes_accessed=4 * rows * width, transcendentals=0),
        name="finish",
    )(rep, half, *others, params)
    return (new_master, new_one, new_two, params, checksum.reshape(rows))


def solution(mesh):
    return jax.shard_map(
        shards,
        mesh=mesh,
        in_specs=(
            P("fsdp", "replica"),
            P("fsdp", "replica"),
            P("fsdp", "replica"),
            P("replica", "fsdp", None),
            P("fsdp"),
        ),
        out_specs=(
            P("fsdp", "replica"),
            P("fsdp", "replica"),
            P("fsdp", "replica"),
            P("fsdp", None),
            P("fsdp"),
        ),
        check_vma=False,
    )
```

```python
import functools
import math

import jax
import jax.numpy as jnp
from jax import lax
from jax.experimental import pallas as pl
from jax.experimental.pallas import tpu as pltpu
from jax.sharding import PartitionSpec as P

LANES = 128
TILE_ROWS = 16
MIB = 1024 * 1024
VMEM_BYTES = 24 * MIB
SHIFT_PEERS = 16
GROUP = 5
F32 = jnp.float32
BF16 = jnp.bfloat16


def iota(shape, axis):
    return lax.broadcasted_iota(jnp.int32, shape, axis)


class Sizes:
    def __init__(self, rows, width, peers, copies):
        self.rows, self.width, self.peers, self.copies = rows, width, peers, copies
        self.cap = max(2, 2 * rows // peers)
        self.split = max(1, TILE_ROWS // self.cap)
        self.lines = self.cap * self.split
        self.slots = peers * self.lines
        self.stacked = self.split * rows
        self.body = width // self.split
        self.cb = math.gcd(self.body, 512)
        self.blocks = self.body // self.cb
        self.span = self.split * self.cb
        self.sub = math.gcd(self.cb, 256)
        self.payload = 3 * self.body + LANES


def prepare_kernel(z, rep_ref, origin_ref, new_row_hbm, full_hbm, pick_ref, info_ref, mask_ref, *refs):
    parts, (full_buf, line_buf, sems, line_sem) = refs[: z.copies - 1], refs[z.copies - 1 :]
    step = z.width // z.blocks
    line_copy = pltpu.make_async_copy(new_row_hbm, line_buf, line_sem)
    line_copy.start()
    copies = []
    for k in range(1, z.copies):
        other = lax.rem(rep_ref[0] + k, z.copies)
        for j in range(z.blocks):
            there = pl.ds(pl.multiple_of(other * z.width + j * step, LANES), step)
            copies.append(
                pltpu.make_async_copy(
                    full_hbm.at[:, there], full_buf.at[k - 1, :, pl.ds(j * step, step)], sems.at[k - 1, j]
                )
            )
            copies[-1].start()
    line_copy.wait()
    line = line_buf[...]
    at_row, at_lane = iota((z.rows, z.rows), 0), iota((z.rows, z.rows), 1)
    column = jnp.sum(jnp.where(at_row == at_lane, line.astype(F32), 0.0), axis=1, keepdims=True).astype(jnp.int32)
    target, target_column = line // z.rows, column // z.rows
    earlier = (target_column == target) & (at_row < at_lane)
    rank = jnp.sum(jnp.where(earlier, 1.0, 0.0), axis=0, keepdims=True).astype(jnp.int32)
    shift = lax.rem(target - origin_ref[0] + z.peers, z.peers)
    shift_column = lax.rem(target_column - origin_ref[0] + z.peers, z.peers)
    for h in range(z.split):
        slot = shift * z.lines + h * z.cap + rank
        pick_ref[h] = jnp.where(iota((z.slots, z.rows), 0) == slot, 1.0, 0.0).astype(BF16)
    lane = iota((z.rows, LANES), 1)
    info_ref[...] = jnp.where(lane == 0, (column - target_column * z.rows + 1).astype(F32), 0.0)
    used = jnp.where(lane == shift_column, 1.0, 0.0)
    mask_ref[...] = jnp.max(used, axis=0, keepdims=True).astype(jnp.int32)
    for k in range(1, z.copies):
        for j in range(z.blocks):
            copies[(k - 1) * z.blocks + j].wait()
            at = slice(j * step, (j + 1) * step)
            parts[k - 1][:, at] = full_buf[k - 1, :, at].astype(BF16)


def agree_kernel(left, right, _, out):
    out[...] = jnp.maximum(left[...], right[...])


def choose_kernel(digits, left, right, *outs):
    total = jnp.maximum(left[...], right[...])
    lane = iota(total.shape, 1)
    for digit, out in zip(digits, outs):
        value = jnp.zeros(total.shape, jnp.int32)
        for i, s in enumerate(digit):
            value = value + jnp.where(lane == s, total << i, 0)
        out[0] = jnp.sum(value.astype(F32)).astype(jnp.int32)


def load_kernel(z, rep_ref, info_ref, master_hbm, one_hbm, two_hbm, full_hbm, master, one, two, own, meta_ref, sems):
    base = rep_ref[0] * z.width
    pieces = sems.shape[1]
    step = z.width // pieces
    copies = []
    for j in range(pieces):
        at = pl.ds(j * step, step)
        mine = pl.ds(pl.multiple_of(base + j * step, LANES), step)
        copies.append(
            [
                pltpu.make_async_copy(master_hbm.at[:, at], master.at[:, at], sems.at[0, j]),
                pltpu.make_async_copy(one_hbm.at[:, at], one.at[:, at], sems.at[1, j]),
                pltpu.make_async_copy(two_hbm.at[:, at], two.at[:, at], sems.at[2, j]),
                pltpu.make_async_copy(full_hbm.at[:, mine], own.at[:, at], sems.at[3, j]),
            ]
        )
    for i in range(4):
        for j in range(pieces):
            copies[j][i].start()
    part = jnp.zeros((z.rows, LANES), F32)
    for j in range(pieces):
        copies[j][0].wait()
        for at in range(j * step, (j + 1) * step, LANES):
            weights = 1.0 + ((iota((1, LANES), 1) + (base + at)) % 7).astype(F32) / 7.0
            part = part + master[:, at : at + LANES] * weights
    total = jnp.sum(part, axis=1, keepdims=True) * (1.0 / math.sqrt(z.width * z.copies))
    high = total.astype(BF16).astype(F32)
    middle = (total - high).astype(BF16).astype(F32)
    low = total - high - middle
    lane = iota((z.rows, LANES), 1)
    meta = jnp.where(lane == 1, high, jnp.where(lane == 2, middle, jnp.where(lane == 3, low, info_ref[...])))
    meta_ref[...] = meta.astype(BF16)
    for j in range(pieces):
        for i in range(1, 4):
            copies[j][i].wait()


def update_kernel(z, pick_ref, meta_ref, master, one, two, own, *refs):
    received, refs = refs[: z.copies - 1], refs[z.copies :]
    outs, rows_buf = refs[: z.peers], refs[z.peers]
    pick = jnp.concatenate([pick_ref[h] for h in range(z.split)], axis=1)
    for j in range(z.blocks):
        for h in range(z.split):
            for c in range(0, z.cb, z.sub):
                at = j * z.span + h * z.cb + c
                cols = slice(at, at + z.sub)
                summed = own[:, cols]
                for other in received:
                    summed = summed + other[:, cols].astype(F32)
                moved = master[:, cols]
                new_one = 0.9 * one[:, cols] + 0.1 * summed
                new_two = 0.95 * two[:, cols] + 0.05 * summed * summed
                update = new_one * (1.0 / (1.0 - 0.9**10)) / (jnp.sqrt(new_two * (1.0 / (1.0 - 0.95**10))) + 1e-08)
                new_master = moved - 0.05 * (update + 0.1 * moved)
                for i, value in enumerate((new_master, new_one, new_two)):
                    to = i * z.body + j * z.cb + c
                    rows_buf[h * z.rows : (h + 1) * z.rows, to : to + z.sub] = value.astype(BF16)
        for i in range(3):
            at = i * z.body + j * z.cb
            packed = jnp.dot(pick, rows_buf[:, at : at + z.cb], preferred_element_type=F32).astype(BF16)
            for s, out in enumerate(outs):
                out[:, at : at + z.cb] = packed[s * z.lines : (s + 1) * z.lines]
    meta = jnp.concatenate([meta_ref[...]] * z.split, axis=0)
    packed = jnp.dot(pick, meta, preferred_element_type=F32).astype(BF16)
    for s, out in enumerate(outs):
        out[:, 3 * z.body :] = packed[s * z.lines : (s + 1) * z.lines]


def gathered(refs, cols):
    return jnp.concatenate([ref[:, cols] for ref in refs], axis=0)


def placing(z, meta):
    offset = meta[:, :1].astype(F32).astype(jnp.int32)
    piece = lax.rem(iota((z.slots, 1), 0), z.lines) // z.cap
    wanted = jnp.where(offset > 0, offset - 1 + piece * z.rows, -1)
    return jnp.where(iota((z.slots, z.stacked), 1) == wanted, 1.0, 0.0).T.astype(BF16)


def placed(place, values):
    return jnp.dot(place, values, preferred_element_type=F32)


def half_kernel(z, *refs):
    got, (half, place_out) = refs[: z.peers], refs[z.peers :]
    meta = gathered(got, slice(3 * z.body, 3 * z.body + LANES))
    place = placing(z, meta)
    place_out[...] = place
    for j in range(z.blocks):
        rows_out = placed(place, gathered(got, slice(j * z.cb, (j + 1) * z.cb))).astype(BF16)
        for h in range(z.split):
            at = j * z.span + h * z.cb
            half[:, at : at + z.cb] = rows_out[h * z.rows : (h + 1) * z.rows]
    half[:, z.width :] = placed(place, meta)[: z.rows].astype(BF16)


def place_moment(z, i, place, got, out, buf, sems):
    copies = []
    for j in range(z.blocks):
        at = i * z.body + j * z.cb
        rows_out = placed(place, gathered(got, slice(at, at + z.cb)))
        for h in range(z.split):
            col = j * z.span + h * z.cb
            buf[:, col : col + z.cb] = rows_out[h * z.rows : (h + 1) * z.rows]
        cols = pl.ds(j * z.span, z.span)
        copies.append(pltpu.make_async_copy(buf.at[:, cols], out.at[:, cols], sems.at[j]))
        copies[-1].start()
    return copies


def rows_kernel(z, rep_ref, half, place, *refs):
    got, (new_master, params, one_out, two_out, master_buf, one_buf, two_buf, sems) = refs[: z.peers], refs[z.peers :]
    there = pl.ds(pl.multiple_of(rep_ref[0] * z.width, LANES), z.width)
    copies = [pltpu.make_async_copy(half.at[:, : z.width], params.at[:, there], sems.at[0, 0])]
    copies[0].start()
    for j in range(z.blocks):
        at = slice(j * z.span, (j + 1) * z.span)
        master_buf[:, at] = half[:, at].astype(F32)
        cols = pl.ds(j * z.span, z.span)
        copies.append(pltpu.make_async_copy(master_buf.at[:, cols], new_master.at[:, cols], sems.at[1, j]))
        copies[-1].start()
    copies += place_moment(z, 1, place[...], got, one_out, one_buf, sems.at[2])
    copies += place_moment(z, 2, place[...], got, two_out, two_buf, sems.at[3])
    for copy in copies:
        copy.wait()


def finish_kernel(z, rep_ref, half, *refs):
    others, (_, params, checksum, sems) = refs[: z.copies - 1], refs[z.copies - 1 :]
    copies = []
    for k, other in enumerate(others):
        replica = lax.rem(rep_ref[0] + z.copies - (k + 1), z.copies)
        there = pl.ds(pl.multiple_of(replica * z.width, LANES), z.width)
        copies.append(pltpu.make_async_copy(other.at[:, : z.width], params.at[:, there], sems.at[k]))
        copies[-1].start()
    sums = half[:, z.width :].astype(F32)
    for other in others:
        sums = sums + other[:, z.width :].astype(F32)
    lane = iota((z.rows, LANES), 1)
    column = jnp.sum(jnp.where((lane >= 1) & (lane <= 3), sums, 0.0), axis=1, keepdims=True)
    diagonal = iota((z.rows, z.rows), 0) == iota((z.rows, z.rows), 1)
    checksum[...] = jnp.sum(jnp.where(diagonal, column, 0.0), axis=0, keepdims=True)
    for copy in copies:
        copy.wait()


def shifted(value, axis, k, count):
    return lax.ppermute(value, axis, [(i, (i + k) % count) for i in range(count)])


def always_sent(peers):
    return [peers // 2, peers // 4 - 1, peers - 1]


def shift_groups(peers):
    always, half = always_sent(peers), peers // 2
    rest = [s for s in range(1, peers) if s not in always]
    rest = sorted(rest, key=lambda s: ((s + half) % peers in always, s % half, s))
    return [rest[i : i + GROUP] for i in range(0, len(rest), GROUP)]


def agree(used, stride, peers, after, compiler_params):
    vmem = pl.BlockSpec(memory_space=pltpu.VMEM)
    other = lax.ppermute(used, "fsdp", [(i, i ^ stride) for i in range(peers)])
    return pl.pallas_call(
        agree_kernel,
        out_shape=jax.ShapeDtypeStruct((1, LANES), jnp.int32),
        in_specs=[vmem, vmem, pl.BlockSpec(memory_space=pl.ANY)],
        out_specs=vmem,
        compiler_params=compiler_params,
        name="agree",
    )(used, other, after)


def choose_branches(used, peers, compiler_params):
    vmem = pl.BlockSpec(memory_space=pltpu.VMEM)
    smem = pl.BlockSpec(memory_space=pltpu.SMEM)
    groups = shift_groups(peers)
    other = lax.ppermute(used, "fsdp", [(i, i ^ (peers // 2)) for i in range(peers)])
    return pl.pallas_call(
        functools.partial(choose_kernel, groups),
        out_shape=[pltpu.SMEM((1,), jnp.int32)] * len(groups),
        in_specs=[vmem, vmem],
        out_specs=[smem] * len(groups),
        compiler_params=compiler_params,
        name="choose",
    )(used, other)


def send_used(peers, group, used, chunks):
    return tuple(
        shifted(chunk, "fsdp", s, peers) if used >> i & 1 else chunk for i, (s, chunk) in enumerate(zip(group, chunks))
    )


def move(z, chunks, used, by_shift, compiler_params):
    if not by_shift:
        got = lax.all_to_all(jnp.concatenate(chunks, axis=0), "fsdp", split_axis=0, concat_axis=0, tiled=True)
        return [got[s * z.lines : (s + 1) * z.lines] for s in range(z.peers)]
    got = list(chunks)
    always = always_sent(z.peers)
    for s in always:
        got[s] = shifted(chunks[s], "fsdp", s, z.peers)
    for stride in (2, 4):
        used = agree(used, stride, z.peers, chunks[0], compiler_params)
    chosen = choose_branches(used, z.peers, compiler_params)
    barred = lax.optimization_barrier((*chosen, *[got[s] for s in always]))
    chosen = barred[: len(chosen)]
    for s, value in zip(always, barred[len(chosen) :]):
        got[s] = value
    for group, number in zip(shift_groups(z.peers), chosen):
        branches = [
            lambda *values, group=group, used=used: send_used(z.peers, group, used, values)
            for used in range(1 << len(group))
        ]
        for s, value in zip(group, lax.switch(number[0], branches, *[chunks[s] for s in group])):
            got[s] = value
    return got


def shards(master, moment_one, moment_two, gradients, new_row):
    rows, width = master.shape
    peers, copies = lax.axis_size("fsdp"), lax.axis_size("replica")
    z = Sizes(rows, width, peers, copies)
    compiler_params = pltpu.CompilerParams(vmem_limit_bytes=VMEM_BYTES)
    smem = pl.BlockSpec(memory_space=pltpu.SMEM)
    vmem = pl.BlockSpec(memory_space=pltpu.VMEM)
    hbm = pl.BlockSpec(memory_space=pl.ANY)
    dma = pltpu.SemaphoreType.DMA

    replica = lax.axis_index("replica").astype(jnp.int32)
    rep = replica.reshape(1)
    by_shift = peers == SHIFT_PEERS
    origin = (lax.axis_index("fsdp").astype(jnp.int32) if by_shift else jnp.int32(0)).reshape(1)
    state_in = [pltpu.with_memory_space_constraint(x, pltpu.HBM) for x in (master, moment_one, moment_two)]
    full = pltpu.with_memory_space_constraint(gradients[0], pltpu.HBM)

    part = jax.ShapeDtypeStruct((rows, width), BF16)
    pick, info, used, *parts = pl.pallas_call(
        functools.partial(prepare_kernel, z),
        out_shape=[
            jax.ShapeDtypeStruct((z.split, z.slots, rows), BF16),
            jax.ShapeDtypeStruct((rows, LANES), F32),
            jax.ShapeDtypeStruct((1, LANES), jnp.int32),
        ]
        + [part] * (copies - 1),
        in_specs=[smem, smem, hbm, hbm],
        out_specs=[vmem] * (copies + 2),
        scratch_shapes=[
            pltpu.VMEM((copies - 1, rows, width), F32),
            pltpu.VMEM((1, rows), jnp.int32),
            dma((copies - 1, z.blocks)),
            dma,
        ],
        compiler_params=compiler_params,
        cost_estimate=pl.CostEstimate(flops=1 << 30, bytes_accessed=1, transcendentals=0),
        name="prepare",
    )(rep, origin, pltpu.with_memory_space_constraint(new_row.reshape(1, rows), pltpu.HBM), full)
    received = [shifted(value, "replica", k + 1, copies) for k, value in enumerate(parts)]

    loaded = jax.ShapeDtypeStruct((rows, width), F32)
    *state, meta = pl.pallas_call(
        functools.partial(load_kernel, z),
        out_shape=[loaded, loaded, loaded, loaded, jax.ShapeDtypeStruct((rows, LANES), BF16)],
        in_specs=[smem, vmem, hbm, hbm, hbm, hbm],
        out_specs=[vmem] * 5,
        scratch_shapes=[dma((4, math.gcd(2, z.blocks)))],
        compiler_params=compiler_params,
        cost_estimate=pl.CostEstimate(flops=1 << 30, bytes_accessed=1, transcendentals=0),
        name="load",
    )(rep, info, *state_in, full)

    if by_shift:
        used = agree(used, 1, peers, meta, compiler_params)
    chunks = pl.pallas_call(
        functools.partial(update_kernel, z),
        out_shape=[jax.ShapeDtypeStruct((z.lines, z.payload), BF16)] * peers,
        in_specs=[vmem] * (5 + copies) + [hbm],
        out_specs=[vmem] * peers,
        scratch_shapes=[pltpu.VMEM((z.stacked, 3 * z.body), BF16)],
        compiler_params=compiler_params,
        cost_estimate=pl.CostEstimate(
            flops=6 * z.slots * z.stacked * z.body, bytes_accessed=24 * rows * width, transcendentals=rows * width
        ),
        name="update",
    )(pick, meta, *state, *received, used)

    got = move(z, chunks, used, by_shift, compiler_params)

    wide = jax.ShapeDtypeStruct((rows, width), F32)
    full_params = jax.ShapeDtypeStruct((rows, width * copies), BF16)
    half, place = pl.pallas_call(
        functools.partial(half_kernel, z),
        out_shape=(
            jax.ShapeDtypeStruct((rows, width + LANES), BF16),
            jax.ShapeDtypeStruct((z.stacked, z.slots), BF16),
        ),
        in_specs=[vmem] * peers,
        out_specs=(vmem, vmem),
        compiler_params=compiler_params,
        name="place_half",
    )(*got)
    others = [shifted(half, "replica", k, copies) for k in range(1, copies)]

    new_master, params, new_one, new_two = pl.pallas_call(
        functools.partial(rows_kernel, z),
        out_shape=(wide, full_params, wide, wide),
        in_specs=[smem] + [vmem] * (peers + 2),
        out_specs=(hbm, hbm, hbm, hbm),
        scratch_shapes=[pltpu.VMEM((rows, width), F32)] * 3 + [dma((4, z.blocks))],
        compiler_params=compiler_params,
        cost_estimate=pl.CostEstimate(
            flops=4 * z.slots * z.stacked * z.body, bytes_accessed=18 * rows * width, transcendentals=0
        ),
        name="place_rows",
    )(rep, half, place, *got)

    params, checksum = pl.pallas_call(
        functools.partial(finish_kernel, z),
        out_shape=(full_params, jax.ShapeDtypeStruct((1, rows), F32)),
        in_specs=[smem] + [vmem] * copies + [hbm],
        out_specs=(hbm, vmem),
        scratch_shapes=[dma((max(1, copies - 1),))],
        input_output_aliases={copies + 1: 0},
        compiler_params=compiler_params,
        cost_estimate=pl.CostEstimate(flops=0, bytes_accessed=4 * rows * width, transcendentals=0),
        name="finish",
    )(rep, half, *others, params)
    return (new_master, new_one, new_two, params, checksum.reshape(rows))


def solution(mesh):
    return jax.shard_map(
        shards,
        mesh=mesh,
        in_specs=(
            P("fsdp", "replica"),
            P("fsdp", "replica"),
            P("fsdp", "replica"),
            P("replica", "fsdp", None),
            P("fsdp"),
        ),
        out_specs=(
            P("fsdp", "replica"),
            P("fsdp", "replica"),
            P("fsdp", "replica"),
            P("fsdp", None),
            P("fsdp"),
        ),
        check_vma=False,
    )
```
